32 devices in a mesh: fsdp: 4 (over z), ctx: 2 (over y), tp: 4 (over x, core).
Axes of the slice: x: 2, y: 2, z: 4, core: 2. Of those that a mesh axis runs over, the one named last changes fastest.
Arguments:
- tokens: bfloat16 [4, 2048, 1024], P('fsdp', ('ctx', 'tp')), may hold values from -6 to 6
- cotangent: bfloat16 [4, 2048, 1024], P('fsdp', ('ctx', 'tp')), may hold values from -6 to 6
- attn_weight: float32 [4, 1024, 1024], P(None, 'fsdp', 'tp'), as said below
- attn_momentum: float32 [4, 1024, 1024], P(None, 'fsdp', 'tp'), may hold values from -56 to 56
- attn_average: float32 [4, 1024, 1024], P(None, 'fsdp', 'tp'), may hold values from -0.1875 to 0.1875
- ffn_weight: float32 [2, 1024, 4096], P(None, 'fsdp', 'tp'), as said below
- ffn_momentum: float32 [2, 1024, 4096], P(None, 'fsdp', 'tp'), may hold values from -128 to 128
- ffn_average: float32 [2, 1024, 4096], P(None, 'fsdp', 'tp'), may hold values from -0.1875 to 0.1875
- vector_weight: float32 [12288], replicated, as said below
- vector_momentum: float32 [12288], replicated, may hold values from -256 to 256
- vector_average: float32 [12288], replicated, as said below
Outputs:
- layer_out: bfloat16 [4, 2048, 1024], P('fsdp', ('ctx', 'tp'))
- input_grad: float32 [4, 2048, 1024], P('fsdp', ('ctx', 'tp'))
- attn_grad: float32 [4, 1024, 1024], P(None, 'fsdp', 'tp')
- attn_new: float32 [4, 1024, 1024], P(None, 'fsdp', 'tp')
- attn_momentum_new: float32 [4, 1024, 1024], P(None, 'fsdp', 'tp')
- attn_average_new: float32 [4, 1024, 1024], P(None, 'fsdp', 'tp')
- attn_copy: bfloat16 [4, 1024, 1024], P(None, 'fsdp', 'tp')
- ffn_grad: float32 [2, 1024, 4096], P(None, 'fsdp', 'tp')
- ffn_new: float32 [2, 1024, 4096], P(None, 'fsdp', 'tp')
- ffn_momentum_new: float32 [2, 1024, 4096], P(None, 'fsdp', 'tp')
- ffn_average_new: float32 [2, 1024, 4096], P(None, 'fsdp', 'tp')
- ffn_copy: bfloat16 [2, 1024, 4096], P(None, 'fsdp', 'tp')
- vector_grad: float32 [12288], replicated
- vector_new: float32 [12288], replicated
- vector_momentum_new: float32 [12288], replicated
- vector_average_new: float32 [12288], replicated
The draws below stay inside these ranges and needn't reach their ends.
Inputs may be any that keep to these rules, and one draw needn't show every extreme that they name: `attn_weight`: four 1024 x 1024 matrices; the fourth is the output projection stored transposed. `ffn_weight`: two 1024 x 4096 matrices; the second is the down projection stored transposed. `vector_weight`: gains are positive. `vector_average`: laid out as vector_weight; gains are positive.
All inputs are finite; a program needn't handle non-finite values.
Results may differ from the reference program's by a relative error of at most 0.02.
Values may be sent and summed in bfloat16 or wider, within the bound.
No kernel may reach another device: no remote copies, remote signals or barrier semaphores. Data moves between devices by JAX's collectives and lax.ppermute only.
A program may use at most 256 MiB of HBM per device.

```python
import math
import jax
import jax.numpy as jnp
from jax import lax

D = 1024
HEADS = 16
FF = 4096
HEAD_DIM = 64
LEN = 2048
SEQS = 4
TOKENS = 8192
VEC = 12288


def vector_law(key):
    gain_key, rest_key = jax.random.split(key)
    gain_rows = jax.random.uniform(gain_key, (2, D), jnp.float32, 0.6, 1.6)
    others = 0.3 * jax.random.normal(rest_key, (6 * D + FF,), jnp.float32)
    return jnp.concatenate([gain_rows[0], others[0:D], gain_rows[1], others[D:]])


def draw_attn_weight(key, part):
    key = jax.random.fold_in(key, 11)
    normal_base = jax.random.normal(key, (4, D, D), jnp.float32) * D ** (-0.5)
    factor = jnp.array([1.0, 1.0, 1.0, 16.0], jnp.float32)
    return normal_base * factor[:, None, None]


def draw_ffn_weight(key, part):
    key = jax.random.fold_in(key, 12)
    normal_base = jax.random.normal(key, (2, D, FF), jnp.float32)
    factor = jnp.array([D ** (-0.5), FF ** (-0.5)], jnp.float32)
    return normal_base * factor[:, None, None]


def draw_vector_weight(key, part):
    key = jax.random.fold_in(key, 13)
    return vector_law(key)


def draw_vector_average(key, part):
    key = jax.random.fold_in(key, 14)
    return vector_law(key)


def levels(rng, extent, cuts, smallest, high):
    def one(axis_at, parts):
        steps = jax.random.uniform(jax.random.fold_in(jax.random.fold_in(rng, 6), axis_at), (parts,), jnp.float32, smallest / len(cuts), high / len(cuts))
        return jnp.repeat(jnp.exp(steps), extent[axis_at] // parts).reshape((-1,) + (1,) * (len(extent) - axis_at - 1))

    loudness = one(*cuts[0])
    for cut in cuts[1:]:
        loudness = loudness * one(*cut)
    return loudness


def gaussian(stream_key, dims, width, reach, cuts=(), dtype=jnp.bfloat16):
    gain = levels(stream_key, dims, cuts, -0.22, 0.18) if cuts else 1.0
    entries = jax.random.normal(stream_key, dims, jnp.float32) * width * gain
    return jnp.minimum(jnp.maximum(entries, -reach), reach).astype(dtype)


def setup_inputs(seed: int = 0) -> dict:
    key_list = jax.random.split(jax.random.key(seed), 12)
    return {
        "tokens": gaussian(key_list[0], (SEQS, LEN, D), 1.0, 6.0, ((0, 4), (1, 8))),
        "cotangent": gaussian(key_list[1], (SEQS, LEN, D), 1.0, 6.0, ((0, 4), (1, 8))),
        "attn_weight": draw_attn_weight(jax.random.fold_in(key_list[11], 71), 0),
        "attn_momentum": gaussian(key_list[3], (4, D, D), (0.1 * TOKENS ** 0.5), 56.0, ((1, 4), (2, 4)), jnp.float32),
        "attn_average": gaussian(key_list[4], (4, D, D), D ** -0.5, 0.1875, ((1, 4), (2, 4)), jnp.float32),
        "ffn_weight": draw_ffn_weight(jax.random.fold_in(key_list[11], 71), 0),
        "ffn_momentum": gaussian(key_list[6], (2, D, FF), (0.25 * TOKENS ** 0.5), 128.0, ((1, 4), (2, 4)), jnp.float32),
        "ffn_average": gaussian(key_list[7], (2, D, FF), D ** -0.5, 0.1875, ((1, 4), (2, 4)), jnp.float32),
        "vector_weight": draw_vector_weight(jax.random.fold_in(key_list[11], 71), 0),
        "vector_momentum": gaussian(key_list[9], (VEC,), (0.5 * TOKENS ** 0.5), 256.0, (), jnp.float32),
        "vector_average": draw_vector_average(jax.random.fold_in(key_list[11], 71), 0),
    }


@jax.custom_vjp
def low(v):
    return lax.optimization_barrier(v.astype(jnp.bfloat16)).astype(jnp.float32)

@jax.custom_vjp
def low_back(v):
    return v

def low_keep(v):
    return (low(v), None)

def low_pass(kept, grad):
    return (grad,)

def back_keep(v):
    return (v, None)

def back_low(kept, grad):
    return (low(grad),)
low.defvjp(low_keep, low_pass)
low_back.defvjp(back_keep, back_low)
NORM_EPSILON = 1e-05
MOMENTUM = 0.5
AVERAGE = 0.5
MATRIX_RATE = 0.1
VECTOR_RATE = 0.3
HIGHEST = lax.Precision.HIGHEST

def layer_norm(values, gain_vec, shift_vec):
    row_mean = lax.optimization_barrier(jnp.mean(values, axis=-1, keepdims=True))
    centered = values - row_mean
    variance = lax.optimization_barrier(jnp.mean(centered * centered, axis=-1, keepdims=True))
    return centered * lax.rsqrt(variance + NORM_EPSILON) * gain_vec + shift_vec

def matmul(left, right):
    return jnp.dot(left, right, precision=HIGHEST, preferred_element_type=jnp.float32)

def one_sequence(sequence, attn_low, ffn_low, vector_weight):
    gain_one = vector_weight[0:D]
    shift_one = vector_weight[D:2 * D]
    gain_two = vector_weight[2 * D:3 * D]
    shift_two = vector_weight[3 * D:4 * D]
    bias_out = vector_weight[4 * D:5 * D]
    bias_down = vector_weight[5 * D:6 * D]
    bias_query = vector_weight[6 * D:7 * D]
    bias_value = vector_weight[7 * D:8 * D]
    bias_hidden = vector_weight[8 * D:8 * D + FF]
    query_pre = matmul(sequence, attn_low[0]) + bias_query
    key_pre = matmul(sequence, attn_low[1])
    value_pre = matmul(sequence, attn_low[2]) + bias_value
    queries = low(low_back(query_pre)).reshape(LEN, HEADS, HEAD_DIM)
    keys_all = low(low_back(key_pre)).reshape(LEN, HEADS, HEAD_DIM)
    values_all = low(low_back(value_pre)).reshape(LEN, HEADS, HEAD_DIM)
    scores = low_back(jnp.einsum('qhe,khe->hqk', queries, keys_all, precision=HIGHEST) * HEAD_DIM ** (-0.5))
    attention = jax.nn.softmax(scores, axis=-1)
    mixed_heads = jnp.einsum('hqk,khe->qhe', low(attention), values_all, precision=HIGHEST)
    mixed_heads = low(low_back(mixed_heads.reshape(LEN, D)))
    attn_out = low_back(matmul(mixed_heads, attn_low[3].T) + bias_out)
    first_norm = layer_norm(sequence + attn_out, gain_one, shift_one)
    hidden_pre = low_back(matmul(low(first_norm), ffn_low[0]) + bias_hidden)
    hidden = low(jax.nn.gelu(hidden_pre, approximate=False))
    down_out = low_back(matmul(hidden, ffn_low[1].T) + bias_down)
    return layer_norm(first_norm + down_out, gain_two, shift_two)

def forward(inputs, attn_weight, ffn_weight, vector_weight):
    attn_low = low(attn_weight)
    ffn_low = low(ffn_weight)
    checked = jax.checkpoint(one_sequence)

    def per_sequence(sequence):
        return checked(sequence, attn_low, ffn_low, vector_weight)
    return lax.map(per_sequence, inputs)

def nesterov(weights, momentum, average, gradient, step_rate):
    momentum_new = MOMENTUM * momentum + gradient
    weight_new = weights - step_rate * (gradient + MOMENTUM * momentum_new)
    average_new = AVERAGE * average + (1.0 - AVERAGE) * weight_new
    return (weight_new, momentum_new, average_new)

def reference(tokens, cotangent, attn_weight, attn_momentum, attn_average, ffn_weight, ffn_momentum, ffn_average, vector_weight, vector_momentum, vector_average):
    inputs = tokens.astype(jnp.float32)
    layer_out, pullback = jax.vjp(forward, inputs, attn_weight, ffn_weight, vector_weight)
    input_grad, attn_grad, ffn_grad, vector_grad = pullback(cotangent.astype(jnp.float32))
    matrix_rate = MATRIX_RATE / math.sqrt(TOKENS)
    vector_rate = VECTOR_RATE / math.sqrt(TOKENS)
    attn_new, attn_momentum_new, attn_average_new = nesterov(attn_weight, attn_momentum, attn_average, attn_grad, matrix_rate)
    ffn_new, ffn_momentum_new, ffn_average_new = nesterov(ffn_weight, ffn_momentum, ffn_average, ffn_grad, matrix_rate)
    vector_new, vector_momentum_new, vector_average_new = nesterov(vector_weight, vector_momentum, vector_average, vector_grad, vector_rate)
    return (layer_out.astype(jnp.bfloat16), input_grad, attn_grad, attn_new, attn_momentum_new, attn_average_new, attn_new.astype(jnp.bfloat16), ffn_grad, ffn_new, ffn_momentum_new, ffn_average_new, ffn_new.astype(jnp.bfloat16), vector_grad, vector_new, vector_momentum_new, vector_average_new)
```

```python
import math

import jax
import jax.numpy as jnp
from jax import lax
from jax.experimental import pallas as pl
from jax.experimental.pallas import tpu as pltpu
from jax.sharding import PartitionSpec as P

D = 1024
FF = 4096
HEAD_DIM = 64
LEN = 2048

NORM_EPSILON = 1e-05
MOMENTUM = 0.5
AVERAGE = 0.5
MATRIX_RATE = 0.1
VECTOR_RATE = 0.3

SCALE = HEAD_DIM ** (-0.5)
LOG2E = math.log2(math.e)
F32 = jnp.float32
BF16 = jnp.bfloat16
NT = (((1,), (1,)), ((), ()))
TN = (((0,), (0,)), ((), ()))
NN = (((1,), (0,)), ((), ()))


def dot(left, right, dims=NN):
    return lax.dot_general(left, right, dims, preferred_element_type=F32)


def head_masks(width):
    lane = lax.broadcasted_iota(jnp.int32, (1, width), 1) // HEAD_DIM
    return [(lane == h).astype(BF16) for h in range(width // HEAD_DIM)]


def attend_kernel(q_ref, k_ref, v_ref, o_ref, lse_ref, vt_ref):
    heads = q_ref.shape[1] // HEAD_DIM

    @pl.when(pl.program_id(0) == 0)
    def _():
        vt_ref[...] = v_ref[...].T

    queries = q_ref[...]
    masks = head_masks(q_ref.shape[1])
    outs = []
    for h in range(heads):
        scores = dot(k_ref[...], queries * masks[h], NT)
        top = jnp.max(scores, axis=0, keepdims=True)
        weights = jnp.exp2((scores - top) * (SCALE * LOG2E))
        total = jnp.sum(weights, axis=0, keepdims=True)
        out = dot(vt_ref[h * HEAD_DIM : (h + 1) * HEAD_DIM, :], weights.astype(BF16))
        outs.append(out / total)
        lse_ref[h : h + 1, :] = top * (SCALE * LOG2E) + jnp.log2(total)
    o_ref[...] = jnp.concatenate(outs, axis=0).T.astype(BF16)


def attend(queries, keys, values):
    rows, width = queries.shape
    block = min(256, rows)
    heads = width // HEAD_DIM
    return pl.pallas_call(
        attend_kernel,
        grid=(rows // block,),
        in_specs=[
            pl.BlockSpec((block, width), lambda i: (i, 0)),
            pl.BlockSpec(keys.shape, lambda i: (0, 0)),
            pl.BlockSpec(values.shape, lambda i: (0, 0)),
        ],
        out_specs=[
            pl.BlockSpec((block, width), lambda i: (i, 0)),
            pl.BlockSpec((heads, block), lambda i: (0, i)),
        ],
        out_shape=[
            jax.ShapeDtypeStruct((rows, width), BF16),
            jax.ShapeDtypeStruct((heads, rows), F32),
        ],
        scratch_shapes=[pltpu.VMEM((width, keys.shape[0]), BF16)],
        compiler_params=pltpu.CompilerParams(vmem_limit_bytes=40 * 1024 * 1024),
        cost_estimate=pl.CostEstimate(
            flops=16 * rows * keys.shape[0] * width,
            bytes_accessed=4 * (rows + keys.shape[0]) * width,
            transcendentals=rows * keys.shape[0] * heads,
        ),
        name="attend",
    )(queries, keys, values)


def attend_back_kernel(
    q_ref, k_ref, v_ref, o_ref, g_ref, lse_ref, dq_ref, dk_ref, dv_ref, kt_ref, dk_acc, dv_acc
):
    heads = q_ref.shape[1] // HEAD_DIM
    step = pl.program_id(0)

    @pl.when(step == 0)
    def _():
        kt_ref[...] = k_ref[...].T
        dk_acc[...] = jnp.zeros_like(dk_acc)
        dv_acc[...] = jnp.zeros_like(dv_acc)

    queries = q_ref[...]
    grads = g_ref[...]
    masks = head_masks(q_ref.shape[1])
    product = (o_ref[...].astype(F32) * grads.astype(F32)).T
    outs, probs, gscores, qms, gms = [], [], [], [], []
    for h in range(heads):
        qm = queries * masks[h]
        gm = grads * masks[h]
        delta = jnp.sum(product[h * HEAD_DIM : (h + 1) * HEAD_DIM, :], axis=0, keepdims=True)
        scores = dot(k_ref[...], qm, NT)
        prob = jnp.exp2(scores * (SCALE * LOG2E) - lse_ref[h : h + 1, :])
        grad_prob = dot(v_ref[...], gm, NT)
        gscore = (prob * (grad_prob - delta)).astype(BF16)
        outs.append(dot(kt_ref[h * HEAD_DIM : (h + 1) * HEAD_DIM, :], gscore))
        probs.append(prob.astype(BF16))
        gscores.append(gscore)
        qms.append(qm)
        gms.append(gm)
    dv_acc[...] += dot(jnp.concatenate(probs, axis=1), jnp.concatenate(gms, axis=0))
    dk_acc[...] += dot(jnp.concatenate(gscores, axis=1), jnp.concatenate(qms, axis=0))
    dq_ref[...] = (jnp.concatenate(outs, axis=0).T * SCALE).astype(BF16)

    @pl.when(step == pl.num_programs(0) - 1)
    def _():
        dk_ref[...] = (dk_acc[...] * SCALE).astype(BF16)
        dv_ref[...] = dv_acc[...].astype(BF16)


def attend_back(queries, keys, values, mixed, grad_mixed, lse):
    rows, width = queries.shape
    block = min(256, rows)
    heads = width // HEAD_DIM
    row_spec = pl.BlockSpec((block, width), lambda i: (i, 0))
    full_spec = pl.BlockSpec(keys.shape, lambda i: (0, 0))
    return pl.pallas_call(
        attend_back_kernel,
        grid=(rows // block,),
        in_specs=[
            row_spec,
            full_spec,
            full_spec,
            row_spec,
            row_spec,
            pl.BlockSpec((heads, block), lambda i: (0, i)),
        ],
        out_specs=[row_spec, full_spec, full_spec],
        out_shape=[
            jax.ShapeDtypeStruct((rows, width), BF16),
            jax.ShapeDtypeStruct(keys.shape, BF16),
            jax.ShapeDtypeStruct(keys.shape, BF16),
        ],
        scratch_shapes=[
            pltpu.VMEM((width, keys.shape[0]), BF16),
            pltpu.VMEM(keys.shape, F32),
            pltpu.VMEM(keys.shape, F32),
        ],
        compiler_params=pltpu.CompilerParams(vmem_limit_bytes=48 * 1024 * 1024),
        cost_estimate=pl.CostEstimate(
            flops=40 * rows * keys.shape[0] * width,
            bytes_accessed=8 * (rows + keys.shape[0]) * width,
            transcendentals=rows * keys.shape[0] * heads,
        ),
        name="attend_back",
    )(queries, keys, values, mixed, grad_mixed, lse)


def norm_forward(values, gain_vec, shift_vec):
    row_mean = jnp.mean(values, axis=-1, keepdims=True)
    centered = values - row_mean
    inverse = lax.rsqrt(jnp.mean(centered * centered, axis=-1, keepdims=True) + NORM_EPSILON)
    normed = centered * inverse
    return (normed * gain_vec + shift_vec, normed, inverse)


def norm_backward(grad_out, normed, inverse, gain_vec):
    grad_normed = grad_out * gain_vec
    grad_in = inverse * (
        grad_normed
        - jnp.mean(grad_normed, axis=-1, keepdims=True)
        - normed * jnp.mean(grad_normed * normed, axis=-1, keepdims=True)
    )
    return (grad_in, jnp.sum(grad_out * normed, axis=0), jnp.sum(grad_out, axis=0))


def gelu_pair(values):
    size = jnp.abs(values)
    t = 1.0 / (1.0 + (0.3275911 * math.sqrt(0.5)) * size)
    bell = jnp.exp2(values * values * (-0.5 * LOG2E))
    poly = t * (
        0.5 * 0.254829592
        + t
        * (
            0.5 * -0.284496736
            + t * (0.5 * 1.421413741 + t * (0.5 * -1.453152027 + t * (0.5 * 1.061405429)))
        )
    )
    tail = poly * bell
    cdf = jnp.where(values < 0, tail, 1.0 - tail)
    return values * cdf, cdf + values * bell * (1.0 / math.sqrt(2.0 * math.pi))


def nesterov(weights, momentum, average, gradient, step_rate):
    momentum_new = MOMENTUM * momentum + gradient
    weight_new = weights - step_rate * (gradient + MOMENTUM * momentum_new)
    return (weight_new, momentum_new, AVERAGE * average + (1.0 - AVERAGE) * weight_new)


def swap_tp(values, bit):
    size = lax.axis_size("tp")
    return lax.ppermute(values, "tp", [(i, i ^ bit) for i in range(size)])


def core(values):
    return swap_tp(values, 1)


def across(values):
    return swap_tp(values, 2)


def swap_ctx(values):
    return lax.ppermute(values, "ctx", [(0, 1), (1, 0)])


def swap_both(values):
    size = lax.axis_size("tp")
    return lax.ppermute(values, ("ctx", "tp"), [(i, i ^ (size + 2)) for i in range(2 * size)])


def sum_all(values):
    for bit in (1, 2):
        values = values + swap_tp(values, bit)
    values = values + swap_ctx(values)
    size = lax.axis_size("fsdp")
    bit = 1
    while bit < size:
        values = values + lax.ppermute(values, "fsdp", [(i, i ^ bit) for i in range(size)])
        bit *= 2
    return values


def on_device(
    tokens,
    cotangent,
    attn_weight,
    attn_momentum,
    attn_average,
    ffn_weight,
    ffn_momentum,
    ffn_average,
    vector_weight,
    vector_momentum,
    vector_average,
):
    tp_rank = lax.axis_index("tp")
    sib_rank = tp_rank ^ 1
    head_width = attn_weight.shape[2]
    unit_width = ffn_weight.shape[2]
    token_count = LEN * lax.axis_size("fsdp")
    matrix_rate = MATRIX_RATE / math.sqrt(token_count)
    vector_rate = VECTOR_RATE / math.sqrt(token_count)

    def gather_weight(shard):
        return lax.all_gather(shard, "fsdp", axis=shard.ndim - 2, tiled=True)

    attn_low = attn_weight.astype(BF16)
    ffn_low = ffn_weight.astype(BF16)
    qkv_w = gather_weight(attn_low[:3])
    out_w = gather_weight(attn_low[3])
    up_w = gather_weight(ffn_low[0])
    down_w = gather_weight(ffn_low[1])

    own = tokens[0]
    rows = own.shape[0]
    near = jnp.concatenate([own, across(own)], axis=0)
    far = jnp.concatenate([swap_ctx(own), swap_both(own)], axis=0)
    token_all = jnp.concatenate([near, core(near), far, core(far)], axis=0)
    pair = 2 * rows
    half = 4 * rows

    gain_one = vector_weight[0:D]
    shift_one = vector_weight[D : 2 * D]
    gain_two = vector_weight[2 * D : 3 * D]
    shift_two = vector_weight[3 * D : 4 * D]
    bias_out = vector_weight[4 * D : 5 * D]
    bias_down = vector_weight[5 * D : 6 * D]

    def piece(start, width, rank):
        return lax.dynamic_slice_in_dim(vector_weight, start + rank * width, width)

    bias_query = piece(6 * D, head_width, tp_rank)
    bias_value = piece(7 * D, head_width, tp_rank)
    bias_hidden = jnp.concatenate(
        [piece(8 * D, unit_width, tp_rank), piece(8 * D, unit_width, sib_rank)]
    )

    queries = (dot(token_all[:half], qkv_w[0]) + bias_query).astype(BF16)
    keys = dot(token_all, qkv_w[1]).astype(BF16)
    values = (dot(token_all, qkv_w[2]) + bias_value).astype(BF16)
    mixed, lse = attend(queries, keys, values)

    out_pair = jnp.concatenate([out_w, core(out_w)], axis=1)
    mixed_pair = jnp.concatenate([mixed[:pair], core(mixed[pair:])], axis=1)
    attn_part = dot(mixed_pair, out_pair, NT)
    attn_out = attn_part[:rows] + across(attn_part[rows:].astype(BF16)).astype(F32) + bias_out
    first, normed_one, inverse_one = norm_forward(own.astype(F32) + attn_out, gain_one, shift_one)
    first_low = first.astype(BF16)
    first_pair = jnp.concatenate([first_low, across(first_low)], axis=0)

    up_pair = jnp.concatenate([up_w, core(up_w)], axis=1)
    down_pair = jnp.concatenate([down_w, core(down_w)], axis=1)
    hidden_act, gelu_slope = gelu_pair(dot(first_pair, up_pair) + bias_hidden)
    hidden = hidden_act.astype(BF16)
    gelu_slope = gelu_slope.astype(BF16)
    down_part = dot(hidden, down_pair, NT)
    down_out = down_part[:rows] + across(down_part[rows:].astype(BF16)).astype(F32) + bias_down
    second, normed_two, inverse_two = norm_forward(first + down_out, gain_two, shift_two)
    layer_out = second.astype(BF16)

    grad_second, grad_gain_two, grad_shift_two = norm_backward(
        cotangent[0].astype(F32), normed_two, inverse_two, gain_two
    )
    grad_down = grad_second.astype(BF16)
    grad_bias_down = jnp.sum(grad_down, axis=0, dtype=F32)
    grad_down_pair = jnp.concatenate([grad_down, across(grad_down)], axis=0)
    grad_up = (dot(grad_down_pair, down_pair) * gelu_slope.astype(F32)).astype(BF16)
    grad_bias_hidden = jnp.sum(grad_up, axis=0, dtype=F32)
    first_part = dot(grad_up, up_pair, NT)
    grad_first = (
        grad_second + first_part[:rows] + across(first_part[rows:].astype(BF16)).astype(F32)
    )
    grad_down_w = dot(grad_down_pair, hidden, TN)
    grad_up_w = dot(first_pair, grad_up, TN)

    def own_units(grads, width):
        return (grads[:, :width] + core(grads[:, width:].astype(BF16)).astype(F32)).astype(BF16)

    def owned(grads):
        part = lax.psum_scatter(grads, "fsdp", scatter_dimension=grads.ndim - 2, tiled=True)
        return part.astype(F32) + swap_ctx(part).astype(F32)

    down_grad = owned(own_units(grad_down_w, unit_width))
    up_grad = owned(own_units(grad_up_w, unit_width))

    grad_res, grad_gain_one, grad_shift_one = norm_backward(
        grad_first, normed_one, inverse_one, gain_one
    )
    grad_attn = grad_res.astype(BF16)
    grad_bias_out = jnp.sum(grad_attn, axis=0, dtype=F32)
    grad_attn_pair = jnp.concatenate([grad_attn, across(grad_attn)], axis=0)
    grad_mixed_pair = dot(grad_attn_pair, out_pair).astype(BF16)
    grad_mixed = jnp.concatenate(
        [grad_mixed_pair[:, :head_width], core(grad_mixed_pair[:, head_width:])], axis=0
    )
    out_grad = owned(own_units(dot(grad_attn_pair, mixed_pair, TN), head_width))

    hidden_vec = lax.dynamic_update_slice(
        jnp.zeros((FF,), F32), grad_bias_hidden[:unit_width], (tp_rank * unit_width,)
    )
    hidden_vec = lax.dynamic_update_slice(
        hidden_vec, grad_bias_hidden[unit_width:], (sib_rank * unit_width,)
    )
    early = sum_all(
        jnp.concatenate(
            [
                grad_gain_one,
                grad_shift_one,
                grad_gain_two,
                grad_shift_two,
                grad_bias_out,
                grad_bias_down,
                hidden_vec,
            ]
        )
    )

    grad_query, grad_key, grad_value = attend_back(queries, keys, values, mixed, grad_mixed, lse)
    grad_kv = jnp.concatenate([grad_key, grad_value], axis=1)
    kv_w = jnp.concatenate([qkv_w[1], qkv_w[2]], axis=1)
    input_near = dot(grad_kv[:half], kv_w, NT) + dot(grad_query, qkv_w[0], NT)
    input_far = dot(grad_kv[half:], kv_w, NT)
    near_sum = input_near[:pair] + core(input_near[pair:].astype(BF16)).astype(F32)
    far_sum = (input_far[:pair] + core(input_far[pair:].astype(BF16)).astype(F32)).astype(BF16)
    input_grad = (
        grad_res
        + near_sum[:rows]
        + across(near_sum[rows:].astype(BF16)).astype(F32)
        + swap_ctx(far_sum[:rows]).astype(F32)
        + swap_both(far_sum[rows:]).astype(F32)
    )
    grad_q_w = dot(token_all[:half], grad_query, TN).astype(BF16)
    grad_k_w = dot(token_all, grad_key, TN).astype(BF16)
    grad_v_w = dot(token_all, grad_value, TN).astype(BF16)
    qkv_grad = owned(jnp.stack([grad_q_w, grad_k_w, grad_v_w]))

    head_part = jnp.stack(
        [jnp.sum(grad_query, axis=0, dtype=F32), jnp.sum(grad_value, axis=0, dtype=F32)]
    )
    late = sum_all(
        lax.dynamic_update_slice(jnp.zeros((2, D), F32), head_part, (0, tp_rank * head_width))
    )

    vector_grad = jnp.concatenate([early[: 6 * D], late.reshape(-1), early[6 * D :]])
    vector_new, vector_momentum_new, vector_average_new = nesterov(
        vector_weight, vector_momentum, vector_average, vector_grad, vector_rate
    )
    attn_grad = jnp.concatenate([qkv_grad, out_grad[None]], axis=0)
    ffn_grad = jnp.stack([up_grad, down_grad])
    attn_new, attn_momentum_new, attn_average_new = nesterov(
        attn_weight, attn_momentum, attn_average, attn_grad, matrix_rate
    )
    ffn_new, ffn_momentum_new, ffn_average_new = nesterov(
        ffn_weight, ffn_momentum, ffn_average, ffn_grad, matrix_rate
    )
    return (
        layer_out[None],
        input_grad[None],
        attn_grad,
        attn_new,
        attn_momentum_new,
        attn_average_new,
        attn_new.astype(BF16),
        ffn_grad,
        ffn_new,
        ffn_momentum_new,
        ffn_average_new,
        ffn_new.astype(BF16),
        vector_grad,
        vector_new,
        vector_momentum_new,
        vector_average_new,
    )


def solution(mesh):
    rows = P("fsdp", ("ctx", "tp"), None)
    weight = P(None, "fsdp", "tp")
    return jax.shard_map(
        on_device,
        mesh=mesh,
        in_specs=(rows, rows) + (weight,) * 6 + (P(),) * 3,
        out_specs=(rows, rows) + (weight,) * 10 + (P(),) * 4,
        check_vma=False,
    )
```

```python
import math

import jax
import jax.numpy as jnp
from jax import lax
from jax.experimental import pallas as pl
from jax.experimental.pallas import tpu as pltpu
from jax.sharding import PartitionSpec as P

D = 1024
FF = 4096
HEAD_DIM = 64
LEN = 2048

NORM_EPSILON = 1e-05
MOMENTUM = 0.5
AVERAGE = 0.5
MATRIX_RATE = 0.1
VECTOR_RATE = 0.3

SCALE = HEAD_DIM ** (-0.5)
LOG2E = math.log2(math.e)
F32 = jnp.float32
BF16 = jnp.bfloat16
NT = (((1,), (1,)), ((), ()))
TN = (((0,), (0,)), ((), ()))
NN = (((1,), (0,)), ((), ()))


def dot(left, right, dims=NN):
    return lax.dot_general(left, right, dims, preferred_element_type=F32)


def head_masks(width):
    lane = lax.broadcasted_iota(jnp.int32, (1, width), 1) // HEAD_DIM
    return [(lane == h).astype(BF16) for h in range(width // HEAD_DIM)]


def attend_kernel(q_ref, k_ref, v_ref, o_ref, lse_ref, vt_ref):
    heads = q_ref.shape[1] // HEAD_DIM

    @pl.when(pl.program_id(0) == 0)
    def _():
        vt_ref[...] = v_ref[...].T

    queries = q_ref[...]
    masks = head_masks(q_ref.shape[1])
    outs = []
    for h in range(heads):
        scores = dot(k_ref[...], queries * masks[h], NT)
        top = jnp.max(scores, axis=0, keepdims=True)
        weights = jnp.exp2((scores - top) * (SCALE * LOG2E))
        total = jnp.sum(weights, axis=0, keepdims=True)
        out = dot(vt_ref[h * HEAD_DIM : (h + 1) * HEAD_DIM, :], weights.astype(BF16))
        outs.append(out / total)
        lse_ref[h : h + 1, :] = top * (SCALE * LOG2E) + jnp.log2(total)
    o_ref[...] = jnp.concatenate(outs, axis=0).T.astype(BF16)


def attend(queries, keys, values):
    rows, width = queries.shape
    block = min(256, rows)
    heads = width // HEAD_DIM
    return pl.pallas_call(
        attend_kernel,
        grid=(rows // block,),
        in_specs=[
            pl.BlockSpec((block, width), lambda i: (i, 0)),
            pl.BlockSpec(keys.shape, lambda i: (0, 0)),
            pl.BlockSpec(values.shape, lambda i: (0, 0)),
        ],
        out_specs=[
            pl.BlockSpec((block, width), lambda i: (i, 0)),
            pl.BlockSpec((heads, block), lambda i: (0, i)),
        ],
        out_shape=[
            jax.ShapeDtypeStruct((rows, width), BF16),
            jax.ShapeDtypeStruct((heads, rows), F32),
        ],
        scratch_shapes=[pltpu.VMEM((width, keys.shape[0]), BF16)],
        compiler_params=pltpu.CompilerParams(vmem_limit_bytes=40 * 1024 * 1024),
        cost_estimate=pl.CostEstimate(
            flops=16 * rows * keys.shape[0] * width,
            bytes_accessed=4 * (rows + keys.shape[0]) * width,
            transcendentals=rows * keys.shape[0] * heads,
        ),
        name="attend",
    )(queries, keys, values)


def attend_back_kernel(
    q_ref, k_ref, v_ref, o_ref, g_ref, lse_ref, dq_ref, dk_ref, dv_ref, kt_ref, dk_acc, dv_acc
):
    heads = q_ref.shape[1] // HEAD_DIM
    step = pl.program_id(0)

    @pl.when(step == 0)
    def _():
        kt_ref[...] = k_ref[...].T
        dk_acc[...] = jnp.zeros_like(dk_acc)
        dv_acc[...] = jnp.zeros_like(dv_acc)

    queries = q_ref[...]
    grads = g_ref[...]
    masks = head_masks(q_ref.shape[1])
    product = (o_ref[...].astype(F32) * grads.astype(F32)).T
    outs, probs, gscores, qms, gms = [], [], [], [], []
    for h in range(heads):
        qm = queries * masks[h]
        gm = grads * masks[h]
        delta = jnp.sum(product[h * HEAD_DIM : (h + 1) * HEAD_DIM, :], axis=0, keepdims=True)
        scores = dot(k_ref[...], qm, NT)
        prob = jnp.exp2(scores * (SCALE * LOG2E) - lse_ref[h : h + 1, :])
        grad_prob = dot(v_ref[...], gm, NT)
        gscore = (prob * (grad_prob - delta)).astype(BF16)
        outs.append(dot(kt_ref[h * HEAD_DIM : (h + 1) * HEAD_DIM, :], gscore))
        probs.append(prob.astype(BF16))
        gscores.append(gscore)
        qms.append(qm)
        gms.append(gm)
    dv_acc[...] += dot(jnp.concatenate(probs, axis=1), jnp.concatenate(gms, axis=0))
    dk_acc[...] += dot(jnp.concatenate(gscores, axis=1), jnp.concatenate(qms, axis=0))
    dq_ref[...] = (jnp.concatenate(outs, axis=0).T * SCALE).astype(BF16)

    @pl.when(step == pl.num_programs(0) - 1)
    def _():
        dk_ref[...] = (dk_acc[...] * SCALE).astype(BF16)
        dv_ref[...] = dv_acc[...].astype(BF16)


def attend_back(queries, keys, values, mixed, grad_mixed, lse):
    rows, width = queries.shape
    block = min(256, rows)
    heads = width // HEAD_DIM
    row_spec = pl.BlockSpec((block, width), lambda i: (i, 0))
    full_spec = pl.BlockSpec(keys.shape, lambda i: (0, 0))
    return pl.pallas_call(
        attend_back_kernel,
        grid=(rows // block,),
        in_specs=[
            row_spec,
            full_spec,
            full_spec,
            row_spec,
            row_spec,
            pl.BlockSpec((heads, block), lambda i: (0, i)),
        ],
        out_specs=[row_spec, full_spec, full_spec],
        out_shape=[
            jax.ShapeDtypeStruct((rows, width), BF16),
            jax.ShapeDtypeStruct(keys.shape, BF16),
            jax.ShapeDtypeStruct(keys.shape, BF16),
        ],
        scratch_shapes=[
            pltpu.VMEM((width, keys.shape[0]), BF16),
            pltpu.VMEM(keys.shape, F32),
            pltpu.VMEM(keys.shape, F32),
        ],
        compiler_params=pltpu.CompilerParams(vmem_limit_bytes=48 * 1024 * 1024),
        cost_estimate=pl.CostEstimate(
            flops=40 * rows * keys.shape[0] * width,
            bytes_accessed=8 * (rows + keys.shape[0]) * width,
            transcendentals=rows * keys.shape[0] * heads,
        ),
        name="attend_back",
    )(queries, keys, values, mixed, grad_mixed, lse)


def norm_forward(values, gain_vec, shift_vec):
    row_mean = jnp.mean(values, axis=-1, keepdims=True)
    centered = values - row_mean
    inverse = lax.rsqrt(jnp.mean(centered * centered, axis=-1, keepdims=True) + NORM_EPSILON)
    normed = centered * inverse
    return (normed * gain_vec + shift_vec, normed, inverse)


def norm_backward(grad_out, normed, inverse, gain_vec):
    grad_normed = grad_out * gain_vec
    grad_in = inverse * (
        grad_normed
        - jnp.mean(grad_normed, axis=-1, keepdims=True)
        - normed * jnp.mean(grad_normed * normed, axis=-1, keepdims=True)
    )
    return (grad_in, jnp.sum(grad_out * normed, axis=0), jnp.sum(grad_out, axis=0))


def gelu_pair(values):
    size = jnp.abs(values)
    t = 1.0 / (1.0 + (0.3275911 * math.sqrt(0.5)) * size)
    bell = jnp.exp2(values * values * (-0.5 * LOG2E))
    poly = t * (
        0.5 * 0.254829592
        + t
        * (
            0.5 * -0.284496736
            + t * (0.5 * 1.421413741 + t * (0.5 * -1.453152027 + t * (0.5 * 1.061405429)))
        )
    )
    tail = poly * bell
    cdf = jnp.where(values < 0, tail, 1.0 - tail)
    return values * cdf, cdf + values * bell * (1.0 / math.sqrt(2.0 * math.pi))


def nesterov(weights, momentum, average, gradient, step_rate):
    momentum_new = MOMENTUM * momentum + gradient
    weight_new = weights - step_rate * (gradient + MOMENTUM * momentum_new)
    return (weight_new, momentum_new, AVERAGE * average + (1.0 - AVERAGE) * weight_new)


def swap_tp(values, bit):
    size = lax.axis_size("tp")
    return lax.ppermute(values, "tp", [(i, i ^ bit) for i in range(size)])


def core(values):
    return swap_tp(values, 1)


def across(values):
    return swap_tp(values, 2)


def swap_ctx(values):
    return lax.ppermute(values, "ctx", [(0, 1), (1, 0)])


def swap_both(values):
    size = lax.axis_size("tp")
    return lax.ppermute(values, ("ctx", "tp"), [(i, i ^ (size + 2)) for i in range(2 * size)])


def sum_all(values):
    for bit in (1, 2):
        values = values + swap_tp(values, bit)
    values = values + swap_ctx(values)
    size = lax.axis_size("fsdp")
    bit = 1
    while bit < size:
        values = values + lax.ppermute(values, "fsdp", [(i, i ^ bit) for i in range(size)])
        bit *= 2
    return values


def on_device(
    tokens,
    cotangent,
    attn_weight,
    attn_momentum,
    attn_average,
    ffn_weight,
    ffn_momentum,
    ffn_average,
    vector_weight,
    vector_momentum,
    vector_average,
):
    tp_rank = lax.axis_index("tp")
    sib_rank = tp_rank ^ 1
    head_width = attn_weight.shape[2]
    unit_width = ffn_weight.shape[2]
    token_count = LEN * lax.axis_size("fsdp")
    matrix_rate = MATRIX_RATE / math.sqrt(token_count)
    vector_rate = VECTOR_RATE / math.sqrt(token_count)

    ctx_rank = lax.axis_index("ctx")

    def gather_weight(shard):
        axis = shard.ndim - 2
        half = shard.shape[axis] // 2
        part = lax.dynamic_slice_in_dim(shard, ctx_rank * half, half, axis)
        return lax.all_gather(part, ("fsdp", "ctx"), axis=axis, tiled=True)

    attn_low = attn_weight.astype(BF16)
    ffn_low = ffn_weight.astype(BF16)
    qkv_w = gather_weight(attn_low[:3])
    out_w = gather_weight(attn_low[3])
    up_w = gather_weight(ffn_low[0])
    down_w = gather_weight(ffn_low[1])

    own = tokens[0]
    rows = own.shape[0]
    near = jnp.concatenate([own, across(own)], axis=0)
    far = jnp.concatenate([swap_ctx(own), swap_both(own)], axis=0)
    token_all = jnp.concatenate([near, core(near), far, core(far)], axis=0)
    pair = 2 * rows
    half = 4 * rows

    gain_one = vector_weight[0:D]
    shift_one = vector_weight[D : 2 * D]
    gain_two = vector_weight[2 * D : 3 * D]
    shift_two = vector_weight[3 * D : 4 * D]
    bias_out = vector_weight[4 * D : 5 * D]
    bias_down = vector_weight[5 * D : 6 * D]

    def piece(start, width, rank):
        return lax.dynamic_slice_in_dim(vector_weight, start + rank * width, width)

    bias_query = piece(6 * D, head_width, tp_rank)
    bias_value = piece(7 * D, head_width, tp_rank)
    bias_hidden = jnp.concatenate(
        [piece(8 * D, unit_width, tp_rank), piece(8 * D, unit_width, sib_rank)]
    )

    queries = (dot(token_all[:half], qkv_w[0]) + bias_query).astype(BF16)
    keys = dot(token_all, qkv_w[1]).astype(BF16)
    values = (dot(token_all, qkv_w[2]) + bias_value).astype(BF16)
    mixed, lse = attend(queries, keys, values)

    out_pair = jnp.concatenate([out_w, core(out_w)], axis=1)
    mixed_pair = jnp.concatenate([mixed[:pair], core(mixed[pair:])], axis=1)
    attn_part = dot(mixed_pair, out_pair, NT)
    attn_out = attn_part[:rows] + across(attn_part[rows:].astype(BF16)).astype(F32) + bias_out
    first, normed_one, inverse_one = norm_forward(own.astype(F32) + attn_out, gain_one, shift_one)
    first_low = first.astype(BF16)
    first_pair = jnp.concatenate([first_low, across(first_low)], axis=0)

    up_pair = jnp.concatenate([up_w, core(up_w)], axis=1)
    down_pair = jnp.concatenate([down_w, core(down_w)], axis=1)
    hidden_act, gelu_slope = gelu_pair(dot(first_pair, up_pair) + bias_hidden)
    hidden = hidden_act.astype(BF16)
    gelu_slope = gelu_slope.astype(BF16)
    down_part = dot(hidden, down_pair, NT)
    down_out = down_part[:rows] + across(down_part[rows:].astype(BF16)).astype(F32) + bias_down
    second, normed_two, inverse_two = norm_forward(first + down_out, gain_two, shift_two)
    layer_out = second.astype(BF16)

    grad_second, grad_gain_two, grad_shift_two = norm_backward(
        cotangent[0].astype(F32), normed_two, inverse_two, gain_two
    )
    grad_down = grad_second.astype(BF16)
    grad_bias_down = jnp.sum(grad_down, axis=0, dtype=F32)
    grad_down_pair = jnp.concatenate([grad_down, across(grad_down)], axis=0)
    grad_up = (dot(grad_down_pair, down_pair) * gelu_slope.astype(F32)).astype(BF16)
    grad_bias_hidden = jnp.sum(grad_up, axis=0, dtype=F32)
    first_part = dot(grad_up, up_pair, NT)
    grad_first = (
        grad_second + first_part[:rows] + across(first_part[rows:].astype(BF16)).astype(F32)
    )
    grad_down_w = dot(grad_down_pair, hidden, TN)
    grad_up_w = dot(first_pair, grad_up, TN)

    def own_units(grads, width):
        return (grads[:, :width] + core(grads[:, width:].astype(BF16)).astype(F32)).astype(BF16)

    def owned(grads):
        axis = grads.ndim - 2
        part = lax.psum_scatter(grads, ("fsdp", "ctx"), scatter_dimension=axis, tiled=True)
        other = swap_ctx(part)
        low, high = jnp.where(ctx_rank == 0, part, other), jnp.where(ctx_rank == 0, other, part)
        return jnp.concatenate([low, high], axis=axis).astype(F32)

    down_grad = owned(own_units(grad_down_w, unit_width))
    up_grad = owned(own_units(grad_up_w, unit_width))

    grad_res, grad_gain_one, grad_shift_one = norm_backward(
        grad_first, normed_one, inverse_one, gain_one
    )
    grad_attn = grad_res.astype(BF16)
    grad_bias_out = jnp.sum(grad_attn, axis=0, dtype=F32)
    grad_attn_pair = jnp.concatenate([grad_attn, across(grad_attn)], axis=0)
    grad_mixed_pair = dot(grad_attn_pair, out_pair).astype(BF16)
    grad_mixed = jnp.concatenate(
        [grad_mixed_pair[:, :head_width], core(grad_mixed_pair[:, head_width:])], axis=0
    )
    out_grad = owned(own_units(dot(grad_attn_pair, mixed_pair, TN), head_width))

    hidden_vec = lax.dynamic_update_slice(
        jnp.zeros((FF,), F32), grad_bias_hidden[:unit_width], (tp_rank * unit_width,)
    )
    hidden_vec = lax.dynamic_update_slice(
        hidden_vec, grad_bias_hidden[unit_width:], (sib_rank * unit_width,)
    )
    early = sum_all(
        jnp.concatenate(
            [
                grad_gain_one,
                grad_shift_one,
                grad_gain_two,
                grad_shift_two,
                grad_bias_out,
                grad_bias_down,
                hidden_vec,
            ]
        )
    )

    grad_query, grad_key, grad_value = attend_back(queries, keys, values, mixed, grad_mixed, lse)
    grad_kv = jnp.concatenate([grad_key, grad_value], axis=1)
    kv_w = jnp.concatenate([qkv_w[1], qkv_w[2]], axis=1)
    input_near = dot(grad_kv[:half], kv_w, NT) + dot(grad_query, qkv_w[0], NT)
    input_far = dot(grad_kv[half:], kv_w, NT)
    near_sum = input_near[:pair] + core(input_near[pair:].astype(BF16)).astype(F32)
    far_sum = (input_far[:pair] + core(input_far[pair:].astype(BF16)).astype(F32)).astype(BF16)
    input_grad = (
        grad_res
        + near_sum[:rows]
        + across(near_sum[rows:].astype(BF16)).astype(F32)
        + swap_ctx(far_sum[:rows]).astype(F32)
        + swap_both(far_sum[rows:]).astype(F32)
    )
    grad_q_w = dot(token_all[:half], grad_query, TN).astype(BF16)
    grad_k_w = dot(token_all, grad_key, TN).astype(BF16)
    grad_v_w = dot(token_all, grad_value, TN).astype(BF16)
    qkv_grad = owned(jnp.stack([grad_q_w, grad_k_w, grad_v_w]))

    head_part = jnp.stack(
        [jnp.sum(grad_query, axis=0, dtype=F32), jnp.sum(grad_value, axis=0, dtype=F32)]
    )
    late = sum_all(
        lax.dynamic_update_slice(jnp.zeros((2, D), F32), head_part, (0, tp_rank * head_width))
    )

    vector_grad = jnp.concatenate([early[: 6 * D], late.reshape(-1), early[6 * D :]])
    vector_new, vector_momentum_new, vector_average_new = nesterov(
        vector_weight, vector_momentum, vector_average, vector_grad, vector_rate
    )
    attn_grad = jnp.concatenate([qkv_grad, out_grad[None]], axis=0)
    ffn_grad = jnp.stack([up_grad, down_grad])
    attn_new, attn_momentum_new, attn_average_new = nesterov(
        attn_weight, attn_momentum, attn_average, attn_grad, matrix_rate
    )
    ffn_new, ffn_momentum_new, ffn_average_new = nesterov(
        ffn_weight, ffn_momentum, ffn_average, ffn_grad, matrix_rate
    )
    return (
        layer_out[None],
        input_grad[None],
        attn_grad,
        attn_new,
        attn_momentum_new,
        attn_average_new,
        attn_new.astype(BF16),
        ffn_grad,
        ffn_new,
        ffn_momentum_new,
        ffn_average_new,
        ffn_new.astype(BF16),
        vector_grad,
        vector_new,
        vector_momentum_new,
        vector_average_new,
    )


def solution(mesh):
    rows = P("fsdp", ("ctx", "tp"), None)
    weight = P(None, "fsdp", "tp")
    return jax.shard_map(
        on_device,
        mesh=mesh,
        in_specs=(rows, rows) + (weight,) * 6 + (P(),) * 3,
        out_specs=(rows, rows) + (weight,) * 10 + (P(),) * 4,
        check_vma=False,
    )
```

```python
import math

import jax
import jax.numpy as jnp
from jax import lax
from jax.experimental import pallas as pl
from jax.experimental.pallas import tpu as pltpu
from jax.sharding import PartitionSpec as P

D = 1024
FF = 4096
HEAD_DIM = 64
LEN = 2048

NORM_EPSILON = 1e-05
MOMENTUM = 0.5
AVERAGE = 0.5
MATRIX_RATE = 0.1
VECTOR_RATE = 0.3

SCALE = HEAD_DIM ** (-0.5)
LOG2E = math.log2(math.e)
F32 = jnp.float32
BF16 = jnp.bfloat16
NT = (((1,), (1,)), ((), ()))
TN = (((0,), (0,)), ((), ()))
NN = (((1,), (0,)), ((), ()))


def dot(left, right, dims=NN):
    return lax.dot_general(left, right, dims, preferred_element_type=F32)


def head_masks(width):
    lane = lax.broadcasted_iota(jnp.int32, (1, width), 1) // HEAD_DIM
    return [(lane == h).astype(BF16) for h in range(width // HEAD_DIM)]


def attend_kernel(q_ref, k_ref, v_ref, o_ref, lse_ref, vt_ref):
    heads = q_ref.shape[1] // HEAD_DIM

    @pl.when(pl.program_id(0) == 0)
    def _():
        vt_ref[...] = v_ref[...].T

    queries = q_ref[...]
    masks = head_masks(q_ref.shape[1])
    outs = []
    for h in range(heads):
        scores = dot(k_ref[...], queries * masks[h], NT)
        top = jnp.max(scores, axis=0, keepdims=True)
        weights = jnp.exp2((scores - top) * (SCALE * LOG2E))
        total = jnp.sum(weights, axis=0, keepdims=True)
        out = dot(vt_ref[h * HEAD_DIM : (h + 1) * HEAD_DIM, :], weights.astype(BF16))
        outs.append(out / total)
        lse_ref[h : h + 1, :] = top * (SCALE * LOG2E) + jnp.log2(total)
    o_ref[...] = jnp.concatenate(outs, axis=0).T.astype(BF16)


def attend(queries, keys, values):
    rows, width = queries.shape
    block = min(256, rows)
    heads = width // HEAD_DIM
    return pl.pallas_call(
        attend_kernel,
        grid=(rows // block,),
        in_specs=[
            pl.BlockSpec((block, width), lambda i: (i, 0)),
            pl.BlockSpec(keys.shape, lambda i: (0, 0)),
            pl.BlockSpec(values.shape, lambda i: (0, 0)),
        ],
        out_specs=[
            pl.BlockSpec((block, width), lambda i: (i, 0)),
            pl.BlockSpec((heads, block), lambda i: (0, i)),
        ],
        out_shape=[
            jax.ShapeDtypeStruct((rows, width), BF16),
            jax.ShapeDtypeStruct((heads, rows), F32),
        ],
        scratch_shapes=[pltpu.VMEM((width, keys.shape[0]), BF16)],
        compiler_params=pltpu.CompilerParams(vmem_limit_bytes=40 * 1024 * 1024),
        cost_estimate=pl.CostEstimate(
            flops=16 * rows * keys.shape[0] * width,
            bytes_accessed=4 * (rows + keys.shape[0]) * width,
            transcendentals=rows * keys.shape[0] * heads,
        ),
        name="attend",
    )(queries, keys, values)


def attend_back_kernel(
    q_ref, k_ref, v_ref, o_ref, g_ref, lse_ref, dq_ref, dk_ref, dv_ref, kt_ref, dk_acc, dv_acc
):
    heads = q_ref.shape[1] // HEAD_DIM
    step = pl.program_id(0)

    @pl.when(step == 0)
    def _():
        kt_ref[...] = k_ref[...].T
        dk_acc[...] = jnp.zeros_like(dk_acc)
        dv_acc[...] = jnp.zeros_like(dv_acc)

    queries = q_ref[...]
    grads = g_ref[...]
    masks = head_masks(q_ref.shape[1])
    product = (o_ref[...].astype(F32) * grads.astype(F32)).T
    outs, probs, gscores, qms, gms = [], [], [], [], []
    for h in range(heads):
        qm = queries * masks[h]
        gm = grads * masks[h]
        delta = jnp.sum(product[h * HEAD_DIM : (h + 1) * HEAD_DIM, :], axis=0, keepdims=True)
        scores = dot(k_ref[...], qm, NT)
        prob = jnp.exp2(scores * (SCALE * LOG2E) - lse_ref[h : h + 1, :])
        grad_prob = dot(v_ref[...], gm, NT)
        gscore = (prob * (grad_prob - delta)).astype(BF16)
        outs.append(dot(kt_ref[h * HEAD_DIM : (h + 1) * HEAD_DIM, :], gscore))
        probs.append(prob.astype(BF16))
        gscores.append(gscore)
        qms.append(qm)
        gms.append(gm)
    dv_acc[...] += dot(jnp.concatenate(probs, axis=1), jnp.concatenate(gms, axis=0))
    dk_acc[...] += dot(jnp.concatenate(gscores, axis=1), jnp.concatenate(qms, axis=0))
    dq_ref[...] = (jnp.concatenate(outs, axis=0).T * SCALE).astype(BF16)

    @pl.when(step == pl.num_programs(0) - 1)
    def _():
        dk_ref[...] = (dk_acc[...] * SCALE).astype(BF16)
        dv_ref[...] = dv_acc[...].astype(BF16)


def attend_back(queries, keys, values, mixed, grad_mixed, lse):
    rows, width = queries.shape
    block = min(256, rows)
    heads = width // HEAD_DIM
    row_spec = pl.BlockSpec((block, width), lambda i: (i, 0))
    full_spec = pl.BlockSpec(keys.shape, lambda i: (0, 0))
    return pl.pallas_call(
        attend_back_kernel,
        grid=(rows // block,),
        in_specs=[
            row_spec,
            full_spec,
            full_spec,
            row_spec,
            row_spec,
            pl.BlockSpec((heads, block), lambda i: (0, i)),
        ],
        out_specs=[row_spec, full_spec, full_spec],
        out_shape=[
            jax.ShapeDtypeStruct((rows, width), BF16),
            jax.ShapeDtypeStruct(keys.shape, BF16),
            jax.ShapeDtypeStruct(keys.shape, BF16),
        ],
        scratch_shapes=[
            pltpu.VMEM((width, keys.shape[0]), BF16),
            pltpu.VMEM(keys.shape, F32),
            pltpu.VMEM(keys.shape, F32),
        ],
        compiler_params=pltpu.CompilerParams(vmem_limit_bytes=48 * 1024 * 1024),
        cost_estimate=pl.CostEstimate(
            flops=40 * rows * keys.shape[0] * width,
            bytes_accessed=8 * (rows + keys.shape[0]) * width,
            transcendentals=rows * keys.shape[0] * heads,
        ),
        name="attend_back",
    )(queries, keys, values, mixed, grad_mixed, lse)


def project_kernel(*refs):
    count = 8
    blocks, weights = refs[:count], refs[count:-7]
    bias_ref, x_ref, w_ref, q_ref, k_ref, v_ref, sem = refs[-7:]
    rows = blocks[0].shape[0]
    width = bias_ref.shape[1]
    deep = weights[0].shape[1]
    for i in range(count):
        x_ref[i * rows : (i + 1) * rows, :] = blocks[i][...]
    for i, part in enumerate(weights):
        for j in range(3):
            w_ref[i * deep : (i + 1) * deep, j * width : (j + 1) * width] = part[j]

    def near(i, carry):
        at = pl.ds(pl.multiple_of(i * 2 * rows, 2 * rows), 2 * rows)
        out = dot(x_ref[at, :], w_ref[...])
        q_ref[at, :] = (out[:, :width] + bias_ref[0:1, :]).astype(BF16)
        k_ref[at, :] = out[:, width : 2 * width].astype(BF16)
        v_ref[at, :] = (out[:, 2 * width :] + bias_ref[1:2, :]).astype(BF16)
        return carry

    def far(i, carry):
        at = pl.ds(pl.multiple_of(i * 2 * rows, 2 * rows), 2 * rows)
        out = dot(x_ref[at, :], w_ref[:, width:])
        k_ref[at, :] = out[:, :width].astype(BF16)
        v_ref[at, :] = (out[:, width:] + bias_ref[1:2, :]).astype(BF16)
        return carry

    lax.fori_loop(0, 2, near, 0)
    lax.fori_loop(2, 4, far, 0)


def project(blocks, weights, biases):
    rows, deep = blocks[0].shape
    width = biases.shape[1]
    whole = pl.BlockSpec(memory_space=pltpu.VMEM)
    return pl.pallas_call(
        project_kernel,
        in_specs=[whole] * (len(blocks) + len(weights) + 1),
        out_specs=[whole] * 5,
        out_shape=[
            jax.ShapeDtypeStruct((8 * rows, deep), BF16),
            jax.ShapeDtypeStruct((deep, 3 * width), BF16),
            jax.ShapeDtypeStruct((4 * rows, width), BF16),
            jax.ShapeDtypeStruct((8 * rows, width), BF16),
            jax.ShapeDtypeStruct((8 * rows, width), BF16),
        ],
        scratch_shapes=[pltpu.SemaphoreType.DMA],
        compiler_params=pltpu.CompilerParams(vmem_limit_bytes=40 * 1024 * 1024),
        cost_estimate=pl.CostEstimate(
            flops=40 * rows * deep * width,
            bytes_accessed=32 * rows * deep,
            transcendentals=0,
        ),
        name="project",
    )(*blocks, *weights, biases)


def norm_forward(values, gain_vec, shift_vec):
    row_mean = jnp.mean(values, axis=-1, keepdims=True)
    centered = values - row_mean
    inverse = lax.rsqrt(jnp.mean(centered * centered, axis=-1, keepdims=True) + NORM_EPSILON)
    normed = centered * inverse
    return (normed * gain_vec + shift_vec, normed, inverse)


def norm_backward(grad_out, normed, inverse, gain_vec):
    grad_normed = grad_out * gain_vec
    grad_in = inverse * (
        grad_normed
        - jnp.mean(grad_normed, axis=-1, keepdims=True)
        - normed * jnp.mean(grad_normed * normed, axis=-1, keepdims=True)
    )
    return (grad_in, jnp.sum(grad_out * normed, axis=0), jnp.sum(grad_out, axis=0))


def gelu_pair(values):
    size = jnp.abs(values)
    t = 1.0 / (1.0 + (0.3275911 * math.sqrt(0.5)) * size)
    bell = jnp.exp2(values * values * (-0.5 * LOG2E))
    poly = t * (
        0.5 * 0.254829592
        + t
        * (
            0.5 * -0.284496736
            + t * (0.5 * 1.421413741 + t * (0.5 * -1.453152027 + t * (0.5 * 1.061405429)))
        )
    )
    tail = poly * bell
    cdf = jnp.where(values < 0, tail, 1.0 - tail)
    return values * cdf, cdf + values * bell * (1.0 / math.sqrt(2.0 * math.pi))


def nesterov(weights, momentum, average, gradient, step_rate):
    momentum_new = MOMENTUM * momentum + gradient
    weight_new = weights - step_rate * (gradient + MOMENTUM * momentum_new)
    return (weight_new, momentum_new, AVERAGE * average + (1.0 - AVERAGE) * weight_new)


def swap_tp(values, bit):
    size = lax.axis_size("tp")
    return lax.ppermute(values, "tp", [(i, i ^ bit) for i in range(size)])


def core(values):
    return swap_tp(values, 1)


def across(values):
    return swap_tp(values, 2)


def swap_ctx(values):
    return lax.ppermute(values, "ctx", [(0, 1), (1, 0)])


def swap_both(values):
    size = lax.axis_size("tp")
    return lax.ppermute(values, ("ctx", "tp"), [(i, i ^ (size + 2)) for i in range(2 * size)])


def sum_all(values):
    for bit in (1, 2):
        values = values + swap_tp(values, bit)
    values = values + swap_ctx(values)
    size = lax.axis_size("fsdp")
    bit = 1
    while bit < size:
        values = values + lax.ppermute(values, "fsdp", [(i, i ^ bit) for i in range(size)])
        bit *= 2
    return values


def ring():
    return lax.axis_size("fsdp") <= 8


def shift_fsdp(values, step):
    size = lax.axis_size("fsdp")
    return lax.ppermute(values, "fsdp", [(i, (i + step) % size) for i in range(size)])


def gather_fsdp(shard, axis):
    if not ring():
        return [lax.all_gather(shard, "fsdp", axis=axis, tiled=True)]
    return [shard] + [shift_fsdp(shard, -s) for s in range(1, lax.axis_size("fsdp"))]


def scatter_fsdp(grads, axis):
    if not ring():
        return lax.psum_scatter(grads, "fsdp", scatter_dimension=axis, tiled=True).astype(F32)
    size = lax.axis_size("fsdp")
    pieces = jnp.split(grads, size, axis=axis)
    total = pieces[0].astype(F32)
    for s in range(1, size):
        total = total + shift_fsdp(pieces[s], s).astype(F32)
    return total


def roll_features(values, back=False):
    if not ring():
        return values
    size = lax.axis_size("fsdp")
    rank = lax.axis_index("fsdp")
    start = (D // size) * (lax.rem(size - rank, size) if back else rank)
    twice = jnp.concatenate([values, values], axis=-1)
    return lax.dynamic_slice_in_dim(twice, start, D, axis=-1)


def after(values, *others):
    return lax.optimization_barrier((values,) + others)[0]


def on_device(
    tokens,
    cotangent,
    attn_weight,
    attn_momentum,
    attn_average,
    ffn_weight,
    ffn_momentum,
    ffn_average,
    vector_weight,
    vector_momentum,
    vector_average,
):
    tp_rank = lax.axis_index("tp")
    sib_rank = tp_rank ^ 1
    ctx_rank = lax.axis_index("ctx")
    head_width = attn_weight.shape[2]
    unit_width = ffn_weight.shape[2]
    half_width = unit_width // 2
    token_count = LEN * lax.axis_size("fsdp")
    matrix_rate = MATRIX_RATE / math.sqrt(token_count)
    vector_rate = VECTOR_RATE / math.sqrt(token_count)

    own = roll_features(tokens[0])
    rows = own.shape[0]
    pair = 2 * rows
    half = 4 * rows
    beside = across(own)
    qkv_parts = gather_fsdp(attn_weight[:3].astype(BF16), 1)
    facing = swap_ctx(own)
    diagonal = swap_both(own)
    blocks = [own, beside, core(own), core(beside), facing, diagonal, core(facing), core(diagonal)]

    def unit_halves(index):
        mine = lax.dynamic_slice_in_dim(ffn_weight[index], ctx_rank * half_width, half_width, 1)
        other = lax.dynamic_slice_in_dim(
            ffn_weight[index], (1 - ctx_rank) * half_width, half_width, 1
        )
        return mine.astype(BF16), other.astype(BF16)

    up_mine, up_other = unit_halves(0)
    down_mine, down_other = unit_halves(1)
    out_up = after(
        jnp.concatenate([attn_weight[3].astype(BF16), up_mine], axis=1), *qkv_parts[1:]
    )
    out_up_parts = gather_fsdp(out_up, 0)
    down_parts = gather_fsdp(after(down_mine, *qkv_parts[1:]), 0)
    out_w = jnp.concatenate([p[:, :head_width] for p in out_up_parts], axis=0)

    def whole_units(mine_parts, other):
        mine = jnp.concatenate(mine_parts, axis=0)
        if ring():
            far = swap_ctx(jnp.concatenate(mine_parts[1:], axis=0))
            far = jnp.concatenate([other, far], axis=0)
        else:
            far = swap_ctx(mine)
        return jnp.concatenate([mine, far], axis=1)

    up_w = whole_units([p[:, head_width:] for p in out_up_parts], up_other)
    down_w = whole_units(down_parts, down_other)

    wide = roll_features(vector_weight[: 6 * D].reshape(6, D))
    gain_one, shift_one, gain_two, shift_two, bias_out, bias_down = (wide[i] for i in range(6))

    def piece(start, width):
        return lax.dynamic_slice_in_dim(vector_weight, start, width)

    biases = jnp.stack(
        [
            piece(6 * D + tp_rank * head_width, head_width),
            piece(7 * D + tp_rank * head_width, head_width),
        ]
    )

    def hidden_bias(rank):
        start = 8 * D + rank * unit_width
        return jnp.concatenate(
            [
                piece(start + ctx_rank * half_width, half_width),
                piece(start + (1 - ctx_rank) * half_width, half_width),
            ]
        )

    token_all, qkv_w, queries, keys, values = project(blocks, qkv_parts, biases)
    mixed, lse = attend(queries, keys, values)

    out_sib = core(out_w)
    mixed_own, mixed_sib = mixed[:pair], core(mixed[pair:])
    attn_part = dot(mixed_own, out_w, NT) + dot(mixed_sib, out_sib, NT)
    attn_out = attn_part[:rows] + across(attn_part[rows:].astype(BF16)).astype(F32) + bias_out
    first, normed_one, inverse_one = norm_forward(own.astype(F32) + attn_out, gain_one, shift_one)
    first_low = first.astype(BF16)
    first_pair = jnp.concatenate([first_low, across(first_low)], axis=0)

    up_sib = core(up_w)
    down_sib = core(down_w)

    def activate(weights, bias):
        act, slope = gelu_pair(dot(first_pair, weights) + bias)
        return act.astype(BF16), slope.astype(BF16)

    hidden_own, slope_own = activate(up_w, hidden_bias(tp_rank))
    hidden_sib, slope_sib = activate(up_sib, hidden_bias(sib_rank))
    down_part = dot(hidden_own, down_w, NT) + dot(hidden_sib, down_sib, NT)
    down_out = down_part[:rows] + across(down_part[rows:].astype(BF16)).astype(F32) + bias_down
    second, normed_two, inverse_two = norm_forward(first + down_out, gain_two, shift_two)
    layer_out = roll_features(second.astype(BF16), back=True)

    grad_second, grad_gain_two, grad_shift_two = norm_backward(
        roll_features(cotangent[0]).astype(F32), normed_two, inverse_two, gain_two
    )
    grad_down = grad_second.astype(BF16)
    grad_bias_down = jnp.sum(grad_down, axis=0, dtype=F32)
    grad_down_pair = jnp.concatenate([grad_down, across(grad_down)], axis=0)
    grad_up_own = (dot(grad_down_pair, down_w) * slope_own.astype(F32)).astype(BF16)
    grad_up_sib = (dot(grad_down_pair, down_sib) * slope_sib.astype(F32)).astype(BF16)
    first_part = dot(grad_up_own, up_w, NT) + dot(grad_up_sib, up_sib, NT)
    first_recv = across(first_part[rows:].astype(BF16))

    def chip_sum(left, right_own, right_sib):
        sent = core(dot(left, right_sib, TN).astype(BF16))
        return (dot(left, right_own, TN) + sent.astype(F32)).astype(BF16)

    down_chip = chip_sum(grad_down_pair, hidden_own, hidden_sib)
    up_chip = chip_sum(first_pair, grad_up_own, grad_up_sib)
    first_recv = after(first_recv, down_chip, up_chip)

    def both_halves(chip):
        facing_part = swap_ctx(chip[:, half_width:])
        return (chip[:, :half_width].astype(F32) + facing_part.astype(F32)).astype(BF16)

    def all_units(mine):
        mine = mine.astype(BF16)
        other = swap_ctx(mine)
        low = jnp.where(ctx_rank == 0, mine, other)
        high = jnp.where(ctx_rank == 0, other, mine)
        return jnp.concatenate([low, high], axis=1).astype(F32)

    down_grad = all_units(scatter_fsdp(both_halves(down_chip), 0))
    up_grad = all_units(scatter_fsdp(both_halves(up_chip), 0))

    grad_first = grad_second + first_part[:rows] + first_recv.astype(F32)
    grad_res, grad_gain_one, grad_shift_one = norm_backward(
        grad_first, normed_one, inverse_one, gain_one
    )
    grad_attn = grad_res.astype(BF16)
    grad_bias_out = jnp.sum(grad_attn, axis=0, dtype=F32)
    grad_attn_pair = jnp.concatenate([grad_attn, across(grad_attn)], axis=0)
    grad_mixed_sib = core(dot(grad_attn_pair, out_sib).astype(BF16))
    grad_mixed_own = dot(grad_attn_pair, out_w).astype(BF16)
    grad_mixed = jnp.concatenate([grad_mixed_own, grad_mixed_sib], axis=0)

    def both_ctx(part):
        part = part.astype(BF16)
        return part.astype(F32) + swap_ctx(part).astype(F32)

    out_chip = chip_sum(grad_attn_pair, mixed_own, mixed_sib)
    grad_mixed = after(grad_mixed, out_chip)
    out_grad = both_ctx(scatter_fsdp(out_chip, 0))

    def place(bias_grads, rank, vec):
        low = jnp.where(ctx_rank == 0, bias_grads[:half_width], bias_grads[half_width:])
        high = jnp.where(ctx_rank == 0, bias_grads[half_width:], bias_grads[:half_width])
        return lax.dynamic_update_slice(
            vec, jnp.concatenate([low, high]), (rank * unit_width,)
        )

    hidden_vec = place(
        jnp.sum(grad_up_own, axis=0, dtype=F32), tp_rank, jnp.zeros((FF,), F32)
    )
    hidden_vec = place(jnp.sum(grad_up_sib, axis=0, dtype=F32), sib_rank, hidden_vec)
    wide_grads = jnp.stack(
        [
            grad_gain_one,
            grad_shift_one,
            grad_gain_two,
            grad_shift_two,
            grad_bias_out,
            grad_bias_down,
        ]
    )
    early = sum_all(
        jnp.concatenate([roll_features(wide_grads, back=True).reshape(-1), hidden_vec])
    )

    grad_query, grad_key, grad_value = attend_back(queries, keys, values, mixed, grad_mixed, lse)
    grad_q_w = dot(token_all[:half], grad_query, TN).astype(BF16)
    grad_k_w = dot(token_all, grad_key, TN).astype(BF16)
    grad_v_w = dot(token_all, grad_value, TN).astype(BF16)
    qkv_grad = both_ctx(scatter_fsdp(jnp.stack([grad_q_w, grad_k_w, grad_v_w]), 1))

    grad_kv = jnp.concatenate([grad_key, grad_value], axis=1)
    kv_w = qkv_w[:, head_width:]
    input_near = dot(grad_kv[:half], kv_w, NT) + dot(grad_query, qkv_w[:, :head_width], NT)
    input_far = dot(grad_kv[half:], kv_w, NT)
    near_sum = input_near[:pair] + core(input_near[pair:].astype(BF16)).astype(F32)
    far_sum = (input_far[:pair] + core(input_far[pair:].astype(BF16)).astype(F32)).astype(BF16)
    input_grad = roll_features(
        grad_res
        + near_sum[:rows]
        + across(near_sum[rows:].astype(BF16)).astype(F32)
        + swap_ctx(far_sum[:rows]).astype(F32)
        + swap_both(far_sum[rows:]).astype(F32),
        back=True,
    )

    head_part = jnp.stack(
        [jnp.sum(grad_query, axis=0, dtype=F32), jnp.sum(grad_value, axis=0, dtype=F32)]
    )
    late = sum_all(
        lax.dynamic_update_slice(jnp.zeros((2, D), F32), head_part, (0, tp_rank * head_width))
    )

    vector_grad = jnp.concatenate([early[: 6 * D], late.reshape(-1), early[6 * D :]])
    vector_new, vector_momentum_new, vector_average_new = nesterov(
        vector_weight, vector_momentum, vector_average, vector_grad, vector_rate
    )
    attn_grad = jnp.concatenate([qkv_grad, out_grad[None]], axis=0)
    ffn_grad = jnp.stack([up_grad, down_grad])
    attn_new, attn_momentum_new, attn_average_new = nesterov(
        attn_weight, attn_momentum, attn_average, attn_grad, matrix_rate
    )
    ffn_new, ffn_momentum_new, ffn_average_new = nesterov(
        ffn_weight, ffn_momentum, ffn_average, ffn_grad, matrix_rate
    )
    return (
        layer_out[None],
        input_grad[None],
        attn_grad,
        attn_new,
        attn_momentum_new,
        attn_average_new,
        attn_new.astype(BF16),
        ffn_grad,
        ffn_new,
        ffn_momentum_new,
        ffn_average_new,
        ffn_new.astype(BF16),
        vector_grad,
        vector_new,
        vector_momentum_new,
        vector_average_new,
    )


def solution(mesh):
    rows = P("fsdp", ("ctx", "tp"), None)
    weight = P(None, "fsdp", "tp")
    return jax.shard_map(
        on_device,
        mesh=mesh,
        in_specs=(rows, rows) + (weight,) * 6 + (P(),) * 3,
        out_specs=(rows, rows) + (weight,) * 10 + (P(),) * 4,
        check_vma=False,
    )
```

```python
import functools
import math

import jax
import jax.numpy as jnp
from jax import lax
from jax.experimental import pallas as pl
from jax.experimental.pallas import tpu as pltpu
from jax.sharding import PartitionSpec as P

D = 1024
FF = 4096
HEAD_DIM = 64
LEN = 2048

NORM_EPSILON = 1e-05
MOMENTUM = 0.5
AVERAGE = 0.5
MATRIX_RATE = 0.1
VECTOR_RATE = 0.3

SCALE = HEAD_DIM ** (-0.5)
LOG2E = math.log2(math.e)
F32 = jnp.float32
BF16 = jnp.bfloat16
NT = (((1,), (1,)), ((), ()))
TN = (((0,), (0,)), ((), ()))
NN = (((1,), (0,)), ((), ()))


def dot(left, right, dims=NN):
    return lax.dot_general(left, right, dims, preferred_element_type=F32)


def head_masks(width):
    lane = lax.broadcasted_iota(jnp.int32, (1, width), 1) // HEAD_DIM
    return [(lane == h).astype(BF16) for h in range(width // HEAD_DIM)]


def attend_kernel(q_ref, k_ref, v_ref, o_ref, lse_ref, vt_ref):
    heads = q_ref.shape[1] // HEAD_DIM

    @pl.when(pl.program_id(0) == 0)
    def _():
        vt_ref[...] = v_ref[...].T

    queries = q_ref[...]
    masks = head_masks(q_ref.shape[1])
    outs = []
    for h in range(heads):
        scores = dot(k_ref[...], queries * masks[h], NT)
        top = jnp.max(scores, axis=0, keepdims=True)
        weights = jnp.exp2((scores - top) * (SCALE * LOG2E))
        total = jnp.sum(weights, axis=0, keepdims=True)
        out = dot(vt_ref[h * HEAD_DIM : (h + 1) * HEAD_DIM, :], weights.astype(BF16))
        outs.append(out / total)
        lse_ref[h : h + 1, :] = top * (SCALE * LOG2E) + jnp.log2(total)
    o_ref[...] = jnp.concatenate(outs, axis=0).T.astype(BF16)


def attend(queries, keys, values):
    rows, width = queries.shape
    block = min(256, rows)
    heads = width // HEAD_DIM
    return pl.pallas_call(
        attend_kernel,
        grid=(rows // block,),
        in_specs=[
            pl.BlockSpec((block, width), lambda i: (i, 0)),
            pl.BlockSpec(keys.shape, lambda i: (0, 0)),
            pl.BlockSpec(values.shape, lambda i: (0, 0)),
        ],
        out_specs=[
            pl.BlockSpec((block, width), lambda i: (i, 0)),
            pl.BlockSpec((heads, block), lambda i: (0, i)),
        ],
        out_shape=[
            jax.ShapeDtypeStruct((rows, width), BF16),
            jax.ShapeDtypeStruct((heads, rows), F32),
        ],
        scratch_shapes=[pltpu.VMEM((width, keys.shape[0]), BF16)],
        compiler_params=pltpu.CompilerParams(vmem_limit_bytes=40 * 1024 * 1024),
        cost_estimate=pl.CostEstimate(flops=1, bytes_accessed=1, transcendentals=0),
        name="attend",
    )(queries, keys, values)


def attend_back_kernel(
    part, q_ref, k_ref, v_ref, o_ref, g_ref, lse_ref, dq_ref, dkv_ref, kt_ref, dk_acc, dv_acc
):
    width = q_ref.shape[1]
    heads = width // HEAD_DIM
    step = pl.program_id(0)

    @pl.when(step == 0)
    def _():
        kt_ref[...] = k_ref[...].T
        dk_acc[...] = jnp.zeros_like(dk_acc)
        dv_acc[...] = jnp.zeros_like(dv_acc)

    queries = q_ref[...]
    grads = g_ref[...]
    masks = head_masks(width)
    product = (o_ref[...].astype(F32) * grads.astype(F32)).T
    outs, probs, gscores, qms, gms = [], [], [], [], []
    for h in range(heads):
        qm = queries * masks[h]
        gm = grads * masks[h]
        delta = jnp.sum(product[h * HEAD_DIM : (h + 1) * HEAD_DIM, :], axis=0, keepdims=True)
        scores = dot(k_ref[...], qm, NT)
        row = part * heads + h
        prob = jnp.exp2(scores * (SCALE * LOG2E) - lse_ref[row : row + 1, :])
        grad_prob = dot(v_ref[...], gm, NT)
        gscore = (prob * (grad_prob - delta)).astype(BF16)
        outs.append(dot(kt_ref[h * HEAD_DIM : (h + 1) * HEAD_DIM, :], gscore))
        probs.append(prob.astype(BF16))
        gscores.append(gscore)
        qms.append(qm)
        gms.append(gm)
    dv_acc[...] += dot(jnp.concatenate(probs, axis=1), jnp.concatenate(gms, axis=0))
    dk_acc[...] += dot(jnp.concatenate(gscores, axis=1), jnp.concatenate(qms, axis=0))
    dq_ref[...] = (jnp.concatenate(outs, axis=0).T * SCALE).astype(BF16)

    @pl.when(step == pl.num_programs(0) - 1)
    def _():
        dkv_ref[:, :width] = (dk_acc[...] * SCALE).astype(BF16)
        dkv_ref[:, width:] = dv_acc[...].astype(BF16)


def attend_back(queries, keys, values, mixed, grad_mixed, lse, part):
    rows, both = queries.shape
    count = keys.shape[0]
    width = both // 2
    block = min(256, rows)
    row_spec = pl.BlockSpec((block, width), lambda i: (i, part))
    full_spec = pl.BlockSpec((count, width), lambda i: (0, part))
    return pl.pallas_call(
        functools.partial(attend_back_kernel, part),
        grid=(rows // block,),
        in_specs=[
            row_spec,
            full_spec,
            full_spec,
            row_spec,
            row_spec,
            pl.BlockSpec((lse.shape[0], block), lambda i: (0, i)),
        ],
        out_specs=[
            pl.BlockSpec((block, width), lambda i: (i, 0)),
            pl.BlockSpec((count, both), lambda i: (0, 0)),
        ],
        out_shape=[shape((rows, width), BF16), shape((count, both), BF16)],
        scratch_shapes=[
            pltpu.VMEM((width, count), BF16),
            pltpu.VMEM((count, width), F32),
            pltpu.VMEM((count, width), F32),
        ],
        compiler_params=pltpu.CompilerParams(vmem_limit_bytes=44 * 1024 * 1024),
        cost_estimate=pl.CostEstimate(flops=1, bytes_accessed=1, transcendentals=0),
        name="attend_back",
    )(queries, keys, values, mixed, grad_mixed, lse)


VMEM = pl.BlockSpec(memory_space=pltpu.VMEM)


def call_whole(kernel, out_shape, args, flops, name, scratch=()):
    nbytes = sum(a.size * a.dtype.itemsize for a in list(args) + list(out_shape))
    return pl.pallas_call(
        kernel,
        in_specs=[VMEM] * len(args),
        out_specs=[VMEM] * len(out_shape),
        out_shape=list(out_shape),
        scratch_shapes=list(scratch),
        compiler_params=pltpu.CompilerParams(vmem_limit_bytes=44 * 1024 * 1024),
        cost_estimate=pl.CostEstimate(flops=1, bytes_accessed=1, transcendentals=0),
        name=name,
    )(*args)


def shape(dims, dtype):
    return jax.ShapeDtypeStruct(tuple(dims), dtype)


def tile(i, size):
    return pl.ds(pl.multiple_of(i * size, size), size)


def project_kernel(*refs):
    blocks, (mine, other, bias_ref, x_ref, w_ref, q_ref, k_ref, v_ref) = refs[:8], refs[8:]
    rows = blocks[0].shape[0]
    part = mine.shape[2]
    width = 2 * part
    for i in range(8):
        x_ref[i * rows : (i + 1) * rows, :] = blocks[i][...]
    for j in range(3):
        w_ref[:, j * width : j * width + part] = mine[j]
        w_ref[:, j * width + part : (j + 1) * width] = other[j]

    def near(i, carry):
        at = tile(i, 2 * rows)
        out = dot(x_ref[at, :], w_ref[...])
        q_ref[at, :] = (out[:, :width] + bias_ref[0:1, :]).astype(BF16)
        k_ref[at, :] = out[:, width : 2 * width].astype(BF16)
        v_ref[at, :] = (out[:, 2 * width :] + bias_ref[1:2, :]).astype(BF16)
        return carry

    def far(i, carry):
        at = tile(i, 2 * rows)
        out = dot(x_ref[at, :], w_ref[:, width:])
        k_ref[at, :] = out[:, :width].astype(BF16)
        v_ref[at, :] = (out[:, width:] + bias_ref[1:2, :]).astype(BF16)
        return carry

    lax.fori_loop(0, 2, near, 0)
    lax.fori_loop(2, 4, far, 0)


def project(blocks, mine, other, biases):
    rows, deep = blocks[0].shape
    width = biases.shape[1]
    out = [
        shape((8 * rows, deep), BF16),
        shape((deep, 3 * width), BF16),
        shape((4 * rows, width), BF16),
        shape((8 * rows, width), BF16),
        shape((8 * rows, width), BF16),
    ]
    args = [*blocks, mine, other, biases]
    return call_whole(project_kernel, out, args, 40 * rows * deep * width, "project")


def input_back_kernel(q0, q1, kv0, kv1, w_ref, near_ref, far_ref, sib_ref, cat_ref):
    half, part = q0.shape
    pair, deep = near_ref.shape
    for j, (ref, at) in enumerate(((q0, 0), (q1, 0), (kv0, 0), (kv1, 0), (kv0, part), (kv1, part))):
        count = ref.shape[0]
        cat_ref[:count, j * part : (j + 1) * part] = ref[:, at : at + part]
    out = dot(cat_ref[:pair, :], w_ref[...], NT)
    near_ref[...] = out
    out = dot(cat_ref[pair:half, :], w_ref[...], NT)
    sib_ref[:pair, :] = out.astype(BF16)
    out = dot(cat_ref[half : half + pair, 2 * part :], w_ref[:, 2 * part :], NT)
    far_ref[...] = out
    out = dot(cat_ref[half + pair :, 2 * part :], w_ref[:, 2 * part :], NT)
    sib_ref[pair:, :] = out.astype(BF16)


def input_back(q0, q1, kv0, kv1, weights):
    half, part = q0.shape
    deep = weights.shape[0]
    pair = half // 2
    out = [shape((pair, deep), F32), shape((pair, deep), F32), shape((half, deep), BF16)]
    return call_whole(
        input_back_kernel,
        out,
        [q0, q1, kv0, kv1, weights],
        20 * half * deep * part,
        "input_back",
        [pltpu.VMEM((kv0.shape[0], 6 * part), BF16)],
    )


def gelu_pair(values):
    size = jnp.abs(values)
    t = 1.0 / (1.0 + (0.3275911 * math.sqrt(0.5)) * size)
    bell = jnp.exp2(values * values * (-0.5 * LOG2E))
    poly = t * (
        0.5 * 0.254829592
        + t
        * (
            0.5 * -0.284496736
            + t * (0.5 * 1.421413741 + t * (0.5 * -1.453152027 + t * (0.5 * 1.061405429)))
        )
    )
    tail = poly * bell
    cdf = jnp.where(values < 0, tail, 1.0 - tail)
    return values * cdf, cdf + values * bell * (1.0 / math.sqrt(2.0 * math.pi))


def up_kernel(
    x0, x1, mine, other, mine_sib, other_sib, bias_ref,
    x_ref, w_ref, act_own, act_sib, slope_own, slope_sib,
):
    rows = x0.shape[0]
    part = mine.shape[2]
    x_ref[:rows, :] = x0[...]
    x_ref[rows:, :] = x1[...]
    at = 0
    for ref, first in ((mine, 1), (other, 0), (mine_sib, 1), (other_sib, 0)):
        for j in range(first, first + 2):
            w_ref[:, at : at + part] = ref[j]
            at += part
    units = act_own.shape[1]
    step = units // 2
    for c in range(4):
        act_ref, slope_ref = ((act_own, slope_own), (act_sib, slope_sib))[c // 2]
        at = slice((c % 2) * step, (c % 2 + 1) * step)

        def body(i, carry):
            r = tile(i, rows)
            pre = dot(x_ref[r, :], w_ref[:, c * step : (c + 1) * step])
            act, slope = gelu_pair(pre + bias_ref[0:1, c * step : (c + 1) * step])
            act_ref[r, at] = act.astype(BF16)
            slope_ref[r, at] = slope.astype(BF16)
            return carry

        lax.fori_loop(0, 2, body, 0)


def feed_up(x0, x1, pieces, bias):
    rows, deep = x0.shape
    units = bias.shape[1]
    out = [shape((2 * rows, deep), BF16), shape((deep, units), BF16)]
    out += [shape((2 * rows, units // 2), BF16)] * 4
    return call_whole(
        up_kernel, out, [x0, x1, *pieces, bias], 4 * rows * deep * units, "feed_up"
    )


def down_kernel(act_own, act_sib, own, sib, w_ref, near_ref, far_ref):
    rows, deep = near_ref.shape
    part = own.shape[2]
    at = 0
    for ref in (own, sib):
        for j in range(4):
            w_ref[:, at : at + part] = ref[j]
            at += part
    units = act_own.shape[1]
    step = deep // 4
    for c in range(4):
        at = slice(c * step, (c + 1) * step)
        out = dot(act_own[...], w_ref[at, :units], NT) + dot(act_sib[...], w_ref[at, units:], NT)
        near_ref[:, at] = out[:rows]
        far_ref[:, at] = out[rows:].astype(BF16)


def feed_down(act_own, act_sib, pieces):
    pair, units = act_own.shape
    deep = pieces[0].shape[1]
    out = [
        shape((deep, 2 * units), BF16),
        shape((pair // 2, deep), F32),
        shape((pair // 2, deep), BF16),
    ]
    return call_whole(
        down_kernel, out, [act_own, act_sib, *pieces], 4 * pair * deep * units, "feed_down"
    )


def feed_back_kernel(
    g0, g1, slope_own, slope_sib, up_ref, down_ref,
    g_ref, gup_own, gup_sib, bias_ref, near_ref, far_ref,
):
    rows, deep = g0.shape
    g_ref[:rows, :] = g0[...]
    g_ref[rows:, :] = g1[...]
    units = gup_own.shape[1]
    step = units // 2
    for c in range(4):
        slope_ref, gup_ref = ((slope_own, gup_own), (slope_sib, gup_sib))[c // 2]
        at = slice((c % 2) * step, (c % 2 + 1) * step)
        grad = dot(g_ref[...], down_ref[:, c * step : (c + 1) * step])
        grad = (grad * slope_ref[:, at].astype(F32)).astype(BF16)
        gup_ref[:, at] = grad
        bias_ref[0:1, c * step : (c + 1) * step] = jnp.sum(
            grad.astype(F32), axis=0, keepdims=True
        )
    step = deep // 4
    for c in range(4):
        at = slice(c * step, (c + 1) * step)
        out = dot(gup_own[...], up_ref[at, :units], NT) + dot(gup_sib[...], up_ref[at, units:], NT)
        near_ref[:, at] = out[:rows]
        far_ref[:, at] = out[rows:].astype(BF16)


def feed_back(g0, g1, slope_own, slope_sib, up_all, down_all):
    rows, deep = g0.shape
    units = slope_own.shape[1]
    out = [shape((2 * rows, deep), BF16)]
    out += [shape((2 * rows, units), BF16)] * 2
    out += [shape((1, 2 * units), F32), shape((rows, deep), F32), shape((rows, deep), BF16)]
    args = [g0, g1, slope_own, slope_sib, up_all, down_all]
    return call_whole(feed_back_kernel, out, args, 16 * rows * deep * units, "feed_back")


def norm_forward(values, gain_vec, shift_vec):
    row_mean = jnp.mean(values, axis=-1, keepdims=True)
    centered = values - row_mean
    inverse = lax.rsqrt(jnp.mean(centered * centered, axis=-1, keepdims=True) + NORM_EPSILON)
    normed = centered * inverse
    return (normed * gain_vec + shift_vec, normed, inverse)


def norm_backward(grad_out, normed, inverse, gain_vec):
    grad_normed = grad_out * gain_vec
    grad_in = inverse * (
        grad_normed
        - jnp.mean(grad_normed, axis=-1, keepdims=True)
        - normed * jnp.mean(grad_normed * normed, axis=-1, keepdims=True)
    )
    return (grad_in, jnp.sum(grad_out * normed, axis=0), jnp.sum(grad_out, axis=0))


def nesterov(weights, momentum, average, gradient, step_rate):
    momentum_new = MOMENTUM * momentum + gradient
    weight_new = weights - step_rate * (gradient + MOMENTUM * momentum_new)
    return (weight_new, momentum_new, AVERAGE * average + (1.0 - AVERAGE) * weight_new)


def swap_tp(values, bit):
    size = lax.axis_size("tp")
    return lax.ppermute(values, "tp", [(i, i ^ bit) for i in range(size)])


def core(values):
    return swap_tp(values, 1)


def across(values):
    return swap_tp(values, 2)


def swap_ctx(values):
    return lax.ppermute(values, "ctx", [(0, 1), (1, 0)])


def swap_both(values):
    size = lax.axis_size("tp")
    return lax.ppermute(values, ("ctx", "tp"), [(i, i ^ (size + 2)) for i in range(2 * size)])


def sum_all(values):
    for bit in (1, 2):
        values = values + swap_tp(values, bit)
    values = values + swap_ctx(values)
    size = lax.axis_size("fsdp")
    bit = 1
    while bit < size:
        values = values + lax.ppermute(values, "fsdp", [(i, i ^ bit) for i in range(size)])
        bit *= 2
    return values


def gather_fsdp(shard, axis):
    return lax.all_gather(shard, "fsdp", axis=axis, tiled=True)


def scatter_fsdp(grads, axis):
    return lax.psum_scatter(grads, "fsdp", scatter_dimension=axis, tiled=True)


def halves(values, axis=-1):
    low, high = jnp.split(values, 2, axis=axis)
    first = lax.axis_index("ctx") == 0
    return jnp.where(first, low, high), jnp.where(first, high, low)


def join(mine, other, axis=-1):
    first = lax.axis_index("ctx") == 0
    low, high = jnp.where(first, mine, other), jnp.where(first, other, mine)
    return jnp.concatenate([low, high], axis=axis)


def quarters(mine):
    return jnp.stack(jnp.split(mine, 2, axis=1))


def after(values, *others):
    return lax.optimization_barrier((values,) + others)[0]


def on_device(
    tokens,
    cotangent,
    attn_weight,
    attn_momentum,
    attn_average,
    ffn_weight,
    ffn_momentum,
    ffn_average,
    vector_weight,
    vector_momentum,
    vector_average,
):
    tp_rank = lax.axis_index("tp")
    sib_rank = tp_rank ^ 1
    head_width = attn_weight.shape[2]
    unit_width = ffn_weight.shape[2]
    token_count = LEN * lax.axis_size("fsdp")
    matrix_rate = MATRIX_RATE / math.sqrt(token_count)
    vector_rate = VECTOR_RATE / math.sqrt(token_count)

    attn_mine, attn_other = halves(attn_weight.astype(BF16))
    qkv_mine = gather_fsdp(attn_mine[:3], 1)
    up_low = halves(ffn_weight[0].astype(BF16))[0]
    down_low = jnp.concatenate([quarters(h) for h in halves(ffn_weight[1].astype(BF16))])
    out_low = jnp.concatenate([attn_mine[3], attn_other[3]], axis=1)
    out_up = gather_fsdp(jnp.concatenate([out_low[None], quarters(up_low)]), 1)
    down_w = gather_fsdp(down_low, 1)

    own = tokens[0]
    rows = own.shape[0]
    pair = 2 * rows
    half = 4 * rows
    beside = across(own)
    facing = swap_ctx(own)
    diagonal = swap_both(own)
    qkv_other = swap_ctx(after(qkv_mine, beside, facing, diagonal))
    blocks = [own, beside, core(own), core(beside), facing, diagonal, core(facing), core(diagonal)]

    gain_one, shift_one, gain_two, shift_two, bias_out, bias_down = (
        vector_weight[i * D : (i + 1) * D] for i in range(6)
    )

    def columns(start, width):
        part = lax.dynamic_slice_in_dim(vector_weight, start, width)
        return jnp.concatenate(halves(part))

    biases = jnp.stack(
        [
            columns(6 * D + tp_rank * head_width, head_width),
            columns(7 * D + tp_rank * head_width, head_width),
        ]
    )
    bias_hidden = jnp.concatenate(
        [
            columns(8 * D + tp_rank * unit_width, unit_width),
            columns(8 * D + sib_rank * unit_width, unit_width),
        ]
    )[None]

    token_all, qkv_w, queries, keys, values = project(blocks, qkv_mine, qkv_other, biases)
    mixed, lse = attend(queries, keys, values)

    out_up = after(out_up, mixed)
    out_up_sib = core(out_up)
    up_other = swap_ctx(out_up[1:])
    up_pieces = [out_up, up_other, out_up_sib, core(up_other)]
    out_w, out_sib = out_up[0], out_up_sib[0]
    mixed_own, mixed_sib = mixed[:pair], core(mixed[pair:])
    attn_part = dot(mixed_own, out_w, NT) + dot(mixed_sib, out_sib, NT)
    attn_out = attn_part[:rows] + across(attn_part[rows:].astype(BF16)).astype(F32) + bias_out
    first, normed_one, inverse_one = norm_forward(own.astype(F32) + attn_out, gain_one, shift_one)
    first_low = first.astype(BF16)
    first_beside = across(first_low)

    down_w = after(down_w, first_beside)
    down_pieces = [down_w, core(down_w)]
    first_pair, up_all, hidden_own, hidden_sib, slope_own, slope_sib = feed_up(
        first_low, first_beside, up_pieces, bias_hidden
    )
    down_all, down_part, down_far = feed_down(hidden_own, hidden_sib, down_pieces)
    down_out = down_part + across(down_far).astype(F32) + bias_down
    second, normed_two, inverse_two = norm_forward(first + down_out, gain_two, shift_two)
    layer_out = second.astype(BF16)

    grad_second, grad_gain_two, grad_shift_two = norm_backward(
        cotangent[0].astype(F32), normed_two, inverse_two, gain_two
    )
    grad_down = grad_second.astype(BF16)
    grad_bias_down = jnp.sum(grad_down, axis=0, dtype=F32)
    grad_down_pair, grad_up_own, grad_up_sib, grad_bias_hidden, first_part, first_far = feed_back(
        grad_down, across(grad_down), slope_own, slope_sib, up_all, down_all
    )
    first_recv = across(first_far)

    def chip_sum(left, right_own, right_sib):
        sent = core(dot(left, right_sib, TN).astype(BF16))
        total = (dot(left, right_own, TN) + sent.astype(F32)).astype(BF16)
        return jnp.split(total, 2, axis=1)

    down_keep, down_send = chip_sum(grad_down_pair, hidden_own, hidden_sib)
    up_keep, up_send = chip_sum(first_pair, grad_up_own, grad_up_sib)
    first_recv = after(first_recv, down_send, up_send)

    def ctx_sum(keep, send):
        return (keep.astype(F32) + swap_ctx(send).astype(F32)).astype(BF16)

    def finish(mine):
        return join(mine, swap_ctx(mine)).astype(F32)

    down_sum = ctx_sum(down_keep, down_send)
    up_sum = ctx_sum(up_keep, up_send)
    down_owned = scatter_fsdp(down_sum, 0)
    up_owned = scatter_fsdp(up_sum, 0)

    grad_first = grad_second + first_part + first_recv.astype(F32)
    grad_res, grad_gain_one, grad_shift_one = norm_backward(
        grad_first, normed_one, inverse_one, gain_one
    )
    grad_attn = grad_res.astype(BF16)
    grad_bias_out = jnp.sum(grad_attn, axis=0, dtype=F32)
    grad_attn_pair = jnp.concatenate([grad_attn, across(grad_attn)], axis=0)
    grad_mixed_sib = core(dot(grad_attn_pair, out_sib).astype(BF16))
    grad_mixed_own = dot(grad_attn_pair, out_w).astype(BF16)
    grad_mixed = jnp.concatenate([grad_mixed_own, grad_mixed_sib], axis=0)
    out_keep, out_send = chip_sum(grad_attn_pair, mixed_own, mixed_sib)

    out_sum = ctx_sum(out_keep, out_send)

    grad_mixed = after(grad_mixed, down_sum)
    heads = (queries, keys, values, mixed)
    query_other, kv_other = attend_back(*heads, grad_mixed, lse, 1)
    send_q = dot(token_all[:half], query_other, TN).astype(BF16)
    send_kv = dot(token_all, kv_other, TN).astype(BF16)
    grad_mixed = after(grad_mixed, up_sum, send_q, send_kv, down_owned)
    recv_q, recv_kv = swap_ctx(send_q), swap_ctx(send_kv)
    query_mine, kv_mine = attend_back(*heads, grad_mixed, lse, 0)
    part = head_width // 2
    keep_q = dot(token_all[:half], query_mine, TN)
    keep_kv = dot(token_all, kv_mine, TN)
    near, far, sibling = input_back(query_mine, query_other, kv_mine, kv_other, qkv_w)
    sibling = core(sibling)
    qkvo_sum = jnp.concatenate(
        [
            (keep_q + recv_q.astype(F32)).astype(BF16),
            (keep_kv + recv_kv.astype(F32)).astype(BF16),
            out_sum,
        ],
        axis=1,
    )
    qkvo_sum = after(qkvo_sum, up_owned, near)
    qkvo_mine = scatter_fsdp(qkvo_sum, 0)
    sibling = after(sibling, qkvo_sum).astype(F32)
    near = near + sibling[:pair]
    far = (far + sibling[pair:]).astype(BF16)
    terms = [across(near[rows:].astype(BF16)), swap_ctx(far[:rows]), swap_both(far[rows:])]
    input_grad = grad_res + near[:rows]
    for term in terms:
        input_grad = input_grad + term.astype(F32)

    down_grad, up_grad = finish(down_owned), finish(up_owned)
    qkvo_mine = after(qkvo_mine, input_grad, down_grad, up_grad)
    qkvo_other = swap_ctx(qkvo_mine)
    attn_grad = jnp.stack(
        [
            join(qkvo_mine[:, j * part : (j + 1) * part], qkvo_other[:, j * part : (j + 1) * part])
            for j in range(4)
        ]
    ).astype(F32)

    def place(vec, start, grads):
        width = grads.shape[0] // 2
        return lax.dynamic_update_slice(vec, join(grads[:width], grads[width:]), (start,))

    def token_sum(mine, other):
        return jnp.concatenate([jnp.sum(g, axis=0, dtype=F32) for g in (mine, other)])

    columns_vec = jnp.zeros((2 * D + FF,), F32)
    columns_vec = place(columns_vec, tp_rank * head_width, token_sum(query_mine, query_other))
    columns_vec = place(
        columns_vec, D + tp_rank * head_width, token_sum(kv_mine[:, part:], kv_other[:, part:])
    )
    columns_vec = place(
        columns_vec, 2 * D + tp_rank * unit_width, grad_bias_hidden[0, :unit_width]
    )
    columns_vec = place(
        columns_vec, 2 * D + sib_rank * unit_width, grad_bias_hidden[0, unit_width:]
    )
    vector_part = jnp.concatenate(
        [
            grad_gain_one,
            grad_shift_one,
            grad_gain_two,
            grad_shift_two,
            grad_bias_out,
            grad_bias_down,
            columns_vec,
        ]
    )
    vector_grad = sum_all(after(vector_part, near))
    vector_new, vector_momentum_new, vector_average_new = nesterov(
        vector_weight, vector_momentum, vector_average, vector_grad, vector_rate
    )
    ffn_grad = jnp.stack([up_grad, down_grad])
    attn_new, attn_momentum_new, attn_average_new = nesterov(
        attn_weight, attn_momentum, attn_average, attn_grad, matrix_rate
    )
    ffn_new, ffn_momentum_new, ffn_average_new = nesterov(
        ffn_weight, ffn_momentum, ffn_average, ffn_grad, matrix_rate
    )
    return (
        layer_out[None],
        input_grad[None],
        attn_grad,
        attn_new,
        attn_momentum_new,
        attn_average_new,
        attn_new.astype(BF16),
        ffn_grad,
        ffn_new,
        ffn_momentum_new,
        ffn_average_new,
        ffn_new.astype(BF16),
        vector_grad,
        vector_new,
        vector_momentum_new,
        vector_average_new,
    )


def solution(mesh):
    rows = P("fsdp", ("ctx", "tp"), None)
    weight = P(None, "fsdp", "tp")
    return jax.shard_map(
        on_device,
        mesh=mesh,
        in_specs=(rows, rows) + (weight,) * 6 + (P(),) * 3,
        out_specs=(rows, rows) + (weight,) * 10 + (P(),) * 4,
        check_vma=False,
    )
```

```python
import functools
import math

import jax
import jax.numpy as jnp
from jax import lax
from jax.experimental import pallas as pl
from jax.experimental.pallas import tpu as pltpu
from jax.sharding import PartitionSpec as P

D = 1024
FF = 4096
HEAD_DIM = 64
LEN = 2048

NORM_EPSILON = 1e-05
MOMENTUM = 0.5
AVERAGE = 0.5
MATRIX_RATE = 0.1
VECTOR_RATE = 0.3

SCALE = HEAD_DIM ** (-0.5)
LOG2E = math.log2(math.e)
F32 = jnp.float32
BF16 = jnp.bfloat16
NT = (((1,), (1,)), ((), ()))
TN = (((0,), (0,)), ((), ()))
NN = (((1,), (0,)), ((), ()))


def dot(left, right, dims=NN):
    return lax.dot_general(left, right, dims, preferred_element_type=F32)


VMEM = pl.BlockSpec(memory_space=pltpu.VMEM)
ANY = pl.BlockSpec(memory_space=pl.ANY)
MEGA = 1024 * 1024
WORK_UNIT = 1.2e10


WORK = {
    "project": 0.001,
    "attend": 0.001,
    "out_project": 0.001,
    "norm_one": 1.5,
    "feed_up": 8,
    "feed_down": 4,
    "norm_two": 2,
    "feed_back": 8,
    "grad_send": 2.5,
    "grad_sum": 3,
    "norm_one_back": 2,
    "out_back": 2,
    "attend_back": 12,
    "head_send": 3,
    "head_sum": 4,
    "input_back": 4,
    "pack": 1,
}


def cost(name):
    flops = int(WORK[name] * WORK_UNIT)
    return pl.CostEstimate(flops=flops, bytes_accessed=1, transcendentals=0)


def shape(dims, dtype):
    return jax.ShapeDtypeStruct(tuple(dims), dtype)


def tile(i, size):
    return pl.ds(pl.multiple_of(i * size, size), size)


def call_whole(kernel, name, out_shape, far_args, near_args, scratch=(), copies=0):
    scratch = list(scratch)
    if copies:
        scratch.append(pltpu.SemaphoreType.DMA((copies,)))
    return pl.pallas_call(
        kernel,
        in_specs=[ANY] * len(far_args) + [VMEM] * len(near_args),
        out_specs=[VMEM] * len(out_shape),
        out_shape=list(out_shape),
        scratch_shapes=scratch,
        compiler_params=pltpu.CompilerParams(vmem_limit_bytes=44 * MEGA),
        cost_estimate=cost(name),
        name=name,
    )(*far_args, *near_args)


def start_all(pairs, sems):
    copies = [pltpu.make_async_copy(src, dst, sems.at[i]) for i, (src, dst) in enumerate(pairs)]
    for copy in copies:
        copy.start()
    return copies


def head_masks(width):
    lane = lax.broadcasted_iota(jnp.int32, (1, width), 1) // HEAD_DIM
    return [(lane == h).astype(BF16) for h in range(width // HEAD_DIM)]


def attend_kernel(chunk, q_ref, k_ref, v_ref, own_ref, sib_ref, lse_ref, vt_ref):
    heads = q_ref.shape[1] // HEAD_DIM
    count = k_ref.shape[0]
    step = pl.program_id(0)

    @pl.when(step == 0)
    def _():
        vt_ref[...] = v_ref[...].T

    queries = q_ref[...]
    masked = [queries * mask for mask in head_masks(q_ref.shape[1])]
    units = [(h, c) for h in range(heads) for c in range(0, count, chunk)]

    def scores_of(unit):
        h, c = unit
        return dot(k_ref[c : c + chunk, :], masked[h], NT)

    tops, totals, outs = {}, {}, {}
    scores = scores_of(units[0])
    for i, unit in enumerate(units):
        current = scores
        if i + 1 < len(units):
            scores = scores_of(units[i + 1])
        h, c = unit
        top = jnp.max(current, axis=0, keepdims=True)
        weights = jnp.exp2((current - top) * (SCALE * LOG2E))
        tops[unit] = top
        totals[unit] = jnp.sum(weights, axis=0, keepdims=True)
        outs[unit] = dot(
            vt_ref[h * HEAD_DIM : (h + 1) * HEAD_DIM, c : c + chunk], weights.astype(BF16)
        )
    heads_out = []
    for h in range(heads):
        mine = [(h, c) for c in range(0, count, chunk)]
        top = functools.reduce(jnp.maximum, [tops[u] for u in mine])
        share = [jnp.exp2((tops[u] - top) * (SCALE * LOG2E)) for u in mine]
        total = sum(totals[u] * f for u, f in zip(mine, share))
        out = sum(outs[u] * f for u, f in zip(mine, share))
        heads_out.append(out / total)
        lse_ref[h : h + 1, :] = top * (SCALE * LOG2E) + jnp.log2(total)
    mixed = jnp.concatenate(heads_out, axis=0).T.astype(BF16)
    steps = pl.num_programs(0)

    @pl.when(step < steps // 2)
    def _():
        own_ref[...] = mixed

    @pl.when(step >= steps // 2)
    def _():
        sib_ref[...] = mixed


def attend(queries, keys, values):
    rows, width = queries.shape
    block = min(256, rows // 2)
    steps = rows // block
    heads = width // HEAD_DIM
    half_blocks = steps // 2
    return pl.pallas_call(
        functools.partial(attend_kernel, min(512, keys.shape[0])),
        grid=(steps,),
        in_specs=[
            pl.BlockSpec((block, width), lambda i: (i, 0)),
            pl.BlockSpec(keys.shape, lambda i: (0, 0)),
            pl.BlockSpec(values.shape, lambda i: (0, 0)),
        ],
        out_specs=[
            pl.BlockSpec((block, width), lambda i: (jnp.minimum(i, half_blocks - 1), 0)),
            pl.BlockSpec((block, width), lambda i: (jnp.maximum(i - half_blocks, 0), 0)),
            pl.BlockSpec((heads, block), lambda i: (0, i)),
        ],
        out_shape=[
            shape((rows // 2, width), BF16),
            shape((rows // 2, width), BF16),
            shape((heads, rows), F32),
        ],
        scratch_shapes=[pltpu.VMEM((width, keys.shape[0]), BF16)],
        compiler_params=pltpu.CompilerParams(vmem_limit_bytes=40 * MEGA),
        cost_estimate=cost("attend"),
        name="attend",
    )(queries, keys, values)


def attend_back_kernel(
    part, q_ref, k_ref, v_ref, o0_ref, o1_ref, g0_ref, g1_ref, lse_ref,
    dq_ref, dkv_ref, kt_ref, dk_acc, dv_acc, o_ref, g_ref,
):
    width = q_ref.shape[1]
    heads = width // HEAD_DIM
    step = pl.program_id(0)
    steps = pl.num_programs(0)

    @pl.when(step == 0)
    def _():
        kt_ref[...] = k_ref[...].T
        dk_acc[...] = jnp.zeros_like(dk_acc)
        dv_acc[...] = jnp.zeros_like(dv_acc)

    @pl.when(step < steps // 2)
    def _():
        o_ref[...] = o0_ref[...]
        g_ref[...] = g0_ref[...]

    @pl.when(step >= steps // 2)
    def _():
        o_ref[...] = o1_ref[...]
        g_ref[...] = g1_ref[...]

    queries = q_ref[...]
    grads = g_ref[...]
    masks = head_masks(width)
    product = (o_ref[...].astype(F32) * grads.astype(F32)).T
    outs, probs, gscores, qms, gms = [], [], [], [], []
    for h in range(heads):
        qm = queries * masks[h]
        gm = grads * masks[h]
        delta = jnp.sum(product[h * HEAD_DIM : (h + 1) * HEAD_DIM, :], axis=0, keepdims=True)
        scores = dot(k_ref[...], qm, NT)
        row = part * heads + h
        prob = jnp.exp2(scores * (SCALE * LOG2E) - lse_ref[row : row + 1, :])
        grad_prob = dot(v_ref[...], gm, NT)
        gscore = (prob * (grad_prob - delta)).astype(BF16)
        outs.append(dot(kt_ref[h * HEAD_DIM : (h + 1) * HEAD_DIM, :], gscore))
        probs.append(prob.astype(BF16))
        gscores.append(gscore)
        qms.append(qm)
        gms.append(gm)
    dv_acc[...] += dot(jnp.concatenate(probs, axis=1), jnp.concatenate(gms, axis=0))
    dk_acc[...] += dot(jnp.concatenate(gscores, axis=1), jnp.concatenate(qms, axis=0))
    dq_ref[...] = (jnp.concatenate(outs, axis=0).T * SCALE).astype(BF16)

    @pl.when(step == steps - 1)
    def _():
        dkv_ref[:, :width] = (dk_acc[...] * SCALE).astype(BF16)
        dkv_ref[:, width:] = dv_acc[...].astype(BF16)


def attend_back(queries, keys, values, mixed, grads, lse, part):
    rows, both = queries.shape
    count = keys.shape[0]
    width = both // 2
    block = min(256, rows // 2)
    half_blocks = rows // 2 // block
    row_spec = pl.BlockSpec((block, width), lambda i: (i, part))
    own_spec = pl.BlockSpec((block, width), lambda i: (jnp.minimum(i, half_blocks - 1), part))
    sib_spec = pl.BlockSpec((block, width), lambda i: (jnp.maximum(i - half_blocks, 0), part))
    full_spec = pl.BlockSpec((count, width), lambda i: (0, part))
    lse_spec = pl.BlockSpec((lse.shape[0], block), lambda i: (0, i))
    return pl.pallas_call(
        functools.partial(attend_back_kernel, part),
        grid=(rows // block,),
        in_specs=[row_spec, full_spec, full_spec] + [own_spec, sib_spec] * 2 + [lse_spec],
        out_specs=[
            pl.BlockSpec((block, width), lambda i: (i, 0)),
            pl.BlockSpec((count, both), lambda i: (0, 0)),
        ],
        out_shape=[shape((rows, width), BF16), shape((count, both), BF16)],
        scratch_shapes=[
            pltpu.VMEM((width, count), BF16),
            pltpu.VMEM((count, width), F32),
            pltpu.VMEM((count, width), F32),
            pltpu.VMEM((block, width), BF16),
            pltpu.VMEM((block, width), BF16),
        ],
        compiler_params=pltpu.CompilerParams(vmem_limit_bytes=44 * MEGA),
        cost_estimate=cost("attend_back"),
        name="attend_back",
    )(queries, keys, values, *mixed, *grads, lse)


def project_kernel(*refs):
    blocks, refs = refs[:8], refs[8:]
    mine, other, bias_ref, xt_ref, w_ref, q_ref, k_ref, v_ref, x_ref, sems = refs
    rows = blocks[0].shape[0]
    part = mine.shape[2]
    width = 2 * part
    pairs = []
    for j in range(3):
        pairs.append((mine.at[j], w_ref.at[:, j * width : j * width + part]))
        pairs.append((other.at[j], w_ref.at[:, j * width + part : (j + 1) * width]))
    for i in range(8):
        pairs.append((blocks[i], x_ref.at[i * rows : (i + 1) * rows, :]))
    copies = start_all(pairs, sems)
    for copy in copies[:6]:
        copy.wait()
    for i in range(4):
        at = slice(i * 2 * rows, (i + 1) * 2 * rows)
        for copy in copies[6 + 2 * i : 8 + 2 * i]:
            copy.wait()
        x = x_ref[at, :]
        if i < 2:
            out = dot(x, w_ref[...])
            q_ref[at, :] = (out[:, :width] + bias_ref[0:1, :]).astype(BF16)
            out = out[:, width:]
        else:
            out = dot(x, w_ref[:, width:])
        k_ref[at, :] = out[:, :width].astype(BF16)
        v_ref[at, :] = (out[:, width:] + bias_ref[1:2, :]).astype(BF16)
        xt_ref[:, at] = x.T


def project(blocks, mine, other, biases):
    rows, deep = blocks[0].shape
    width = biases.shape[1]
    out = [
        shape((deep, 8 * rows), BF16),
        shape((deep, 3 * width), BF16),
        shape((4 * rows, width), BF16),
        shape((8 * rows, width), BF16),
        shape((8 * rows, width), BF16),
    ]
    scratch = [pltpu.VMEM((8 * rows, deep), BF16)]
    return call_whole(
        project_kernel, "project", out, [*blocks, mine, other], [biases], scratch, 14
    )


def split_store(out, near_ref, far_ref, at):
    rows = near_ref.shape[0]
    near_ref[:, at] = out[:rows]
    far_ref[:, at] = out[rows:].astype(BF16)


def out_kernel(w0, w1, w2, w3, own, sib, w_ref, near_ref, far_ref, sems):
    part = w0.shape[1]
    width = own.shape[1]
    deep = w0.shape[0]
    pairs = [(w, w_ref.at[:, j * part : (j + 1) * part]) for j, w in enumerate((w0, w1, w2, w3))]
    for copy in start_all(pairs, sems):
        copy.wait()
    for c in range(4):
        at = slice(c * deep // 4, (c + 1) * deep // 4)
        out = dot(own[...], w_ref[at, :width], NT) + dot(sib[...], w_ref[at, width:], NT)
        split_store(out, near_ref, far_ref, at)


def out_project(own, sib, pieces):
    pair, width = own.shape
    deep = pieces[0].shape[0]
    out = [
        shape((deep, 2 * width), BF16),
        shape((pair // 2, deep), F32),
        shape((pair // 2, deep), BF16),
    ]
    return call_whole(out_kernel, "out_project", out, pieces, [own, sib], copies=4)


def out_back_kernel(g0, g1, w_ref, gt_ref, own_ref, sib_ref):
    rows = g0.shape[0]
    width = own_ref.shape[1]
    for i, ref in enumerate((g0, g1)):
        at = slice(i * rows, (i + 1) * rows)
        g = ref[...]
        out = dot(g, w_ref[...])
        own_ref[at, :] = out[:, :width].astype(BF16)
        sib_ref[at, :] = out[:, width:].astype(BF16)
        gt_ref[:, at] = g.T


def out_back(g0, g1, weights):
    rows, deep = g0.shape
    width = weights.shape[1] // 2
    out = [
        shape((deep, 2 * rows), BF16),
        shape((2 * rows, width), BF16),
        shape((2 * rows, width), BF16),
    ]
    return call_whole(out_back_kernel, "out_back", out, [], [g0, g1, weights])


def input_back_kernel(q0, q1, kv0, kv1, w_ref, near_ref, far_ref, sib_ref, cat_ref):
    half, part = q0.shape
    pair, deep = near_ref.shape
    for j, (ref, at) in enumerate(((q0, 0), (q1, 0), (kv0, 0), (kv1, 0), (kv0, part), (kv1, part))):
        count = ref.shape[0]
        cat_ref[:count, j * part : (j + 1) * part] = ref[:, at : at + part]
    sib_ref[:pair, :] = dot(cat_ref[pair:half, :], w_ref[...], NT).astype(BF16)
    out = dot(cat_ref[half + pair :, 2 * part :], w_ref[:, 2 * part :], NT)
    sib_ref[pair:, :] = out.astype(BF16)
    near_ref[...] = dot(cat_ref[:pair, :], w_ref[...], NT)
    far_ref[...] = dot(cat_ref[half : half + pair, 2 * part :], w_ref[:, 2 * part :], NT)


def input_back(q0, q1, kv0, kv1, weights):
    half, part = q0.shape
    deep = weights.shape[0]
    pair = half // 2
    out = [shape((pair, deep), F32), shape((pair, deep), F32), shape((half, deep), BF16)]
    scratch = [pltpu.VMEM((kv0.shape[0], 6 * part), BF16)]
    return call_whole(
        input_back_kernel, "input_back", out, [], [q0, q1, kv0, kv1, weights], scratch
    )


def grad_send_kernel(left, right, out_ref):
    out_ref[...] = dot(left[...], right[...]).astype(BF16)


def grad_send(left, right):
    out = [shape((left.shape[0], right.shape[1]), BF16)]
    return call_whole(grad_send_kernel, "grad_send", out, [], [left, right])[0]


def grad_sum_kernel(left, right, recv, keep_ref, send_ref):
    part = keep_ref.shape[1]
    for ref, at in ((send_ref, slice(part, 2 * part)), (keep_ref, slice(0, part))):
        ref[...] = (dot(left[...], right[:, at]) + recv[:, at].astype(F32)).astype(BF16)


def grad_sum(left, right, recv):
    half = shape((left.shape[0], right.shape[1] // 2), BF16)
    return call_whole(grad_sum_kernel, "grad_sum", [half, half], [], [left, right, recv])


def head_grads(left, query, pair):
    half = query.shape[0]
    return jnp.concatenate([dot(left[:, :half], query[...]), dot(left[...], pair[...])], axis=1)


def head_send_kernel(left, query, pair, out_ref):
    out_ref[...] = head_grads(left, query, pair).astype(BF16)


def head_send(left, query, pair):
    out = [shape((left.shape[0], query.shape[1] + pair.shape[1]), BF16)]
    return call_whole(head_send_kernel, "head_send", out, [], [left, query, pair])[0]


def head_sum_kernel(left, query, pair, recv, keep, keep_recv, out_ref):
    width = recv.shape[1]
    total = head_grads(left, query, pair) + recv[...].astype(F32)
    out_ref[:, :width] = total.astype(BF16)
    out_ref[:, width:] = (keep[...].astype(F32) + keep_recv[...].astype(F32)).astype(BF16)


def head_sum(left, query, pair, recv, keep, keep_recv):
    out = [shape((left.shape[0], recv.shape[1] + keep.shape[1]), BF16)]
    args = [left, query, pair, recv, keep, keep_recv]
    return call_whole(head_sum_kernel, "head_sum", out, [], args)[0]


def gelu_pair(values):
    size = jnp.abs(values)
    t = 1.0 / (1.0 + (0.3275911 * math.sqrt(0.5)) * size)
    bell = jnp.exp2(values * values * (-0.5 * LOG2E))
    poly = t * (
        0.5 * 0.254829592
        + t
        * (
            0.5 * -0.284496736
            + t * (0.5 * 1.421413741 + t * (0.5 * -1.453152027 + t * (0.5 * 1.061405429)))
        )
    )
    tail = poly * bell
    cdf = jnp.where(values < 0, tail, 1.0 - tail)
    return values * cdf, cdf + values * bell * (1.0 / math.sqrt(2.0 * math.pi))


def gather_units(refs, w_ref):
    pairs = []
    part = refs[0][0].shape[2]
    for ref, first in refs:
        for j in range(first, first + 2):
            at = len(pairs) * part
            pairs.append((ref.at[j], w_ref.at[:, at : at + part]))
    return pairs


def up_kernel(
    x0, x1, mine, other, mine_sib, other_sib, bias_ref,
    xt_ref, w_ref, act_own, act_sib, slope_own, slope_sib, x_ref, sems,
):
    rows = x0.shape[0]
    pairs = [(x0, x_ref.at[:rows, :]), (x1, x_ref.at[rows:, :])]
    pairs += gather_units(((mine, 0), (other, 0), (mine_sib, 0), (other_sib, 0)), w_ref)
    copies = start_all(pairs, sems)
    copies[0].wait()
    copies[1].wait()
    units = act_own.shape[1]
    step = mine.shape[2]
    for c in range(8):
        act_ref, slope_ref = ((act_own, slope_own), (act_sib, slope_sib))[c // 4]
        copies[2 + c].wait()
        at = slice((c % 4) * step, (c % 4 + 1) * step)
        pre = dot(x_ref[...], w_ref[:, c * step : (c + 1) * step])
        act, slope = gelu_pair(pre + bias_ref[0:1, c * step : (c + 1) * step])
        act_ref[:, at] = act.astype(BF16)
        slope_ref[:, at] = slope.astype(BF16)
    xt_ref[...] = x_ref[...].T


def feed_up(x0, x1, pieces, bias):
    rows, deep = x0.shape
    units = bias.shape[1]
    out = [shape((deep, 2 * rows), BF16), shape((deep, units), BF16)]
    out += [shape((2 * rows, units // 2), BF16)] * 4
    scratch = [pltpu.VMEM((2 * rows, deep), BF16)]
    return call_whole(up_kernel, "feed_up", out, [x0, x1, *pieces], [bias], scratch, 10)


def down_kernel(mine, other, mine_sib, other_sib, act_own, act_sib, w_ref, near_ref, far_ref, sems):
    deep = near_ref.shape[1]
    refs = ((mine, 2), (other, 0), (mine_sib, 2), (other_sib, 0))
    for copy in start_all(gather_units(refs, w_ref), sems):
        copy.wait()
    units = act_own.shape[1]
    for c in range(4):
        at = slice(c * deep // 4, (c + 1) * deep // 4)
        out = dot(act_own[...], w_ref[at, :units], NT) + dot(act_sib[...], w_ref[at, units:], NT)
        split_store(out, near_ref, far_ref, at)


def feed_down(act_own, act_sib, pieces):
    pair, units = act_own.shape
    deep = pieces[0].shape[1]
    out = [
        shape((deep, 2 * units), BF16),
        shape((pair // 2, deep), F32),
        shape((pair // 2, deep), BF16),
    ]
    return call_whole(down_kernel, "feed_down", out, pieces, [act_own, act_sib], copies=8)


def feed_back_kernel(
    g0, g1, slope_own, slope_sib, up_ref, down_ref,
    gt_ref, gup_own, gup_sib, bias_ref, near_ref, far_ref, g_ref,
):
    rows, deep = g0.shape
    g_ref[:rows, :] = g0[...]
    g_ref[rows:, :] = g1[...]
    units = gup_own.shape[1]
    step = units // 2
    for c in range(4):
        slope_ref, gup_ref = ((slope_own, gup_own), (slope_sib, gup_sib))[c // 2]
        at = slice((c % 2) * step, (c % 2 + 1) * step)
        grad = dot(g_ref[...], down_ref[:, c * step : (c + 1) * step])
        grad = (grad * slope_ref[:, at].astype(F32)).astype(BF16)
        gup_ref[:, at] = grad
        bias_ref[0:1, c * step : (c + 1) * step] = jnp.sum(
            grad.astype(F32), axis=0, keepdims=True
        )
    for c in range(4):
        at = slice(c * deep // 4, (c + 1) * deep // 4)
        out = dot(gup_own[...], up_ref[at, :units], NT) + dot(gup_sib[...], up_ref[at, units:], NT)
        split_store(out, near_ref, far_ref, at)
    gt_ref[...] = g_ref[...].T


def feed_back(g0, g1, slope_own, slope_sib, up_all, down_all):
    rows, deep = g0.shape
    units = slope_own.shape[1]
    out = [shape((deep, 2 * rows), BF16)]
    out += [shape((2 * rows, units), BF16)] * 2
    out += [shape((1, 2 * units), F32), shape((rows, deep), F32), shape((rows, deep), BF16)]
    args = [g0, g1, slope_own, slope_sib, up_all, down_all]
    scratch = [pltpu.VMEM((2 * rows, deep), BF16)]
    return call_whole(feed_back_kernel, "feed_back", out, [], args, scratch)


def row_mean(values):
    return jnp.mean(values, axis=-1, keepdims=True)


def col_sum(values):
    return jnp.sum(values, axis=0, keepdims=True)


def normalize(values):
    centered = values - row_mean(values)
    inverse = lax.rsqrt(row_mean(centered * centered) + NORM_EPSILON)
    return centered * inverse, inverse


def norm_back(grad_out, normed, inverse, gain):
    grad = grad_out * gain
    return inverse * (grad - row_mean(grad) - normed * row_mean(grad * normed))


def norm_one_kernel(own, part, recv, vec, first_ref, low_ref, normed_ref, inverse_ref):
    attn_out = part[...] + recv[...].astype(F32) + vec[4:5, :]
    normed, inverse = normalize(own[...].astype(F32) + attn_out)
    first = normed * vec[0:1, :] + vec[1:2, :]
    first_ref[...] = first
    low_ref[...] = first.astype(BF16)
    normed_ref[...] = normed
    inverse_ref[...] = inverse


def norm_one(own, part, recv, vec):
    rows, deep = own.shape
    out = [shape((rows, deep), t) for t in (F32, BF16, F32)] + [shape((rows, 1), F32)]
    return call_whole(norm_one_kernel, "norm_one", out, [], [own, part, recv, vec])


def norm_two_kernel(first, part, recv, cotangent, vec, out_ref, grad_ref, low_ref, sums_ref):
    down_out = part[...] + recv[...].astype(F32) + vec[5:6, :]
    normed, inverse = normalize(first[...] + down_out)
    out_ref[...] = (normed * vec[2:3, :] + vec[3:4, :]).astype(BF16)
    given = cotangent[...].astype(F32)
    grad = norm_back(given, normed, inverse, vec[2:3, :])
    grad_ref[...] = grad
    low = grad.astype(BF16)
    low_ref[...] = low
    sums_ref[0:1, :] = col_sum(given * normed)
    sums_ref[1:2, :] = col_sum(given)
    sums_ref[2:3, :] = col_sum(low.astype(F32))


def norm_two(first, part, recv, cotangent, vec):
    rows, deep = first.shape
    out = [shape((rows, deep), t) for t in (BF16, F32, BF16)] + [shape((3, deep), F32)]
    return call_whole(norm_two_kernel, "norm_two", out, [], [first, part, recv, cotangent, vec])


def norm_one_back_kernel(
    grad_second, part, recv, normed, inverse, vec, grad_ref, low_ref, sums_ref
):
    given = grad_second[...] + part[...] + recv[...].astype(F32)
    grad = norm_back(given, normed[...], inverse[...], vec[0:1, :])
    grad_ref[...] = grad
    low = grad.astype(BF16)
    low_ref[...] = low
    sums_ref[0:1, :] = col_sum(given * normed[...])
    sums_ref[1:2, :] = col_sum(given)
    sums_ref[2:3, :] = col_sum(low.astype(F32))


def norm_one_back(grad_second, part, recv, normed, inverse, vec):
    rows, deep = part.shape
    out = [shape((rows, deep), t) for t in (F32, BF16)] + [shape((3, deep), F32)]
    args = [grad_second, part, recv, normed, inverse, vec]
    return call_whole(norm_one_back_kernel, "norm_one_back", out, [], args)


def pack_kernel(one, two, q0, q1, kv0, kv1, hidden, out_ref):
    size = 4
    rank = lax.axis_index("tp")
    first = lax.axis_index("ctx") == 0
    part = q0.shape[1]
    units = hidden.shape[1] // 2
    out_ref[0:2, :] = one[0:2, :]
    out_ref[2:4, :] = two[0:2, :]
    out_ref[4:5, :] = one[2:3, :]
    out_ref[5:6, :] = two[2:3, :]
    for row, (mine, other, at) in ((6, (q0, q1, 0)), (7, (kv0, kv1, part))):
        mine = col_sum(mine[:, at : at + part].astype(F32))
        other = col_sum(other[:, at : at + part].astype(F32))
        low, high = jnp.where(first, mine, other), jnp.where(first, other, mine)
        for t in range(size):
            keep = rank == t
            start = 2 * t * part
            out_ref[row : row + 1, start : start + part] = jnp.where(keep, low, 0.0)
            out_ref[row : row + 1, start + part : start + 2 * part] = jnp.where(keep, high, 0.0)
    for t in range(size):
        row = 8 + t
        total = jnp.where(rank == t, hidden[:, :units], 0.0)
        total = total + jnp.where((rank ^ 1) == t, hidden[:, units:], 0.0)
        mine, other = total[:, : units // 2], total[:, units // 2 :]
        out_ref[row : row + 1, : units // 2] = jnp.where(first, mine, other)
        out_ref[row : row + 1, units // 2 :] = jnp.where(first, other, mine)


def pack(one, two, q0, q1, kv0, kv1, hidden):
    out = [shape((12, one.shape[1]), F32)]
    return call_whole(pack_kernel, "pack", out, [], [one, two, q0, q1, kv0, kv1, hidden])[0]


def nesterov(weights, momentum, average, gradient, step_rate):
    momentum_new = MOMENTUM * momentum + gradient
    weight_new = weights - step_rate * (gradient + MOMENTUM * momentum_new)
    return (weight_new, momentum_new, AVERAGE * average + (1.0 - AVERAGE) * weight_new)


def swap_tp(values, bit):
    size = lax.axis_size("tp")
    return lax.ppermute(values, "tp", [(i, i ^ bit) for i in range(size)])


def core(values):
    return swap_tp(values, 1)


def across(values):
    return swap_tp(values, 2)


def swap_ctx(values):
    return lax.ppermute(values, "ctx", [(0, 1), (1, 0)])


def swap_both(values):
    size = lax.axis_size("tp")
    return lax.ppermute(values, ("ctx", "tp"), [(i, i ^ (size + 2)) for i in range(2 * size)])


def sum_plane(values):
    for bit in (1, 2):
        values = values + swap_tp(values, bit)
    return values + swap_ctx(values)


def sum_fsdp(values):
    size = lax.axis_size("fsdp")
    bit = 1
    while bit < size:
        values = values + lax.ppermute(values, "fsdp", [(i, i ^ bit) for i in range(size)])
        bit *= 2
    return values


def gather_fsdp(shard, axis):
    return lax.all_gather(shard, "fsdp", axis=axis, tiled=True)


def scatter_fsdp(grads, axis):
    return lax.psum_scatter(grads, "fsdp", scatter_dimension=axis, tiled=True)


def halves(values, axis=-1):
    low, high = jnp.split(values, 2, axis=axis)
    first = lax.axis_index("ctx") == 0
    return jnp.where(first, low, high), jnp.where(first, high, low)


def join(mine, other, axis=-1):
    first = lax.axis_index("ctx") == 0
    low, high = jnp.where(first, mine, other), jnp.where(first, other, mine)
    return jnp.concatenate([low, high], axis=axis)


def quarters(mine):
    return jnp.stack(jnp.split(mine, 2, axis=1))


def after(values, *others):
    return lax.optimization_barrier((values,) + others)[0]


def on_device(
    tokens,
    cotangent,
    attn_weight,
    attn_momentum,
    attn_average,
    ffn_weight,
    ffn_momentum,
    ffn_average,
    vector_weight,
    vector_momentum,
    vector_average,
):
    tp_rank = lax.axis_index("tp")
    sib_rank = tp_rank ^ 1
    head_width = attn_weight.shape[2]
    unit_width = ffn_weight.shape[2]
    token_count = LEN * lax.axis_size("fsdp")
    matrix_rate = MATRIX_RATE / math.sqrt(token_count)
    vector_rate = VECTOR_RATE / math.sqrt(token_count)

    attn_mine = gather_fsdp(halves(attn_weight.astype(BF16))[0], 1)

    own = tokens[0]
    rows = own.shape[0]
    pair = 2 * rows
    half = 4 * rows
    beside = across(own)
    facing = swap_ctx(own)
    diagonal = swap_both(own)
    attn_mine = after(attn_mine, beside, facing, diagonal)
    qkv_other = swap_ctx(attn_mine[:3])
    out_mine = attn_mine[3]
    out_other = swap_ctx(after(out_mine, qkv_other))
    ffn_low = halves(ffn_weight.astype(BF16))[0]
    ffn_low = after(jnp.concatenate([quarters(ffn_low[0]), quarters(ffn_low[1])]), attn_mine)
    ffn_mine = gather_fsdp(ffn_low, 1)
    blocks = [own, beside, core(own), core(beside), facing, diagonal, core(facing), core(diagonal)]

    vec = vector_weight[: 6 * D].reshape(6, D)

    def columns(start, width):
        part = lax.dynamic_slice_in_dim(vector_weight, start, width)
        return jnp.concatenate(halves(part))

    biases = jnp.stack(
        [
            columns(6 * D + tp_rank * head_width, head_width),
            columns(7 * D + tp_rank * head_width, head_width),
        ]
    )
    bias_hidden = jnp.concatenate(
        [
            columns(8 * D + tp_rank * unit_width, unit_width),
            columns(8 * D + sib_rank * unit_width, unit_width),
        ]
    )[None]

    token_t, qkv_w, queries, keys, values = project(blocks, attn_mine, qkv_other, biases)
    out_other = after(out_other, queries)
    out_pieces = [out_mine, out_other, core(out_mine), core(out_other)]
    mixed_own, mixed_sib, lse = attend(after(queries, *out_pieces), keys, values)
    mixed_recv = core(mixed_sib)
    out_w, attn_part, attn_far = out_project(mixed_own, mixed_recv, out_pieces)
    ffn_mine = after(ffn_mine, attn_far)
    up_other = swap_ctx(ffn_mine[:2])
    down_other = swap_ctx(ffn_mine[2:])
    first, first_low, normed_one, inverse_one = norm_one(own, attn_part, across(attn_far), vec)
    first_beside = across(first_low)

    up_other = after(up_other, first_low)
    down_other = after(down_other, first_beside)
    ffn_sib = core(after(ffn_mine, first_low))
    first_t, up_all, hidden_own, hidden_sib, slope_own, slope_sib = feed_up(
        first_low, first_beside, [ffn_mine, up_other, ffn_sib, core(up_other)], bias_hidden
    )
    down_all, down_part, down_far = feed_down(
        hidden_own, hidden_sib, [ffn_mine, down_other, ffn_sib, core(down_other)]
    )
    layer_out, grad_second, grad_down, sums_two = norm_two(
        first, down_part, across(down_far), cotangent[0], vec
    )
    grad_down_t, grad_up_own, grad_up_sib, grad_bias_hidden, first_part, first_far = feed_back(
        grad_down, across(grad_down), slope_own, slope_sib, up_all, down_all
    )
    down_sib = grad_send(grad_down_t, hidden_sib)
    up_sib = grad_send(first_t, grad_up_sib)
    first_recv = after(across(first_far), down_sib, up_sib)
    grad_res, grad_attn, sums_one = norm_one_back(
        grad_second, first_part, first_recv, normed_one, inverse_one, vec
    )
    grad_attn_beside = across(grad_attn)
    down_keep, down_send = grad_sum(grad_down_t, hidden_own, after(core(down_sib), grad_attn))
    up_keep, up_send = grad_sum(first_t, grad_up_own, after(core(up_sib), grad_attn))

    def ctx_sum(keep, send):
        return (keep.astype(F32) + swap_ctx(send).astype(F32)).astype(BF16)

    def finish(mine):
        return join(mine, swap_ctx(mine)).astype(F32)

    down_sum = ctx_sum(down_keep, down_send)
    up_sum = ctx_sum(up_keep, up_send)
    down_owned = scatter_fsdp(down_sum, 0)
    up_owned = scatter_fsdp(up_sum, 0)

    grad_attn_beside = after(grad_attn_beside, down_send, up_send)
    grad_attn_t, grad_mixed_own, grad_mixed_sib = out_back(grad_attn, grad_attn_beside, out_w)
    grad_mixed = (grad_mixed_own, core(grad_mixed_sib))

    mixed = (mixed_own, mixed_sib)
    heads = (queries, keys, values, mixed)
    grad_mixed = (grad_mixed[0], after(grad_mixed[1], down_sum))
    query_other, kv_other = attend_back(*heads, grad_mixed, lse, 1)
    send = head_send(token_t, query_other, kv_other)
    out_sib = grad_send(after(grad_attn_t, query_other), mixed_recv)
    out_keep, out_send = grad_sum(grad_attn_t, mixed_own, core(out_sib))
    grad_mixed = (grad_mixed[0], after(grad_mixed[1], up_sum, send, out_send))
    recv = swap_ctx(send)
    query_mine, kv_mine = attend_back(*heads, grad_mixed, lse, 0)
    part = head_width // 2
    near, far, sibling = input_back(query_mine, query_other, kv_mine, kv_other, qkv_w)
    sibling = core(sibling)
    qkvo_sum = head_sum(token_t, query_mine, kv_mine, recv, out_keep, swap_ctx(out_send))
    qkvo_sum = after(qkvo_sum, up_owned)
    qkvo_mine = scatter_fsdp(qkvo_sum, 0)

    vector_part = pack(
        after(sums_one, qkvo_sum), sums_two, query_mine, query_other, kv_mine, kv_other, grad_bias_hidden
    )
    vector_plane = sum_plane(vector_part)
    sibling = after(sibling, qkvo_sum, vector_plane).astype(F32)
    near = near + sibling[:pair]
    far = (far + sibling[pair:]).astype(BF16)
    terms = [across(near[rows:].astype(BF16)), swap_ctx(far[:rows]), swap_both(far[rows:])]
    vector_grad = sum_fsdp(vector_plane).reshape(-1)
    input_grad = grad_res + near[:rows]
    for term in terms:
        input_grad = input_grad + term.astype(F32)

    down_grad, up_grad = finish(down_owned), finish(up_owned)
    qkvo_mine = after(qkvo_mine, input_grad, down_grad, up_grad, vector_grad)
    qkvo_other = swap_ctx(qkvo_mine)
    attn_grad = jnp.stack(
        [
            join(qkvo_mine[:, j * part : (j + 1) * part], qkvo_other[:, j * part : (j + 1) * part])
            for j in range(4)
        ]
    ).astype(F32)
    vector_new, vector_momentum_new, vector_average_new = nesterov(
        vector_weight, vector_momentum, vector_average, vector_grad, vector_rate
    )
    ffn_grad = jnp.stack([up_grad, down_grad])
    attn_new, attn_momentum_new, attn_average_new = nesterov(
        attn_weight, attn_momentum, attn_average, attn_grad, matrix_rate
    )
    ffn_new, ffn_momentum_new, ffn_average_new = nesterov(
        ffn_weight, ffn_momentum, ffn_average, ffn_grad, matrix_rate
    )
    return (
        layer_out[None],
        input_grad[None],
        attn_grad,
        attn_new,
        attn_momentum_new,
        attn_average_new,
        attn_new.astype(BF16),
        ffn_grad,
        ffn_new,
        ffn_momentum_new,
        ffn_average_new,
        ffn_new.astype(BF16),
        vector_grad,
        vector_new,
        vector_momentum_new,
        vector_average_new,
    )


def solution(mesh):
    rows = P("fsdp", ("ctx", "tp"), None)
    weight = P(None, "fsdp", "tp")
    return jax.shard_map(
        on_device,
        mesh=mesh,
        in_specs=(rows, rows) + (weight,) * 6 + (P(),) * 3,
        out_specs=(rows, rows) + (weight,) * 10 + (P(),) * 4,
        check_vma=False,
    )
```

```python
import functools
import math

import jax
import jax.numpy as jnp
from jax import lax
from jax.experimental import pallas as pl
from jax.experimental.pallas import tpu as pltpu
from jax.sharding import PartitionSpec as P

D = 1024
FF = 4096
HEAD_DIM = 64
LEN = 2048

NORM_EPSILON = 1e-05
MOMENTUM = 0.5
AVERAGE = 0.5
MATRIX_RATE = 0.1
VECTOR_RATE = 0.3

SCALE = HEAD_DIM ** (-0.5)
LOG2E = math.log2(math.e)
F32 = jnp.float32
BF16 = jnp.bfloat16
NT = (((1,), (1,)), ((), ()))
TN = (((0,), (0,)), ((), ()))
NN = (((1,), (0,)), ((), ()))


def dot(left, right, dims=NN):
    return lax.dot_general(left, right, dims, preferred_element_type=F32)


VMEM = pl.BlockSpec(memory_space=pltpu.VMEM)
ANY = pl.BlockSpec(memory_space=pl.ANY)
MEGA = 1024 * 1024
WORK_UNIT = 1.2e10


WORK = {
    "project": 0.001,
    "attend": 0.001,
    "out_project": 0.001,
    "norm_one": 1.5,
    "feed_up": 8,
    "feed_down": 4,
    "norm_two": 2,
    "feed_back": 8,
    "grad_send": 10,
    "grad_sum": 3,
    "norm_one_back": 2,
    "out_back": 2,
    "attend_back": 12,
    "head_send": 3,
    "head_sum": 4,
    "input_back": 4,
    "fold": 1.5,
    "grad_total": 3,
}


def cost(name):
    flops = int(WORK[name] * WORK_UNIT)
    return pl.CostEstimate(flops=flops, bytes_accessed=1, transcendentals=0)


def shape(dims, dtype):
    return jax.ShapeDtypeStruct(tuple(dims), dtype)


def tile(i, size):
    return pl.ds(pl.multiple_of(i * size, size), size)


def call_whole(kernel, name, out_shape, far_args, near_args, scratch=(), copies=0):
    scratch = list(scratch)
    if copies:
        scratch.append(pltpu.SemaphoreType.DMA((copies,)))
    return pl.pallas_call(
        kernel,
        in_specs=[ANY] * len(far_args) + [VMEM] * len(near_args),
        out_specs=[VMEM] * len(out_shape),
        out_shape=list(out_shape),
        scratch_shapes=scratch,
        compiler_params=pltpu.CompilerParams(vmem_limit_bytes=32 * MEGA),
        cost_estimate=cost(name),
        name=name,
    )(*far_args, *near_args)


def start_all(pairs, sems):
    copies = [pltpu.make_async_copy(src, dst, sems.at[i]) for i, (src, dst) in enumerate(pairs)]
    for copy in copies:
        copy.start()
    return copies


def head_masks(width):
    lane = lax.broadcasted_iota(jnp.int32, (1, width), 1) // HEAD_DIM
    return [(lane == h).astype(BF16) for h in range(width // HEAD_DIM)]


def attend_kernel(chunk, q_ref, k_ref, v_ref, own_ref, sib_ref, lse_ref, vt_ref):
    heads = q_ref.shape[1] // HEAD_DIM
    count = k_ref.shape[0]
    step = pl.program_id(0)

    @pl.when(step == 0)
    def _():
        vt_ref[...] = v_ref[...].T

    queries = q_ref[...]
    masked = [queries * mask for mask in head_masks(q_ref.shape[1])]
    units = [(h, c) for h in range(heads) for c in range(0, count, chunk)]

    def scores_of(unit):
        h, c = unit
        return dot(k_ref[c : c + chunk, :], masked[h], NT)

    tops, totals, outs = {}, {}, {}
    scores = scores_of(units[0])
    for i, unit in enumerate(units):
        current = scores
        if i + 1 < len(units):
            scores = scores_of(units[i + 1])
        h, c = unit
        top = jnp.max(current, axis=0, keepdims=True)
        weights = jnp.exp2((current - top) * (SCALE * LOG2E))
        tops[unit] = top
        totals[unit] = jnp.sum(weights, axis=0, keepdims=True)
        outs[unit] = dot(
            vt_ref[h * HEAD_DIM : (h + 1) * HEAD_DIM, c : c + chunk], weights.astype(BF16)
        )
    heads_out = []
    for h in range(heads):
        mine = [(h, c) for c in range(0, count, chunk)]
        top = functools.reduce(jnp.maximum, [tops[u] for u in mine])
        share = [jnp.exp2((tops[u] - top) * (SCALE * LOG2E)) for u in mine]
        total = sum(totals[u] * f for u, f in zip(mine, share))
        out = sum(outs[u] * f for u, f in zip(mine, share))
        heads_out.append(out / total)
        lse_ref[h : h + 1, :] = top * (SCALE * LOG2E) + jnp.log2(total)
    mixed = jnp.concatenate(heads_out, axis=0).T.astype(BF16)
    steps = pl.num_programs(0)

    @pl.when(step < steps // 2)
    def _():
        own_ref[...] = mixed

    @pl.when(step >= steps // 2)
    def _():
        sib_ref[...] = mixed


def attend(queries, keys, values):
    rows, width = queries.shape
    block = min(256, rows // 2)
    steps = rows // block
    heads = width // HEAD_DIM
    half_blocks = steps // 2
    return pl.pallas_call(
        functools.partial(attend_kernel, min(512, keys.shape[0])),
        grid=(steps,),
        in_specs=[
            pl.BlockSpec((block, width), lambda i: (i, 0)),
            pl.BlockSpec(keys.shape, lambda i: (0, 0)),
            pl.BlockSpec(values.shape, lambda i: (0, 0)),
        ],
        out_specs=[
            pl.BlockSpec((block, width), lambda i: (jnp.minimum(i, half_blocks - 1), 0)),
            pl.BlockSpec((block, width), lambda i: (jnp.maximum(i - half_blocks, 0), 0)),
            pl.BlockSpec((heads, block), lambda i: (0, i)),
        ],
        out_shape=[
            shape((rows // 2, width), BF16),
            shape((rows // 2, width), BF16),
            shape((heads, rows), F32),
        ],
        scratch_shapes=[pltpu.VMEM((width, keys.shape[0]), BF16)],
        compiler_params=pltpu.CompilerParams(vmem_limit_bytes=32 * MEGA),
        cost_estimate=cost("attend"),
        name="attend",
    )(queries, keys, values)


def attend_back_kernel(
    part, q_ref, k_ref, v_ref, o0_ref, o1_ref, g0_ref, g1_ref, lse_ref,
    dq_ref, dkv_ref, kt_ref, dk_acc, dv_acc, o_ref, g_ref,
):
    width = q_ref.shape[1]
    heads = width // HEAD_DIM
    step = pl.program_id(0)
    steps = pl.num_programs(0)

    @pl.when(step == 0)
    def _():
        kt_ref[...] = k_ref[...].T
        dk_acc[...] = jnp.zeros_like(dk_acc)
        dv_acc[...] = jnp.zeros_like(dv_acc)

    @pl.when(step < steps // 2)
    def _():
        o_ref[...] = o0_ref[...]
        g_ref[...] = g0_ref[...]

    @pl.when(step >= steps // 2)
    def _():
        o_ref[...] = o1_ref[...]
        g_ref[...] = g1_ref[...]

    queries = q_ref[...]
    grads = g_ref[...]
    masks = head_masks(width)
    product = (o_ref[...].astype(F32) * grads.astype(F32)).T
    outs, probs, gscores, qms, gms = [], [], [], [], []
    for h in range(heads):
        qm = queries * masks[h]
        gm = grads * masks[h]
        delta = jnp.sum(product[h * HEAD_DIM : (h + 1) * HEAD_DIM, :], axis=0, keepdims=True)
        scores = dot(k_ref[...], qm, NT)
        row = part * heads + h
        prob = jnp.exp2(scores * (SCALE * LOG2E) - lse_ref[row : row + 1, :])
        grad_prob = dot(v_ref[...], gm, NT)
        gscore = (prob * (grad_prob - delta)).astype(BF16)
        outs.append(dot(kt_ref[h * HEAD_DIM : (h + 1) * HEAD_DIM, :], gscore))
        probs.append(prob.astype(BF16))
        gscores.append(gscore)
        qms.append(qm)
        gms.append(gm)
    dv_acc[...] += dot(jnp.concatenate(probs, axis=1), jnp.concatenate(gms, axis=0))
    dk_acc[...] += dot(jnp.concatenate(gscores, axis=1), jnp.concatenate(qms, axis=0))
    dq_ref[...] = (jnp.concatenate(outs, axis=0).T * SCALE).astype(BF16)

    @pl.when(step == steps - 1)
    def _():
        dkv_ref[:, :width] = (dk_acc[...] * SCALE).astype(BF16)
        dkv_ref[:, width:] = dv_acc[...].astype(BF16)


def attend_back(queries, keys, values, mixed, grads, lse, part):
    rows, both = queries.shape
    count = keys.shape[0]
    width = both // 2
    block = min(256, rows // 2)
    half_blocks = rows // 2 // block
    row_spec = pl.BlockSpec((block, width), lambda i: (i, part))
    own_spec = pl.BlockSpec((block, width), lambda i: (jnp.minimum(i, half_blocks - 1), part))
    sib_spec = pl.BlockSpec((block, width), lambda i: (jnp.maximum(i - half_blocks, 0), part))
    full_spec = pl.BlockSpec((count, width), lambda i: (0, part))
    lse_spec = pl.BlockSpec((lse.shape[0], block), lambda i: (0, i))
    return pl.pallas_call(
        functools.partial(attend_back_kernel, part),
        grid=(rows // block,),
        in_specs=[row_spec, full_spec, full_spec] + [own_spec, sib_spec] * 2 + [lse_spec],
        out_specs=[
            pl.BlockSpec((block, width), lambda i: (i, 0)),
            pl.BlockSpec((count, both), lambda i: (0, 0)),
        ],
        out_shape=[shape((rows, width), BF16), shape((count, both), BF16)],
        scratch_shapes=[
            pltpu.VMEM((width, count), BF16),
            pltpu.VMEM((count, width), F32),
            pltpu.VMEM((count, width), F32),
            pltpu.VMEM((block, width), BF16),
            pltpu.VMEM((block, width), BF16),
        ],
        compiler_params=pltpu.CompilerParams(vmem_limit_bytes=32 * MEGA),
        cost_estimate=cost("attend_back"),
        name="attend_back",
    )(queries, keys, values, *mixed, *grads, lse)


def ring_rows(count, deep):
    size = deep // count
    rank = lax.axis_index("fsdp")
    return [tile(lax.rem(rank + s, count), size) if count > 1 else tile(0, size) for s in range(count)]


def project_kernel(count, *refs):
    blocks, refs = refs[:8], refs[8:]
    mine, refs = refs[:count], refs[count:]
    other, refs = refs[:count], refs[count:]
    bias_ref, xt_ref, w_ref, q_ref, k_ref, v_ref, x_ref, sems = refs
    rows = blocks[0].shape[0]
    deep = x_ref.shape[1]
    part = mine[0].shape[2]
    width = 2 * part
    pairs = []
    for at, low, high in zip(ring_rows(count, deep), mine, other):
        for j in range(3):
            pairs.append((low.at[j], w_ref.at[at, j * width : j * width + part]))
            pairs.append((high.at[j], w_ref.at[at, j * width + part : (j + 1) * width]))
    weights = len(pairs)
    for i in range(8):
        pairs.append((blocks[i], x_ref.at[i * rows : (i + 1) * rows, :]))
    copies = start_all(pairs, sems)
    for copy in copies[:weights]:
        copy.wait()
    for i in range(4):
        at = slice(i * 2 * rows, (i + 1) * 2 * rows)
        for copy in copies[weights + 2 * i : weights + 2 * i + 2]:
            copy.wait()
        x = x_ref[at, :]
        if i < 2:
            out = dot(x, w_ref[...])
            q_ref[at, :] = (out[:, :width] + bias_ref[0:1, :]).astype(BF16)
            out = out[:, width:]
        else:
            out = dot(x, w_ref[:, width:])
        k_ref[at, :] = out[:, :width].astype(BF16)
        v_ref[at, :] = (out[:, width:] + bias_ref[1:2, :]).astype(BF16)
        xt_ref[:, at] = x.T


def project(blocks, mine, other, biases):
    rows, deep = blocks[0].shape
    width = biases.shape[1]
    out = [
        shape((deep, 8 * rows), BF16),
        shape((deep, 3 * width), BF16),
        shape((4 * rows, width), BF16),
        shape((8 * rows, width), BF16),
        shape((8 * rows, width), BF16),
    ]
    scratch = [pltpu.VMEM((8 * rows, deep), BF16)]
    kernel = functools.partial(project_kernel, len(mine))
    args = [*blocks, *mine, *other]
    return call_whole(kernel, "project", out, args, [biases], scratch, 8 + 6 * len(mine))


def split_store(out, near_ref, far_ref, at):
    rows = near_ref.shape[0]
    near_ref[:, at] = out[:rows]
    far_ref[:, at] = out[rows:].astype(BF16)


def out_kernel(w0, w1, own, sib, w_ref, near_ref, far_ref, sems):
    width = own.shape[1]
    deep = w_ref.shape[0]
    pairs = [(w0.at[0], w_ref.at[:, :width]), (w1.at[0], w_ref.at[:, width:])]
    for copy in start_all(pairs, sems):
        copy.wait()
    for c in range(4):
        at = slice(c * deep // 4, (c + 1) * deep // 4)
        out = dot(own[...], w_ref[at, :width], NT) + dot(sib[...], w_ref[at, width:], NT)
        split_store(out, near_ref, far_ref, at)


def out_project(own, sib, pieces):
    pair, width = own.shape
    deep = pieces[0].shape[1]
    out = [
        shape((deep, 2 * width), BF16),
        shape((pair // 2, deep), F32),
        shape((pair // 2, deep), BF16),
    ]
    return call_whole(out_kernel, "out_project", out, pieces, [own, sib], copies=2)


def out_back_kernel(g0, g1, w_ref, gt_ref, own_ref, sib_ref):
    rows = g0.shape[0]
    width = own_ref.shape[1]
    for i, ref in enumerate((g0, g1)):
        at = slice(i * rows, (i + 1) * rows)
        g = ref[...]
        out = dot(g, w_ref[...])
        own_ref[at, :] = out[:, :width].astype(BF16)
        sib_ref[at, :] = out[:, width:].astype(BF16)
        gt_ref[:, at] = g.T


def out_back(g0, g1, weights):
    rows, deep = g0.shape
    width = weights.shape[1] // 2
    out = [
        shape((deep, 2 * rows), BF16),
        shape((2 * rows, width), BF16),
        shape((2 * rows, width), BF16),
    ]
    return call_whole(out_back_kernel, "out_back", out, [], [g0, g1, weights])


EXTRA = 16


def pack_rows(out_ref, one, two, q0, q1, kv0, kv1, hidden):
    rank = lax.axis_index("tp")
    size = lax.axis_size("tp")
    first = lax.axis_index("ctx") == 0
    part = q0.shape[1]
    units = hidden.shape[1] // 2
    out_ref[...] = jnp.zeros_like(out_ref)
    out_ref[0:2, :] = one[0:2, :]
    out_ref[2:4, :] = two[0:2, :]
    out_ref[4:5, :] = one[2:3, :]
    out_ref[5:6, :] = two[2:3, :]
    for row, (mine, other, at) in ((6, (q0, q1, 0)), (7, (kv0, kv1, part))):
        mine = col_sum(mine[:, at : at + part].astype(F32))
        other = col_sum(other[:, at : at + part].astype(F32))
        low, high = jnp.where(first, mine, other), jnp.where(first, other, mine)
        for t in range(size):
            keep = rank == t
            start = 2 * t * part
            out_ref[row : row + 1, start : start + part] = jnp.where(keep, low, 0.0)
            out_ref[row : row + 1, start + part : start + 2 * part] = jnp.where(keep, high, 0.0)
    for t in range(size):
        row = 8 + t
        total = jnp.where(rank == t, hidden[:, :units], 0.0)
        total = total + jnp.where((rank ^ 1) == t, hidden[:, units:], 0.0)
        mine, other = total[:, : units // 2], total[:, units // 2 :]
        out_ref[row : row + 1, : units // 2] = jnp.where(first, mine, other)
        out_ref[row : row + 1, units // 2 :] = jnp.where(first, other, mine)


def input_back_kernel(
    q0, q1, kv0, kv1, w_ref, one, two, hidden, near_ref, far_ref, sib_ref, cat_ref, vec_ref
):
    half, part = q0.shape
    pair, deep = near_ref.shape
    for j, (ref, at) in enumerate(((q0, 0), (q1, 0), (kv0, 0), (kv1, 0), (kv0, part), (kv1, part))):
        count = ref.shape[0]
        cat_ref[:count, j * part : (j + 1) * part] = ref[:, at : at + part]
    sib_ref[:pair, :] = dot(cat_ref[pair:half, :], w_ref[...], NT).astype(BF16)
    out = dot(cat_ref[half + pair :, 2 * part :], w_ref[:, 2 * part :], NT)
    sib_ref[pair:half, :] = out.astype(BF16)
    near_ref[...] = dot(cat_ref[:pair, :], w_ref[...], NT)
    far_ref[...] = dot(cat_ref[half : half + pair, 2 * part :], w_ref[:, 2 * part :], NT)
    pack_rows(vec_ref, one, two, q0, q1, kv0, kv1, hidden)
    sib_ref[half:, :] = vec_ref[...].astype(BF16)


def input_back(q0, q1, kv0, kv1, weights, one, two, hidden):
    half, part = q0.shape
    deep = weights.shape[0]
    pair = half // 2
    out = [shape((pair, deep), F32), shape((pair, deep), F32), shape((half + EXTRA, deep), BF16)]
    scratch = [pltpu.VMEM((kv0.shape[0], 6 * part), BF16), pltpu.VMEM((EXTRA, deep), F32)]
    args = [q0, q1, kv0, kv1, weights, one, two, hidden]
    return call_whole(input_back_kernel, "input_back", out, [], args, scratch)


def fold_kernel(near, far, sent, recv, rest, own_ref, x_ref, y_ref, d_ref, vec_ref):
    rows = own_ref.shape[0]
    pair = 2 * rows
    own_ref[...] = rest[...] + near[:rows, :] + recv[:rows, :].astype(F32)
    vec = sent[2 * pair :, :].astype(F32) + recv[2 * pair :, :].astype(F32)
    vec_ref[...] = vec.astype(BF16)
    for ref, term, at in ((x_ref, near, rows), (y_ref, far, 0), (d_ref, far, rows)):
        start = at if term is near else pair + at
        total = term[at : at + rows, :] + recv[start : start + rows, :].astype(F32)
        ref[:rows, :] = total.astype(BF16)
        ref[rows:, :] = vec.astype(BF16)


def fold(near, far, sent, recv, rest):
    rows, deep = rest.shape
    out = [shape((rows, deep), F32)] + [shape((rows + EXTRA, deep), BF16)] * 3
    out += [shape((EXTRA, deep), BF16)]
    return call_whole(fold_kernel, "fold", out, [], [near, far, sent, recv, rest])


def grad_send_kernel(left, right, out_ref):
    out_ref[...] = dot(left[...], right[...]).astype(BF16)


def grad_send(left, right):
    out = [shape((left.shape[0], right.shape[1]), BF16)]
    return call_whole(grad_send_kernel, "grad_send", out, [], [left, right])[0]


def grad_sum_kernel(left, right, recv, keep_ref, send_ref):
    part = keep_ref.shape[1]
    for ref, at in ((send_ref, slice(part, 2 * part)), (keep_ref, slice(0, part))):
        ref[...] = (dot(left[...], right[:, at]) + recv[:, at].astype(F32)).astype(BF16)


def grad_sum(left, right, recv):
    half = shape((left.shape[0], right.shape[1] // 2), BF16)
    return call_whole(grad_sum_kernel, "grad_sum", [half, half], [], [left, right, recv])


def grad_total_kernel(left, right, recv, out_ref):
    out_ref[...] = (dot(left[...], right[...]) + recv[...].astype(F32)).astype(BF16)


def grad_total(left, right, recv):
    out = [shape((left.shape[0], right.shape[1]), BF16)]
    return call_whole(grad_total_kernel, "grad_total", out, [], [left, right, recv])[0]


def head_grads(left, query, pair):
    half = query.shape[0]
    return jnp.concatenate([dot(left[:, :half], query[...]), dot(left[...], pair[...])], axis=1)


def head_send_kernel(left, query, pair, out_ref):
    out_ref[...] = head_grads(left, query, pair).astype(BF16)


def head_send(left, query, pair):
    out = [shape((left.shape[0], query.shape[1] + pair.shape[1]), BF16)]
    return call_whole(head_send_kernel, "head_send", out, [], [left, query, pair])[0]


def head_sum_kernel(left, query, pair, recv, keep, keep_recv, out_ref):
    width = recv.shape[1]
    total = head_grads(left, query, pair) + recv[...].astype(F32)
    out_ref[:, :width] = total.astype(BF16)
    out_ref[:, width:] = (keep[...].astype(F32) + keep_recv[...].astype(F32)).astype(BF16)


def head_sum(left, query, pair, recv, keep, keep_recv):
    out = [shape((left.shape[0], recv.shape[1] + keep.shape[1]), BF16)]
    args = [left, query, pair, recv, keep, keep_recv]
    return call_whole(head_sum_kernel, "head_sum", out, [], args)[0]


def gelu_pair(values):
    size = jnp.abs(values)
    t = 1.0 / (1.0 + (0.3275911 * math.sqrt(0.5)) * size)
    bell = jnp.exp2(values * values * (-0.5 * LOG2E))
    poly = t * (
        0.5 * 0.254829592
        + t
        * (
            0.5 * -0.284496736
            + t * (0.5 * 1.421413741 + t * (0.5 * -1.453152027 + t * (0.5 * 1.061405429)))
        )
    )
    tail = poly * bell
    cdf = jnp.where(values < 0, tail, 1.0 - tail)
    return values * cdf, cdf + values * bell * (1.0 / math.sqrt(2.0 * math.pi))


def gather_units(refs, w_ref):
    pairs = []
    part = refs[0][0].shape[2]
    for ref, first in refs:
        for j in range(first, ref.shape[0]):
            at = len(pairs) * part
            pairs.append((ref.at[j], w_ref.at[:, at : at + part]))
    return pairs


def up_kernel(
    x0, x1, mine, other, mine_sib, other_sib, bias_ref,
    xt_ref, w_ref, act_own, act_sib, slope_own, slope_sib, x_ref, sems,
):
    rows = x0.shape[0]
    pairs = [(x0, x_ref.at[:rows, :]), (x1, x_ref.at[rows:, :])]
    pairs += gather_units(((mine, 1), (other, 0), (mine_sib, 1), (other_sib, 0)), w_ref)
    copies = start_all(pairs, sems)
    copies[0].wait()
    copies[1].wait()
    units = act_own.shape[1]
    step = mine.shape[2]

    def matmul(c):
        copies[2 + c].wait()
        return dot(x_ref[...], w_ref[:, c * step : (c + 1) * step])

    following = matmul(0)
    for c in range(8):
        pre = following
        if c < 7:
            following = matmul(c + 1)
        act_ref, slope_ref = ((act_own, slope_own), (act_sib, slope_sib))[c // 4]
        at = slice((c % 4) * step, (c % 4 + 1) * step)
        act, slope = gelu_pair(pre + bias_ref[0:1, c * step : (c + 1) * step])
        act_ref[:, at] = act.astype(BF16)
        slope_ref[:, at] = slope.astype(BF16)
    xt_ref[...] = x_ref[...].T


def feed_up(x0, x1, pieces, bias):
    rows, deep = x0.shape
    units = bias.shape[1]
    out = [shape((deep, 2 * rows), BF16), shape((deep, units), BF16)]
    out += [shape((2 * rows, units // 2), BF16)] * 4
    scratch = [pltpu.VMEM((2 * rows, deep), BF16)]
    return call_whole(up_kernel, "feed_up", out, [x0, x1, *pieces], [bias], scratch, 10)


def down_kernel(spots, *refs):
    count = len(spots)
    own, sib, refs = refs[:count], refs[count : 2 * count], refs[2 * count :]
    act_own, act_sib, w_ref, near_ref, far_ref, sems = refs
    deep = near_ref.shape[1]
    units = act_own.shape[1]
    pairs = []
    rows = ring_rows(deep // own[0].shape[0], deep)
    for (piece, start), left, right in zip(spots, own, sib):
        width = left.shape[1]
        pairs.append((left, w_ref.at[rows[piece], start : start + width]))
        pairs.append((right, w_ref.at[rows[piece], units + start : units + start + width]))
    for copy in start_all(pairs, sems):
        copy.wait()
    for c in range(4):
        at = slice(c * deep // 4, (c + 1) * deep // 4)
        out = dot(act_own[...], w_ref[at, :units], NT) + dot(act_sib[...], w_ref[at, units:], NT)
        split_store(out, near_ref, far_ref, at)


def feed_down(act_own, act_sib, spots, own, sib):
    pair, units = act_own.shape
    deep = D
    out = [
        shape((deep, 2 * units), BF16),
        shape((pair // 2, deep), F32),
        shape((pair // 2, deep), BF16),
    ]
    kernel = functools.partial(down_kernel, spots)
    args = [*own, *sib]
    return call_whole(
        kernel, "feed_down", out, args, [act_own, act_sib], copies=2 * len(own)
    )


def feed_back_kernel(
    g0, g1, slope_own, slope_sib, up_ref, down_ref,
    gt_ref, gup_own, gup_sib, bias_ref, near_ref, far_ref, g_ref,
):
    rows, deep = g0.shape
    g_ref[:rows, :] = g0[...]
    g_ref[rows:, :] = g1[...]
    units = gup_own.shape[1]
    step = units // 2
    for c in range(4):
        slope_ref, gup_ref = ((slope_own, gup_own), (slope_sib, gup_sib))[c // 2]
        at = slice((c % 2) * step, (c % 2 + 1) * step)
        grad = dot(g_ref[...], down_ref[:, c * step : (c + 1) * step])
        grad = (grad * slope_ref[:, at].astype(F32)).astype(BF16)
        gup_ref[:, at] = grad
        bias_ref[0:1, c * step : (c + 1) * step] = jnp.sum(
            grad.astype(F32), axis=0, keepdims=True
        )
    for c in range(4):
        at = slice(c * deep // 4, (c + 1) * deep // 4)
        out = dot(gup_own[...], up_ref[at, :units], NT) + dot(gup_sib[...], up_ref[at, units:], NT)
        split_store(out, near_ref, far_ref, at)
    gt_ref[...] = g_ref[...].T


def feed_back(g0, g1, slope_own, slope_sib, up_all, down_all):
    rows, deep = g0.shape
    units = slope_own.shape[1]
    out = [shape((deep, 2 * rows), BF16)]
    out += [shape((2 * rows, units), BF16)] * 2
    out += [shape((1, 2 * units), F32), shape((rows, deep), F32), shape((rows, deep), BF16)]
    args = [g0, g1, slope_own, slope_sib, up_all, down_all]
    scratch = [pltpu.VMEM((2 * rows, deep), BF16)]
    return call_whole(feed_back_kernel, "feed_back", out, [], args, scratch)


def row_mean(values):
    return jnp.mean(values, axis=-1, keepdims=True)


def col_sum(values):
    return jnp.sum(values, axis=0, keepdims=True)


def normalize(values):
    centered = values - row_mean(values)
    inverse = lax.rsqrt(row_mean(centered * centered) + NORM_EPSILON)
    return centered * inverse, inverse


def norm_back(grad_out, normed, inverse, gain):
    grad = grad_out * gain
    return inverse * (grad - row_mean(grad) - normed * row_mean(grad * normed))


def norm_one_kernel(own, part, recv, vec, first_ref, low_ref, normed_ref, inverse_ref):
    attn_out = part[...] + recv[...].astype(F32) + vec[4:5, :]
    normed, inverse = normalize(own[...].astype(F32) + attn_out)
    first = normed * vec[0:1, :] + vec[1:2, :]
    first_ref[...] = first
    low_ref[...] = first.astype(BF16)
    normed_ref[...] = normed
    inverse_ref[...] = inverse


def norm_one(own, part, recv, vec):
    rows, deep = own.shape
    out = [shape((rows, deep), t) for t in (F32, BF16, F32)] + [shape((rows, 1), F32)]
    return call_whole(norm_one_kernel, "norm_one", out, [], [own, part, recv, vec])


def norm_two_kernel(first, part, recv, cotangent, vec, out_ref, grad_ref, low_ref, sums_ref):
    down_out = part[...] + recv[...].astype(F32) + vec[5:6, :]
    normed, inverse = normalize(first[...] + down_out)
    out_ref[...] = (normed * vec[2:3, :] + vec[3:4, :]).astype(BF16)
    given = cotangent[...].astype(F32)
    grad = norm_back(given, normed, inverse, vec[2:3, :])
    grad_ref[...] = grad
    low = grad.astype(BF16)
    low_ref[...] = low
    sums_ref[0:1, :] = col_sum(given * normed)
    sums_ref[1:2, :] = col_sum(given)
    sums_ref[2:3, :] = col_sum(low.astype(F32))


def norm_two(first, part, recv, cotangent, vec):
    rows, deep = first.shape
    out = [shape((rows, deep), t) for t in (BF16, F32, BF16)] + [shape((3, deep), F32)]
    return call_whole(norm_two_kernel, "norm_two", out, [], [first, part, recv, cotangent, vec])


def norm_one_back_kernel(
    grad_second, part, recv, normed, inverse, vec, grad_ref, low_ref, sums_ref
):
    given = grad_second[...] + part[...] + recv[...].astype(F32)
    grad = norm_back(given, normed[...], inverse[...], vec[0:1, :])
    grad_ref[...] = grad
    low = grad.astype(BF16)
    low_ref[...] = low
    sums_ref[0:1, :] = col_sum(given * normed[...])
    sums_ref[1:2, :] = col_sum(given)
    sums_ref[2:3, :] = col_sum(low.astype(F32))


def norm_one_back(grad_second, part, recv, normed, inverse, vec):
    rows, deep = part.shape
    out = [shape((rows, deep), t) for t in (F32, BF16)] + [shape((3, deep), F32)]
    args = [grad_second, part, recv, normed, inverse, vec]
    return call_whole(norm_one_back_kernel, "norm_one_back", out, [], args)


def nesterov(weights, momentum, average, gradient, step_rate):
    momentum_new = MOMENTUM * momentum + gradient
    weight_new = weights - step_rate * (gradient + MOMENTUM * momentum_new)
    return (weight_new, momentum_new, AVERAGE * average + (1.0 - AVERAGE) * weight_new)


def swap_tp(values, bit):
    size = lax.axis_size("tp")
    return lax.ppermute(values, "tp", [(i, i ^ bit) for i in range(size)])


def core(values):
    return swap_tp(values, 1)


def across(values):
    return swap_tp(values, 2)


def swap_ctx(values):
    return lax.ppermute(values, "ctx", [(0, 1), (1, 0)])


def swap_both(values):
    size = lax.axis_size("tp")
    return lax.ppermute(values, ("ctx", "tp"), [(i, i ^ (size + 2)) for i in range(2 * size)])


def sum_fsdp(values):
    size = lax.axis_size("fsdp")

    def swap(values, bit):
        return lax.ppermute(values, "fsdp", [(i, i ^ bit) for i in range(size)])

    if size == 4:
        one, two, three = (swap(values, bit) for bit in (1, 2, 3))
        return (values + one) + (two + three)
    bit = 1
    while bit < size:
        values = values + swap(values, bit)
        bit *= 2
    return values


def gather_fsdp(shard, axis):
    return lax.all_gather(shard, "fsdp", axis=axis, tiled=True)


def ring():
    return lax.axis_size("fsdp") == 4


def shift_fsdp(values, step):
    size = lax.axis_size("fsdp")
    return lax.ppermute(values, "fsdp", [(i, (i + step) % size) for i in range(size)])


def gather_pieces(shard, axis):
    if not ring():
        return [gather_fsdp(shard, axis)]
    return [shard] + [shift_fsdp(shard, -s) for s in range(1, lax.axis_size("fsdp"))]


def scatter_pieces(grads):
    if not ring():
        return scatter_fsdp(grads, 0).astype(F32)
    size = lax.axis_size("fsdp")
    rank = lax.axis_index("fsdp")
    rows = grads.shape[0] // size
    pieces = [
        lax.dynamic_slice_in_dim(grads, lax.rem(rank + s, size) * rows, rows) for s in range(size)
    ]
    total = pieces[0].astype(F32)
    for s in (2, 1, 3):
        total = total + shift_fsdp(pieces[s], s).astype(F32)
    return total


def scatter_fsdp(grads, axis):
    return lax.psum_scatter(grads, "fsdp", scatter_dimension=axis, tiled=True)


def halves(values, axis=-1):
    low, high = jnp.split(values, 2, axis=axis)
    first = lax.axis_index("ctx") == 0
    return jnp.where(first, low, high), jnp.where(first, high, low)


def join(mine, other, axis=-1):
    first = lax.axis_index("ctx") == 0
    low, high = jnp.where(first, mine, other), jnp.where(first, other, mine)
    return jnp.concatenate([low, high], axis=axis)


def quarters(mine):
    return jnp.stack(jnp.split(mine, 2, axis=1))


def after(values, *others):
    return lax.optimization_barrier((values,) + others)[0]


def on_device(
    tokens,
    cotangent,
    attn_weight,
    attn_momentum,
    attn_average,
    ffn_weight,
    ffn_momentum,
    ffn_average,
    vector_weight,
    vector_momentum,
    vector_average,
):
    tp_rank = lax.axis_index("tp")
    sib_rank = tp_rank ^ 1
    head_width = attn_weight.shape[2]
    unit_width = ffn_weight.shape[2]
    token_count = LEN * lax.axis_size("fsdp")
    matrix_rate = MATRIX_RATE / math.sqrt(token_count)
    vector_rate = VECTOR_RATE / math.sqrt(token_count)

    attn_low, attn_high = halves(attn_weight.astype(BF16))
    qkv_mine = gather_pieces(attn_low[:3], 1)

    own = tokens[0]
    rows = own.shape[0]
    pair = 2 * rows
    half = 4 * rows
    beside = across(own)
    facing = swap_ctx(own)
    diagonal = swap_both(own)
    if ring():
        others = swap_ctx(after(jnp.stack(qkv_mine[1:]), beside, facing))
        qkv_other = [attn_high[:3]] + [others[s] for s in range(len(qkv_mine) - 1)]
    else:
        qkv_other = [swap_ctx(qkv_mine[0])]
    up_low = quarters(halves(ffn_weight[0].astype(BF16))[0])
    out_low = jnp.concatenate([attn_low[3], attn_high[3]], axis=1)
    out_up = gather_fsdp(after(jnp.concatenate([out_low[None], up_low]), *qkv_mine[-3:]), 1)
    blocks = [own, beside, core(own), core(beside), facing, diagonal, core(facing), core(diagonal)]

    vec = vector_weight[: 6 * D].reshape(6, D)

    def columns(start, width):
        part = lax.dynamic_slice_in_dim(vector_weight, start, width)
        return jnp.concatenate(halves(part))

    biases = jnp.stack(
        [
            columns(6 * D + tp_rank * head_width, head_width),
            columns(7 * D + tp_rank * head_width, head_width),
        ]
    )
    bias_hidden = jnp.concatenate(
        [
            columns(8 * D + tp_rank * unit_width, unit_width),
            columns(8 * D + sib_rank * unit_width, unit_width),
        ]
    )[None]

    token_t, qkv_w, queries, keys, values = project(blocks, qkv_mine, qkv_other, biases)
    down_low = jnp.concatenate(halves(ffn_weight[1].astype(BF16)), axis=1)
    mixed_own, mixed_sib, lse = attend(queries, keys, values)
    down_low = after(down_low, mixed_own)
    if ring():
        low, high = jnp.split(down_low, 2, axis=1)
        spots = ((0, 0), (1, 0), (3, 0), (2, 0), (2, low.shape[1]))
        down_w = [down_low, shift_fsdp(down_low, -1), shift_fsdp(down_low, -3)]
        down_w += [shift_fsdp(low, -2), shift_fsdp(high, -2)]
    else:
        spots = ((0, 0),)
        down_w = [gather_fsdp(down_low, 0)]
    mixed_recv = core(mixed_sib)
    out_up = after(out_up, mixed_own)
    out_up_sib = core(out_up)
    up_other = swap_ctx(out_up[1:])
    out_w, attn_part, attn_far = out_project(mixed_own, mixed_recv, [out_up, out_up_sib])
    attn_recv = across(attn_far)
    if ring():
        attn_recv = after(attn_recv, down_w[1], down_w[2])
    first, first_low, normed_one, inverse_one = norm_one(own, attn_part, attn_recv, vec)
    first_beside = across(first_low)

    if ring():
        first_beside = after(first_beside, down_w[3])
    up_other = after(up_other, first_beside)
    first_t, up_all, hidden_own, hidden_sib, slope_own, slope_sib = feed_up(
        first_low, first_beside, [out_up, up_other, out_up_sib, core(up_other)], bias_hidden
    )
    if ring():
        down_w[4] = after(down_w[4], hidden_own)
    down_all, down_part, down_far = feed_down(
        hidden_own, hidden_sib, spots, down_w, [core(w) for w in down_w]
    )
    layer_out, grad_second, grad_down, sums_two = norm_two(
        first, down_part, across(down_far), cotangent[0], vec
    )
    grad_down_t, grad_up_own, grad_up_sib, grad_bias_hidden, first_part, first_far = feed_back(
        grad_down, across(grad_down), slope_own, slope_sib, up_all, down_all
    )
    down_sib = grad_send(grad_down_t, hidden_sib)
    up_sib = grad_send(first_t, grad_up_sib)
    first_recv = after(across(first_far), down_sib, up_sib)
    grad_res, grad_attn, sums_one = norm_one_back(
        grad_second, first_part, first_recv, normed_one, inverse_one, vec
    )
    grad_attn_beside = across(grad_attn)
    down_sum = grad_total(grad_down_t, hidden_own, after(core(down_sib), grad_attn))
    up_keep, up_send = grad_sum(first_t, grad_up_own, after(core(up_sib), grad_attn))

    def finish(mine):
        return join(mine, swap_ctx(mine)).astype(F32)

    def finish_whole(part):
        mine, other = jnp.split(part.astype(F32), 2, axis=1)
        recv_other, recv_mine = jnp.split(swap_ctx(part).astype(F32), 2, axis=1)
        return join(mine + recv_mine, other + recv_other)

    down_owned = scatter_fsdp(down_sum, 0)
    up_recv = swap_ctx(up_send)

    grad_attn_beside = after(grad_attn_beside, down_sum, up_send)
    grad_attn_t, grad_mixed_own, grad_mixed_sib = out_back(grad_attn, grad_attn_beside, out_w)
    grad_mixed = (grad_mixed_own, core(grad_mixed_sib))

    up_recv = after(up_recv, grad_mixed_sib)
    up_sum = (up_keep.astype(F32) + up_recv.astype(F32)).astype(BF16)
    up_owned = scatter_pieces(up_sum).astype(BF16)
    mixed = (mixed_own, mixed_sib)
    heads = (queries, keys, values, mixed)
    grad_mixed = (grad_mixed[0], after(grad_mixed[1], up_sum))
    query_other, kv_other = attend_back(*heads, grad_mixed, lse, 1)
    send = head_send(token_t, query_other, kv_other)
    out_sib = grad_send(after(grad_attn_t, query_other), mixed_recv)
    out_keep, out_send = grad_sum(grad_attn_t, mixed_own, core(out_sib))
    grad_mixed = (grad_mixed[0], after(grad_mixed[1], up_sum, send, out_send))
    recv = swap_ctx(send)
    query_mine, kv_mine = attend_back(*heads, grad_mixed, lse, 0)
    query_mine = after(query_mine, up_owned)
    part = head_width // 2
    near, far, sibling = input_back(
        query_mine, query_other, kv_mine, kv_other, qkv_w, sums_one, sums_two, grad_bias_hidden
    )
    sib_recv = core(sibling)
    qkvo_sum = head_sum(token_t, query_mine, kv_mine, recv, out_keep, swap_ctx(out_send))
    qkvo_mine = scatter_fsdp(qkvo_sum, 0)
    sib_recv = after(sib_recv, qkvo_sum)
    input_part, to_x, to_y, to_d, vec_part = fold(near, far, sibling, sib_recv, grad_res)
    from_x, from_y, from_d = across(to_x), swap_ctx(to_y), swap_both(to_d)
    input_grad = input_part
    for term in (from_x, from_y, from_d):
        input_grad = input_grad + term[:rows].astype(F32)
    vec_x, vec_y, vec_d = (term[rows:].astype(F32) for term in (from_x, from_y, from_d))
    vec_plane = (vec_part.astype(F32) + vec_x) + (vec_y + vec_d)
    vector_grad = sum_fsdp(vec_plane[:12]).reshape(-1)

    down_grad, up_grad = finish_whole(down_owned), finish(up_owned)
    qkvo_mine = after(qkvo_mine, input_grad, down_grad, up_grad, vec_plane)
    qkvo_other = swap_ctx(qkvo_mine)
    attn_grad = jnp.stack(
        [
            join(qkvo_mine[:, j * part : (j + 1) * part], qkvo_other[:, j * part : (j + 1) * part])
            for j in range(4)
        ]
    ).astype(F32)
    vector_new, vector_momentum_new, vector_average_new = nesterov(
        vector_weight, vector_momentum, vector_average, vector_grad, vector_rate
    )
    ffn_grad = jnp.stack([up_grad, down_grad])
    attn_new, attn_momentum_new, attn_average_new = nesterov(
        attn_weight, attn_momentum, attn_average, attn_grad, matrix_rate
    )
    ffn_new, ffn_momentum_new, ffn_average_new = nesterov(
        ffn_weight, ffn_momentum, ffn_average, ffn_grad, matrix_rate
    )
    return (
        layer_out[None],
        input_grad[None],
        attn_grad,
        attn_new,
        attn_momentum_new,
        attn_average_new,
        attn_new.astype(BF16),
        ffn_grad,
        ffn_new,
        ffn_momentum_new,
        ffn_average_new,
        ffn_new.astype(BF16),
        vector_grad,
        vector_new,
        vector_momentum_new,
        vector_average_new,
    )


def solution(mesh):
    rows = P("fsdp", ("ctx", "tp"), None)
    weight = P(None, "fsdp", "tp")
    return jax.shard_map(
        on_device,
        mesh=mesh,
        in_specs=(rows, rows) + (weight,) * 6 + (P(),) * 3,
        out_specs=(rows, rows) + (weight,) * 10 + (P(),) * 4,
        check_vma=False,
    )
```

```python
import functools
import math

import jax
import jax.numpy as jnp
from jax import lax
from jax.experimental import pallas as pl
from jax.experimental.pallas import tpu as pltpu
from jax.sharding import PartitionSpec as P

D = 1024
FF = 4096
HEAD_DIM = 64
LEN = 2048

NORM_EPSILON = 1e-05
MOMENTUM = 0.5
AVERAGE = 0.5
MATRIX_RATE = 0.1
VECTOR_RATE = 0.3

SCALE = HEAD_DIM ** (-0.5)
LOG2E = math.log2(math.e)
F32 = jnp.float32
BF16 = jnp.bfloat16
NT = (((1,), (1,)), ((), ()))
TN = (((0,), (0,)), ((), ()))
NN = (((1,), (0,)), ((), ()))


def dot(left, right, dims=NN):
    return lax.dot_general(left, right, dims, preferred_element_type=F32)


VMEM = pl.BlockSpec(memory_space=pltpu.VMEM)
ANY = pl.BlockSpec(memory_space=pl.ANY)
MEGA = 1024 * 1024
WORK_UNIT = 1.2e10


WORK = {
    "project": 0.001,
    "attend": 0.001,
    "out_project": 0.001,
    "norm_one": 1.5,
    "feed_up": 8,
    "feed_down": 4,
    "norm_two": 2,
    "feed_back": 8,
    "grad_send": 10,
    "grad_sum": 3,
    "norm_one_back": 2,
    "out_back": 2,
    "attend_back": 12,
    "head_send": 3,
    "head_sum": 4,
    "input_back": 4,
    "fold": 1.5,
    "grad_total": 3,
}


def cost(name):
    flops = int(WORK[name] * WORK_UNIT)
    return pl.CostEstimate(flops=flops, bytes_accessed=1, transcendentals=0)


def shape(dims, dtype):
    return jax.ShapeDtypeStruct(tuple(dims), dtype)


def tile(i, size):
    return pl.ds(pl.multiple_of(i * size, size), size)


def call_whole(kernel, name, out_shape, far_args, near_args, scratch=(), copies=0):
    scratch = list(scratch)
    if copies:
        scratch.append(pltpu.SemaphoreType.DMA((copies,)))
    return pl.pallas_call(
        kernel,
        in_specs=[ANY] * len(far_args) + [VMEM] * len(near_args),
        out_specs=[VMEM] * len(out_shape),
        out_shape=list(out_shape),
        scratch_shapes=scratch,
        compiler_params=pltpu.CompilerParams(vmem_limit_bytes=8 * MEGA),
        cost_estimate=cost(name),
        name=name,
    )(*far_args, *near_args)


def start_all(pairs, sems):
    copies = [pltpu.make_async_copy(src, dst, sems.at[i]) for i, (src, dst) in enumerate(pairs)]
    for copy in copies:
        copy.start()
    return copies


def head_masks(width):
    lane = lax.broadcasted_iota(jnp.int32, (1, width), 1) // HEAD_DIM
    return [(lane == h).astype(BF16) for h in range(width // HEAD_DIM)]


def attend_kernel(chunk, q_ref, k_ref, v_ref, own_ref, sib_ref, lse_ref, vt_ref):
    heads = q_ref.shape[1] // HEAD_DIM
    count = k_ref.shape[0]
    step = pl.program_id(0)

    @pl.when(step == 0)
    def _():
        vt_ref[...] = v_ref[...].T

    queries = q_ref[...]
    masked = [queries * mask for mask in head_masks(q_ref.shape[1])]
    units = [(h, c) for h in range(heads) for c in range(0, count, chunk)]

    def scores_of(unit):
        h, c = unit
        return dot(k_ref[c : c + chunk, :], masked[h], NT)

    tops, totals, outs = {}, {}, {}
    scores = scores_of(units[0])
    for i, unit in enumerate(units):
        current = scores
        if i + 1 < len(units):
            scores = scores_of(units[i + 1])
        h, c = unit
        top = jnp.max(current, axis=0, keepdims=True)
        weights = jnp.exp2((current - top) * (SCALE * LOG2E))
        tops[unit] = top
        totals[unit] = jnp.sum(weights, axis=0, keepdims=True)
        outs[unit] = dot(
            vt_ref[h * HEAD_DIM : (h + 1) * HEAD_DIM, c : c + chunk], weights.astype(BF16)
        )
    heads_out = []
    for h in range(heads):
        mine = [(h, c) for c in range(0, count, chunk)]
        top = functools.reduce(jnp.maximum, [tops[u] for u in mine])
        share = [jnp.exp2((tops[u] - top) * (SCALE * LOG2E)) for u in mine]
        total = sum(totals[u] * f for u, f in zip(mine, share))
        out = sum(outs[u] * f for u, f in zip(mine, share))
        heads_out.append(out / total)
        lse_ref[h : h + 1, :] = top * (SCALE * LOG2E) + jnp.log2(total)
    mixed = jnp.concatenate(heads_out, axis=0).T.astype(BF16)
    steps = pl.num_programs(0)

    @pl.when(step < steps // 2)
    def _():
        own_ref[...] = mixed

    @pl.when(step >= steps // 2)
    def _():
        sib_ref[...] = mixed


def attend(queries, keys, values):
    rows, width = queries.shape
    block = min(256, rows // 2)
    steps = rows // block
    heads = width // HEAD_DIM
    half_blocks = steps // 2
    return pl.pallas_call(
        functools.partial(attend_kernel, min(512, keys.shape[0])),
        grid=(steps,),
        in_specs=[
            pl.BlockSpec((block, width), lambda i: (i, 0)),
            pl.BlockSpec(keys.shape, lambda i: (0, 0)),
            pl.BlockSpec(values.shape, lambda i: (0, 0)),
        ],
        out_specs=[
            pl.BlockSpec((block, width), lambda i: (jnp.minimum(i, half_blocks - 1), 0)),
            pl.BlockSpec((block, width), lambda i: (jnp.maximum(i - half_blocks, 0), 0)),
            pl.BlockSpec((heads, block), lambda i: (0, i)),
        ],
        out_shape=[
            shape((rows // 2, width), BF16),
            shape((rows // 2, width), BF16),
            shape((heads, rows), F32),
        ],
        scratch_shapes=[pltpu.VMEM((width, keys.shape[0]), BF16)],
        compiler_params=pltpu.CompilerParams(vmem_limit_bytes=16 * MEGA),
        cost_estimate=cost("attend"),
        name="attend",
    )(queries, keys, values)


def attend_back_kernel(
    part, q_ref, k_ref, v_ref, o0_ref, o1_ref, g0_ref, g1_ref, lse_ref,
    dq_ref, dkv_ref, kt_ref, dk_acc, dv_acc, o_ref, g_ref,
):
    width = q_ref.shape[1]
    heads = width // HEAD_DIM
    step = pl.program_id(0)
    steps = pl.num_programs(0)

    @pl.when(step == 0)
    def _():
        kt_ref[...] = k_ref[...].T
        dk_acc[...] = jnp.zeros_like(dk_acc)
        dv_acc[...] = jnp.zeros_like(dv_acc)

    @pl.when(step < steps // 2)
    def _():
        o_ref[...] = o0_ref[...]
        g_ref[...] = g0_ref[...]

    @pl.when(step >= steps // 2)
    def _():
        o_ref[...] = o1_ref[...]
        g_ref[...] = g1_ref[...]

    queries = q_ref[...]
    grads = g_ref[...]
    masks = head_masks(width)
    product = (o_ref[...].astype(F32) * grads.astype(F32)).T
    outs, probs, gscores, qms, gms = [], [], [], [], []
    for h in range(heads):
        qm = queries * masks[h]
        gm = grads * masks[h]
        delta = jnp.sum(product[h * HEAD_DIM : (h + 1) * HEAD_DIM, :], axis=0, keepdims=True)
        scores = dot(k_ref[...], qm, NT)
        row = part * heads + h
        prob = jnp.exp2(scores * (SCALE * LOG2E) - lse_ref[row : row + 1, :])
        grad_prob = dot(v_ref[...], gm, NT)
        gscore = (prob * (grad_prob - delta)).astype(BF16)
        outs.append(dot(kt_ref[h * HEAD_DIM : (h + 1) * HEAD_DIM, :], gscore))
        probs.append(prob.astype(BF16))
        gscores.append(gscore)
        qms.append(qm)
        gms.append(gm)
    dv_acc[...] += dot(jnp.concatenate(probs, axis=1), jnp.concatenate(gms, axis=0))
    dk_acc[...] += dot(jnp.concatenate(gscores, axis=1), jnp.concatenate(qms, axis=0))
    dq_ref[...] = (jnp.concatenate(outs, axis=0).T * SCALE).astype(BF16)

    @pl.when(step == steps - 1)
    def _():
        dkv_ref[:, :width] = (dk_acc[...] * SCALE).astype(BF16)
        dkv_ref[:, width:] = dv_acc[...].astype(BF16)


def attend_back(queries, keys, values, mixed, grads, lse, part):
    rows, both = queries.shape
    count = keys.shape[0]
    width = both // 2
    block = min(256, rows // 2)
    half_blocks = rows // 2 // block
    row_spec = pl.BlockSpec((block, width), lambda i: (i, part))
    own_spec = pl.BlockSpec((block, width), lambda i: (jnp.minimum(i, half_blocks - 1), part))
    sib_spec = pl.BlockSpec((block, width), lambda i: (jnp.maximum(i - half_blocks, 0), part))
    full_spec = pl.BlockSpec((count, width), lambda i: (0, part))
    lse_spec = pl.BlockSpec((lse.shape[0], block), lambda i: (0, i))
    return pl.pallas_call(
        functools.partial(attend_back_kernel, part),
        grid=(rows // block,),
        in_specs=[row_spec, full_spec, full_spec] + [own_spec, sib_spec] * 2 + [lse_spec],
        out_specs=[
            pl.BlockSpec((block, width), lambda i: (i, 0)),
            pl.BlockSpec((count, both), lambda i: (0, 0)),
        ],
        out_shape=[shape((rows, width), BF16), shape((count, both), BF16)],
        scratch_shapes=[
            pltpu.VMEM((width, count), BF16),
            pltpu.VMEM((count, width), F32),
            pltpu.VMEM((count, width), F32),
            pltpu.VMEM((block, width), BF16),
            pltpu.VMEM((block, width), BF16),
        ],
        compiler_params=pltpu.CompilerParams(vmem_limit_bytes=16 * MEGA),
        cost_estimate=cost("attend_back"),
        name="attend_back",
    )(queries, keys, values, *mixed, *grads, lse)


def ring_rows(count, deep):
    size = deep // count
    rank = lax.axis_index("fsdp")
    return [tile(lax.rem(rank + s, count), size) if count > 1 else tile(0, size) for s in range(count)]


def project_kernel(count, *refs):
    blocks, refs = refs[:8], refs[8:]
    mine, refs = refs[:count], refs[count:]
    other, refs = refs[:count], refs[count:]
    bias_ref, xt_ref, w_ref, q_ref, k_ref, v_ref, x_ref, sems = refs
    rows = blocks[0].shape[0]
    deep = x_ref.shape[1]
    part = mine[0].shape[2]
    width = 2 * part
    pairs = []
    for at, low, high in zip(ring_rows(count, deep), mine, other):
        for j in range(3):
            pairs.append((low.at[j], w_ref.at[at, j * width : j * width + part]))
            pairs.append((high.at[j], w_ref.at[at, j * width + part : (j + 1) * width]))
    weights = len(pairs)
    for i in range(8):
        pairs.append((blocks[i], x_ref.at[i * rows : (i + 1) * rows, :]))
    copies = start_all(pairs, sems)
    for copy in copies[:weights]:
        copy.wait()
    for i in range(4):
        at = slice(i * 2 * rows, (i + 1) * 2 * rows)
        for copy in copies[weights + 2 * i : weights + 2 * i + 2]:
            copy.wait()
        x = x_ref[at, :]
        if i < 2:
            out = dot(x, w_ref[...])
            q_ref[at, :] = (out[:, :width] + bias_ref[0:1, :]).astype(BF16)
            out = out[:, width:]
        else:
            out = dot(x, w_ref[:, width:])
        k_ref[at, :] = out[:, :width].astype(BF16)
        v_ref[at, :] = (out[:, width:] + bias_ref[1:2, :]).astype(BF16)
        xt_ref[:, at] = x.T


def project(blocks, mine, other, biases):
    rows, deep = blocks[0].shape
    width = biases.shape[1]
    out = [
        shape((deep, 8 * rows), BF16),
        shape((deep, 3 * width), BF16),
        shape((4 * rows, width), BF16),
        shape((8 * rows, width), BF16),
        shape((8 * rows, width), BF16),
    ]
    scratch = [pltpu.VMEM((8 * rows, deep), BF16)]
    kernel = functools.partial(project_kernel, len(mine))
    args = [*blocks, *mine, *other]
    return call_whole(kernel, "project", out, args, [biases], scratch, 8 + 6 * len(mine))


def split_store(out, near_ref, far_ref, at):
    rows = near_ref.shape[0]
    near_ref[:, at] = out[:rows]
    far_ref[:, at] = out[rows:].astype(BF16)


def out_kernel(w0, w1, own, sib, w_ref, near_ref, far_ref, sems):
    width = own.shape[1]
    deep = w_ref.shape[0]
    pairs = [(w0.at[0], w_ref.at[:, :width]), (w1.at[0], w_ref.at[:, width:])]
    for copy in start_all(pairs, sems):
        copy.wait()
    for c in range(4):
        at = slice(c * deep // 4, (c + 1) * deep // 4)
        out = dot(own[...], w_ref[at, :width], NT) + dot(sib[...], w_ref[at, width:], NT)
        split_store(out, near_ref, far_ref, at)


def out_project(own, sib, pieces):
    pair, width = own.shape
    deep = pieces[0].shape[1]
    out = [
        shape((deep, 2 * width), BF16),
        shape((pair // 2, deep), F32),
        shape((pair // 2, deep), BF16),
    ]
    return call_whole(out_kernel, "out_project", out, pieces, [own, sib], copies=2)


def out_back_kernel(g0, g1, w_ref, gt_ref, own_ref, sib_ref):
    rows = g0.shape[0]
    width = own_ref.shape[1]
    for i, ref in enumerate((g0, g1)):
        at = slice(i * rows, (i + 1) * rows)
        g = ref[...]
        out = dot(g, w_ref[...])
        own_ref[at, :] = out[:, :width].astype(BF16)
        sib_ref[at, :] = out[:, width:].astype(BF16)
        gt_ref[:, at] = g.T


def out_back(g0, g1, weights):
    rows, deep = g0.shape
    width = weights.shape[1] // 2
    out = [
        shape((deep, 2 * rows), BF16),
        shape((2 * rows, width), BF16),
        shape((2 * rows, width), BF16),
    ]
    return call_whole(out_back_kernel, "out_back", out, [], [g0, g1, weights])


EXTRA = 16


def pack_rows(out_ref, one, two, q0, q1, kv0, kv1, hidden):
    rank = lax.axis_index("tp")
    size = lax.axis_size("tp")
    first = lax.axis_index("ctx") == 0
    part = q0.shape[1]
    units = hidden.shape[1] // 2
    out_ref[...] = jnp.zeros_like(out_ref)
    out_ref[0:2, :] = one[0:2, :]
    out_ref[2:4, :] = two[0:2, :]
    out_ref[4:5, :] = one[2:3, :]
    out_ref[5:6, :] = two[2:3, :]
    for row, (mine, other, at) in ((6, (q0, q1, 0)), (7, (kv0, kv1, part))):
        mine = col_sum(mine[:, at : at + part].astype(F32))
        other = col_sum(other[:, at : at + part].astype(F32))
        low, high = jnp.where(first, mine, other), jnp.where(first, other, mine)
        for t in range(size):
            keep = rank == t
            start = 2 * t * part
            out_ref[row : row + 1, start : start + part] = jnp.where(keep, low, 0.0)
            out_ref[row : row + 1, start + part : start + 2 * part] = jnp.where(keep, high, 0.0)
    for t in range(size):
        row = 8 + t
        total = jnp.where(rank == t, hidden[:, :units], 0.0)
        total = total + jnp.where((rank ^ 1) == t, hidden[:, units:], 0.0)
        mine, other = total[:, : units // 2], total[:, units // 2 :]
        out_ref[row : row + 1, : units // 2] = jnp.where(first, mine, other)
        out_ref[row : row + 1, units // 2 :] = jnp.where(first, other, mine)


def input_back_kernel(
    q0, q1, kv0, kv1, w_ref, one, two, hidden, near_ref, far_ref, sib_ref, cat_ref, vec_ref
):
    half, part = q0.shape
    pair, deep = near_ref.shape
    for j, (ref, at) in enumerate(((q0, 0), (q1, 0), (kv0, 0), (kv1, 0), (kv0, part), (kv1, part))):
        count = ref.shape[0]
        cat_ref[:count, j * part : (j + 1) * part] = ref[:, at : at + part]
    sib_ref[:pair, :] = dot(cat_ref[pair:half, :], w_ref[...], NT).astype(BF16)
    out = dot(cat_ref[half + pair :, 2 * part :], w_ref[:, 2 * part :], NT)
    sib_ref[pair:half, :] = out.astype(BF16)
    near_ref[...] = dot(cat_ref[:pair, :], w_ref[...], NT)
    far_ref[...] = dot(cat_ref[half : half + pair, 2 * part :], w_ref[:, 2 * part :], NT)
    pack_rows(vec_ref, one, two, q0, q1, kv0, kv1, hidden)
    sib_ref[half:, :] = vec_ref[...].astype(BF16)


def input_back(q0, q1, kv0, kv1, weights, one, two, hidden):
    half, part = q0.shape
    deep = weights.shape[0]
    pair = half // 2
    out = [shape((pair, deep), F32), shape((pair, deep), F32), shape((half + EXTRA, deep), BF16)]
    scratch = [pltpu.VMEM((kv0.shape[0], 6 * part), BF16), pltpu.VMEM((EXTRA, deep), F32)]
    args = [q0, q1, kv0, kv1, weights, one, two, hidden]
    return call_whole(input_back_kernel, "input_back", out, [], args, scratch)


def fold_kernel(near, far, sent, recv, rest, own_ref, x_ref, y_ref, d_ref, vec_ref):
    rows = own_ref.shape[0]
    pair = 2 * rows
    own_ref[...] = rest[...] + near[:rows, :] + recv[:rows, :].astype(F32)
    vec = sent[2 * pair :, :].astype(F32) + recv[2 * pair :, :].astype(F32)
    vec_ref[...] = vec.astype(BF16)
    for ref, term, at in ((x_ref, near, rows), (y_ref, far, 0), (d_ref, far, rows)):
        start = at if term is near else pair + at
        total = term[at : at + rows, :] + recv[start : start + rows, :].astype(F32)
        ref[:rows, :] = total.astype(BF16)
        ref[rows:, :] = vec.astype(BF16)


def fold(near, far, sent, recv, rest):
    rows, deep = rest.shape
    out = [shape((rows, deep), F32)] + [shape((rows + EXTRA, deep), BF16)] * 3
    out += [shape((EXTRA, deep), BF16)]
    return call_whole(fold_kernel, "fold", out, [], [near, far, sent, recv, rest])


def grad_send_kernel(left, right, out_ref):
    out_ref[...] = dot(left[...], right[...]).astype(BF16)


def grad_send(left, right):
    out = [shape((left.shape[0], right.shape[1]), BF16)]
    return call_whole(grad_send_kernel, "grad_send", out, [], [left, right])[0]


def grad_sum_kernel(left, right, recv, keep_ref, send_ref):
    part = keep_ref.shape[1]
    for ref, at in ((send_ref, slice(part, 2 * part)), (keep_ref, slice(0, part))):
        ref[...] = (dot(left[...], right[:, at]) + recv[:, at].astype(F32)).astype(BF16)


def grad_sum(left, right, recv):
    half = shape((left.shape[0], right.shape[1] // 2), BF16)
    return call_whole(grad_sum_kernel, "grad_sum", [half, half], [], [left, right, recv])


def grad_total_kernel(left, right, recv, out_ref):
    out_ref[...] = (dot(left[...], right[...]) + recv[...].astype(F32)).astype(BF16)


def grad_total(left, right, recv):
    out = [shape((left.shape[0], right.shape[1]), BF16)]
    return call_whole(grad_total_kernel, "grad_total", out, [], [left, right, recv])[0]


def head_grads(left, query, pair):
    half = query.shape[0]
    return jnp.concatenate([dot(left[:, :half], query[...]), dot(left[...], pair[...])], axis=1)


def head_send_kernel(left, query, pair, out_ref):
    out_ref[...] = head_grads(left, query, pair).astype(BF16)


def head_send(left, query, pair):
    out = [shape((left.shape[0], query.shape[1] + pair.shape[1]), BF16)]
    return call_whole(head_send_kernel, "head_send", out, [], [left, query, pair])[0]


def head_sum_kernel(left, query, pair, recv, keep, keep_recv, out_ref):
    width = recv.shape[1]
    total = head_grads(left, query, pair) + recv[...].astype(F32)
    out_ref[:, :width] = total.astype(BF16)
    out_ref[:, width:] = (keep[...].astype(F32) + keep_recv[...].astype(F32)).astype(BF16)


def head_sum(left, query, pair, recv, keep, keep_recv):
    out = [shape((left.shape[0], recv.shape[1] + keep.shape[1]), BF16)]
    args = [left, query, pair, recv, keep, keep_recv]
    return call_whole(head_sum_kernel, "head_sum", out, [], args)[0]


def gelu_pair(values):
    size = jnp.abs(values)
    t = 1.0 / (1.0 + (0.3275911 * math.sqrt(0.5)) * size)
    bell = jnp.exp2(values * values * (-0.5 * LOG2E))
    poly = t * (
        0.5 * 0.254829592
        + t
        * (
            0.5 * -0.284496736
            + t * (0.5 * 1.421413741 + t * (0.5 * -1.453152027 + t * (0.5 * 1.061405429)))
        )
    )
    tail = poly * bell
    cdf = jnp.where(values < 0, tail, 1.0 - tail)
    return values * cdf, cdf + values * bell * (1.0 / math.sqrt(2.0 * math.pi))


def gather_units(refs, w_ref):
    pairs = []
    part = refs[0][0].shape[2]
    for ref, first in refs:
        for j in range(first, ref.shape[0]):
            at = len(pairs) * part
            pairs.append((ref.at[j], w_ref.at[:, at : at + part]))
    return pairs


def up_kernel(
    x0, x1, mine, other, mine_sib, other_sib, bias_ref,
    xt_ref, w_ref, act_own, act_sib, slope_own, slope_sib, x_ref, sems,
):
    rows = x0.shape[0]
    pairs = [(x0, x_ref.at[:rows, :]), (x1, x_ref.at[rows:, :])]
    pairs += gather_units(((mine, 1), (other, 0), (mine_sib, 1), (other_sib, 0)), w_ref)
    copies = start_all(pairs, sems)
    copies[0].wait()
    copies[1].wait()
    units = act_own.shape[1]
    step = mine.shape[2]

    def matmul(c):
        copies[2 + c].wait()
        return dot(x_ref[...], w_ref[:, c * step : (c + 1) * step])

    following = matmul(0)
    for c in range(8):
        pre = following
        if c < 7:
            following = matmul(c + 1)
        act_ref, slope_ref = ((act_own, slope_own), (act_sib, slope_sib))[c // 4]
        at = slice((c % 4) * step, (c % 4 + 1) * step)
        act, slope = gelu_pair(pre + bias_ref[0:1, c * step : (c + 1) * step])
        act_ref[:, at] = act.astype(BF16)
        slope_ref[:, at] = slope.astype(BF16)
    xt_ref[...] = x_ref[...].T


def feed_up(x0, x1, pieces, bias):
    rows, deep = x0.shape
    units = bias.shape[1]
    out = [shape((deep, 2 * rows), BF16), shape((deep, units), BF16)]
    out += [shape((2 * rows, units // 2), BF16)] * 4
    scratch = [pltpu.VMEM((2 * rows, deep), BF16)]
    return call_whole(up_kernel, "feed_up", out, [x0, x1, *pieces], [bias], scratch, 10)


def down_kernel(spots, *refs):
    count = len(spots)
    own, sib, refs = refs[:count], refs[count : 2 * count], refs[2 * count :]
    act_own, act_sib, w_ref, near_ref, far_ref, sems = refs
    deep = near_ref.shape[1]
    units = act_own.shape[1]
    pairs = []
    rows = ring_rows(deep // own[0].shape[0], deep)
    for (piece, start), left, right in zip(spots, own, sib):
        width = left.shape[1]
        pairs.append((left, w_ref.at[rows[piece], start : start + width]))
        pairs.append((right, w_ref.at[rows[piece], units + start : units + start + width]))
    for copy in start_all(pairs, sems):
        copy.wait()
    for c in range(4):
        at = slice(c * deep // 4, (c + 1) * deep // 4)
        out = dot(act_own[...], w_ref[at, :units], NT) + dot(act_sib[...], w_ref[at, units:], NT)
        split_store(out, near_ref, far_ref, at)


def feed_down(act_own, act_sib, spots, own, sib):
    pair, units = act_own.shape
    deep = D
    out = [
        shape((deep, 2 * units), BF16),
        shape((pair // 2, deep), F32),
        shape((pair // 2, deep), BF16),
    ]
    kernel = functools.partial(down_kernel, spots)
    args = [*own, *sib]
    return call_whole(
        kernel, "feed_down", out, args, [act_own, act_sib], copies=2 * len(own)
    )


def feed_back_kernel(
    g0, g1, slope_own, slope_sib, up_ref, down_ref,
    gt_ref, gup_own, gup_sib, bias_ref, near_ref, far_ref, g_ref,
):
    rows, deep = g0.shape
    g_ref[:rows, :] = g0[...]
    g_ref[rows:, :] = g1[...]
    units = gup_own.shape[1]
    step = units // 2
    for c in range(4):
        slope_ref, gup_ref = ((slope_own, gup_own), (slope_sib, gup_sib))[c // 2]
        at = slice((c % 2) * step, (c % 2 + 1) * step)
        grad = dot(g_ref[...], down_ref[:, c * step : (c + 1) * step])
        grad = (grad * slope_ref[:, at].astype(F32)).astype(BF16)
        gup_ref[:, at] = grad
        bias_ref[0:1, c * step : (c + 1) * step] = jnp.sum(
            grad.astype(F32), axis=0, keepdims=True
        )
    for c in range(4):
        at = slice(c * deep // 4, (c + 1) * deep // 4)
        out = dot(gup_own[...], up_ref[at, :units], NT) + dot(gup_sib[...], up_ref[at, units:], NT)
        split_store(out, near_ref, far_ref, at)
    gt_ref[...] = g_ref[...].T


def feed_back(g0, g1, slope_own, slope_sib, up_all, down_all):
    rows, deep = g0.shape
    units = slope_own.shape[1]
    out = [shape((deep, 2 * rows), BF16)]
    out += [shape((2 * rows, units), BF16)] * 2
    out += [shape((1, 2 * units), F32), shape((rows, deep), F32), shape((rows, deep), BF16)]
    args = [g0, g1, slope_own, slope_sib, up_all, down_all]
    scratch = [pltpu.VMEM((2 * rows, deep), BF16)]
    return call_whole(feed_back_kernel, "feed_back", out, [], args, scratch)


def row_mean(values):
    return jnp.mean(values, axis=-1, keepdims=True)


def col_sum(values):
    return jnp.sum(values, axis=0, keepdims=True)


def normalize(values):
    centered = values - row_mean(values)
    inverse = lax.rsqrt(row_mean(centered * centered) + NORM_EPSILON)
    return centered * inverse, inverse


def norm_back(grad_out, normed, inverse, gain):
    grad = grad_out * gain
    return inverse * (grad - row_mean(grad) - normed * row_mean(grad * normed))


def norm_one_kernel(own, part, recv, vec, first_ref, low_ref, normed_ref, inverse_ref):
    attn_out = part[...] + recv[...].astype(F32) + vec[4:5, :]
    normed, inverse = normalize(own[...].astype(F32) + attn_out)
    first = normed * vec[0:1, :] + vec[1:2, :]
    first_ref[...] = first
    low_ref[...] = first.astype(BF16)
    normed_ref[...] = normed
    inverse_ref[...] = inverse


def norm_one(own, part, recv, vec):
    rows, deep = own.shape
    out = [shape((rows, deep), t) for t in (F32, BF16, F32)] + [shape((rows, 1), F32)]
    return call_whole(norm_one_kernel, "norm_one", out, [], [own, part, recv, vec])


def norm_two_kernel(first, part, recv, cotangent, vec, out_ref, grad_ref, low_ref, sums_ref):
    down_out = part[...] + recv[...].astype(F32) + vec[5:6, :]
    normed, inverse = normalize(first[...] + down_out)
    out_ref[...] = (normed * vec[2:3, :] + vec[3:4, :]).astype(BF16)
    given = cotangent[...].astype(F32)
    grad = norm_back(given, normed, inverse, vec[2:3, :])
    grad_ref[...] = grad
    low = grad.astype(BF16)
    low_ref[...] = low
    sums_ref[0:1, :] = col_sum(given * normed)
    sums_ref[1:2, :] = col_sum(given)
    sums_ref[2:3, :] = col_sum(low.astype(F32))


def norm_two(first, part, recv, cotangent, vec):
    rows, deep = first.shape
    out = [shape((rows, deep), t) for t in (BF16, F32, BF16)] + [shape((3, deep), F32)]
    return call_whole(norm_two_kernel, "norm_two", out, [], [first, part, recv, cotangent, vec])


def norm_one_back_kernel(
    grad_second, part, recv, normed, inverse, vec, grad_ref, low_ref, sums_ref
):
    given = grad_second[...] + part[...] + recv[...].astype(F32)
    grad = norm_back(given, normed[...], inverse[...], vec[0:1, :])
    grad_ref[...] = grad
    low = grad.astype(BF16)
    low_ref[...] = low
    sums_ref[0:1, :] = col_sum(given * normed[...])
    sums_ref[1:2, :] = col_sum(given)
    sums_ref[2:3, :] = col_sum(low.astype(F32))


def norm_one_back(grad_second, part, recv, normed, inverse, vec):
    rows, deep = part.shape
    out = [shape((rows, deep), t) for t in (F32, BF16)] + [shape((3, deep), F32)]
    args = [grad_second, part, recv, normed, inverse, vec]
    return call_whole(norm_one_back_kernel, "norm_one_back", out, [], args)


def nesterov(weights, momentum, average, gradient, step_rate):
    momentum_new = MOMENTUM * momentum + gradient
    weight_new = weights - step_rate * (gradient + MOMENTUM * momentum_new)
    return (weight_new, momentum_new, AVERAGE * average + (1.0 - AVERAGE) * weight_new)


def swap_tp(values, bit):
    size = lax.axis_size("tp")
    return lax.ppermute(values, "tp", [(i, i ^ bit) for i in range(size)])


def core(values):
    return swap_tp(values, 1)


def across(values):
    return swap_tp(values, 2)


def swap_ctx(values):
    return lax.ppermute(values, "ctx", [(0, 1), (1, 0)])


def swap_both(values):
    size = lax.axis_size("tp")
    return lax.ppermute(values, ("ctx", "tp"), [(i, i ^ (size + 2)) for i in range(2 * size)])


def sum_fsdp(values):
    size = lax.axis_size("fsdp")

    def swap(values, bit):
        return lax.ppermute(values, "fsdp", [(i, i ^ bit) for i in range(size)])

    if size == 4:
        one, two, three = (swap(values, bit) for bit in (1, 2, 3))
        return (values + one) + (two + three)
    bit = 1
    while bit < size:
        values = values + swap(values, bit)
        bit *= 2
    return values


def gather_fsdp(shard, axis):
    return lax.all_gather(shard, "fsdp", axis=axis, tiled=True)


def ring():
    return lax.axis_size("fsdp") == 4


def shift_fsdp(values, step):
    size = lax.axis_size("fsdp")
    return lax.ppermute(values, "fsdp", [(i, (i + step) % size) for i in range(size)])


def gather_pieces(shard, axis):
    if not ring():
        return [gather_fsdp(shard, axis)]
    return [shard] + [shift_fsdp(shard, -s) for s in range(1, lax.axis_size("fsdp"))]


def scatter_pieces(grads):
    if not ring():
        return scatter_fsdp(grads, 0).astype(F32)
    size = lax.axis_size("fsdp")
    rank = lax.axis_index("fsdp")
    rows = grads.shape[0] // size
    pieces = [
        lax.dynamic_slice_in_dim(grads, lax.rem(rank + s, size) * rows, rows) for s in range(size)
    ]
    total = pieces[0].astype(F32)
    for s in (2, 1, 3):
        total = total + shift_fsdp(pieces[s], s).astype(F32)
    return total


def scatter_fsdp(grads, axis):
    return lax.psum_scatter(grads, "fsdp", scatter_dimension=axis, tiled=True)


def halves(values, axis=-1):
    low, high = jnp.split(values, 2, axis=axis)
    first = lax.axis_index("ctx") == 0
    return jnp.where(first, low, high), jnp.where(first, high, low)


def join(mine, other, axis=-1):
    first = lax.axis_index("ctx") == 0
    low, high = jnp.where(first, mine, other), jnp.where(first, other, mine)
    return jnp.concatenate([low, high], axis=axis)


def quarters(mine):
    return jnp.stack(jnp.split(mine, 2, axis=1))


def after(values, *others):
    return lax.optimization_barrier((values,) + others)[0]


def on_device(
    tokens,
    cotangent,
    attn_weight,
    attn_momentum,
    attn_average,
    ffn_weight,
    ffn_momentum,
    ffn_average,
    vector_weight,
    vector_momentum,
    vector_average,
):
    tp_rank = lax.axis_index("tp")
    sib_rank = tp_rank ^ 1
    head_width = attn_weight.shape[2]
    unit_width = ffn_weight.shape[2]
    token_count = LEN * lax.axis_size("fsdp")
    matrix_rate = MATRIX_RATE / math.sqrt(token_count)
    vector_rate = VECTOR_RATE / math.sqrt(token_count)

    attn_low, attn_high = halves(attn_weight.astype(BF16))
    qkv_mine = gather_pieces(attn_low[:3], 1)

    own = tokens[0]
    rows = own.shape[0]
    pair = 2 * rows
    half = 4 * rows
    beside = across(own)
    facing = swap_ctx(own)
    diagonal = swap_both(own)
    if ring():
        others = swap_ctx(after(jnp.stack(qkv_mine[1:]), beside, facing))
        qkv_other = [attn_high[:3]] + [others[s] for s in range(len(qkv_mine) - 1)]
    else:
        qkv_other = [swap_ctx(qkv_mine[0])]
    up_low = quarters(halves(ffn_weight[0].astype(BF16))[0])
    out_low = jnp.concatenate([attn_low[3], attn_high[3]], axis=1)
    out_up_low = jnp.concatenate([out_low[None], up_low])
    out_up = gather_fsdp(after(out_up_low, *qkv_mine[-3:], beside, facing), 1)
    blocks = [own, beside, core(own), core(beside), facing, diagonal, core(facing), core(diagonal)]

    vec = vector_weight[: 6 * D].reshape(6, D)

    def columns(start, width):
        part = lax.dynamic_slice_in_dim(vector_weight, start, width)
        return jnp.concatenate(halves(part))

    biases = jnp.stack(
        [
            columns(6 * D + tp_rank * head_width, head_width),
            columns(7 * D + tp_rank * head_width, head_width),
        ]
    )
    bias_hidden = jnp.concatenate(
        [
            columns(8 * D + tp_rank * unit_width, unit_width),
            columns(8 * D + sib_rank * unit_width, unit_width),
        ]
    )[None]

    token_t, qkv_w, queries, keys, values = project(blocks, qkv_mine, qkv_other, biases)
    down_low = jnp.concatenate(halves(ffn_weight[1].astype(BF16)), axis=1)
    mixed_own, mixed_sib, lse = attend(queries, keys, values)
    down_low = after(down_low, mixed_own)
    if ring():
        low, high = jnp.split(down_low, 2, axis=1)
        spots = ((0, 0), (1, 0), (3, 0), (2, 0), (2, low.shape[1]))
        down_w = [down_low, shift_fsdp(down_low, -1), shift_fsdp(down_low, -3)]
        down_w += [shift_fsdp(low, -2), shift_fsdp(high, -2)]
    else:
        spots = ((0, 0),)
        down_w = [gather_fsdp(down_low, 0)]
    mixed_recv = core(mixed_sib)
    out_up = after(out_up, mixed_own)
    out_up_sib = core(out_up)
    up_other = swap_ctx(out_up[1:])
    out_w, attn_part, attn_far = out_project(mixed_own, mixed_recv, [out_up, out_up_sib])
    attn_recv = across(attn_far)
    if ring():
        attn_recv = after(attn_recv, down_w[1], down_w[2])
    first, first_low, normed_one, inverse_one = norm_one(own, attn_part, attn_recv, vec)
    first_beside = across(first_low)

    if ring():
        first_beside = after(first_beside, down_w[3])
    up_other = after(up_other, first_beside)
    first_t, up_all, hidden_own, hidden_sib, slope_own, slope_sib = feed_up(
        first_low, first_beside, [out_up, up_other, out_up_sib, core(up_other)], bias_hidden
    )
    if ring():
        down_w[4] = after(down_w[4], hidden_own)
    down_all, down_part, down_far = feed_down(
        hidden_own, hidden_sib, spots, down_w, [core(w) for w in down_w]
    )
    layer_out, grad_second, grad_down, sums_two = norm_two(
        first, down_part, across(down_far), cotangent[0], vec
    )
    grad_down_t, grad_up_own, grad_up_sib, grad_bias_hidden, first_part, first_far = feed_back(
        grad_down, across(grad_down), slope_own, slope_sib, up_all, down_all
    )
    down_sib = grad_send(grad_down_t, hidden_sib)
    up_sib = grad_send(first_t, grad_up_sib)
    first_recv = after(across(first_far), down_sib, up_sib)
    grad_res, grad_attn, sums_one = norm_one_back(
        grad_second, first_part, first_recv, normed_one, inverse_one, vec
    )
    grad_attn_beside = across(grad_attn)
    down_sum = grad_total(grad_down_t, hidden_own, after(core(down_sib), grad_attn))
    up_keep, up_send = grad_sum(first_t, grad_up_own, after(core(up_sib), grad_attn))

    def finish(mine):
        return join(mine, swap_ctx(mine)).astype(F32)

    def finish_whole(part):
        mine, other = jnp.split(part.astype(F32), 2, axis=1)
        recv_other, recv_mine = jnp.split(swap_ctx(part).astype(F32), 2, axis=1)
        return join(mine + recv_mine, other + recv_other)

    down_owned = scatter_fsdp(down_sum, 0)
    up_recv = swap_ctx(up_send)

    grad_attn_beside = after(grad_attn_beside, down_sum, up_send)
    grad_attn_t, grad_mixed_own, grad_mixed_sib = out_back(grad_attn, grad_attn_beside, out_w)
    grad_mixed = (grad_mixed_own, core(grad_mixed_sib))

    up_recv = after(up_recv, grad_mixed_sib)
    up_sum = (up_keep.astype(F32) + up_recv.astype(F32)).astype(BF16)
    up_owned = scatter_pieces(up_sum).astype(BF16)
    mixed = (mixed_own, mixed_sib)
    heads = (queries, keys, values, mixed)
    query_other, kv_other = attend_back(*heads, grad_mixed, lse, 1)
    send = head_send(token_t, query_other, kv_other)
    out_sib = grad_send(after(grad_attn_t, query_other), mixed_recv)
    out_keep, out_send = grad_sum(grad_attn_t, mixed_own, core(out_sib))
    grad_mixed = (grad_mixed[0], after(grad_mixed[1], up_sum, send, out_send))
    recv = swap_ctx(send)
    query_mine, kv_mine = attend_back(*heads, grad_mixed, lse, 0)
    query_mine = after(query_mine, up_owned)
    part = head_width // 2
    near, far, sibling = input_back(
        query_mine, query_other, kv_mine, kv_other, qkv_w, sums_one, sums_two, grad_bias_hidden
    )
    sib_recv = core(sibling)
    qkvo_sum = head_sum(token_t, query_mine, kv_mine, recv, out_keep, swap_ctx(out_send))
    qkvo_mine = scatter_fsdp(qkvo_sum, 0)
    sib_recv = after(sib_recv, qkvo_sum)
    input_part, to_x, to_y, to_d, vec_part = fold(near, far, sibling, sib_recv, grad_res)
    from_x, from_y, from_d = across(to_x), swap_ctx(to_y), swap_both(to_d)
    input_grad = input_part
    for term in (from_x, from_y, from_d):
        input_grad = input_grad + term[:rows].astype(F32)
    vec_x, vec_y, vec_d = (term[rows:].astype(F32) for term in (from_x, from_y, from_d))
    vec_plane = (vec_part.astype(F32) + vec_x) + (vec_y + vec_d)
    vector_grad = sum_fsdp(vec_plane[:12]).reshape(-1)

    down_grad, up_grad = finish_whole(after(down_owned, to_y)), finish(after(up_owned, to_y))
    ffn_grad = jnp.stack([up_grad, down_grad])
    ffn_new, ffn_momentum_new, ffn_average_new = nesterov(
        ffn_weight, ffn_momentum, ffn_average, ffn_grad, matrix_rate
    )
    qkvo_mine = after(qkvo_mine, input_grad, ffn_new, ffn_average_new, vec_plane)
    qkvo_other = swap_ctx(qkvo_mine)
    attn_grad = jnp.stack(
        [
            join(qkvo_mine[:, j * part : (j + 1) * part], qkvo_other[:, j * part : (j + 1) * part])
            for j in range(4)
        ]
    ).astype(F32)
    vector_new, vector_momentum_new, vector_average_new = nesterov(
        vector_weight, vector_momentum, vector_average, vector_grad, vector_rate
    )
    attn_new, attn_momentum_new, attn_average_new = nesterov(
        attn_weight, attn_momentum, attn_average, attn_grad, matrix_rate
    )
    return (
        layer_out[None],
        input_grad[None],
        attn_grad,
        attn_new,
        attn_momentum_new,
        attn_average_new,
        attn_new.astype(BF16),
        ffn_grad,
        ffn_new,
        ffn_momentum_new,
        ffn_average_new,
        ffn_new.astype(BF16),
        vector_grad,
        vector_new,
        vector_momentum_new,
        vector_average_new,
    )


def solution(mesh):
    rows = P("fsdp", ("ctx", "tp"), None)
    weight = P(None, "fsdp", "tp")
    return jax.shard_map(
        on_device,
        mesh=mesh,
        in_specs=(rows, rows) + (weight,) * 6 + (P(),) * 3,
        out_specs=(rows, rows) + (weight,) * 10 + (P(),) * 4,
        check_vma=False,
    )
```

```python
import functools
import math

import jax
import jax.numpy as jnp
from jax import lax
from jax.experimental import pallas as pl
from jax.experimental.pallas import tpu as pltpu
from jax.sharding import PartitionSpec as P

D = 1024
FF = 4096
HEAD_DIM = 64
LEN = 2048

NORM_EPSILON = 1e-05
MOMENTUM = 0.5
AVERAGE = 0.5
MATRIX_RATE = 0.1
VECTOR_RATE = 0.3

SCALE = HEAD_DIM ** (-0.5)
LOG2E = math.log2(math.e)
F32 = jnp.float32
BF16 = jnp.bfloat16
NT = (((1,), (1,)), ((), ()))
TN = (((0,), (0,)), ((), ()))
NN = (((1,), (0,)), ((), ()))


def dot(left, right, dims=NN):
    return lax.dot_general(left, right, dims, preferred_element_type=F32)


VMEM = pl.BlockSpec(memory_space=pltpu.VMEM)
FAR = pl.BlockSpec(memory_space=pltpu.HBM)
MEGA = 1024 * 1024
WORK_UNIT = 1.2e10
WORK = {
    "attend": 0.001,
    "out_project": 0.001,
    "norm_one": 1.5,
    "feed_up": 8,
    "feed_down": 4,
    "norm_two": 2,
    "feed_back": 8,
    "grad_send": 10,
    "grad_sum": 3,
    "grad_total": 3,
    "norm_one_back": 2,
    "out_back": 2,
    "attend_back": 12,
    "head_sum": 0.01,
    "input_back": 0.01,
    "out_send": 0.01,
    "out_sum": 0.01,
    "fold": 0.01,
}


def cost(name):
    flops = int(WORK[name] * WORK_UNIT)
    return pl.CostEstimate(flops=flops, bytes_accessed=1, transcendentals=0)


def shape(dims, dtype):
    return jax.ShapeDtypeStruct(tuple(dims), dtype)


def tile(i, size):
    return pl.ds(pl.multiple_of(i * size, size), size)


class Copies:
    def __init__(self, sems):
        self.sems = sems
        self.begun = []
        self.open = []

    def start(self, src, dst):
        copy = pltpu.make_async_copy(src, dst, self.sems.at[len(self.begun)])
        copy.start()
        self.begun.append(copy)
        self.open.append(copy)
        return copy

    def wait(self, copies=None):
        for copy in list(self.open) if copies is None else copies:
            copy.wait()
            self.open.remove(copy)


def call(kernel, name, outs, far, near, scratch=(), copies=1, vmem=10):
    def body(*refs):
        io = Copies(refs[-1])
        kernel(io, *refs[:-1])
        io.wait()

    return pl.pallas_call(
        body,
        in_specs=[FAR] * len(far) + [VMEM] * len(near),
        out_specs=[FAR if is_far else VMEM for _, is_far in outs],
        out_shape=[out for out, _ in outs],
        scratch_shapes=[*scratch, pltpu.SemaphoreType.DMA((copies,))],
        compiler_params=pltpu.CompilerParams(vmem_limit_bytes=vmem * MEGA),
        cost_estimate=cost(name),
        name=name,
    )(*far, *near)


def ring_rows(count, deep):
    size = deep // count
    rank = lax.axis_index("fsdp")
    return [tile(lax.rem(rank + s, count), size) if count > 1 else tile(0, size) for s in range(count)]


def head_masks(width):
    lane = lax.broadcasted_iota(jnp.int32, (1, width), 1) // HEAD_DIM
    return [(lane == h).astype(BF16) for h in range(width // HEAD_DIM)]


def attend_block(queries, k_ref, vt_ref, chunk):
    width = queries.shape[1]
    count = k_ref.shape[0]
    masked = [queries * mask for mask in head_masks(width)]
    units = [(h, c) for h in range(width // HEAD_DIM) for c in range(0, count, chunk)]

    def scores_of(unit):
        h, c = unit
        return dot(k_ref[c : c + chunk, :], masked[h], NT)

    tops, totals, outs = {}, {}, {}
    scores = scores_of(units[0])
    for i, unit in enumerate(units):
        current = scores
        if i + 1 < len(units):
            scores = scores_of(units[i + 1])
        h, c = unit
        top = jnp.max(current, axis=0, keepdims=True)
        weights = jnp.exp2((current - top) * (SCALE * LOG2E))
        tops[unit] = top
        totals[unit] = jnp.sum(weights, axis=0, keepdims=True)
        outs[unit] = dot(
            vt_ref[h * HEAD_DIM : (h + 1) * HEAD_DIM, c : c + chunk], weights.astype(BF16)
        )
    heads_out, lses = [], []
    for h in range(width // HEAD_DIM):
        mine = [(h, c) for c in range(0, count, chunk)]
        top = functools.reduce(jnp.maximum, [tops[u] for u in mine])
        share = [jnp.exp2((tops[u] - top) * (SCALE * LOG2E)) for u in mine]
        total = sum(totals[u] * f for u, f in zip(mine, share))
        out = sum(outs[u] * f for u, f in zip(mine, share))
        heads_out.append(out / total)
        lses.append(top * (SCALE * LOG2E) + jnp.log2(total))
    return jnp.concatenate(heads_out, axis=0), lses


def attend_kernel(count, io, *refs):
    blocks, refs = refs[:8], refs[8:]
    mine, refs = refs[:count], refs[count:]
    other, refs = refs[:count], refs[count:]
    bias_ref, refs = refs[0], refs[1:]
    xt_out, w_out, q_out, k_out, v_out, own_out, sib_out, lse_ref = refs[:8]
    x_ref, xt_ref, w_ref, q_ref, k_ref, v_ref, vt_ref, mixed_ref = refs[8:]
    rows, deep = blocks[0].shape
    part = mine[0].shape[2]
    width = 2 * part
    weights, tokens = [], []
    for at, low, high in zip(ring_rows(count, deep), mine, other):
        for j in range(3):
            weights.append(io.start(low.at[j], w_ref.at[at, j * width : j * width + part]))
            weights.append(
                io.start(high.at[j], w_ref.at[at, j * width + part : (j + 1) * width])
            )
    for i in range(8):
        tokens.append(io.start(blocks[i], x_ref.at[i * rows : (i + 1) * rows, :]))
    io.wait(weights)
    io.start(w_ref, w_out)
    for i in range(4):
        at = slice(i * 2 * rows, (i + 1) * 2 * rows)
        io.wait(tokens[2 * i : 2 * i + 2])
        x = x_ref[at, :]
        if i < 2:
            out = dot(x, w_ref[...])
            q_ref[at, :] = (out[:, :width] + bias_ref[0:1, :]).astype(BF16)
            out = out[:, width:]
        else:
            out = dot(x, w_ref[:, width:])
        values = (out[:, width:] + bias_ref[1:2, :]).astype(BF16)
        k_ref[at, :] = out[:, :width].astype(BF16)
        v_ref[at, :] = values
        vt_ref[:, at] = values.T
        xt_ref[:, at] = x.T
    for src, dst in ((xt_ref, xt_out), (q_ref, q_out), (k_ref, k_out), (v_ref, v_out)):
        io.start(src, dst)
    half = 4 * rows
    block = min(256, half // 2)
    chunk = min(512, 8 * rows)

    def body(i, carry):
        at = tile(i, block)
        out, lses = attend_block(q_ref[at, :], k_ref, vt_ref, chunk)
        mixed_ref[at, :] = out.T.astype(BF16)
        for h, lse in enumerate(lses):
            lse_ref[h : h + 1, at] = lse
        return carry

    lax.fori_loop(0, half // block // 2, body, 0)
    io.start(mixed_ref.at[: half // 2, :], own_out)
    lax.fori_loop(half // block // 2, half // block, body, 0)
    io.start(mixed_ref.at[half // 2 :, :], sib_out)


def attend(blocks, mine, other, biases):
    rows, deep = blocks[0].shape
    width = biases.shape[1]
    outs = [
        (shape((deep, 8 * rows), BF16), True),
        (shape((deep, 3 * width), BF16), True),
        (shape((4 * rows, width), BF16), True),
        (shape((8 * rows, width), BF16), True),
        (shape((8 * rows, width), BF16), True),
        (shape((2 * rows, width), BF16), True),
        (shape((2 * rows, width), BF16), True),
        (shape((width // HEAD_DIM, 4 * rows), F32), False),
    ]
    scratch = [
        pltpu.VMEM((8 * rows, deep), BF16),
        pltpu.VMEM((deep, 8 * rows), BF16),
        pltpu.VMEM((deep, 3 * width), BF16),
        pltpu.VMEM((4 * rows, width), BF16),
        pltpu.VMEM((8 * rows, width), BF16),
        pltpu.VMEM((8 * rows, width), BF16),
        pltpu.VMEM((width, 8 * rows), BF16),
        pltpu.VMEM((4 * rows, width), BF16),
    ]
    kernel = functools.partial(attend_kernel, len(mine))
    far = [*blocks, *mine, *other]
    count = 6 * len(mine) + 8 + 7
    return call(kernel, "attend", outs, far, [biases], scratch, count, 28)


def attend_back_kernel(part, io, *refs):
    ins, refs = refs[:8], refs[8:]
    lse_ref, refs = refs[0], refs[1:]
    dq_out, dkv_out, dw_ref = refs[:3]
    q_ref, k_ref, v_ref, o_ref, g_ref, xt_ref, kt_ref, dq_ref, dkv_ref, dk_acc, dv_acc = refs[3:]
    rows, width = q_ref.shape
    pair = rows // 2
    heads = width // HEAD_DIM
    cols = slice(part * width, (part + 1) * width)
    q_in, k_in, v_in, o0, o1, g0, g1, xt_in = ins
    loads = [
        io.start(k_in.at[:, cols], k_ref),
        io.start(q_in.at[:, cols], q_ref),
        io.start(g0.at[:, cols], g_ref.at[:pair, :]),
        io.start(g1.at[:, cols], g_ref.at[pair:, :]),
        io.start(o0.at[:, cols], o_ref.at[:pair, :]),
        io.start(o1.at[:, cols], o_ref.at[pair:, :]),
        io.start(v_in.at[:, cols], v_ref),
    ]
    late = [io.start(xt_in, xt_ref)]
    dk_acc[...] = jnp.zeros_like(dk_acc)
    dv_acc[...] = jnp.zeros_like(dv_acc)
    io.wait(loads)
    kt_ref[...] = k_ref[...].T
    masks = head_masks(width)
    block = min(256, pair)

    def body(i, carry):
        at = tile(i, block)
        queries = q_ref[at, :]
        grads = g_ref[at, :]
        product = (o_ref[at, :].astype(F32) * grads.astype(F32)).T
        outs, probs, gscores, qms, gms = [], [], [], [], []
        for h in range(heads):
            qm = queries * masks[h]
            gm = grads * masks[h]
            delta = col_sum(product[h * HEAD_DIM : (h + 1) * HEAD_DIM, :])
            scores = dot(k_ref[...], qm, NT)
            row = part * heads + h
            prob = jnp.exp2(scores * (SCALE * LOG2E) - lse_ref[row : row + 1, at])
            grad_prob = dot(v_ref[...], gm, NT)
            gscore = (prob * (grad_prob - delta)).astype(BF16)
            outs.append(dot(kt_ref[h * HEAD_DIM : (h + 1) * HEAD_DIM, :], gscore))
            probs.append(prob.astype(BF16))
            gscores.append(gscore)
            qms.append(qm)
            gms.append(gm)
        dv_acc[...] += dot(jnp.concatenate(probs, axis=1), jnp.concatenate(gms, axis=0))
        dk_acc[...] += dot(jnp.concatenate(gscores, axis=1), jnp.concatenate(qms, axis=0))
        dq_ref[at, :] = (jnp.concatenate(outs, axis=0).T * SCALE).astype(BF16)
        return carry

    lax.fori_loop(0, rows // block, body, 0)
    io.start(dq_ref, dq_out)
    dkv_ref[:, :width] = (dk_acc[...] * SCALE).astype(BF16)
    dkv_ref[:, width:] = dv_acc[...].astype(BF16)
    io.start(dkv_ref, dkv_out)
    io.wait(late)
    dw_ref[:, :width] = dot(xt_ref[:, :rows], dq_ref[...]).astype(BF16)
    dw_ref[:, width:] = dot(xt_ref[...], dkv_ref[...]).astype(BF16)


def attend_back(queries, keys, values, mixed, grads, tokens_t, lse, part):
    rows, both = queries.shape
    count = keys.shape[0]
    deep = tokens_t.shape[0]
    width = both // 2
    outs = [
        (shape((rows, width), BF16), True),
        (shape((count, both), BF16), True),
        (shape((deep, width + both), BF16), False),
    ]
    scratch = [
        pltpu.VMEM((rows, width), BF16),
        pltpu.VMEM((count, width), BF16),
        pltpu.VMEM((count, width), BF16),
        pltpu.VMEM((rows, width), BF16),
        pltpu.VMEM((rows, width), BF16),
        pltpu.VMEM((deep, count), BF16),
        pltpu.VMEM((width, count), BF16),
        pltpu.VMEM((rows, width), BF16),
        pltpu.VMEM((count, both), BF16),
        pltpu.VMEM((count, width), F32),
        pltpu.VMEM((count, width), F32),
    ]
    far = [queries, keys, values, *mixed, *grads, tokens_t]
    kernel = functools.partial(attend_back_kernel, part)
    return call(kernel, "attend_back", outs, far, [lse], scratch, 10, 28)


def split_store(out, near_ref, far_ref, at):
    rows = near_ref.shape[0]
    near_ref[:, at] = out[:rows]
    far_ref[:, at] = out[rows:].astype(BF16)


def out_kernel(io, w0, w1, own_in, recv, w_out, near_out, far_ref, w_ref, own, near_ref):
    width = own.shape[1]
    deep = w_ref.shape[0]
    io.start(own_in, own)
    io.start(w0.at[0], w_ref.at[:, :width])
    io.start(w1.at[0], w_ref.at[:, width:])
    io.wait()
    io.start(w_ref, w_out)
    for c in range(4):
        at = slice(c * deep // 4, (c + 1) * deep // 4)
        out = dot(own[...], w_ref[at, :width], NT) + dot(recv[...], w_ref[at, width:], NT)
        split_store(out, near_ref, far_ref, at)
        io.start(near_ref.at[:, at], near_out.at[:, at])


def out_project(own, recv, pieces):
    pair, width = own.shape
    deep = pieces[0].shape[1]
    outs = [
        (shape((deep, 2 * width), BF16), True),
        (shape((pair // 2, deep), F32), True),
        (shape((pair // 2, deep), BF16), False),
    ]
    scratch = [
        pltpu.VMEM((deep, 2 * width), BF16),
        pltpu.VMEM((pair, width), BF16),
        pltpu.VMEM((pair // 2, deep), F32),
    ]
    return call(out_kernel, "out_project", outs, [*pieces, own], [recv], scratch, 8)


def out_back_kernel(io, w_in, g0, g1, gt_out, own_out, sib_ref, w_ref, gt_ref, own_ref):
    rows = g0.shape[0]
    width = own_ref.shape[1]
    io.start(w_in, w_ref)
    io.wait()
    for i, ref in enumerate((g0, g1)):
        at = slice(i * rows, (i + 1) * rows)
        g = ref[...]
        out = dot(g, w_ref[...])
        own_ref[at, :] = out[:, :width].astype(BF16)
        sib_ref[at, :] = out[:, width:].astype(BF16)
        gt_ref[:, at] = g.T
        io.start(own_ref.at[at, :], own_out.at[at, :])
    io.start(gt_ref, gt_out)


def out_back(g0, g1, weights):
    rows, deep = g0.shape
    width = weights.shape[1] // 2
    outs = [
        (shape((deep, 2 * rows), BF16), True),
        (shape((2 * rows, width), BF16), True),
        (shape((2 * rows, width), BF16), False),
    ]
    scratch = [
        pltpu.VMEM(weights.shape, BF16),
        pltpu.VMEM((deep, 2 * rows), BF16),
        pltpu.VMEM((2 * rows, width), BF16),
    ]
    return call(out_back_kernel, "out_back", outs, [weights], [g0, g1], scratch, 4)


EXTRA = 16


def pack_rows(out_ref, one, two, sums, hidden):
    rank = lax.axis_index("tp")
    size = lax.axis_size("tp")
    first = lax.axis_index("ctx") == 0
    part = sums[0].shape[1]
    units = hidden.shape[1] // 2
    out_ref[...] = jnp.zeros_like(out_ref)
    out_ref[0:2, :] = one[0:2, :]
    out_ref[2:4, :] = two[0:2, :]
    out_ref[4:5, :] = one[2:3, :]
    out_ref[5:6, :] = two[2:3, :]
    for row, (mine, other) in ((6, sums[:2]), (7, sums[2:])):
        low, high = jnp.where(first, mine, other), jnp.where(first, other, mine)
        for t in range(size):
            keep = rank == t
            start = 2 * t * part
            out_ref[row : row + 1, start : start + part] = jnp.where(keep, low, 0.0)
            out_ref[row : row + 1, start + part : start + 2 * part] = jnp.where(keep, high, 0.0)
    for t in range(size):
        row = 8 + t
        total = jnp.where(rank == t, hidden[:, :units], 0.0)
        total = total + jnp.where((rank ^ 1) == t, hidden[:, units:], 0.0)
        mine, other = total[:, : units // 2], total[:, units // 2 :]
        out_ref[row : row + 1, : units // 2] = jnp.where(first, mine, other)
        out_ref[row : row + 1, units // 2 :] = jnp.where(first, other, mine)


def input_back_kernel(
    io, q0, q1, kv0, kv1, w_in, one, two, hidden, near_out, far_out, sib_ref,
    cat_ref, w_ref, near_ref, far_ref, vec_ref,
):
    half, part = q0.shape
    pair, deep = near_ref.shape
    io.start(w_in, w_ref)
    for j, (ref, at) in enumerate(((q0, 0), (q1, 0), (kv0, 0), (kv1, 0), (kv0, part), (kv1, part))):
        count = ref.shape[0]
        io.start(ref.at[:, at : at + part], cat_ref.at[:count, j * part : (j + 1) * part])
    io.wait()
    sib_ref[:pair, :] = dot(cat_ref[pair:half, :], w_ref[...], NT).astype(BF16)
    out = dot(cat_ref[half + pair :, 2 * part :], w_ref[:, 2 * part :], NT)
    sib_ref[pair:half, :] = out.astype(BF16)
    near_ref[...] = dot(cat_ref[:pair, :], w_ref[...], NT)
    io.start(near_ref, near_out)
    far_ref[...] = dot(cat_ref[half : half + pair, 2 * part :], w_ref[:, 2 * part :], NT)
    io.start(far_ref, far_out)
    sums = []
    for j, count in ((0, half), (1, half), (4, 2 * half), (5, 2 * half)):
        sums.append(col_sum(cat_ref[:count, j * part : (j + 1) * part].astype(F32)))
    pack_rows(vec_ref, one, two, sums, hidden)
    sib_ref[half:, :] = vec_ref[...].astype(BF16)


def input_back(q0, q1, kv0, kv1, weights, one, two, hidden):
    half, part = q0.shape
    deep = weights.shape[0]
    pair = half // 2
    outs = [
        (shape((pair, deep), F32), True),
        (shape((pair, deep), F32), True),
        (shape((half + EXTRA, deep), BF16), False),
    ]
    scratch = [
        pltpu.VMEM((kv0.shape[0], 6 * part), BF16),
        pltpu.VMEM(weights.shape, BF16),
        pltpu.VMEM((pair, deep), F32),
        pltpu.VMEM((pair, deep), F32),
        pltpu.VMEM((EXTRA, deep), F32),
    ]
    far = [q0, q1, kv0, kv1, weights]
    return call(input_back_kernel, "input_back", outs, far, [one, two, hidden], scratch, 9, 20)


def fold_kernel(
    io, near_in, far_in, rest_in, sent, recv, own_out, x_ref, y_ref, d_ref, vec_ref,
    near, far, rest, own_ref,
):
    rows = rest.shape[0]
    pair = 2 * rows
    for src, dst in ((near_in, near), (far_in, far), (rest_in, rest)):
        io.start(src, dst)
    io.wait()
    vec = sent[2 * pair :, :].astype(F32) + recv[2 * pair :, :].astype(F32)
    vec_ref[...] = vec.astype(BF16)
    for ref, term, at in ((x_ref, near, rows), (y_ref, far, 0), (d_ref, far, rows)):
        start = at if term is near else pair + at
        total = term[at : at + rows, :] + recv[start : start + rows, :].astype(F32)
        ref[:rows, :] = total.astype(BF16)
        ref[rows:, :] = vec.astype(BF16)
    own_ref[...] = rest[...] + near[:rows, :] + recv[:rows, :].astype(F32)
    io.start(own_ref, own_out)


def fold(near, far, sent, recv, rest):
    rows, deep = rest.shape
    outs = [(shape((rows, deep), F32), True)] + [(shape((rows + EXTRA, deep), BF16), False)] * 3
    outs += [(shape((EXTRA, deep), BF16), False)]
    scratch = [pltpu.VMEM((n * rows, deep), F32) for n in (2, 2, 1, 1)]
    return call(fold_kernel, "fold", outs, [near, far, rest], [sent, recv], scratch, 4, 12)


def grad_send_kernel(io, left, right, out_ref):
    out_ref[...] = dot(left[...], right[...]).astype(BF16)


def grad_send(left, right, name="grad_send"):
    outs = [(shape((left.shape[0], right.shape[1]), BF16), False)]
    return call(grad_send_kernel, name, outs, [], [left, right])[0]


def grad_sum_kernel(io, left, right, recv, keep_ref, send_ref):
    part = keep_ref.shape[1]
    for ref, at in ((send_ref, slice(part, 2 * part)), (keep_ref, slice(0, part))):
        ref[...] = (dot(left[...], right[:, at]) + recv[:, at].astype(F32)).astype(BF16)


def grad_sum(left, right, recv, name="grad_sum"):
    half = (shape((left.shape[0], right.shape[1] // 2), BF16), False)
    return call(grad_sum_kernel, name, [half] * 2, [], [left, right, recv])


def grad_total_kernel(io, left, right, recv, out_ref):
    out_ref[...] = (dot(left[...], right[...]) + recv[...].astype(F32)).astype(BF16)


def grad_total(left, right, recv):
    outs = [(shape((left.shape[0], right.shape[1]), BF16), False)]
    return call(grad_total_kernel, "grad_total", outs, [], [left, right, recv])[0]


def head_sum_kernel(io, grad, recv, keep, keep_recv, out_ref):
    width = recv.shape[1]
    out_ref[:, :width] = (grad[...].astype(F32) + recv[...].astype(F32)).astype(BF16)
    out_ref[:, width:] = (keep[...].astype(F32) + keep_recv[...].astype(F32)).astype(BF16)


def head_sum(grad, recv, keep, keep_recv):
    outs = [(shape((grad.shape[0], recv.shape[1] + keep.shape[1]), BF16), False)]
    return call(head_sum_kernel, "head_sum", outs, [], [grad, recv, keep, keep_recv])[0]


def gelu_pair(values):
    size = jnp.abs(values)
    t = 1.0 / (1.0 + (0.3275911 * math.sqrt(0.5)) * size)
    bell = jnp.exp2(values * values * (-0.5 * LOG2E))
    poly = t * (
        0.5 * 0.254829592
        + t
        * (
            0.5 * -0.284496736
            + t * (0.5 * 1.421413741 + t * (0.5 * -1.453152027 + t * (0.5 * 1.061405429)))
        )
    )
    tail = poly * bell
    cdf = jnp.where(values < 0, tail, 1.0 - tail)
    return values * cdf, cdf + values * bell * (1.0 / math.sqrt(2.0 * math.pi))


def up_kernel(
    io, mine, other, mine_sib, other_sib, x0, x1, bias_ref,
    xt_out, w_ref, act_own, act_sib, slope_own, slope_sib, xt_ref, x_ref,
):
    rows = x0.shape[0]
    step = mine.shape[2]
    loads = []
    for ref, first in ((mine, 1), (other, 0), (mine_sib, 1), (other_sib, 0)):
        for j in range(first, ref.shape[0]):
            at = len(loads) * step
            loads.append(io.start(ref.at[j], w_ref.at[:, at : at + step]))
    x_ref[:rows, :] = x0[...]
    x_ref[rows:, :] = x1[...]

    def matmul(c):
        io.wait(loads[c : c + 1])
        return dot(x_ref[...], w_ref[:, c * step : (c + 1) * step])

    following = matmul(0)
    for c in range(8):
        pre = following
        if c < 7:
            following = matmul(c + 1)
        act_ref, slope_ref = ((act_own, slope_own), (act_sib, slope_sib))[c // 4]
        at = slice((c % 4) * step, (c % 4 + 1) * step)
        act, slope = gelu_pair(pre + bias_ref[0:1, c * step : (c + 1) * step])
        act_ref[:, at] = act.astype(BF16)
        slope_ref[:, at] = slope.astype(BF16)
        if c == 0:
            xt_ref[...] = x_ref[...].T
            io.start(xt_ref, xt_out)


def feed_up(x0, x1, pieces, bias):
    rows, deep = x0.shape
    units = bias.shape[1]
    outs = [(shape((deep, 2 * rows), BF16), True), (shape((deep, units), BF16), False)]
    outs += [(shape((2 * rows, units // 2), BF16), False)] * 4
    scratch = [pltpu.VMEM((deep, 2 * rows), BF16), pltpu.VMEM((2 * rows, deep), BF16)]
    return call(up_kernel, "feed_up", outs, pieces, [x0, x1, bias], scratch, 9)


def down_kernel(spots, io, *refs):
    count = len(spots)
    own, sib, refs = refs[:count], refs[count : 2 * count], refs[2 * count :]
    act_own, act_sib, w_ref, near_out, far_ref, near_ref = refs
    deep = near_ref.shape[1]
    units = act_own.shape[1]
    rows = ring_rows(deep // own[0].shape[0], deep)
    for (piece, start), left, right in zip(spots, own, sib):
        width = left.shape[1]
        io.start(left, w_ref.at[rows[piece], start : start + width])
        io.start(right, w_ref.at[rows[piece], units + start : units + start + width])
    io.wait()
    for c in range(4):
        at = slice(c * deep // 4, (c + 1) * deep // 4)
        out = dot(act_own[...], w_ref[at, :units], NT) + dot(act_sib[...], w_ref[at, units:], NT)
        split_store(out, near_ref, far_ref, at)
        io.start(near_ref.at[:, at], near_out.at[:, at])


def feed_down(act_own, act_sib, spots, own, sib):
    pair, units = act_own.shape
    outs = [
        (shape((D, 2 * units), BF16), False),
        (shape((pair // 2, D), F32), True),
        (shape((pair // 2, D), BF16), False),
    ]
    kernel = functools.partial(down_kernel, spots)
    scratch = [pltpu.VMEM((pair // 2, D), F32)]
    near = [act_own, act_sib]
    return call(kernel, "feed_down", outs, [*own, *sib], near, scratch, 2 * len(own) + 4)


def feed_back_kernel(
    io, g0, g1, slope_own, slope_sib, up_ref, down_ref,
    gt_ref, gup_own, gup_sib, bias_ref, near_out, far_ref, g_ref, near_ref,
):
    rows, deep = g0.shape
    g_ref[:rows, :] = g0[...]
    g_ref[rows:, :] = g1[...]
    units = gup_own.shape[1]
    step = units // 2
    for c in range(4):
        slope_ref, gup_ref = ((slope_own, gup_own), (slope_sib, gup_sib))[c // 2]
        at = slice((c % 2) * step, (c % 2 + 1) * step)
        grad = dot(g_ref[...], down_ref[:, c * step : (c + 1) * step])
        grad = (grad * slope_ref[:, at].astype(F32)).astype(BF16)
        gup_ref[:, at] = grad
        bias_ref[0:1, c * step : (c + 1) * step] = col_sum(grad.astype(F32))
    for c in range(4):
        at = slice(c * deep // 4, (c + 1) * deep // 4)
        out = dot(gup_own[...], up_ref[at, :units], NT) + dot(gup_sib[...], up_ref[at, units:], NT)
        split_store(out, near_ref, far_ref, at)
        io.start(near_ref.at[:, at], near_out.at[:, at])
    gt_ref[...] = g_ref[...].T


def feed_back(g0, g1, slope_own, slope_sib, up_all, down_all):
    rows, deep = g0.shape
    units = slope_own.shape[1]
    outs = [(shape((deep, 2 * rows), BF16), False)]
    outs += [(shape((2 * rows, units), BF16), False)] * 2
    outs += [(shape((1, 2 * units), F32), False), (shape((rows, deep), F32), True)]
    outs += [(shape((rows, deep), BF16), False)]
    near = [g0, g1, slope_own, slope_sib, up_all, down_all]
    scratch = [pltpu.VMEM((2 * rows, deep), BF16), pltpu.VMEM((rows, deep), F32)]
    return call(feed_back_kernel, "feed_back", outs, [], near, scratch, 4)


def row_mean(values):
    return jnp.mean(values, axis=-1, keepdims=True)


def col_sum(values):
    return jnp.sum(values, axis=0, keepdims=True)


def normalize(values):
    centered = values - row_mean(values)
    inverse = lax.rsqrt(row_mean(centered * centered) + NORM_EPSILON)
    return centered * inverse, inverse


def norm_back(grad_out, normed, inverse, gain):
    grad = grad_out * gain
    return inverse * (grad - row_mean(grad) - normed * row_mean(grad * normed))


def load_rows(io, *pairs):
    for src, dst in pairs:
        io.start(src, dst)
    io.wait()


def norm_one_kernel(io, own_in, part_in, recv, vec, res_out, low_ref, own, part, res_ref):
    load_rows(io, (own_in, own), (part_in, part))
    attn_out = part[...] + recv[...].astype(F32) + vec[4:5, :]
    res = own[...].astype(F32) + attn_out
    res_ref[...] = res
    io.start(res_ref, res_out)
    low_ref[...] = (normalize(res)[0] * vec[0:1, :] + vec[1:2, :]).astype(BF16)


def norm_one(own, part, recv, vec):
    dims = own.shape
    outs = [(shape(dims, F32), True), (shape(dims, BF16), False)]
    scratch = [pltpu.VMEM(dims, t) for t in (BF16, F32, F32)]
    return call(norm_one_kernel, "norm_one", outs, [own, part], [recv, vec], scratch, 3)


def norm_two_kernel(
    io, res_in, part_in, given_in, recv, vec, out_out, grad_out, low_ref, sums_ref,
    res, part, given_ref, out_ref, grad_ref,
):
    load_rows(io, (res_in, res), (part_in, part), (given_in, given_ref))
    first = normalize(res[...])[0] * vec[0:1, :] + vec[1:2, :]
    down_out = part[...] + recv[...].astype(F32) + vec[5:6, :]
    normed, inverse = normalize(first + down_out)
    given = given_ref[...].astype(F32)
    grad = norm_back(given, normed, inverse, vec[2:3, :])
    low = grad.astype(BF16)
    low_ref[...] = low
    grad_ref[...] = grad
    io.start(grad_ref, grad_out)
    out_ref[...] = (normed * vec[2:3, :] + vec[3:4, :]).astype(BF16)
    io.start(out_ref, out_out)
    sums_ref[0:1, :] = col_sum(given * normed)
    sums_ref[1:2, :] = col_sum(given)
    sums_ref[2:3, :] = col_sum(low.astype(F32))


def norm_two(res, part, recv, cotangent, vec):
    rows, deep = dims = res.shape
    outs = [(shape(dims, BF16), True), (shape(dims, F32), True), (shape(dims, BF16), False)]
    outs += [(shape((3, deep), F32), False)]
    scratch = [pltpu.VMEM(dims, t) for t in (F32, F32, BF16, BF16, F32)]
    far = [res, part, cotangent]
    return call(norm_two_kernel, "norm_two", outs, far, [recv, vec], scratch, 5)


def norm_one_back_kernel(
    io, second_in, part_in, res_in, recv, vec, grad_out, low_ref, sums_ref,
    second, part, res, grad_ref,
):
    load_rows(io, (second_in, second), (part_in, part), (res_in, res))
    normed, inverse = normalize(res[...])
    given = second[...] + part[...] + recv[...].astype(F32)
    grad = norm_back(given, normed, inverse, vec[0:1, :])
    low = grad.astype(BF16)
    low_ref[...] = low
    grad_ref[...] = grad
    io.start(grad_ref, grad_out)
    sums_ref[0:1, :] = col_sum(given * normed)
    sums_ref[1:2, :] = col_sum(given)
    sums_ref[2:3, :] = col_sum(low.astype(F32))


def norm_one_back(grad_second, part, recv, res, vec):
    rows, deep = dims = part.shape
    outs = [(shape(dims, F32), True), (shape(dims, BF16), False), (shape((3, deep), F32), False)]
    scratch = [pltpu.VMEM(dims, F32)] * 4
    far = [grad_second, part, res]
    return call(norm_one_back_kernel, "norm_one_back", outs, far, [recv, vec], scratch, 4)


def nesterov(weights, momentum, average, gradient, step_rate):
    momentum_new = MOMENTUM * momentum + gradient
    weight_new = weights - step_rate * (gradient + MOMENTUM * momentum_new)
    return (weight_new, momentum_new, AVERAGE * average + (1.0 - AVERAGE) * weight_new)


def swap_tp(values, bit):
    size = lax.axis_size("tp")
    return lax.ppermute(values, "tp", [(i, i ^ bit) for i in range(size)])


def core(values):
    return swap_tp(values, 1)


def across(values):
    return swap_tp(values, 2)


def swap_ctx(values):
    return lax.ppermute(values, "ctx", [(0, 1), (1, 0)])


def swap_both(values):
    size = lax.axis_size("tp")
    return lax.ppermute(values, ("ctx", "tp"), [(i, i ^ (size + 2)) for i in range(2 * size)])


def sum_fsdp(values):
    size = lax.axis_size("fsdp")

    def swap(values, bit):
        return lax.ppermute(values, "fsdp", [(i, i ^ bit) for i in range(size)])

    if size == 4:
        one, two, three = (swap(values, bit) for bit in (1, 2, 3))
        return (values + one) + (two + three)
    bit = 1
    while bit < size:
        values = values + swap(values, bit)
        bit *= 2
    return values


def gather_fsdp(shard, axis):
    return lax.all_gather(shard, "fsdp", axis=axis, tiled=True)


def ring():
    return lax.axis_size("fsdp") == 4


def shift_fsdp(values, step):
    size = lax.axis_size("fsdp")
    return lax.ppermute(values, "fsdp", [(i, (i + step) % size) for i in range(size)])


def gather_pieces(shard, axis):
    if not ring():
        return [gather_fsdp(shard, axis)]
    return [shard] + [shift_fsdp(shard, -s) for s in range(1, lax.axis_size("fsdp"))]


def scatter_pieces(grads):
    if not ring():
        return [scatter_fsdp(grads, 0)]
    size = lax.axis_size("fsdp")
    rank = lax.axis_index("fsdp")
    rows = grads.shape[0] // size
    pieces = [
        lax.dynamic_slice_in_dim(grads, lax.rem(rank + s, size) * rows, rows) for s in range(size)
    ]
    low, high = jnp.split(pieces[2], 2, axis=1)
    return [pieces[0]] + [
        shift_fsdp(piece, s) for piece, s in ((pieces[1], 1), (low, 2), (high, 2), (pieces[3], 3))
    ]


def total_pieces(terms):
    if len(terms) == 1:
        return terms[0]
    own, one, low, high, three = terms
    two = jnp.concatenate([low, high], axis=1)
    return sum(term.astype(F32) for term in (own, two, one, three)).astype(BF16)


def scatter_fsdp(grads, axis):
    return lax.psum_scatter(grads, "fsdp", scatter_dimension=axis, tiled=True)


def halves(values, axis=-1):
    low, high = jnp.split(values, 2, axis=axis)
    first = lax.axis_index("ctx") == 0
    return jnp.where(first, low, high), jnp.where(first, high, low)


def join(mine, other, axis=-1):
    first = lax.axis_index("ctx") == 0
    low, high = jnp.where(first, mine, other), jnp.where(first, other, mine)
    return jnp.concatenate([low, high], axis=axis)


def quarters(mine):
    return jnp.stack(jnp.split(mine, 2, axis=1))


def after(values, *others):
    return lax.optimization_barrier((values,) + others)[0]


def on_device(
    tokens,
    cotangent,
    attn_weight,
    attn_momentum,
    attn_average,
    ffn_weight,
    ffn_momentum,
    ffn_average,
    vector_weight,
    vector_momentum,
    vector_average,
):
    tp_rank = lax.axis_index("tp")
    sib_rank = tp_rank ^ 1
    head_width = attn_weight.shape[2]
    unit_width = ffn_weight.shape[2]
    token_count = LEN * lax.axis_size("fsdp")
    matrix_rate = MATRIX_RATE / math.sqrt(token_count)
    vector_rate = VECTOR_RATE / math.sqrt(token_count)

    attn_low, attn_high = halves(attn_weight.astype(BF16))
    qkv_mine = gather_pieces(attn_low[:3], 1)

    own = tokens[0]
    rows = own.shape[0]
    pair = 2 * rows
    half = 4 * rows
    beside = across(own)
    facing = swap_ctx(own)
    diagonal = swap_both(own)
    if ring():
        others = swap_ctx(after(jnp.stack(qkv_mine[1:]), facing, diagonal))
        qkv_other = [attn_high[:3]] + [others[s] for s in range(len(qkv_mine) - 1)]
    else:
        qkv_other = [swap_ctx(qkv_mine[0])]
    up_low = quarters(halves(ffn_weight[0].astype(BF16))[0])
    out_low = jnp.concatenate([attn_low[3], attn_high[3]], axis=1)
    out_up_low = jnp.concatenate([out_low[None], up_low])
    out_up = gather_fsdp(after(out_up_low, *qkv_mine[-3:], facing, diagonal), 1)
    blocks = [own, beside, core(own), core(beside), facing, diagonal, core(facing), core(diagonal)]

    vec = vector_weight[: 6 * D].reshape(6, D)

    def columns(start, width):
        part = lax.dynamic_slice_in_dim(vector_weight, start, width)
        return jnp.concatenate(halves(part))

    biases = jnp.stack(
        [
            columns(6 * D + tp_rank * head_width, head_width),
            columns(7 * D + tp_rank * head_width, head_width),
        ]
    )
    bias_hidden = jnp.concatenate(
        [
            columns(8 * D + tp_rank * unit_width, unit_width),
            columns(8 * D + sib_rank * unit_width, unit_width),
        ]
    )[None]

    token_t, qkv_w, queries, keys, values, mixed_own, mixed_sib, lse = attend(
        blocks, qkv_mine, qkv_other, biases
    )
    down_low = jnp.concatenate(halves(ffn_weight[1].astype(BF16)), axis=1)
    down_low = after(down_low, mixed_own)
    if ring():
        low, high = jnp.split(down_low, 2, axis=1)
        spots = ((0, 0), (1, 0), (3, 0), (2, 0), (2, low.shape[1]))
        down_w = [down_low, shift_fsdp(down_low, -1), shift_fsdp(down_low, -3)]
        down_w += [shift_fsdp(low, -2), shift_fsdp(high, -2)]
    else:
        spots = ((0, 0),)
        down_w = [gather_fsdp(down_low, 0)]
    mixed_recv = core(mixed_sib)
    out_up = after(out_up, mixed_own)
    out_up_sib = core(out_up)
    up_other = swap_ctx(out_up[1:])
    out_w, attn_part, attn_far = out_project(mixed_own, mixed_recv, [out_up, out_up_sib])
    attn_recv = across(attn_far)
    if ring():
        attn_recv = after(attn_recv, down_w[1], down_w[2])
    res, first_low = norm_one(own, attn_part, attn_recv, vec)
    first_beside = across(first_low)

    if ring():
        first_beside = after(first_beside, down_w[3])
    up_other = after(up_other, first_beside)
    first_t, up_all, hidden_own, hidden_sib, slope_own, slope_sib = feed_up(
        first_low, first_beside, [out_up, up_other, out_up_sib, core(up_other)], bias_hidden
    )
    if ring():
        down_w[4] = after(down_w[4], hidden_own)
    down_all, down_part, down_far = feed_down(
        hidden_own, hidden_sib, spots, down_w, [core(w) for w in down_w]
    )
    layer_out, grad_second, grad_down, sums_two = norm_two(
        res, down_part, across(down_far), cotangent[0], vec
    )
    grad_down_t, grad_up_own, grad_up_sib, grad_bias_hidden, first_part, first_far = feed_back(
        grad_down, across(grad_down), slope_own, slope_sib, up_all, down_all
    )
    down_sib = grad_send(grad_down_t, hidden_sib)
    up_sib = grad_send(first_t, grad_up_sib)
    first_recv = after(across(first_far), down_sib, up_sib)
    grad_res, grad_attn, sums_one = norm_one_back(
        grad_second, first_part, first_recv, res, vec
    )
    grad_attn_beside = across(grad_attn)
    down_sum = grad_total(grad_down_t, hidden_own, after(core(down_sib), grad_attn))
    up_keep, up_send = grad_sum(first_t, grad_up_own, after(core(up_sib), grad_attn))

    def finish(mine):
        return join(mine, swap_ctx(mine)).astype(F32)

    def finish_whole(part):
        mine, other = jnp.split(part.astype(F32), 2, axis=1)
        recv_other, recv_mine = jnp.split(swap_ctx(part).astype(F32), 2, axis=1)
        return join(mine + recv_mine, other + recv_other)

    down_terms = scatter_pieces(down_sum)
    up_recv = swap_ctx(up_send)

    grad_attn_beside = after(grad_attn_beside, down_sum, up_send, *down_terms[1:2])
    grad_attn_t, grad_mixed_own, grad_mixed_sib = out_back(grad_attn, grad_attn_beside, out_w)
    grad_mixed = (grad_mixed_own, core(grad_mixed_sib))

    up_recv = after(up_recv, grad_mixed_sib)
    up_sum = (up_keep.astype(F32) + up_recv.astype(F32)).astype(BF16)
    up_terms = scatter_pieces(up_sum)
    mixed = (mixed_own, mixed_sib)
    heads = (queries, keys, values, mixed)
    query_other, kv_other, send = attend_back(*heads, grad_mixed, token_t, lse, 1)
    recv = swap_ctx(send)
    out_sib = grad_send(after(grad_attn_t, send, *down_terms[2:3]), mixed_recv, "out_send")
    out_keep, out_send = grad_sum(grad_attn_t, mixed_own, core(out_sib), "out_sum")
    grad_mixed = (grad_mixed[0], after(grad_mixed[1], up_sum, send, out_send))
    query_mine, kv_mine, grad_heads = attend_back(*heads, grad_mixed, token_t, lse, 0)
    query_mine = after(query_mine, recv, *down_terms[4:5], *up_terms[1:2])
    part = head_width // 2
    near, far, sibling = input_back(
        query_mine, query_other, kv_mine, kv_other, qkv_w, sums_one, sums_two, grad_bias_hidden
    )
    sib_recv = core(sibling)
    qkvo_sum = head_sum(grad_heads, recv, out_keep, swap_ctx(out_send))
    qkvo_mine = scatter_fsdp(qkvo_sum, 0)
    sib_recv = after(sib_recv, qkvo_sum)
    input_part, to_x, to_y, to_d, vec_part = fold(near, far, sibling, sib_recv, grad_res)
    from_x, from_y, from_d = across(to_x), swap_ctx(to_y), swap_both(to_d)
    input_grad = input_part
    for term in (from_x, from_y, from_d):
        input_grad = input_grad + term[:rows].astype(F32)
    vec_x, vec_y, vec_d = (term[rows:].astype(F32) for term in (from_x, from_y, from_d))
    vec_plane = (vec_part.astype(F32) + vec_x) + (vec_y + vec_d)
    vector_grad = sum_fsdp(vec_plane[:12]).reshape(-1)

    down_owned, up_owned = (
        total_pieces([after(term, from_y) for term in terms]) for terms in (down_terms, up_terms)
    )
    down_grad, up_grad = finish_whole(down_owned), finish(up_owned)
    ffn_grad = jnp.stack([up_grad, down_grad])
    ffn_new, ffn_momentum_new, ffn_average_new = nesterov(
        ffn_weight, ffn_momentum, ffn_average, ffn_grad, matrix_rate
    )
    qkvo_mine = after(qkvo_mine, input_grad, ffn_new, ffn_average_new, vec_plane)
    qkvo_other = swap_ctx(qkvo_mine)
    attn_grad = jnp.stack(
        [
            join(qkvo_mine[:, j * part : (j + 1) * part], qkvo_other[:, j * part : (j + 1) * part])
            for j in range(4)
        ]
    ).astype(F32)
    vector_new, vector_momentum_new, vector_average_new = nesterov(
        vector_weight, vector_momentum, vector_average, vector_grad, vector_rate
    )
    attn_new, attn_momentum_new, attn_average_new = nesterov(
        attn_weight, attn_momentum, attn_average, attn_grad, matrix_rate
    )
    return (
        layer_out[None],
        input_grad[None],
        attn_grad,
        attn_new,
        attn_momentum_new,
        attn_average_new,
        attn_new.astype(BF16),
        ffn_grad,
        ffn_new,
        ffn_momentum_new,
        ffn_average_new,
        ffn_new.astype(BF16),
        vector_grad,
        vector_new,
        vector_momentum_new,
        vector_average_new,
    )


def solution(mesh):
    rows = P("fsdp", ("ctx", "tp"), None)
    weight = P(None, "fsdp", "tp")
    return jax.shard_map(
        on_device,
        mesh=mesh,
        in_specs=(rows, rows) + (weight,) * 6 + (P(),) * 3,
        out_specs=(rows, rows) + (weight,) * 10 + (P(),) * 4,
        check_vma=False,
    )
```

```python
import functools
import math

import jax
import jax.numpy as jnp
from jax import lax
from jax.experimental import pallas as pl
from jax.experimental.pallas import tpu as pltpu
from jax.sharding import PartitionSpec as P

D = 1024
FF = 4096
HEAD_DIM = 64
LEN = 2048

NORM_EPSILON = 1e-05
MOMENTUM = 0.5
AVERAGE = 0.5
MATRIX_RATE = 0.1
VECTOR_RATE = 0.3

SCALE = HEAD_DIM ** (-0.5)
LOG2E = math.log2(math.e)
F32 = jnp.float32
BF16 = jnp.bfloat16
NT = (((1,), (1,)), ((), ()))
TN = (((0,), (0,)), ((), ()))
NN = (((1,), (0,)), ((), ()))


def dot(left, right, dims=NN):
    return lax.dot_general(left, right, dims, preferred_element_type=F32)


VMEM = pl.BlockSpec(memory_space=pltpu.VMEM)
FAR = pl.BlockSpec(memory_space=pltpu.HBM)
MEGA = 1024 * 1024
BUDGET = 56 * MEGA
WORK_UNIT = 1.2e10
WORK = {
    "attend": 0.001,
    "out_project": 0.001,
    "norm_one": 1.5,
    "feed_up": 8,
    "feed_down": 4,
    "norm_two": 2,
    "feed_back": 8,
    "grad_send": 10,
    "grad_sum": 3,
    "grad_total": 3,
    "norm_one_back": 2,
    "out_back": 2,
    "attend_back": 12,
    "head_sum": 0.01,
    "input_back": 0.01,
    "out_send": 0.01,
    "out_sum": 0.01,
    "fold": 0.01,
}


def cost(name):
    flops = int(WORK[name] * WORK_UNIT)
    return pl.CostEstimate(flops=flops, bytes_accessed=1, transcendentals=0)


def shape(dims, dtype):
    return jax.ShapeDtypeStruct(tuple(dims), dtype)


def tile(i, size):
    return pl.ds(pl.multiple_of(i * size, size), size)


class Copies:
    def __init__(self, sems):
        self.sems = sems
        self.begun = []
        self.open = []

    def start(self, src, dst):
        copy = pltpu.make_async_copy(src, dst, self.sems.at[len(self.begun)])
        copy.start()
        self.begun.append(copy)
        self.open.append(copy)
        return copy

    def wait(self, copies=None):
        for copy in list(self.open) if copies is None else copies:
            copy.wait()
            self.open.remove(copy)


def call(kernel, name, outs, far, near, scratch=(), copies=1, vmem=10):
    def body(*refs):
        io = Copies(refs[-1])
        kernel(io, *refs[:-1])
        io.wait()

    resident = list(near) + [out for out, is_far in outs if not is_far]
    resident = sum(max(MEGA // 16, a.size * a.dtype.itemsize) for a in resident)
    grant = max(vmem * MEGA, BUDGET - resident)
    return pl.pallas_call(
        body,
        in_specs=[FAR] * len(far) + [VMEM] * len(near),
        out_specs=[FAR if is_far else VMEM for _, is_far in outs],
        out_shape=[out for out, _ in outs],
        scratch_shapes=[*scratch, pltpu.SemaphoreType.DMA((copies,))],
        compiler_params=pltpu.CompilerParams(vmem_limit_bytes=grant),
        cost_estimate=cost(name),
        name=name,
    )(*far, *near)


def ring_rows(count, deep):
    size = deep // count
    rank = lax.axis_index("fsdp")
    return [tile(lax.rem(rank + s, count), size) if count > 1 else tile(0, size) for s in range(count)]


def head_masks(width):
    lane = lax.broadcasted_iota(jnp.int32, (1, width), 1) // HEAD_DIM
    return [(lane == h).astype(BF16) for h in range(width // HEAD_DIM)]


def attend_block(queries, k_ref, vt_ref, chunk):
    width = queries.shape[1]
    count = k_ref.shape[0]
    masked = [queries * mask for mask in head_masks(width)]
    units = [(h, c) for h in range(width // HEAD_DIM) for c in range(0, count, chunk)]

    def scores_of(unit):
        h, c = unit
        return dot(k_ref[c : c + chunk, :], masked[h], NT)

    tops, totals, outs = {}, {}, {}
    scores = scores_of(units[0])
    for i, unit in enumerate(units):
        current = scores
        if i + 1 < len(units):
            scores = scores_of(units[i + 1])
        h, c = unit
        top = jnp.max(current, axis=0, keepdims=True)
        weights = jnp.exp2((current - top) * (SCALE * LOG2E))
        tops[unit] = top
        totals[unit] = jnp.sum(weights, axis=0, keepdims=True)
        outs[unit] = dot(
            vt_ref[h * HEAD_DIM : (h + 1) * HEAD_DIM, c : c + chunk], weights.astype(BF16)
        )
    heads_out, lses = [], []
    for h in range(width // HEAD_DIM):
        mine = [(h, c) for c in range(0, count, chunk)]
        top = functools.reduce(jnp.maximum, [tops[u] for u in mine])
        share = [jnp.exp2((tops[u] - top) * (SCALE * LOG2E)) for u in mine]
        total = sum(totals[u] * f for u, f in zip(mine, share))
        out = sum(outs[u] * f for u, f in zip(mine, share))
        heads_out.append(out / total)
        lses.append(top * (SCALE * LOG2E) + jnp.log2(total))
    return jnp.concatenate(heads_out, axis=0), lses


def attend_kernel(count, io, *refs):
    blocks, refs = refs[:8], refs[8:]
    mine, refs = refs[:count], refs[count:]
    other, refs = refs[:count], refs[count:]
    bias_ref, refs = refs[0], refs[1:]
    xt_out, w_out, q_out, k_out, v_out, own_out, sib_out, lse_ref = refs[:8]
    x_ref, xt_ref, w_ref, q_ref, k_ref, v_ref, vt_ref, mixed_ref = refs[8:]
    rows, deep = blocks[0].shape
    part = mine[0].shape[2]
    width = 2 * part
    weights, tokens = [], []
    for at, low, high in zip(ring_rows(count, deep), mine, other):
        for j in range(3):
            weights.append(io.start(low.at[j], w_ref.at[at, j * width : j * width + part]))
            weights.append(
                io.start(high.at[j], w_ref.at[at, j * width + part : (j + 1) * width])
            )
    for i in range(8):
        tokens.append(io.start(blocks[i], x_ref.at[i * rows : (i + 1) * rows, :]))
    io.wait(weights)
    io.start(w_ref, w_out)
    for i in range(4):
        at = slice(i * 2 * rows, (i + 1) * 2 * rows)
        io.wait(tokens[2 * i : 2 * i + 2])
        x = x_ref[at, :]
        if i < 2:
            out = dot(x, w_ref[...])
            q_ref[at, :] = (out[:, :width] + bias_ref[0:1, :]).astype(BF16)
            out = out[:, width:]
        else:
            out = dot(x, w_ref[:, width:])
        values = (out[:, width:] + bias_ref[1:2, :]).astype(BF16)
        k_ref[at, :] = out[:, :width].astype(BF16)
        v_ref[at, :] = values
        vt_ref[:, at] = values.T
        xt_ref[:, at] = x.T
    for src, dst in ((xt_ref, xt_out), (q_ref, q_out), (k_ref, k_out), (v_ref, v_out)):
        io.start(src, dst)
    half = 4 * rows
    block = min(256, half // 2)
    chunk = min(512, 8 * rows)

    def body(i, carry):
        at = tile(i, block)
        out, lses = attend_block(q_ref[at, :], k_ref, vt_ref, chunk)
        mixed_ref[at, :] = out.T.astype(BF16)
        for h, lse in enumerate(lses):
            lse_ref[h : h + 1, at] = lse
        return carry

    lax.fori_loop(0, half // block // 2, body, 0)
    io.start(mixed_ref.at[: half // 2, :], own_out)
    lax.fori_loop(half // block // 2, half // block, body, 0)
    io.start(mixed_ref.at[half // 2 :, :], sib_out)


def attend(blocks, mine, other, biases):
    rows, deep = blocks[0].shape
    width = biases.shape[1]
    outs = [
        (shape((deep, 8 * rows), BF16), True),
        (shape((deep, 3 * width), BF16), True),
        (shape((4 * rows, width), BF16), True),
        (shape((8 * rows, width), BF16), True),
        (shape((8 * rows, width), BF16), True),
        (shape((2 * rows, width), BF16), True),
        (shape((2 * rows, width), BF16), True),
        (shape((width // HEAD_DIM, 4 * rows), F32), False),
    ]
    scratch = [
        pltpu.VMEM((8 * rows, deep), BF16),
        pltpu.VMEM((deep, 8 * rows), BF16),
        pltpu.VMEM((deep, 3 * width), BF16),
        pltpu.VMEM((4 * rows, width), BF16),
        pltpu.VMEM((8 * rows, width), BF16),
        pltpu.VMEM((8 * rows, width), BF16),
        pltpu.VMEM((width, 8 * rows), BF16),
        pltpu.VMEM((4 * rows, width), BF16),
    ]
    kernel = functools.partial(attend_kernel, len(mine))
    far = [*blocks, *mine, *other]
    count = 6 * len(mine) + 8 + 7
    return call(kernel, "attend", outs, far, [biases], scratch, count, 28)


def attend_back_kernel(part, io, *refs):
    ins, refs = refs[:8], refs[8:]
    lse_ref, refs = refs[0], refs[1:]
    dq_out, dkv_out, dw_ref = refs[:3]
    q_ref, k_ref, v_ref, o_ref, g_ref, xt_ref, kt_ref, dq_ref, dkv_ref, dk_acc, dv_acc = refs[3:]
    rows, width = q_ref.shape
    pair = rows // 2
    heads = width // HEAD_DIM
    cols = slice(part * width, (part + 1) * width)
    q_in, k_in, v_in, o0, o1, g0, g1, xt_in = ins
    loads = [
        io.start(k_in.at[:, cols], k_ref),
        io.start(q_in.at[:, cols], q_ref),
        io.start(g0.at[:, cols], g_ref.at[:pair, :]),
        io.start(g1.at[:, cols], g_ref.at[pair:, :]),
        io.start(o0.at[:, cols], o_ref.at[:pair, :]),
        io.start(o1.at[:, cols], o_ref.at[pair:, :]),
        io.start(v_in.at[:, cols], v_ref),
    ]
    late = [io.start(xt_in, xt_ref)]
    dk_acc[...] = jnp.zeros_like(dk_acc)
    dv_acc[...] = jnp.zeros_like(dv_acc)
    io.wait(loads)
    kt_ref[...] = k_ref[...].T
    masks = head_masks(width)
    block = min(256, pair)

    def body(i, carry):
        at = tile(i, block)
        queries = q_ref[at, :]
        grads = g_ref[at, :]
        product = (o_ref[at, :].astype(F32) * grads.astype(F32)).T
        outs, probs, gscores, qms, gms = [], [], [], [], []
        for h in range(heads):
            qm = queries * masks[h]
            gm = grads * masks[h]
            delta = col_sum(product[h * HEAD_DIM : (h + 1) * HEAD_DIM, :])
            scores = dot(k_ref[...], qm, NT)
            row = part * heads + h
            prob = jnp.exp2(scores * (SCALE * LOG2E) - lse_ref[row : row + 1, at])
            grad_prob = dot(v_ref[...], gm, NT)
            gscore = (prob * (grad_prob - delta)).astype(BF16)
            outs.append(dot(kt_ref[h * HEAD_DIM : (h + 1) * HEAD_DIM, :], gscore))
            probs.append(prob.astype(BF16))
            gscores.append(gscore)
            qms.append(qm)
            gms.append(gm)
        dv_acc[...] += dot(jnp.concatenate(probs, axis=1), jnp.concatenate(gms, axis=0))
        dk_acc[...] += dot(jnp.concatenate(gscores, axis=1), jnp.concatenate(qms, axis=0))
        dq_ref[at, :] = (jnp.concatenate(outs, axis=0).T * SCALE).astype(BF16)
        return carry

    lax.fori_loop(0, rows // block, body, 0)
    io.start(dq_ref, dq_out)
    dkv_ref[:, :width] = (dk_acc[...] * SCALE).astype(BF16)
    dkv_ref[:, width:] = dv_acc[...].astype(BF16)
    io.start(dkv_ref, dkv_out)
    io.wait(late)
    dw_ref[:, :width] = dot(xt_ref[:, :rows], dq_ref[...]).astype(BF16)
    dw_ref[:, width:] = dot(xt_ref[...], dkv_ref[...]).astype(BF16)


def attend_back(queries, keys, values, mixed, grads, tokens_t, lse, part):
    rows, both = queries.shape
    count = keys.shape[0]
    deep = tokens_t.shape[0]
    width = both // 2
    outs = [
        (shape((rows, width), BF16), True),
        (shape((count, both), BF16), True),
        (shape((deep, width + both), BF16), False),
    ]
    scratch = [
        pltpu.VMEM((rows, width), BF16),
        pltpu.VMEM((count, width), BF16),
        pltpu.VMEM((count, width), BF16),
        pltpu.VMEM((rows, width), BF16),
        pltpu.VMEM((rows, width), BF16),
        pltpu.VMEM((deep, count), BF16),
        pltpu.VMEM((width, count), BF16),
        pltpu.VMEM((rows, width), BF16),
        pltpu.VMEM((count, both), BF16),
        pltpu.VMEM((count, width), F32),
        pltpu.VMEM((count, width), F32),
    ]
    far = [queries, keys, values, *mixed, *grads, tokens_t]
    kernel = functools.partial(attend_back_kernel, part)
    return call(kernel, "attend_back", outs, far, [lse], scratch, 10, 28)


def split_store(out, near_ref, far_ref, at):
    rows = near_ref.shape[0]
    near_ref[:, at] = out[:rows]
    far_ref[:, at] = out[rows:].astype(BF16)


def out_kernel(io, w0, w1, own_in, recv, w_out, near_out, far_ref, w_ref, own, near_ref):
    width = own.shape[1]
    deep = w_ref.shape[0]
    io.start(own_in, own)
    io.start(w0.at[0], w_ref.at[:, :width])
    io.start(w1.at[0], w_ref.at[:, width:])
    io.wait()
    io.start(w_ref, w_out)
    for c in range(4):
        at = slice(c * deep // 4, (c + 1) * deep // 4)
        out = dot(own[...], w_ref[at, :width], NT) + dot(recv[...], w_ref[at, width:], NT)
        split_store(out, near_ref, far_ref, at)
        io.start(near_ref.at[:, at], near_out.at[:, at])


def out_project(own, recv, pieces):
    pair, width = own.shape
    deep = pieces[0].shape[1]
    outs = [
        (shape((deep, 2 * width), BF16), True),
        (shape((pair // 2, deep), F32), True),
        (shape((pair // 2, deep), BF16), False),
    ]
    scratch = [
        pltpu.VMEM((deep, 2 * width), BF16),
        pltpu.VMEM((pair, width), BF16),
        pltpu.VMEM((pair // 2, deep), F32),
    ]
    return call(out_kernel, "out_project", outs, [*pieces, own], [recv], scratch, 8)


def out_back_kernel(io, w_in, g0, g1, gt_out, own_out, sib_ref, w_ref, gt_ref, own_ref):
    rows = g0.shape[0]
    width = own_ref.shape[1]
    io.start(w_in, w_ref)
    io.wait()
    for i, ref in enumerate((g0, g1)):
        at = slice(i * rows, (i + 1) * rows)
        g = ref[...]
        out = dot(g, w_ref[...])
        own_ref[at, :] = out[:, :width].astype(BF16)
        sib_ref[at, :] = out[:, width:].astype(BF16)
        gt_ref[:, at] = g.T
        io.start(own_ref.at[at, :], own_out.at[at, :])
    io.start(gt_ref, gt_out)


def out_back(g0, g1, weights):
    rows, deep = g0.shape
    width = weights.shape[1] // 2
    outs = [
        (shape((deep, 2 * rows), BF16), True),
        (shape((2 * rows, width), BF16), True),
        (shape((2 * rows, width), BF16), False),
    ]
    scratch = [
        pltpu.VMEM(weights.shape, BF16),
        pltpu.VMEM((deep, 2 * rows), BF16),
        pltpu.VMEM((2 * rows, width), BF16),
    ]
    return call(out_back_kernel, "out_back", outs, [weights], [g0, g1], scratch, 4)


EXTRA = 16


def pack_rows(out_ref, one, two, sums, hidden):
    rank = lax.axis_index("tp")
    size = lax.axis_size("tp")
    first = lax.axis_index("ctx") == 0
    part = sums[0].shape[1]
    units = hidden.shape[1] // 2
    out_ref[...] = jnp.zeros_like(out_ref)
    out_ref[0:2, :] = one[0:2, :]
    out_ref[2:4, :] = two[0:2, :]
    out_ref[4:5, :] = one[2:3, :]
    out_ref[5:6, :] = two[2:3, :]
    for row, (mine, other) in ((6, sums[:2]), (7, sums[2:])):
        low, high = jnp.where(first, mine, other), jnp.where(first, other, mine)
        for t in range(size):
            keep = rank == t
            start = 2 * t * part
            out_ref[row : row + 1, start : start + part] = jnp.where(keep, low, 0.0)
            out_ref[row : row + 1, start + part : start + 2 * part] = jnp.where(keep, high, 0.0)
    for t in range(size):
        row = 8 + t
        total = jnp.where(rank == t, hidden[:, :units], 0.0)
        total = total + jnp.where((rank ^ 1) == t, hidden[:, units:], 0.0)
        mine, other = total[:, : units // 2], total[:, units // 2 :]
        out_ref[row : row + 1, : units // 2] = jnp.where(first, mine, other)
        out_ref[row : row + 1, units // 2 :] = jnp.where(first, other, mine)


def input_back_kernel(
    io, q0, q1, kv0, kv1, w_in, one, two, hidden, near_out, far_out, sib_ref,
    cat_ref, w_ref, near_ref, far_ref, vec_ref,
):
    half, part = q0.shape
    pair, deep = near_ref.shape
    io.start(w_in, w_ref)
    for j, (ref, at) in enumerate(((q0, 0), (q1, 0), (kv0, 0), (kv1, 0), (kv0, part), (kv1, part))):
        count = ref.shape[0]
        io.start(ref.at[:, at : at + part], cat_ref.at[:count, j * part : (j + 1) * part])
    io.wait()
    sib_ref[:pair, :] = dot(cat_ref[pair:half, :], w_ref[...], NT).astype(BF16)
    out = dot(cat_ref[half + pair :, 2 * part :], w_ref[:, 2 * part :], NT)
    sib_ref[pair:half, :] = out.astype(BF16)
    near_ref[...] = dot(cat_ref[:pair, :], w_ref[...], NT)
    io.start(near_ref, near_out)
    far_ref[...] = dot(cat_ref[half : half + pair, 2 * part :], w_ref[:, 2 * part :], NT)
    io.start(far_ref, far_out)
    sums = []
    for j, count in ((0, half), (1, half), (4, 2 * half), (5, 2 * half)):
        sums.append(col_sum(cat_ref[:count, j * part : (j + 1) * part].astype(F32)))
    pack_rows(vec_ref, one, two, sums, hidden)
    sib_ref[half:, :] = vec_ref[...].astype(BF16)


def input_back(q0, q1, kv0, kv1, weights, one, two, hidden):
    half, part = q0.shape
    deep = weights.shape[0]
    pair = half // 2
    outs = [
        (shape((pair, deep), F32), True),
        (shape((pair, deep), F32), True),
        (shape((half + EXTRA, deep), BF16), False),
    ]
    scratch = [
        pltpu.VMEM((kv0.shape[0], 6 * part), BF16),
        pltpu.VMEM(weights.shape, BF16),
        pltpu.VMEM((pair, deep), F32),
        pltpu.VMEM((pair, deep), F32),
        pltpu.VMEM((EXTRA, deep), F32),
    ]
    far = [q0, q1, kv0, kv1, weights]
    return call(input_back_kernel, "input_back", outs, far, [one, two, hidden], scratch, 9, 20)


def fold_kernel(
    io, near_in, far_in, rest_in, sent, recv, own_out, x_ref, y_ref, d_ref, vec_ref,
    near, far, rest, own_ref,
):
    rows = rest.shape[0]
    pair = 2 * rows
    for src, dst in ((near_in, near), (far_in, far), (rest_in, rest)):
        io.start(src, dst)
    io.wait()
    vec = sent[2 * pair :, :].astype(F32) + recv[2 * pair :, :].astype(F32)
    vec_ref[...] = vec.astype(BF16)
    for ref, term, at in ((x_ref, near, rows), (y_ref, far, 0), (d_ref, far, rows)):
        start = at if term is near else pair + at
        total = term[at : at + rows, :] + recv[start : start + rows, :].astype(F32)
        ref[:rows, :] = total.astype(BF16)
        ref[rows:, :] = vec.astype(BF16)
    own_ref[...] = rest[...] + near[:rows, :] + recv[:rows, :].astype(F32)
    io.start(own_ref, own_out)


def fold(near, far, sent, recv, rest):
    rows, deep = rest.shape
    outs = [(shape((rows, deep), F32), True)] + [(shape((rows + EXTRA, deep), BF16), False)] * 3
    outs += [(shape((EXTRA, deep), BF16), False)]
    scratch = [pltpu.VMEM((n * rows, deep), F32) for n in (2, 2, 1, 1)]
    return call(fold_kernel, "fold", outs, [near, far, rest], [sent, recv], scratch, 4, 12)


def grad_send_kernel(io, left, right, out_ref):
    out_ref[...] = dot(left[...], right[...]).astype(BF16)


def grad_send(left, right, name="grad_send"):
    outs = [(shape((left.shape[0], right.shape[1]), BF16), False)]
    return call(grad_send_kernel, name, outs, [], [left, right])[0]


def grad_sum_kernel(io, left, right, recv, keep_ref, send_ref):
    part = keep_ref.shape[1]
    for ref, at in ((send_ref, slice(part, 2 * part)), (keep_ref, slice(0, part))):
        ref[...] = (dot(left[...], right[:, at]) + recv[:, at].astype(F32)).astype(BF16)


def grad_sum(left, right, recv, name="grad_sum"):
    half = (shape((left.shape[0], right.shape[1] // 2), BF16), False)
    return call(grad_sum_kernel, name, [half] * 2, [], [left, right, recv])


def grad_total_kernel(io, left, right, recv, out_ref):
    out_ref[...] = (dot(left[...], right[...]) + recv[...].astype(F32)).astype(BF16)


def grad_total(left, right, recv):
    outs = [(shape((left.shape[0], right.shape[1]), BF16), False)]
    return call(grad_total_kernel, "grad_total", outs, [], [left, right, recv])[0]


def head_sum_kernel(io, grad, recv, keep, keep_recv, out_ref):
    width = recv.shape[1]
    out_ref[:, :width] = (grad[...].astype(F32) + recv[...].astype(F32)).astype(BF16)
    out_ref[:, width:] = (keep[...].astype(F32) + keep_recv[...].astype(F32)).astype(BF16)


def head_sum(grad, recv, keep, keep_recv):
    outs = [(shape((grad.shape[0], recv.shape[1] + keep.shape[1]), BF16), False)]
    return call(head_sum_kernel, "head_sum", outs, [], [grad, recv, keep, keep_recv])[0]


def gelu_pair(values):
    size = jnp.abs(values)
    t = 1.0 / (1.0 + (0.3275911 * math.sqrt(0.5)) * size)
    bell = jnp.exp2(values * values * (-0.5 * LOG2E))
    poly = t * (
        0.5 * 0.254829592
        + t
        * (
            0.5 * -0.284496736
            + t * (0.5 * 1.421413741 + t * (0.5 * -1.453152027 + t * (0.5 * 1.061405429)))
        )
    )
    tail = poly * bell
    cdf = jnp.where(values < 0, tail, 1.0 - tail)
    return values * cdf, cdf + values * bell * (1.0 / math.sqrt(2.0 * math.pi))


def up_kernel(
    io, mine, other, mine_sib, other_sib, x0, x1, bias_ref,
    xt_out, w_ref, act_own, act_sib, slope_own, slope_sib, xt_ref, x_ref,
):
    rows = x0.shape[0]
    step = mine.shape[2]
    loads = []
    for ref, first in ((mine, 1), (other, 0), (mine_sib, 1), (other_sib, 0)):
        for j in range(first, ref.shape[0]):
            at = len(loads) * step
            loads.append(io.start(ref.at[j], w_ref.at[:, at : at + step]))
    x_ref[:rows, :] = x0[...]
    x_ref[rows:, :] = x1[...]

    def matmul(c):
        io.wait(loads[c : c + 1])
        return dot(x_ref[...], w_ref[:, c * step : (c + 1) * step])

    following = matmul(0)
    for c in range(8):
        pre = following
        if c < 7:
            following = matmul(c + 1)
        act_ref, slope_ref = ((act_own, slope_own), (act_sib, slope_sib))[c // 4]
        at = slice((c % 4) * step, (c % 4 + 1) * step)
        act, slope = gelu_pair(pre + bias_ref[0:1, c * step : (c + 1) * step])
        act_ref[:, at] = act.astype(BF16)
        slope_ref[:, at] = slope.astype(BF16)
        if c == 0:
            xt_ref[...] = x_ref[...].T
            io.start(xt_ref, xt_out)


def feed_up(x0, x1, pieces, bias):
    rows, deep = x0.shape
    units = bias.shape[1]
    outs = [(shape((deep, 2 * rows), BF16), True), (shape((deep, units), BF16), False)]
    outs += [(shape((2 * rows, units // 2), BF16), False)] * 4
    scratch = [pltpu.VMEM((deep, 2 * rows), BF16), pltpu.VMEM((2 * rows, deep), BF16)]
    return call(up_kernel, "feed_up", outs, pieces, [x0, x1, bias], scratch, 9)


def down_kernel(spots, io, *refs):
    count = len(spots)
    own, sib, refs = refs[:count], refs[count : 2 * count], refs[2 * count :]
    act_own, act_sib, w_ref, near_out, far_ref, near_ref = refs
    deep = near_ref.shape[1]
    units = act_own.shape[1]
    rows = ring_rows(deep // own[0].shape[0], deep)
    for (piece, start), left, right in zip(spots, own, sib):
        width = left.shape[1]
        io.start(left, w_ref.at[rows[piece], start : start + width])
        io.start(right, w_ref.at[rows[piece], units + start : units + start + width])
    io.wait()
    for c in range(4):
        at = slice(c * deep // 4, (c + 1) * deep // 4)
        out = dot(act_own[...], w_ref[at, :units], NT) + dot(act_sib[...], w_ref[at, units:], NT)
        split_store(out, near_ref, far_ref, at)
        io.start(near_ref.at[:, at], near_out.at[:, at])


def feed_down(act_own, act_sib, spots, own, sib):
    pair, units = act_own.shape
    outs = [
        (shape((D, 2 * units), BF16), False),
        (shape((pair // 2, D), F32), True),
        (shape((pair // 2, D), BF16), False),
    ]
    kernel = functools.partial(down_kernel, spots)
    scratch = [pltpu.VMEM((pair // 2, D), F32)]
    near = [act_own, act_sib]
    return call(kernel, "feed_down", outs, [*own, *sib], near, scratch, 2 * len(own) + 4)


def feed_back_kernel(
    io, g0, g1, slope_own, slope_sib, up_ref, down_ref,
    gt_ref, gup_own, gup_sib, bias_ref, near_out, far_ref, g_ref, near_ref,
):
    rows, deep = g0.shape
    g_ref[:rows, :] = g0[...]
    g_ref[rows:, :] = g1[...]
    units = gup_own.shape[1]
    step = units // 2
    for c in range(4):
        slope_ref, gup_ref = ((slope_own, gup_own), (slope_sib, gup_sib))[c // 2]
        at = slice((c % 2) * step, (c % 2 + 1) * step)
        grad = dot(g_ref[...], down_ref[:, c * step : (c + 1) * step])
        grad = (grad * slope_ref[:, at].astype(F32)).astype(BF16)
        gup_ref[:, at] = grad
        bias_ref[0:1, c * step : (c + 1) * step] = col_sum(grad.astype(F32))
    for c in range(4):
        at = slice(c * deep // 4, (c + 1) * deep // 4)
        out = dot(gup_own[...], up_ref[at, :units], NT) + dot(gup_sib[...], up_ref[at, units:], NT)
        split_store(out, near_ref, far_ref, at)
        io.start(near_ref.at[:, at], near_out.at[:, at])
    gt_ref[...] = g_ref[...].T


def feed_back(g0, g1, slope_own, slope_sib, up_all, down_all):
    rows, deep = g0.shape
    units = slope_own.shape[1]
    outs = [(shape((deep, 2 * rows), BF16), False)]
    outs += [(shape((2 * rows, units), BF16), False)] * 2
    outs += [(shape((1, 2 * units), F32), False), (shape((rows, deep), F32), True)]
    outs += [(shape((rows, deep), BF16), False)]
    near = [g0, g1, slope_own, slope_sib, up_all, down_all]
    scratch = [pltpu.VMEM((2 * rows, deep), BF16), pltpu.VMEM((rows, deep), F32)]
    return call(feed_back_kernel, "feed_back", outs, [], near, scratch, 4)


def row_mean(values):
    return jnp.mean(values, axis=-1, keepdims=True)


def col_sum(values):
    return jnp.sum(values, axis=0, keepdims=True)


def normalize(values):
    centered = values - row_mean(values)
    inverse = lax.rsqrt(row_mean(centered * centered) + NORM_EPSILON)
    return centered * inverse, inverse


def norm_back(grad_out, normed, inverse, gain):
    grad = grad_out * gain
    return inverse * (grad - row_mean(grad) - normed * row_mean(grad * normed))


def load_rows(io, *pairs):
    for src, dst in pairs:
        io.start(src, dst)
    io.wait()


def norm_one_kernel(io, own_in, part_in, recv, vec, res_out, low_ref, own, part, res_ref):
    load_rows(io, (own_in, own), (part_in, part))
    attn_out = part[...] + recv[...].astype(F32) + vec[4:5, :]
    res = own[...].astype(F32) + attn_out
    res_ref[...] = res
    io.start(res_ref, res_out)
    low_ref[...] = (normalize(res)[0] * vec[0:1, :] + vec[1:2, :]).astype(BF16)


def norm_one(own, part, recv, vec):
    dims = own.shape
    outs = [(shape(dims, F32), True), (shape(dims, BF16), False)]
    scratch = [pltpu.VMEM(dims, t) for t in (BF16, F32, F32)]
    return call(norm_one_kernel, "norm_one", outs, [own, part], [recv, vec], scratch, 3)


def norm_two_kernel(
    io, res_in, part_in, given_in, recv, vec, out_out, grad_out, low_ref, sums_ref,
    res, part, given_ref, out_ref, grad_ref,
):
    load_rows(io, (res_in, res), (part_in, part), (given_in, given_ref))
    first = normalize(res[...])[0] * vec[0:1, :] + vec[1:2, :]
    down_out = part[...] + recv[...].astype(F32) + vec[5:6, :]
    normed, inverse = normalize(first + down_out)
    given = given_ref[...].astype(F32)
    grad = norm_back(given, normed, inverse, vec[2:3, :])
    low = grad.astype(BF16)
    low_ref[...] = low
    grad_ref[...] = grad
    io.start(grad_ref, grad_out)
    out_ref[...] = (normed * vec[2:3, :] + vec[3:4, :]).astype(BF16)
    io.start(out_ref, out_out)
    sums_ref[0:1, :] = col_sum(given * normed)
    sums_ref[1:2, :] = col_sum(given)
    sums_ref[2:3, :] = col_sum(low.astype(F32))


def norm_two(res, part, recv, cotangent, vec):
    rows, deep = dims = res.shape
    outs = [(shape(dims, BF16), True), (shape(dims, F32), True), (shape(dims, BF16), False)]
    outs += [(shape((3, deep), F32), False)]
    scratch = [pltpu.VMEM(dims, t) for t in (F32, F32, BF16, BF16, F32)]
    far = [res, part, cotangent]
    return call(norm_two_kernel, "norm_two", outs, far, [recv, vec], scratch, 5)


def norm_one_back_kernel(
    io, second_in, part_in, res_in, recv, vec, grad_out, low_ref, sums_ref,
    second, part, res, grad_ref,
):
    load_rows(io, (second_in, second), (part_in, part), (res_in, res))
    normed, inverse = normalize(res[...])
    given = second[...] + part[...] + recv[...].astype(F32)
    grad = norm_back(given, normed, inverse, vec[0:1, :])
    low = grad.astype(BF16)
    low_ref[...] = low
    grad_ref[...] = grad
    io.start(grad_ref, grad_out)
    sums_ref[0:1, :] = col_sum(given * normed)
    sums_ref[1:2, :] = col_sum(given)
    sums_ref[2:3, :] = col_sum(low.astype(F32))


def norm_one_back(grad_second, part, recv, res, vec):
    rows, deep = dims = part.shape
    outs = [(shape(dims, F32), True), (shape(dims, BF16), False), (shape((3, deep), F32), False)]
    scratch = [pltpu.VMEM(dims, F32)] * 4
    far = [grad_second, part, res]
    return call(norm_one_back_kernel, "norm_one_back", outs, far, [recv, vec], scratch, 4)


def nesterov(weights, momentum, average, gradient, step_rate):
    momentum_new = MOMENTUM * momentum + gradient
    weight_new = weights - step_rate * (gradient + MOMENTUM * momentum_new)
    return (weight_new, momentum_new, AVERAGE * average + (1.0 - AVERAGE) * weight_new)


def swap_tp(values, bit):
    size = lax.axis_size("tp")
    return lax.ppermute(values, "tp", [(i, i ^ bit) for i in range(size)])


def core(values):
    return swap_tp(values, 1)


def across(values):
    return swap_tp(values, 2)


def swap_ctx(values):
    return lax.ppermute(values, "ctx", [(0, 1), (1, 0)])


def swap_both(values):
    size = lax.axis_size("tp")
    return lax.ppermute(values, ("ctx", "tp"), [(i, i ^ (size + 2)) for i in range(2 * size)])


def gather_fsdp(shard, axis):
    return lax.all_gather(shard, "fsdp", axis=axis, tiled=True)


def ring():
    return lax.axis_size("fsdp") == 4


def shift_fsdp(values, step):
    size = lax.axis_size("fsdp")
    return lax.ppermute(values, "fsdp", [(i, (i + step) % size) for i in range(size)])


def gather_pieces(shard, axis):
    if not ring():
        return [gather_fsdp(shard, axis)]
    return [shard] + [shift_fsdp(shard, -s) for s in range(1, lax.axis_size("fsdp"))]


def scatter_pieces(grads):
    if not ring():
        return [scatter_fsdp(grads, 0)]
    size = lax.axis_size("fsdp")
    rank = lax.axis_index("fsdp")
    rows = grads.shape[0] // size
    pieces = [
        lax.dynamic_slice_in_dim(grads, lax.rem(rank + s, size) * rows, rows) for s in range(size)
    ]
    low, high = jnp.split(pieces[2], 2, axis=1)
    return [pieces[0]] + [
        shift_fsdp(piece, s) for piece, s in ((pieces[1], 1), (low, 2), (high, 2), (pieces[3], 3))
    ]


def total_pieces(terms):
    if len(terms) == 1:
        return terms[0]
    own, one, low, high, three = terms
    two = jnp.concatenate([low, high], axis=1)
    return sum(term.astype(F32) for term in (own, two, one, three)).astype(BF16)


def scatter_fsdp(grads, axis):
    return lax.psum_scatter(grads, "fsdp", scatter_dimension=axis, tiled=True)


def halves(values, axis=-1):
    low, high = jnp.split(values, 2, axis=axis)
    first = lax.axis_index("ctx") == 0
    return jnp.where(first, low, high), jnp.where(first, high, low)


def join(mine, other, axis=-1):
    first = lax.axis_index("ctx") == 0
    low, high = jnp.where(first, mine, other), jnp.where(first, other, mine)
    return jnp.concatenate([low, high], axis=axis)


def quarters(mine):
    return jnp.stack(jnp.split(mine, 2, axis=1))


def after(values, *others):
    return lax.optimization_barrier((values,) + others)[0]


def on_device(
    tokens,
    cotangent,
    attn_weight,
    attn_momentum,
    attn_average,
    ffn_weight,
    ffn_momentum,
    ffn_average,
    vector_weight,
    vector_momentum,
    vector_average,
):
    tp_rank = lax.axis_index("tp")
    sib_rank = tp_rank ^ 1
    head_width = attn_weight.shape[2]
    unit_width = ffn_weight.shape[2]
    token_count = LEN * lax.axis_size("fsdp")
    matrix_rate = MATRIX_RATE / math.sqrt(token_count)
    vector_rate = VECTOR_RATE / math.sqrt(token_count)

    attn_low, attn_high = halves(attn_weight.astype(BF16))
    qkv_mine = gather_pieces(attn_low[:3], 1)

    own = tokens[0]
    rows = own.shape[0]
    pair = 2 * rows
    half = 4 * rows
    beside = across(own)
    facing = swap_ctx(own)
    diagonal = swap_both(own)
    if ring():
        others = swap_ctx(after(jnp.stack(qkv_mine[1:]), facing, diagonal))
        qkv_other = [attn_high[:3]] + [others[s] for s in range(len(qkv_mine) - 1)]
    else:
        qkv_other = [swap_ctx(qkv_mine[0])]
    up_low = quarters(halves(ffn_weight[0].astype(BF16))[0])
    out_low = jnp.concatenate([attn_low[3], attn_high[3]], axis=1)
    out_up_low = jnp.concatenate([out_low[None], up_low])
    out_up = gather_fsdp(after(out_up_low, *qkv_mine[-3:]), 1)
    blocks = [own, beside, core(own), core(beside), facing, diagonal, core(facing), core(diagonal)]

    vec = vector_weight[: 6 * D].reshape(6, D)

    def columns(start, width):
        part = lax.dynamic_slice_in_dim(vector_weight, start, width)
        return jnp.concatenate(halves(part))

    biases = jnp.stack(
        [
            columns(6 * D + tp_rank * head_width, head_width),
            columns(7 * D + tp_rank * head_width, head_width),
        ]
    )
    bias_hidden = jnp.concatenate(
        [
            columns(8 * D + tp_rank * unit_width, unit_width),
            columns(8 * D + sib_rank * unit_width, unit_width),
        ]
    )[None]

    token_t, qkv_w, queries, keys, values, mixed_own, mixed_sib, lse = attend(
        blocks, qkv_mine, qkv_other, biases
    )
    down_low = jnp.concatenate(halves(ffn_weight[1].astype(BF16)), axis=1)
    down_low = after(down_low, mixed_own)
    if ring():
        low, high = jnp.split(down_low, 2, axis=1)
        spots = ((0, 0), (1, 0), (3, 0), (2, 0), (2, low.shape[1]))
        down_w = [down_low, shift_fsdp(down_low, -1), shift_fsdp(down_low, -3)]
        down_w += [shift_fsdp(low, -2), shift_fsdp(high, -2)]
    else:
        spots = ((0, 0),)
        down_w = [gather_fsdp(down_low, 0)]
    mixed_recv = core(mixed_sib)
    out_up = after(out_up, mixed_own)
    out_up_sib = core(out_up)
    up_other = swap_ctx(out_up[1:])
    out_w, attn_part, attn_far = out_project(mixed_own, mixed_recv, [out_up, out_up_sib])
    attn_recv = across(attn_far)
    if ring():
        attn_recv = after(attn_recv, down_w[1], down_w[2])
    res, first_low = norm_one(own, attn_part, attn_recv, vec)
    first_beside = across(first_low)

    if ring():
        first_beside = after(first_beside, down_w[3])
    up_other = after(up_other, first_beside)
    first_t, up_all, hidden_own, hidden_sib, slope_own, slope_sib = feed_up(
        first_low, first_beside, [out_up, up_other, out_up_sib, core(up_other)], bias_hidden
    )
    if ring():
        down_w[4] = after(down_w[4], hidden_own)
    down_all, down_part, down_far = feed_down(
        hidden_own, hidden_sib, spots, down_w, [core(w) for w in down_w]
    )
    layer_out, grad_second, grad_down, sums_two = norm_two(
        res, down_part, across(down_far), cotangent[0], vec
    )
    grad_down_t, grad_up_own, grad_up_sib, grad_bias_hidden, first_part, first_far = feed_back(
        grad_down, across(grad_down), slope_own, slope_sib, up_all, down_all
    )
    down_sib = grad_send(grad_down_t, hidden_sib)
    up_sib = grad_send(first_t, grad_up_sib)
    first_recv = after(across(first_far), down_sib, up_sib)
    grad_res, grad_attn, sums_one = norm_one_back(
        grad_second, first_part, first_recv, res, vec
    )
    grad_attn_beside = across(grad_attn)
    down_sum = grad_total(grad_down_t, hidden_own, after(core(down_sib), grad_attn))
    up_keep, up_send = grad_sum(first_t, grad_up_own, after(core(up_sib), grad_attn))

    def finish(mine):
        return join(mine, swap_ctx(mine)).astype(F32)

    def finish_whole(part):
        mine, other = jnp.split(part.astype(F32), 2, axis=1)
        recv_other, recv_mine = jnp.split(swap_ctx(part).astype(F32), 2, axis=1)
        return join(mine + recv_mine, other + recv_other)

    down_terms = scatter_pieces(down_sum)
    up_recv = swap_ctx(up_send)

    grad_attn_beside = after(grad_attn_beside, down_sum, up_send, *down_terms[1:2])
    grad_attn_t, grad_mixed_own, grad_mixed_sib = out_back(grad_attn, grad_attn_beside, out_w)
    grad_mixed = (grad_mixed_own, core(grad_mixed_sib))

    up_recv = after(up_recv, grad_mixed_sib)
    up_sum = (up_keep.astype(F32) + up_recv.astype(F32)).astype(BF16)
    up_terms = scatter_pieces(up_sum)
    mixed = (mixed_own, mixed_sib)
    heads = (queries, keys, values, mixed)
    query_other, kv_other, send = attend_back(*heads, grad_mixed, token_t, lse, 1)
    recv = swap_ctx(send)
    out_sib = grad_send(after(grad_attn_t, send, *down_terms[2:3]), mixed_recv, "out_send")
    out_keep, out_send = grad_sum(grad_attn_t, mixed_own, core(out_sib), "out_sum")
    grad_mixed = (grad_mixed[0], after(grad_mixed[1], up_sum, send, out_send))
    query_mine, kv_mine, grad_heads = attend_back(*heads, grad_mixed, token_t, lse, 0)
    query_mine = after(query_mine, recv, *down_terms[4:5], *up_terms[1:2])
    part = head_width // 2
    near, far, sibling = input_back(
        query_mine, query_other, kv_mine, kv_other, qkv_w, sums_one, sums_two, grad_bias_hidden
    )
    sib_recv = core(sibling)
    qkvo_sum = head_sum(grad_heads, recv, out_keep, swap_ctx(out_send))
    qkvo_mine = scatter_fsdp(qkvo_sum, 0)
    sib_recv = after(sib_recv, qkvo_sum)
    input_part, to_x, to_y, to_d, vec_part = fold(near, far, sibling, sib_recv, grad_res)
    down_owned = total_pieces([after(term, to_y) for term in down_terms])
    down_grad = finish_whole(down_owned)
    from_x, from_y, from_d = across(to_x), swap_ctx(to_y), swap_both(to_d)
    up_owned = total_pieces([after(term, from_y) for term in up_terms])
    up_grad = finish(up_owned)
    input_grad = input_part
    for term in (from_x, from_y, from_d):
        input_grad = input_grad + term[:rows].astype(F32)
    vec_x, vec_y, vec_d = (term[rows:].astype(F32) for term in (from_x, from_y, from_d))
    vec_plane = (vec_part.astype(F32) + vec_x) + (vec_y + vec_d)
    vector_grad = lax.psum(vec_plane[:12], "fsdp").reshape(-1)

    ffn_grad = jnp.stack([up_grad, down_grad])
    ffn_new, ffn_momentum_new, ffn_average_new = nesterov(
        ffn_weight, ffn_momentum, ffn_average, ffn_grad, matrix_rate
    )
    qkvo_mine = after(qkvo_mine, from_x, from_y, from_d)
    qkvo_other = swap_ctx(qkvo_mine)
    attn_grad = jnp.stack(
        [
            join(qkvo_mine[:, j * part : (j + 1) * part], qkvo_other[:, j * part : (j + 1) * part])
            for j in range(4)
        ]
    ).astype(F32)
    vector_new, vector_momentum_new, vector_average_new = nesterov(
        vector_weight, vector_momentum, vector_average, vector_grad, vector_rate
    )
    attn_new, attn_momentum_new, attn_average_new = nesterov(
        attn_weight, attn_momentum, attn_average, attn_grad, matrix_rate
    )
    return (
        layer_out[None],
        input_grad[None],
        attn_grad,
        attn_new,
        attn_momentum_new,
        attn_average_new,
        attn_new.astype(BF16),
        ffn_grad,
        ffn_new,
        ffn_momentum_new,
        ffn_average_new,
        ffn_new.astype(BF16),
        vector_grad,
        vector_new,
        vector_momentum_new,
        vector_average_new,
    )


def solution(mesh):
    rows = P("fsdp", ("ctx", "tp"), None)
    weight = P(None, "fsdp", "tp")
    return jax.shard_map(
        on_device,
        mesh=mesh,
        in_specs=(rows, rows) + (weight,) * 6 + (P(),) * 3,
        out_specs=(rows, rows) + (weight,) * 10 + (P(),) * 4,
        check_vma=False,
    )
```

```python
import functools
import math

import jax
import jax.numpy as jnp
from jax import lax
from jax.experimental import pallas as pl
from jax.experimental.pallas import tpu as pltpu
from jax.sharding import PartitionSpec as P

D = 1024
FF = 4096
HEAD_DIM = 64
LEN = 2048

NORM_EPSILON = 1e-05
MOMENTUM = 0.5
AVERAGE = 0.5
MATRIX_RATE = 0.1
VECTOR_RATE = 0.3

SCALE = HEAD_DIM ** (-0.5)
LOG2E = math.log2(math.e)
F32 = jnp.float32
BF16 = jnp.bfloat16
NT = (((1,), (1,)), ((), ()))
TN = (((0,), (0,)), ((), ()))
NN = (((1,), (0,)), ((), ()))


def dot(left, right, dims=NN):
    return lax.dot_general(left, right, dims, preferred_element_type=F32)


VMEM = pl.BlockSpec(memory_space=pltpu.VMEM)
ANY = pl.BlockSpec(memory_space=pl.ANY)
MEGA = 1024 * 1024
WORK_UNIT = 1.2e10


WORK = {
    "project": 0.001,
    "attend": 0.001,
    "out_project": 0.001,
    "norm_one": 1.5,
    "feed_up": 8,
    "feed_down": 4,
    "norm_two": 2,
    "feed_back": 8,
    "grad_send": 10,
    "grad_sum": 3,
    "norm_one_back": 2,
    "out_back": 2,
    "attend_back": 12,
    "head_send": 3,
    "head_sum": 4,
    "input_back": 4,
    "fold": 1.5,
    "grad_total": 3,
}


def cost(name):
    flops = int(WORK[name] * WORK_UNIT)
    return pl.CostEstimate(flops=flops, bytes_accessed=1, transcendentals=0)


def shape(dims, dtype):
    return jax.ShapeDtypeStruct(tuple(dims), dtype)


def tile(i, size):
    return pl.ds(pl.multiple_of(i * size, size), size)


def call_whole(kernel, name, out_shape, far_args, near_args, scratch=(), copies=0):
    scratch = list(scratch)
    if copies:
        scratch.append(pltpu.SemaphoreType.DMA((copies,)))
    return pl.pallas_call(
        kernel,
        in_specs=[ANY] * len(far_args) + [VMEM] * len(near_args),
        out_specs=[VMEM] * len(out_shape),
        out_shape=list(out_shape),
        scratch_shapes=scratch,
        compiler_params=pltpu.CompilerParams(vmem_limit_bytes=8 * MEGA),
        cost_estimate=cost(name),
        name=name,
    )(*far_args, *near_args)


def start_all(pairs, sems):
    copies = [pltpu.make_async_copy(src, dst, sems.at[i]) for i, (src, dst) in enumerate(pairs)]
    for copy in copies:
        copy.start()
    return copies


def head_masks(width):
    lane = lax.broadcasted_iota(jnp.int32, (1, width), 1) // HEAD_DIM
    return [(lane == h).astype(BF16) for h in range(width // HEAD_DIM)]


def attend_kernel(chunk, q_ref, k_ref, v_ref, own_ref, sib_ref, lse_ref, vt_ref):
    heads = q_ref.shape[1] // HEAD_DIM
    count = k_ref.shape[0]
    step = pl.program_id(0)

    @pl.when(step == 0)
    def _():
        vt_ref[...] = v_ref[...].T

    queries = q_ref[...]
    masked = [queries * mask for mask in head_masks(q_ref.shape[1])]
    units = [(h, c) for h in range(heads) for c in range(0, count, chunk)]

    def scores_of(unit):
        h, c = unit
        return dot(k_ref[c : c + chunk, :], masked[h], NT)

    tops, totals, outs = {}, {}, {}
    scores = scores_of(units[0])
    for i, unit in enumerate(units):
        current = scores
        if i + 1 < len(units):
            scores = scores_of(units[i + 1])
        h, c = unit
        top = jnp.max(current, axis=0, keepdims=True)
        weights = jnp.exp2((current - top) * (SCALE * LOG2E))
        tops[unit] = top
        totals[unit] = jnp.sum(weights, axis=0, keepdims=True)
        outs[unit] = dot(
            vt_ref[h * HEAD_DIM : (h + 1) * HEAD_DIM, c : c + chunk], weights.astype(BF16)
        )
    heads_out = []
    for h in range(heads):
        mine = [(h, c) for c in range(0, count, chunk)]
        top = functools.reduce(jnp.maximum, [tops[u] for u in mine])
        share = [jnp.exp2((tops[u] - top) * (SCALE * LOG2E)) for u in mine]
        total = sum(totals[u] * f for u, f in zip(mine, share))
        out = sum(outs[u] * f for u, f in zip(mine, share))
        heads_out.append(out / total)
        lse_ref[h : h + 1, :] = top * (SCALE * LOG2E) + jnp.log2(total)
    mixed = jnp.concatenate(heads_out, axis=0).T.astype(BF16)
    steps = pl.num_programs(0)

    @pl.when(step < steps // 2)
    def _():
        own_ref[...] = mixed

    @pl.when(step >= steps // 2)
    def _():
        sib_ref[...] = mixed


def attend(queries, keys, values):
    rows, width = queries.shape
    block = min(256, rows // 2)
    steps = rows // block
    heads = width // HEAD_DIM
    half_blocks = steps // 2
    return pl.pallas_call(
        functools.partial(attend_kernel, min(512, keys.shape[0])),
        grid=(steps,),
        in_specs=[
            pl.BlockSpec((block, width), lambda i: (i, 0)),
            pl.BlockSpec(keys.shape, lambda i: (0, 0)),
            pl.BlockSpec(values.shape, lambda i: (0, 0)),
        ],
        out_specs=[
            pl.BlockSpec((block, width), lambda i: (jnp.minimum(i, half_blocks - 1), 0)),
            pl.BlockSpec((block, width), lambda i: (jnp.maximum(i - half_blocks, 0), 0)),
            pl.BlockSpec((heads, block), lambda i: (0, i)),
        ],
        out_shape=[
            shape((rows // 2, width), BF16),
            shape((rows // 2, width), BF16),
            shape((heads, rows), F32),
        ],
        scratch_shapes=[pltpu.VMEM((width, keys.shape[0]), BF16)],
        compiler_params=pltpu.CompilerParams(vmem_limit_bytes=16 * MEGA),
        cost_estimate=cost("attend"),
        name="attend",
    )(queries, keys, values)


def attend_back_kernel(
    part, q_ref, k_ref, v_ref, o0_ref, o1_ref, g0_ref, g1_ref, lse_ref,
    dq_ref, dkv_ref, kt_ref, dk_acc, dv_acc, o_ref, g_ref,
):
    width = q_ref.shape[1]
    heads = width // HEAD_DIM
    step = pl.program_id(0)
    steps = pl.num_programs(0)

    @pl.when(step == 0)
    def _():
        kt_ref[...] = k_ref[...].T
        dk_acc[...] = jnp.zeros_like(dk_acc)
        dv_acc[...] = jnp.zeros_like(dv_acc)

    @pl.when(step < steps // 2)
    def _():
        o_ref[...] = o0_ref[...]
        g_ref[...] = g0_ref[...]

    @pl.when(step >= steps // 2)
    def _():
        o_ref[...] = o1_ref[...]
        g_ref[...] = g1_ref[...]

    queries = q_ref[...]
    grads = g_ref[...]
    masks = head_masks(width)
    product = (o_ref[...].astype(F32) * grads.astype(F32)).T
    outs, probs, gscores, qms, gms = [], [], [], [], []
    for h in range(heads):
        qm = queries * masks[h]
        gm = grads * masks[h]
        delta = jnp.sum(product[h * HEAD_DIM : (h + 1) * HEAD_DIM, :], axis=0, keepdims=True)
        scores = dot(k_ref[...], qm, NT)
        row = part * heads + h
        prob = jnp.exp2(scores * (SCALE * LOG2E) - lse_ref[row : row + 1, :])
        grad_prob = dot(v_ref[...], gm, NT)
        gscore = (prob * (grad_prob - delta)).astype(BF16)
        outs.append(dot(kt_ref[h * HEAD_DIM : (h + 1) * HEAD_DIM, :], gscore))
        probs.append(prob.astype(BF16))
        gscores.append(gscore)
        qms.append(qm)
        gms.append(gm)
    dv_acc[...] += dot(jnp.concatenate(probs, axis=1), jnp.concatenate(gms, axis=0))
    dk_acc[...] += dot(jnp.concatenate(gscores, axis=1), jnp.concatenate(qms, axis=0))
    dq_ref[...] = (jnp.concatenate(outs, axis=0).T * SCALE).astype(BF16)

    @pl.when(step == steps - 1)
    def _():
        dkv_ref[:, :width] = (dk_acc[...] * SCALE).astype(BF16)
        dkv_ref[:, width:] = dv_acc[...].astype(BF16)


def attend_back(queries, keys, values, mixed, grads, lse, part):
    rows, both = queries.shape
    count = keys.shape[0]
    width = both // 2
    block = min(256, rows // 2)
    half_blocks = rows // 2 // block
    row_spec = pl.BlockSpec((block, width), lambda i: (i, part))
    own_spec = pl.BlockSpec((block, width), lambda i: (jnp.minimum(i, half_blocks - 1), part))
    sib_spec = pl.BlockSpec((block, width), lambda i: (jnp.maximum(i - half_blocks, 0), part))
    full_spec = pl.BlockSpec((count, width), lambda i: (0, part))
    lse_spec = pl.BlockSpec((lse.shape[0], block), lambda i: (0, i))
    return pl.pallas_call(
        functools.partial(attend_back_kernel, part),
        grid=(rows // block,),
        in_specs=[row_spec, full_spec, full_spec] + [own_spec, sib_spec] * 2 + [lse_spec],
        out_specs=[
            pl.BlockSpec((block, width), lambda i: (i, 0)),
            pl.BlockSpec((count, both), lambda i: (0, 0)),
        ],
        out_shape=[shape((rows, width), BF16), shape((count, both), BF16)],
        scratch_shapes=[
            pltpu.VMEM((width, count), BF16),
            pltpu.VMEM((count, width), F32),
            pltpu.VMEM((count, width), F32),
            pltpu.VMEM((block, width), BF16),
            pltpu.VMEM((block, width), BF16),
        ],
        compiler_params=pltpu.CompilerParams(vmem_limit_bytes=16 * MEGA),
        cost_estimate=cost("attend_back"),
        name="attend_back",
    )(queries, keys, values, *mixed, *grads, lse)


def ring_rows(count, deep):
    size = deep // count
    rank = lax.axis_index("fsdp")
    return [tile(lax.rem(rank + s, count), size) if count > 1 else tile(0, size) for s in range(count)]


def project_kernel(count, *refs):
    blocks, refs = refs[:8], refs[8:]
    mine, refs = refs[:count], refs[count:]
    other, refs = refs[:count], refs[count:]
    bias_ref, xt_ref, w_ref, q_ref, k_ref, v_ref, x_ref, sems = refs
    rows = blocks[0].shape[0]
    deep = x_ref.shape[1]
    part = mine[0].shape[2]
    width = 2 * part
    pairs = []
    for at, low, high in zip(ring_rows(count, deep), mine, other):
        for j in range(3):
            pairs.append((low.at[j], w_ref.at[at, j * width : j * width + part]))
            pairs.append((high.at[j], w_ref.at[at, j * width + part : (j + 1) * width]))
    weights = len(pairs)
    for i in range(8):
        pairs.append((blocks[i], x_ref.at[i * rows : (i + 1) * rows, :]))
    copies = start_all(pairs, sems)
    for copy in copies[:weights]:
        copy.wait()
    for i in range(4):
        at = slice(i * 2 * rows, (i + 1) * 2 * rows)
        for copy in copies[weights + 2 * i : weights + 2 * i + 2]:
            copy.wait()
        x = x_ref[at, :]
        if i < 2:
            out = dot(x, w_ref[...])
            q_ref[at, :] = (out[:, :width] + bias_ref[0:1, :]).astype(BF16)
            out = out[:, width:]
        else:
            out = dot(x, w_ref[:, width:])
        k_ref[at, :] = out[:, :width].astype(BF16)
        v_ref[at, :] = (out[:, width:] + bias_ref[1:2, :]).astype(BF16)
        xt_ref[:, at] = x.T


def project(blocks, mine, other, biases):
    rows, deep = blocks[0].shape
    width = biases.shape[1]
    out = [
        shape((deep, 8 * rows), BF16),
        shape((deep, 3 * width), BF16),
        shape((4 * rows, width), BF16),
        shape((8 * rows, width), BF16),
        shape((8 * rows, width), BF16),
    ]
    scratch = [pltpu.VMEM((8 * rows, deep), BF16)]
    kernel = functools.partial(project_kernel, len(mine))
    args = [*blocks, *mine, *other]
    return call_whole(kernel, "project", out, args, [biases], scratch, 8 + 6 * len(mine))


def split_store(out, near_ref, far_ref, at):
    rows = near_ref.shape[0]
    near_ref[:, at] = out[:rows]
    far_ref[:, at] = out[rows:].astype(BF16)


def out_kernel(w0, w1, own, sib, w_ref, near_ref, far_ref, sems):
    width = own.shape[1]
    deep = w_ref.shape[0]
    pairs = [(w0.at[0], w_ref.at[:, :width]), (w1.at[0], w_ref.at[:, width:])]
    for copy in start_all(pairs, sems):
        copy.wait()
    for c in range(4):
        at = slice(c * deep // 4, (c + 1) * deep // 4)
        out = dot(own[...], w_ref[at, :width], NT) + dot(sib[...], w_ref[at, width:], NT)
        split_store(out, near_ref, far_ref, at)


def out_project(own, sib, pieces):
    pair, width = own.shape
    deep = pieces[0].shape[1]
    out = [
        shape((deep, 2 * width), BF16),
        shape((pair // 2, deep), F32),
        shape((pair // 2, deep), BF16),
    ]
    return call_whole(out_kernel, "out_project", out, pieces, [own, sib], copies=2)


def out_back_kernel(g0, g1, w_ref, gt_ref, own_ref, sib_ref):
    rows = g0.shape[0]
    width = own_ref.shape[1]
    for i, ref in enumerate((g0, g1)):
        at = slice(i * rows, (i + 1) * rows)
        g = ref[...]
        out = dot(g, w_ref[...])
        own_ref[at, :] = out[:, :width].astype(BF16)
        sib_ref[at, :] = out[:, width:].astype(BF16)
        gt_ref[:, at] = g.T


def out_back(g0, g1, weights):
    rows, deep = g0.shape
    width = weights.shape[1] // 2
    out = [
        shape((deep, 2 * rows), BF16),
        shape((2 * rows, width), BF16),
        shape((2 * rows, width), BF16),
    ]
    return call_whole(out_back_kernel, "out_back", out, [], [g0, g1, weights])


EXTRA = 16


def pack_rows(out_ref, one, two, q0, q1, kv0, kv1, hidden):
    rank = lax.axis_index("tp")
    size = lax.axis_size("tp")
    first = lax.axis_index("ctx") == 0
    part = q0.shape[1]
    units = hidden.shape[1] // 2
    out_ref[...] = jnp.zeros_like(out_ref)
    out_ref[0:2, :] = one[0:2, :]
    out_ref[2:4, :] = two[0:2, :]
    out_ref[4:5, :] = one[2:3, :]
    out_ref[5:6, :] = two[2:3, :]
    for row, (mine, other, at) in ((6, (q0, q1, 0)), (7, (kv0, kv1, part))):
        mine = col_sum(mine[:, at : at + part].astype(F32))
        other = col_sum(other[:, at : at + part].astype(F32))
        low, high = jnp.where(first, mine, other), jnp.where(first, other, mine)
        for t in range(size):
            keep = rank == t
            start = 2 * t * part
            out_ref[row : row + 1, start : start + part] = jnp.where(keep, low, 0.0)
            out_ref[row : row + 1, start + part : start + 2 * part] = jnp.where(keep, high, 0.0)
    for t in range(size):
        row = 8 + t
        total = jnp.where(rank == t, hidden[:, :units], 0.0)
        total = total + jnp.where((rank ^ 1) == t, hidden[:, units:], 0.0)
        mine, other = total[:, : units // 2], total[:, units // 2 :]
        out_ref[row : row + 1, : units // 2] = jnp.where(first, mine, other)
        out_ref[row : row + 1, units // 2 :] = jnp.where(first, other, mine)


def input_back_kernel(
    q0, q1, kv0, kv1, w_ref, one, two, hidden, near_ref, far_ref, sib_ref, cat_ref, vec_ref
):
    half, part = q0.shape
    pair, deep = near_ref.shape
    for j, (ref, at) in enumerate(((q0, 0), (q1, 0), (kv0, 0), (kv1, 0), (kv0, part), (kv1, part))):
        count = ref.shape[0]
        cat_ref[:count, j * part : (j + 1) * part] = ref[:, at : at + part]
    sib_ref[:pair, :] = dot(cat_ref[pair:half, :], w_ref[...], NT).astype(BF16)
    out = dot(cat_ref[half + pair :, 2 * part :], w_ref[:, 2 * part :], NT)
    sib_ref[pair:half, :] = out.astype(BF16)
    near_ref[...] = dot(cat_ref[:pair, :], w_ref[...], NT)
    far_ref[...] = dot(cat_ref[half : half + pair, 2 * part :], w_ref[:, 2 * part :], NT)
    pack_rows(vec_ref, one, two, q0, q1, kv0, kv1, hidden)
    sib_ref[half:, :] = vec_ref[...].astype(BF16)


def input_back(q0, q1, kv0, kv1, weights, one, two, hidden):
    half, part = q0.shape
    deep = weights.shape[0]
    pair = half // 2
    out = [shape((pair, deep), F32), shape((pair, deep), F32), shape((half + EXTRA, deep), BF16)]
    scratch = [pltpu.VMEM((kv0.shape[0], 6 * part), BF16), pltpu.VMEM((EXTRA, deep), F32)]
    args = [q0, q1, kv0, kv1, weights, one, two, hidden]
    return call_whole(input_back_kernel, "input_back", out, [], args, scratch)


def fold_kernel(near, far, sent, recv, rest, own_ref, x_ref, y_ref, d_ref, vec_ref):
    rows = own_ref.shape[0]
    pair = 2 * rows
    own_ref[...] = rest[...] + near[:rows, :] + recv[:rows, :].astype(F32)
    vec = sent[2 * pair :, :].astype(F32) + recv[2 * pair :, :].astype(F32)
    vec_ref[...] = vec.astype(BF16)
    for ref, term, at in ((x_ref, near, rows), (y_ref, far, 0), (d_ref, far, rows)):
        start = at if term is near else pair + at
        total = term[at : at + rows, :] + recv[start : start + rows, :].astype(F32)
        ref[:rows, :] = total.astype(BF16)
        ref[rows:, :] = vec.astype(BF16)


def fold(near, far, sent, recv, rest):
    rows, deep = rest.shape
    out = [shape((rows, deep), F32)] + [shape((rows + EXTRA, deep), BF16)] * 3
    out += [shape((EXTRA, deep), BF16)]
    return call_whole(fold_kernel, "fold", out, [], [near, far, sent, recv, rest])


def grad_send_kernel(left, right, out_ref):
    out_ref[...] = dot(left[...], right[...]).astype(BF16)


def grad_send(left, right):
    out = [shape((left.shape[0], right.shape[1]), BF16)]
    return call_whole(grad_send_kernel, "grad_send", out, [], [left, right])[0]


def grad_sum_kernel(left, right, recv, keep_ref, send_ref):
    part = keep_ref.shape[1]
    for ref, at in ((send_ref, slice(part, 2 * part)), (keep_ref, slice(0, part))):
        ref[...] = (dot(left[...], right[:, at]) + recv[:, at].astype(F32)).astype(BF16)


def grad_sum(left, right, recv):
    half = shape((left.shape[0], right.shape[1] // 2), BF16)
    return call_whole(grad_sum_kernel, "grad_sum", [half, half], [], [left, right, recv])


def grad_total_kernel(left, right, recv, out_ref):
    out_ref[...] = (dot(left[...], right[...]) + recv[...].astype(F32)).astype(BF16)


def grad_total(left, right, recv):
    out = [shape((left.shape[0], right.shape[1]), BF16)]
    return call_whole(grad_total_kernel, "grad_total", out, [], [left, right, recv])[0]


def head_grads(left, query, pair):
    half = query.shape[0]
    return jnp.concatenate([dot(left[:, :half], query[...]), dot(left[...], pair[...])], axis=1)


def head_send_kernel(left, query, pair, out_ref):
    out_ref[...] = head_grads(left, query, pair).astype(BF16)


def head_send(left, query, pair):
    out = [shape((left.shape[0], query.shape[1] + pair.shape[1]), BF16)]
    return call_whole(head_send_kernel, "head_send", out, [], [left, query, pair])[0]


def head_sum_kernel(left, query, pair, recv, keep, keep_recv, out_ref):
    width = recv.shape[1]
    total = head_grads(left, query, pair) + recv[...].astype(F32)
    out_ref[:, :width] = total.astype(BF16)
    out_ref[:, width:] = (keep[...].astype(F32) + keep_recv[...].astype(F32)).astype(BF16)


def head_sum(left, query, pair, recv, keep, keep_recv):
    out = [shape((left.shape[0], recv.shape[1] + keep.shape[1]), BF16)]
    args = [left, query, pair, recv, keep, keep_recv]
    return call_whole(head_sum_kernel, "head_sum", out, [], args)[0]


def gelu_pair(values):
    size = jnp.abs(values)
    t = 1.0 / (1.0 + (0.3275911 * math.sqrt(0.5)) * size)
    bell = jnp.exp2(values * values * (-0.5 * LOG2E))
    poly = t * (
        0.5 * 0.254829592
        + t
        * (
            0.5 * -0.284496736
            + t * (0.5 * 1.421413741 + t * (0.5 * -1.453152027 + t * (0.5 * 1.061405429)))
        )
    )
    tail = poly * bell
    cdf = jnp.where(values < 0, tail, 1.0 - tail)
    return values * cdf, cdf + values * bell * (1.0 / math.sqrt(2.0 * math.pi))


def gather_units(refs, w_ref):
    pairs = []
    part = refs[0][0].shape[2]
    for ref, first in refs:
        for j in range(first, ref.shape[0]):
            at = len(pairs) * part
            pairs.append((ref.at[j], w_ref.at[:, at : at + part]))
    return pairs


def up_kernel(
    x0, x1, mine, other, mine_sib, other_sib, bias_ref,
    xt_ref, w_ref, act_own, act_sib, slope_own, slope_sib, x_ref, sems,
):
    rows = x0.shape[0]
    pairs = [(x0, x_ref.at[:rows, :]), (x1, x_ref.at[rows:, :])]
    pairs += gather_units(((mine, 1), (other, 0), (mine_sib, 1), (other_sib, 0)), w_ref)
    copies = start_all(pairs, sems)
    copies[0].wait()
    copies[1].wait()
    units = act_own.shape[1]
    step = mine.shape[2]

    def matmul(c):
        copies[2 + c].wait()
        return dot(x_ref[...], w_ref[:, c * step : (c + 1) * step])

    following = matmul(0)
    for c in range(8):
        pre = following
        if c < 7:
            following = matmul(c + 1)
        act_ref, slope_ref = ((act_own, slope_own), (act_sib, slope_sib))[c // 4]
        at = slice((c % 4) * step, (c % 4 + 1) * step)
        act, slope = gelu_pair(pre + bias_ref[0:1, c * step : (c + 1) * step])
        act_ref[:, at] = act.astype(BF16)
        slope_ref[:, at] = slope.astype(BF16)
    xt_ref[...] = x_ref[...].T


def feed_up(x0, x1, pieces, bias):
    rows, deep = x0.shape
    units = bias.shape[1]
    out = [shape((deep, 2 * rows), BF16), shape((deep, units), BF16)]
    out += [shape((2 * rows, units // 2), BF16)] * 4
    scratch = [pltpu.VMEM((2 * rows, deep), BF16)]
    return call_whole(up_kernel, "feed_up", out, [x0, x1, *pieces], [bias], scratch, 10)


def down_kernel(spots, *refs):
    count = len(spots)
    own, sib, refs = refs[:count], refs[count : 2 * count], refs[2 * count :]
    act_own, act_sib, w_ref, near_ref, far_ref, sems = refs
    deep = near_ref.shape[1]
    units = act_own.shape[1]
    pairs = []
    rows = ring_rows(deep // own[0].shape[0], deep)
    for (piece, start), left, right in zip(spots, own, sib):
        width = left.shape[1]
        pairs.append((left, w_ref.at[rows[piece], start : start + width]))
        pairs.append((right, w_ref.at[rows[piece], units + start : units + start + width]))
    for copy in start_all(pairs, sems):
        copy.wait()
    for c in range(4):
        at = slice(c * deep // 4, (c + 1) * deep // 4)
        out = dot(act_own[...], w_ref[at, :units], NT) + dot(act_sib[...], w_ref[at, units:], NT)
        split_store(out, near_ref, far_ref, at)


def feed_down(act_own, act_sib, spots, own, sib):
    pair, units = act_own.shape
    deep = D
    out = [
        shape((deep, 2 * units), BF16),
        shape((pair // 2, deep), F32),
        shape((pair // 2, deep), BF16),
    ]
    kernel = functools.partial(down_kernel, spots)
    args = [*own, *sib]
    return call_whole(
        kernel, "feed_down", out, args, [act_own, act_sib], copies=2 * len(own)
    )


def feed_back_kernel(
    g0, g1, slope_own, slope_sib, up_ref, down_ref,
    gt_ref, gup_own, gup_sib, bias_ref, near_ref, far_ref, g_ref,
):
    rows, deep = g0.shape
    g_ref[:rows, :] = g0[...]
    g_ref[rows:, :] = g1[...]
    units = gup_own.shape[1]
    step = units // 2
    for c in range(4):
        slope_ref, gup_ref = ((slope_own, gup_own), (slope_sib, gup_sib))[c // 2]
        at = slice((c % 2) * step, (c % 2 + 1) * step)
        grad = dot(g_ref[...], down_ref[:, c * step : (c + 1) * step])
        grad = (grad * slope_ref[:, at].astype(F32)).astype(BF16)
        gup_ref[:, at] = grad
        bias_ref[0:1, c * step : (c + 1) * step] = jnp.sum(
            grad.astype(F32), axis=0, keepdims=True
        )
    for c in range(4):
        at = slice(c * deep // 4, (c + 1) * deep // 4)
        out = dot(gup_own[...], up_ref[at, :units], NT) + dot(gup_sib[...], up_ref[at, units:], NT)
        split_store(out, near_ref, far_ref, at)
    gt_ref[...] = g_ref[...].T


def feed_back(g0, g1, slope_own, slope_sib, up_all, down_all):
    rows, deep = g0.shape
    units = slope_own.shape[1]
    out = [shape((deep, 2 * rows), BF16)]
    out += [shape((2 * rows, units), BF16)] * 2
    out += [shape((1, 2 * units), F32), shape((rows, deep), F32), shape((rows, deep), BF16)]
    args = [g0, g1, slope_own, slope_sib, up_all, down_all]
    scratch = [pltpu.VMEM((2 * rows, deep), BF16)]
    return call_whole(feed_back_kernel, "feed_back", out, [], args, scratch)


def row_mean(values):
    return jnp.mean(values, axis=-1, keepdims=True)


def col_sum(values):
    return jnp.sum(values, axis=0, keepdims=True)


def normalize(values):
    centered = values - row_mean(values)
    inverse = lax.rsqrt(row_mean(centered * centered) + NORM_EPSILON)
    return centered * inverse, inverse


def norm_back(grad_out, normed, inverse, gain):
    grad = grad_out * gain
    return inverse * (grad - row_mean(grad) - normed * row_mean(grad * normed))


def norm_one_kernel(own, part, recv, vec, first_ref, low_ref, normed_ref, inverse_ref):
    attn_out = part[...] + recv[...].astype(F32) + vec[4:5, :]
    normed, inverse = normalize(own[...].astype(F32) + attn_out)
    first = normed * vec[0:1, :] + vec[1:2, :]
    first_ref[...] = first
    low_ref[...] = first.astype(BF16)
    normed_ref[...] = normed
    inverse_ref[...] = inverse


def norm_one(own, part, recv, vec):
    rows, deep = own.shape
    out = [shape((rows, deep), t) for t in (F32, BF16, F32)] + [shape((rows, 1), F32)]
    return call_whole(norm_one_kernel, "norm_one", out, [], [own, part, recv, vec])


def norm_two_kernel(first, part, recv, cotangent, vec, out_ref, grad_ref, low_ref, sums_ref):
    down_out = part[...] + recv[...].astype(F32) + vec[5:6, :]
    normed, inverse = normalize(first[...] + down_out)
    out_ref[...] = (normed * vec[2:3, :] + vec[3:4, :]).astype(BF16)
    given = cotangent[...].astype(F32)
    grad = norm_back(given, normed, inverse, vec[2:3, :])
    grad_ref[...] = grad
    low = grad.astype(BF16)
    low_ref[...] = low
    sums_ref[0:1, :] = col_sum(given * normed)
    sums_ref[1:2, :] = col_sum(given)
    sums_ref[2:3, :] = col_sum(low.astype(F32))


def norm_two(first, part, recv, cotangent, vec):
    rows, deep = first.shape
    out = [shape((rows, deep), t) for t in (BF16, F32, BF16)] + [shape((3, deep), F32)]
    return call_whole(norm_two_kernel, "norm_two", out, [], [first, part, recv, cotangent, vec])


def norm_one_back_kernel(
    grad_second, part, recv, normed, inverse, vec, grad_ref, low_ref, sums_ref
):
    given = grad_second[...] + part[...] + recv[...].astype(F32)
    grad = norm_back(given, normed[...], inverse[...], vec[0:1, :])
    grad_ref[...] = grad
    low = grad.astype(BF16)
    low_ref[...] = low
    sums_ref[0:1, :] = col_sum(given * normed[...])
    sums_ref[1:2, :] = col_sum(given)
    sums_ref[2:3, :] = col_sum(low.astype(F32))


def norm_one_back(grad_second, part, recv, normed, inverse, vec):
    rows, deep = part.shape
    out = [shape((rows, deep), t) for t in (F32, BF16)] + [shape((3, deep), F32)]
    args = [grad_second, part, recv, normed, inverse, vec]
    return call_whole(norm_one_back_kernel, "norm_one_back", out, [], args)


def nesterov(weights, momentum, average, gradient, step_rate):
    momentum_new = MOMENTUM * momentum + gradient
    weight_new = weights - step_rate * (gradient + MOMENTUM * momentum_new)
    return (weight_new, momentum_new, AVERAGE * average + (1.0 - AVERAGE) * weight_new)


def swap_tp(values, bit):
    size = lax.axis_size("tp")
    return lax.ppermute(values, "tp", [(i, i ^ bit) for i in range(size)])


def core(values):
    return swap_tp(values, 1)


def across(values):
    return swap_tp(values, 2)


def swap_ctx(values):
    return lax.ppermute(values, "ctx", [(0, 1), (1, 0)])


def swap_both(values):
    size = lax.axis_size("tp")
    return lax.ppermute(values, ("ctx", "tp"), [(i, i ^ (size + 2)) for i in range(2 * size)])


def sum_fsdp(values):
    size = lax.axis_size("fsdp")

    def swap(values, bit):
        return lax.ppermute(values, "fsdp", [(i, i ^ bit) for i in range(size)])

    if size == 4:
        one, two, three = (swap(values, bit) for bit in (1, 2, 3))
        return (values + one) + (two + three)
    bit = 1
    while bit < size:
        values = values + swap(values, bit)
        bit *= 2
    return values


def gather_fsdp(shard, axis):
    return lax.all_gather(shard, "fsdp", axis=axis, tiled=True)


def ring():
    return lax.axis_size("fsdp") == 4


def shift_fsdp(values, step):
    size = lax.axis_size("fsdp")
    return lax.ppermute(values, "fsdp", [(i, (i + step) % size) for i in range(size)])


def gather_pieces(shard, axis):
    if not ring():
        return [gather_fsdp(shard, axis)]
    return [shard] + [shift_fsdp(shard, -s) for s in range(1, lax.axis_size("fsdp"))]


def scatter_pieces(grads):
    if not ring():
        return scatter_fsdp(grads, 0).astype(F32)
    size = lax.axis_size("fsdp")
    rank = lax.axis_index("fsdp")
    rows = grads.shape[0] // size
    pieces = [
        lax.dynamic_slice_in_dim(grads, lax.rem(rank + s, size) * rows, rows) for s in range(size)
    ]
    total = pieces[0].astype(F32)
    for s in (2, 1, 3):
        total = total + shift_fsdp(pieces[s], s).astype(F32)
    return total


def scatter_fsdp(grads, axis):
    return lax.psum_scatter(grads, "fsdp", scatter_dimension=axis, tiled=True)


def halves(values, axis=-1):
    low, high = jnp.split(values, 2, axis=axis)
    first = lax.axis_index("ctx") == 0
    return jnp.where(first, low, high), jnp.where(first, high, low)


def join(mine, other, axis=-1):
    first = lax.axis_index("ctx") == 0
    low, high = jnp.where(first, mine, other), jnp.where(first, other, mine)
    return jnp.concatenate([low, high], axis=axis)


def quarters(mine):
    return jnp.stack(jnp.split(mine, 2, axis=1))


def after(values, *others):
    return lax.optimization_barrier((values,) + others)[0]


def on_device(
    tokens,
    cotangent,
    attn_weight,
    attn_momentum,
    attn_average,
    ffn_weight,
    ffn_momentum,
    ffn_average,
    vector_weight,
    vector_momentum,
    vector_average,
):
    tp_rank = lax.axis_index("tp")
    sib_rank = tp_rank ^ 1
    head_width = attn_weight.shape[2]
    unit_width = ffn_weight.shape[2]
    token_count = LEN * lax.axis_size("fsdp")
    matrix_rate = MATRIX_RATE / math.sqrt(token_count)
    vector_rate = VECTOR_RATE / math.sqrt(token_count)

    attn_low, attn_high = halves(attn_weight.astype(BF16))
    qkv_mine = gather_pieces(attn_low[:3], 1)

    own = tokens[0]
    rows = own.shape[0]
    pair = 2 * rows
    half = 4 * rows
    beside = across(own)
    facing = swap_ctx(own)
    diagonal = swap_both(own)
    if ring():
        others = swap_ctx(after(jnp.stack(qkv_mine[1:]), beside, facing))
        qkv_other = [attn_high[:3]] + [others[s] for s in range(len(qkv_mine) - 1)]
    else:
        qkv_other = [swap_ctx(qkv_mine[0])]
    up_low = quarters(halves(ffn_weight[0].astype(BF16))[0])
    out_low = jnp.concatenate([attn_low[3], attn_high[3]], axis=1)
    out_up_low = jnp.concatenate([out_low[None], up_low])
    out_up = gather_fsdp(after(out_up_low, *qkv_mine[-3:], beside, facing), 1)
    blocks = [own, beside, core(own), core(beside), facing, diagonal, core(facing), core(diagonal)]

    vec = vector_weight[: 6 * D].reshape(6, D)

    def columns(start, width):
        part = lax.dynamic_slice_in_dim(vector_weight, start, width)
        return jnp.concatenate(halves(part))

    biases = jnp.stack(
        [
            columns(6 * D + tp_rank * head_width, head_width),
            columns(7 * D + tp_rank * head_width, head_width),
        ]
    )
    bias_hidden = jnp.concatenate(
        [
            columns(8 * D + tp_rank * unit_width, unit_width),
            columns(8 * D + sib_rank * unit_width, unit_width),
        ]
    )[None]

    token_t, qkv_w, queries, keys, values = project(blocks, qkv_mine, qkv_other, biases)
    down_low = jnp.concatenate(halves(ffn_weight[1].astype(BF16)), axis=1)
    mixed_own, mixed_sib, lse = attend(queries, keys, values)
    down_low = after(down_low, mixed_own)
    if ring():
        low, high = jnp.split(down_low, 2, axis=1)
        spots = ((0, 0), (1, 0), (3, 0), (2, 0), (2, low.shape[1]))
        down_w = [down_low, shift_fsdp(down_low, -1), shift_fsdp(down_low, -3)]
        down_w += [shift_fsdp(low, -2), shift_fsdp(high, -2)]
    else:
        spots = ((0, 0),)
        down_w = [gather_fsdp(down_low, 0)]
    mixed_recv = core(mixed_sib)
    out_up = after(out_up, mixed_own)
    out_up_sib = core(out_up)
    up_other = swap_ctx(out_up[1:])
    out_w, attn_part, attn_far = out_project(mixed_own, mixed_recv, [out_up, out_up_sib])
    attn_recv = across(attn_far)
    if ring():
        attn_recv = after(attn_recv, down_w[1], down_w[2])
    first, first_low, normed_one, inverse_one = norm_one(own, attn_part, attn_recv, vec)
    first_beside = across(first_low)

    if ring():
        first_beside = after(first_beside, down_w[3])
    up_other = after(up_other, first_beside)
    first_t, up_all, hidden_own, hidden_sib, slope_own, slope_sib = feed_up(
        first_low, first_beside, [out_up, up_other, out_up_sib, core(up_other)], bias_hidden
    )
    if ring():
        down_w[4] = after(down_w[4], hidden_own)
    down_all, down_part, down_far = feed_down(
        hidden_own, hidden_sib, spots, down_w, [core(w) for w in down_w]
    )
    layer_out, grad_second, grad_down, sums_two = norm_two(
        first, down_part, across(down_far), cotangent[0], vec
    )
    grad_down_t, grad_up_own, grad_up_sib, grad_bias_hidden, first_part, first_far = feed_back(
        grad_down, across(grad_down), slope_own, slope_sib, up_all, down_all
    )
    down_sib = grad_send(grad_down_t, hidden_sib)
    up_sib = grad_send(first_t, grad_up_sib)
    first_recv = after(across(first_far), down_sib, up_sib)
    grad_res, grad_attn, sums_one = norm_one_back(
        grad_second, first_part, first_recv, normed_one, inverse_one, vec
    )
    grad_attn_beside = across(grad_attn)
    down_sum = grad_total(grad_down_t, hidden_own, after(core(down_sib), grad_attn))
    up_keep, up_send = grad_sum(first_t, grad_up_own, after(core(up_sib), grad_attn))

    def finish(mine):
        return join(mine, swap_ctx(mine)).astype(F32)

    def finish_whole(part):
        mine, other = jnp.split(part.astype(F32), 2, axis=1)
        recv_other, recv_mine = jnp.split(swap_ctx(part).astype(F32), 2, axis=1)
        return join(mine + recv_mine, other + recv_other)

    down_owned = scatter_fsdp(down_sum, 0)
    up_recv = swap_ctx(up_send)

    grad_attn_beside = after(grad_attn_beside, down_sum, up_send)
    grad_attn_t, grad_mixed_own, grad_mixed_sib = out_back(grad_attn, grad_attn_beside, out_w)
    grad_mixed = (grad_mixed_own, core(grad_mixed_sib))

    up_recv = after(up_recv, grad_mixed_sib)
    up_sum = (up_keep.astype(F32) + up_recv.astype(F32)).astype(BF16)
    up_owned = scatter_pieces(up_sum).astype(BF16)
    mixed = (mixed_own, mixed_sib)
    heads = (queries, keys, values, mixed)
    query_other, kv_other = attend_back(*heads, grad_mixed, lse, 1)
    send = head_send(token_t, query_other, kv_other)
    out_sib = grad_send(after(grad_attn_t, query_other), mixed_recv)
    out_keep, out_send = grad_sum(grad_attn_t, mixed_own, core(out_sib))
    grad_mixed = (grad_mixed[0], after(grad_mixed[1], up_sum, send, out_send))
    recv = swap_ctx(send)
    query_mine, kv_mine = attend_back(*heads, grad_mixed, lse, 0)
    part = head_width // 2
    near, far, sibling = input_back(
        query_mine, query_other, kv_mine, kv_other, qkv_w, sums_one, sums_two, grad_bias_hidden
    )
    sib_recv = core(sibling)
    qkvo_sum = head_sum(token_t, query_mine, kv_mine, recv, out_keep, swap_ctx(out_send))
    qkvo_mine = scatter_fsdp(qkvo_sum, 0)
    up_owned = after(up_owned, qkvo_sum)
    sib_recv = after(sib_recv, qkvo_sum, up_owned)
    input_part, to_x, to_y, to_d, vec_part = fold(near, far, sibling, sib_recv, grad_res)
    from_x, from_y, from_d = across(to_x), swap_ctx(to_y), swap_both(to_d)
    down_grad, up_grad = finish_whole(after(down_owned, qkvo_sum)), finish(up_owned)
    ffn_grad = jnp.stack([up_grad, down_grad])
    ffn_new, ffn_momentum_new, ffn_average_new = nesterov(
        ffn_weight, ffn_momentum, ffn_average, ffn_grad, matrix_rate
    )
    input_grad = input_part
    for term in (from_x, from_y, from_d):
        input_grad = input_grad + term[:rows].astype(F32)
    vec_x, vec_y, vec_d = (term[rows:].astype(F32) for term in (from_x, from_y, from_d))
    vec_plane = (vec_part.astype(F32) + vec_x) + (vec_y + vec_d)

    qkvo_mine = after(qkvo_mine, from_x, from_y, from_d)
    qkvo_other = swap_ctx(qkvo_mine)
    vector_grad = sum_fsdp(after(vec_plane, qkvo_mine)[:12]).reshape(-1)
    attn_grad = jnp.stack(
        [
            join(qkvo_mine[:, j * part : (j + 1) * part], qkvo_other[:, j * part : (j + 1) * part])
            for j in range(4)
        ]
    ).astype(F32)
    vector_new, vector_momentum_new, vector_average_new = nesterov(
        vector_weight, vector_momentum, vector_average, vector_grad, vector_rate
    )
    attn_new, attn_momentum_new, attn_average_new = nesterov(
        attn_weight, attn_momentum, attn_average, attn_grad, matrix_rate
    )
    return (
        layer_out[None],
        input_grad[None],
        attn_grad,
        attn_new,
        attn_momentum_new,
        attn_average_new,
        attn_new.astype(BF16),
        ffn_grad,
        ffn_new,
        ffn_momentum_new,
        ffn_average_new,
        ffn_new.astype(BF16),
        vector_grad,
        vector_new,
        vector_momentum_new,
        vector_average_new,
    )


def solution(mesh):
    rows = P("fsdp", ("ctx", "tp"), None)
    weight = P(None, "fsdp", "tp")
    return jax.shard_map(
        on_device,
        mesh=mesh,
        in_specs=(rows, rows) + (weight,) * 6 + (P(),) * 3,
        out_specs=(rows, rows) + (weight,) * 10 + (P(),) * 4,
        check_vma=False,
    )
```

```python
import functools
import math

import jax
import jax.numpy as jnp
from jax import lax
from jax.experimental import pallas as pl
from jax.experimental.pallas import tpu as pltpu
from jax.sharding import PartitionSpec as P

D = 1024
FF = 4096
HEAD_DIM = 64
LEN = 2048

NORM_EPSILON = 1e-05
MOMENTUM = 0.5
AVERAGE = 0.5
MATRIX_RATE = 0.1
VECTOR_RATE = 0.3

SCALE = HEAD_DIM ** (-0.5)
LOG2E = math.log2(math.e)
F32 = jnp.float32
BF16 = jnp.bfloat16
NT = (((1,), (1,)), ((), ()))
TN = (((0,), (0,)), ((), ()))
NN = (((1,), (0,)), ((), ()))


def dot(left, right, dims=NN):
    return lax.dot_general(left, right, dims, preferred_element_type=F32)


VMEM = pl.BlockSpec(memory_space=pltpu.VMEM)
ANY = pl.BlockSpec(memory_space=pl.ANY)
MEGA = 1024 * 1024
WORK_UNIT = 1.2e10


WORK = {
    "project": 0.001,
    "attend": 0.001,
    "out_project": 0.001,
    "norm_one": 1.5,
    "feed_up": 8,
    "feed_down": 4,
    "norm_two": 2,
    "feed_back": 8,
    "grad_send": 10,
    "grad_sum": 3,
    "norm_one_back": 2,
    "out_back": 2,
    "attend_back": 12,
    "head_send": 3,
    "head_sum": 4,
    "input_back": 4,
    "fold": 1.5,
    "grad_total": 3,
}


def cost(name):
    flops = int(WORK[name] * WORK_UNIT)
    return pl.CostEstimate(flops=flops, bytes_accessed=1, transcendentals=0)


def shape(dims, dtype):
    return jax.ShapeDtypeStruct(tuple(dims), dtype)


def tile(i, size):
    return pl.ds(pl.multiple_of(i * size, size), size)


def call_whole(kernel, name, out_shape, far_args, near_args, scratch=(), copies=0):
    scratch = list(scratch)
    if copies:
        scratch.append(pltpu.SemaphoreType.DMA((copies,)))
    return pl.pallas_call(
        kernel,
        in_specs=[ANY] * len(far_args) + [VMEM] * len(near_args),
        out_specs=[VMEM] * len(out_shape),
        out_shape=list(out_shape),
        scratch_shapes=scratch,
        compiler_params=pltpu.CompilerParams(vmem_limit_bytes=8 * MEGA),
        cost_estimate=cost(name),
        name=name,
    )(*far_args, *near_args)


def start_all(pairs, sems):
    copies = [pltpu.make_async_copy(src, dst, sems.at[i]) for i, (src, dst) in enumerate(pairs)]
    for copy in copies:
        copy.start()
    return copies


def head_masks(width):
    lane = lax.broadcasted_iota(jnp.int32, (1, width), 1) // HEAD_DIM
    return [(lane == h).astype(BF16) for h in range(width // HEAD_DIM)]


def attend_kernel(chunk, q_ref, k_ref, v_ref, own_ref, sib_ref, lse_ref, vt_ref):
    heads = q_ref.shape[1] // HEAD_DIM
    count = k_ref.shape[0]
    step = pl.program_id(0)

    @pl.when(step == 0)
    def _():
        vt_ref[...] = v_ref[...].T

    queries = q_ref[...]
    masked = [queries * mask for mask in head_masks(q_ref.shape[1])]
    units = [(h, c) for h in range(heads) for c in range(0, count, chunk)]

    def scores_of(unit):
        h, c = unit
        return dot(k_ref[c : c + chunk, :], masked[h], NT)

    tops, totals, outs = {}, {}, {}
    scores = scores_of(units[0])
    for i, unit in enumerate(units):
        current = scores
        if i + 1 < len(units):
            scores = scores_of(units[i + 1])
        h, c = unit
        top = jnp.max(current, axis=0, keepdims=True)
        weights = jnp.exp2((current - top) * (SCALE * LOG2E))
        tops[unit] = top
        totals[unit] = jnp.sum(weights, axis=0, keepdims=True)
        outs[unit] = dot(
            vt_ref[h * HEAD_DIM : (h + 1) * HEAD_DIM, c : c + chunk], weights.astype(BF16)
        )
    heads_out = []
    for h in range(heads):
        mine = [(h, c) for c in range(0, count, chunk)]
        top = functools.reduce(jnp.maximum, [tops[u] for u in mine])
        share = [jnp.exp2((tops[u] - top) * (SCALE * LOG2E)) for u in mine]
        total = sum(totals[u] * f for u, f in zip(mine, share))
        out = sum(outs[u] * f for u, f in zip(mine, share))
        heads_out.append(out / total)
        lse_ref[h : h + 1, :] = top * (SCALE * LOG2E) + jnp.log2(total)
    mixed = jnp.concatenate(heads_out, axis=0).T.astype(BF16)
    steps = pl.num_programs(0)

    @pl.when(step < steps // 2)
    def _():
        own_ref[...] = mixed

    @pl.when(step >= steps // 2)
    def _():
        sib_ref[...] = mixed


def attend(queries, keys, values):
    rows, width = queries.shape
    block = min(256, rows // 2)
    steps = rows // block
    heads = width // HEAD_DIM
    half_blocks = steps // 2
    return pl.pallas_call(
        functools.partial(attend_kernel, min(512, keys.shape[0])),
        grid=(steps,),
        in_specs=[
            pl.BlockSpec((block, width), lambda i: (i, 0)),
            pl.BlockSpec(keys.shape, lambda i: (0, 0)),
            pl.BlockSpec(values.shape, lambda i: (0, 0)),
        ],
        out_specs=[
            pl.BlockSpec((block, width), lambda i: (jnp.minimum(i, half_blocks - 1), 0)),
            pl.BlockSpec((block, width), lambda i: (jnp.maximum(i - half_blocks, 0), 0)),
            pl.BlockSpec((heads, block), lambda i: (0, i)),
        ],
        out_shape=[
            shape((rows // 2, width), BF16),
            shape((rows // 2, width), BF16),
            shape((heads, rows), F32),
        ],
        scratch_shapes=[pltpu.VMEM((width, keys.shape[0]), BF16)],
        compiler_params=pltpu.CompilerParams(vmem_limit_bytes=16 * MEGA),
        cost_estimate=cost("attend"),
        name="attend",
    )(queries, keys, values)


def attend_back_kernel(
    part, q_ref, k_ref, v_ref, o0_ref, o1_ref, g0_ref, g1_ref, lse_ref,
    dq_ref, dkv_ref, kt_ref, dk_acc, dv_acc, o_ref, g_ref,
):
    width = q_ref.shape[1]
    heads = width // HEAD_DIM
    step = pl.program_id(0)
    steps = pl.num_programs(0)

    @pl.when(step == 0)
    def _():
        kt_ref[...] = k_ref[...].T
        dk_acc[...] = jnp.zeros_like(dk_acc)
        dv_acc[...] = jnp.zeros_like(dv_acc)

    @pl.when(step < steps // 2)
    def _():
        o_ref[...] = o0_ref[...]
        g_ref[...] = g0_ref[...]

    @pl.when(step >= steps // 2)
    def _():
        o_ref[...] = o1_ref[...]
        g_ref[...] = g1_ref[...]

    queries = q_ref[...]
    grads = g_ref[...]
    masks = head_masks(width)
    product = (o_ref[...].astype(F32) * grads.astype(F32)).T
    outs, probs, gscores, qms, gms = [], [], [], [], []
    for h in range(heads):
        qm = queries * masks[h]
        gm = grads * masks[h]
        delta = jnp.sum(product[h * HEAD_DIM : (h + 1) * HEAD_DIM, :], axis=0, keepdims=True)
        scores = dot(k_ref[...], qm, NT)
        row = part * heads + h
        prob = jnp.exp2(scores * (SCALE * LOG2E) - lse_ref[row : row + 1, :])
        grad_prob = dot(v_ref[...], gm, NT)
        gscore = (prob * (grad_prob - delta)).astype(BF16)
        outs.append(dot(kt_ref[h * HEAD_DIM : (h + 1) * HEAD_DIM, :], gscore))
        probs.append(prob.astype(BF16))
        gscores.append(gscore)
        qms.append(qm)
        gms.append(gm)
    dv_acc[...] += dot(jnp.concatenate(probs, axis=1), jnp.concatenate(gms, axis=0))
    dk_acc[...] += dot(jnp.concatenate(gscores, axis=1), jnp.concatenate(qms, axis=0))
    dq_ref[...] = (jnp.concatenate(outs, axis=0).T * SCALE).astype(BF16)

    @pl.when(step == steps - 1)
    def _():
        dkv_ref[:, :width] = (dk_acc[...] * SCALE).astype(BF16)
        dkv_ref[:, width:] = dv_acc[...].astype(BF16)


def attend_back(queries, keys, values, mixed, grads, lse, part):
    rows, both = queries.shape
    count = keys.shape[0]
    width = both // 2
    block = min(256, rows // 2)
    half_blocks = rows // 2 // block
    row_spec = pl.BlockSpec((block, width), lambda i: (i, part))
    own_spec = pl.BlockSpec((block, width), lambda i: (jnp.minimum(i, half_blocks - 1), part))
    sib_spec = pl.BlockSpec((block, width), lambda i: (jnp.maximum(i - half_blocks, 0), part))
    full_spec = pl.BlockSpec((count, width), lambda i: (0, part))
    lse_spec = pl.BlockSpec((lse.shape[0], block), lambda i: (0, i))
    return pl.pallas_call(
        functools.partial(attend_back_kernel, part),
        grid=(rows // block,),
        in_specs=[row_spec, full_spec, full_spec] + [own_spec, sib_spec] * 2 + [lse_spec],
        out_specs=[
            pl.BlockSpec((block, width), lambda i: (i, 0)),
            pl.BlockSpec((count, both), lambda i: (0, 0)),
        ],
        out_shape=[shape((rows, width), BF16), shape((count, both), BF16)],
        scratch_shapes=[
            pltpu.VMEM((width, count), BF16),
            pltpu.VMEM((count, width), F32),
            pltpu.VMEM((count, width), F32),
            pltpu.VMEM((block, width), BF16),
            pltpu.VMEM((block, width), BF16),
        ],
        compiler_params=pltpu.CompilerParams(vmem_limit_bytes=16 * MEGA),
        cost_estimate=cost("attend_back"),
        name="attend_back",
    )(queries, keys, values, *mixed, *grads, lse)


def ring_rows(count, deep):
    size = deep // count
    rank = lax.axis_index("fsdp")
    return [tile(lax.rem(rank + s, count), size) if count > 1 else tile(0, size) for s in range(count)]


def project_kernel(count, *refs):
    blocks, refs = refs[:8], refs[8:]
    mine, refs = refs[:count], refs[count:]
    other, refs = refs[:count], refs[count:]
    bias_ref, xt_ref, w_ref, q_ref, k_ref, v_ref, x_ref, sems = refs
    rows = blocks[0].shape[0]
    deep = x_ref.shape[1]
    part = mine[0].shape[2]
    width = 2 * part
    pairs = []
    for at, low, high in zip(ring_rows(count, deep), mine, other):
        for j in range(3):
            pairs.append((low.at[j], w_ref.at[at, j * width : j * width + part]))
            pairs.append((high.at[j], w_ref.at[at, j * width + part : (j + 1) * width]))
    weights = len(pairs)
    for i in range(8):
        pairs.append((blocks[i], x_ref.at[i * rows : (i + 1) * rows, :]))
    copies = start_all(pairs, sems)
    for copy in copies[:weights]:
        copy.wait()
    for i in range(4):
        at = slice(i * 2 * rows, (i + 1) * 2 * rows)
        for copy in copies[weights + 2 * i : weights + 2 * i + 2]:
            copy.wait()
        x = x_ref[at, :]
        if i < 2:
            out = dot(x, w_ref[...])
            q_ref[at, :] = (out[:, :width] + bias_ref[0:1, :]).astype(BF16)
            out = out[:, width:]
        else:
            out = dot(x, w_ref[:, width:])
        k_ref[at, :] = out[:, :width].astype(BF16)
        v_ref[at, :] = (out[:, width:] + bias_ref[1:2, :]).astype(BF16)
        xt_ref[:, at] = x.T


def project(blocks, mine, other, biases):
    rows, deep = blocks[0].shape
    width = biases.shape[1]
    out = [
        shape((deep, 8 * rows), BF16),
        shape((deep, 3 * width), BF16),
        shape((4 * rows, width), BF16),
        shape((8 * rows, width), BF16),
        shape((8 * rows, width), BF16),
    ]
    scratch = [pltpu.VMEM((8 * rows, deep), BF16)]
    kernel = functools.partial(project_kernel, len(mine))
    args = [*blocks, *mine, *other]
    return call_whole(kernel, "project", out, args, [biases], scratch, 8 + 6 * len(mine))


def split_store(out, near_ref, far_ref, at):
    rows = near_ref.shape[0]
    near_ref[:, at] = out[:rows]
    far_ref[:, at] = out[rows:].astype(BF16)


def out_kernel(w0, w1, own, sib, w_ref, near_ref, far_ref, sems):
    width = own.shape[1]
    deep = w_ref.shape[0]
    pairs = [(w0.at[0], w_ref.at[:, :width]), (w1.at[0], w_ref.at[:, width:])]
    for copy in start_all(pairs, sems):
        copy.wait()
    for c in range(4):
        at = slice(c * deep // 4, (c + 1) * deep // 4)
        out = dot(own[...], w_ref[at, :width], NT) + dot(sib[...], w_ref[at, width:], NT)
        split_store(out, near_ref, far_ref, at)


def out_project(own, sib, pieces):
    pair, width = own.shape
    deep = pieces[0].shape[1]
    out = [
        shape((deep, 2 * width), BF16),
        shape((pair // 2, deep), F32),
        shape((pair // 2, deep), BF16),
    ]
    return call_whole(out_kernel, "out_project", out, pieces, [own, sib], copies=2)


def out_back_kernel(g0, g1, w_ref, gt_ref, own_ref, sib_ref):
    rows = g0.shape[0]
    width = own_ref.shape[1]
    for i, ref in enumerate((g0, g1)):
        at = slice(i * rows, (i + 1) * rows)
        g = ref[...]
        out = dot(g, w_ref[...])
        own_ref[at, :] = out[:, :width].astype(BF16)
        sib_ref[at, :] = out[:, width:].astype(BF16)
        gt_ref[:, at] = g.T


def out_back(g0, g1, weights):
    rows, deep = g0.shape
    width = weights.shape[1] // 2
    out = [
        shape((deep, 2 * rows), BF16),
        shape((2 * rows, width), BF16),
        shape((2 * rows, width), BF16),
    ]
    return call_whole(out_back_kernel, "out_back", out, [], [g0, g1, weights])


EXTRA = 16


def pack_rows(out_ref, one, two, q0, q1, kv0, kv1, hidden):
    rank = lax.axis_index("tp")
    size = lax.axis_size("tp")
    first = lax.axis_index("ctx") == 0
    part = q0.shape[1]
    units = hidden.shape[1] // 2
    out_ref[...] = jnp.zeros_like(out_ref)
    out_ref[0:2, :] = one[0:2, :]
    out_ref[2:4, :] = two[0:2, :]
    out_ref[4:5, :] = one[2:3, :]
    out_ref[5:6, :] = two[2:3, :]
    for row, (mine, other, at) in ((6, (q0, q1, 0)), (7, (kv0, kv1, part))):
        mine = col_sum(mine[:, at : at + part].astype(F32))
        other = col_sum(other[:, at : at + part].astype(F32))
        low, high = jnp.where(first, mine, other), jnp.where(first, other, mine)
        for t in range(size):
            keep = rank == t
            start = 2 * t * part
            out_ref[row : row + 1, start : start + part] = jnp.where(keep, low, 0.0)
            out_ref[row : row + 1, start + part : start + 2 * part] = jnp.where(keep, high, 0.0)
    for t in range(size):
        row = 8 + t
        total = jnp.where(rank == t, hidden[:, :units], 0.0)
        total = total + jnp.where((rank ^ 1) == t, hidden[:, units:], 0.0)
        mine, other = total[:, : units // 2], total[:, units // 2 :]
        out_ref[row : row + 1, : units // 2] = jnp.where(first, mine, other)
        out_ref[row : row + 1, units // 2 :] = jnp.where(first, other, mine)


def input_back_kernel(
    q0, q1, kv0, kv1, w_ref, one, two, hidden, near_ref, far_ref, sib_ref, cat_ref, vec_ref
):
    half, part = q0.shape
    pair, deep = near_ref.shape
    for j, (ref, at) in enumerate(((q0, 0), (q1, 0), (kv0, 0), (kv1, 0), (kv0, part), (kv1, part))):
        count = ref.shape[0]
        cat_ref[:count, j * part : (j + 1) * part] = ref[:, at : at + part]
    sib_ref[:pair, :] = dot(cat_ref[pair:half, :], w_ref[...], NT).astype(BF16)
    out = dot(cat_ref[half + pair :, 2 * part :], w_ref[:, 2 * part :], NT)
    sib_ref[pair:half, :] = out.astype(BF16)
    near_ref[...] = dot(cat_ref[:pair, :], w_ref[...], NT)
    far_ref[...] = dot(cat_ref[half : half + pair, 2 * part :], w_ref[:, 2 * part :], NT)
    pack_rows(vec_ref, one, two, q0, q1, kv0, kv1, hidden)
    sib_ref[half:, :] = vec_ref[...].astype(BF16)


def input_back(q0, q1, kv0, kv1, weights, one, two, hidden):
    half, part = q0.shape
    deep = weights.shape[0]
    pair = half // 2
    out = [shape((pair, deep), F32), shape((pair, deep), F32), shape((half + EXTRA, deep), BF16)]
    scratch = [pltpu.VMEM((kv0.shape[0], 6 * part), BF16), pltpu.VMEM((EXTRA, deep), F32)]
    args = [q0, q1, kv0, kv1, weights, one, two, hidden]
    return call_whole(input_back_kernel, "input_back", out, [], args, scratch)


def fold_kernel(near, far, sent, recv, rest, own_ref, x_ref, y_ref, d_ref, vec_ref):
    rows = own_ref.shape[0]
    pair = 2 * rows
    own_ref[...] = rest[...] + near[:rows, :] + recv[:rows, :].astype(F32)
    vec = sent[2 * pair :, :].astype(F32) + recv[2 * pair :, :].astype(F32)
    vec_ref[...] = vec.astype(BF16)
    for ref, term, at in ((x_ref, near, rows), (y_ref, far, 0), (d_ref, far, rows)):
        start = at if term is near else pair + at
        total = term[at : at + rows, :] + recv[start : start + rows, :].astype(F32)
        ref[:rows, :] = total.astype(BF16)
        ref[rows:, :] = vec.astype(BF16)


def fold(near, far, sent, recv, rest):
    rows, deep = rest.shape
    out = [shape((rows, deep), F32)] + [shape((rows + EXTRA, deep), BF16)] * 3
    out += [shape((EXTRA, deep), BF16)]
    return call_whole(fold_kernel, "fold", out, [], [near, far, sent, recv, rest])


def grad_send_kernel(left, right, out_ref):
    out_ref[...] = dot(left[...], right[...]).astype(BF16)


def grad_send(left, right):
    out = [shape((left.shape[0], right.shape[1]), BF16)]
    return call_whole(grad_send_kernel, "grad_send", out, [], [left, right])[0]


def grad_sum_kernel(left, right, recv, keep_ref, send_ref):
    part = keep_ref.shape[1]
    for ref, at in ((send_ref, slice(part, 2 * part)), (keep_ref, slice(0, part))):
        ref[...] = (dot(left[...], right[:, at]) + recv[:, at].astype(F32)).astype(BF16)


def grad_sum(left, right, recv):
    half = shape((left.shape[0], right.shape[1] // 2), BF16)
    return call_whole(grad_sum_kernel, "grad_sum", [half, half], [], [left, right, recv])


def grad_total_kernel(left, right, recv, out_ref):
    out_ref[...] = (dot(left[...], right[...]) + recv[...].astype(F32)).astype(BF16)


def grad_total(left, right, recv):
    out = [shape((left.shape[0], right.shape[1]), BF16)]
    return call_whole(grad_total_kernel, "grad_total", out, [], [left, right, recv])[0]


def head_grads(left, query, pair):
    half = query.shape[0]
    return jnp.concatenate([dot(left[:, :half], query[...]), dot(left[...], pair[...])], axis=1)


def head_send_kernel(left, query, pair, out_ref):
    out_ref[...] = head_grads(left, query, pair).astype(BF16)


def head_send(left, query, pair):
    out = [shape((left.shape[0], query.shape[1] + pair.shape[1]), BF16)]
    return call_whole(head_send_kernel, "head_send", out, [], [left, query, pair])[0]


def head_sum_kernel(left, query, pair, recv, keep, keep_recv, out_ref):
    width = recv.shape[1]
    total = head_grads(left, query, pair) + recv[...].astype(F32)
    out_ref[:, :width] = total.astype(BF16)
    out_ref[:, width:] = (keep[...].astype(F32) + keep_recv[...].astype(F32)).astype(BF16)


def head_sum(left, query, pair, recv, keep, keep_recv):
    out = [shape((left.shape[0], recv.shape[1] + keep.shape[1]), BF16)]
    args = [left, query, pair, recv, keep, keep_recv]
    return call_whole(head_sum_kernel, "head_sum", out, [], args)[0]


def gelu_pair(values):
    size = jnp.abs(values)
    t = 1.0 / (1.0 + (0.3275911 * math.sqrt(0.5)) * size)
    bell = jnp.exp2(values * values * (-0.5 * LOG2E))
    poly = t * (
        0.5 * 0.254829592
        + t
        * (
            0.5 * -0.284496736
            + t * (0.5 * 1.421413741 + t * (0.5 * -1.453152027 + t * (0.5 * 1.061405429)))
        )
    )
    tail = poly * bell
    cdf = jnp.where(values < 0, tail, 1.0 - tail)
    return values * cdf, cdf + values * bell * (1.0 / math.sqrt(2.0 * math.pi))


def gather_units(refs, w_ref):
    pairs = []
    part = refs[0][0].shape[2]
    for ref, first in refs:
        for j in range(first, ref.shape[0]):
            at = len(pairs) * part
            pairs.append((ref.at[j], w_ref.at[:, at : at + part]))
    return pairs


def up_kernel(
    x0, x1, mine, other, mine_sib, other_sib, bias_ref,
    xt_ref, w_ref, act_own, act_sib, slope_own, slope_sib, x_ref, sems,
):
    rows = x0.shape[0]
    pairs = [(x0, x_ref.at[:rows, :]), (x1, x_ref.at[rows:, :])]
    pairs += gather_units(((mine, 1), (other, 0), (mine_sib, 1), (other_sib, 0)), w_ref)
    copies = start_all(pairs, sems)
    copies[0].wait()
    copies[1].wait()
    units = act_own.shape[1]
    step = mine.shape[2]

    def matmul(c):
        copies[2 + c].wait()
        return dot(x_ref[...], w_ref[:, c * step : (c + 1) * step])

    following = matmul(0)
    for c in range(8):
        pre = following
        if c < 7:
            following = matmul(c + 1)
        act_ref, slope_ref = ((act_own, slope_own), (act_sib, slope_sib))[c // 4]
        at = slice((c % 4) * step, (c % 4 + 1) * step)
        act, slope = gelu_pair(pre + bias_ref[0:1, c * step : (c + 1) * step])
        act_ref[:, at] = act.astype(BF16)
        slope_ref[:, at] = slope.astype(BF16)
    xt_ref[...] = x_ref[...].T


def feed_up(x0, x1, pieces, bias):
    rows, deep = x0.shape
    units = bias.shape[1]
    out = [shape((deep, 2 * rows), BF16), shape((deep, units), BF16)]
    out += [shape((2 * rows, units // 2), BF16)] * 4
    scratch = [pltpu.VMEM((2 * rows, deep), BF16)]
    return call_whole(up_kernel, "feed_up", out, [x0, x1, *pieces], [bias], scratch, 10)


def down_kernel(spots, *refs):
    count = len(spots)
    own, sib, refs = refs[:count], refs[count : 2 * count], refs[2 * count :]
    act_own, act_sib, w_ref, near_ref, far_ref, sems = refs
    deep = near_ref.shape[1]
    units = act_own.shape[1]
    pairs = []
    rows = ring_rows(deep // own[0].shape[0], deep)
    for (piece, start), left, right in zip(spots, own, sib):
        width = left.shape[1]
        pairs.append((left, w_ref.at[rows[piece], start : start + width]))
        pairs.append((right, w_ref.at[rows[piece], units + start : units + start + width]))
    for copy in start_all(pairs, sems):
        copy.wait()
    for c in range(4):
        at = slice(c * deep // 4, (c + 1) * deep // 4)
        out = dot(act_own[...], w_ref[at, :units], NT) + dot(act_sib[...], w_ref[at, units:], NT)
        split_store(out, near_ref, far_ref, at)


def feed_down(act_own, act_sib, spots, own, sib):
    pair, units = act_own.shape
    deep = D
    out = [
        shape((deep, 2 * units), BF16),
        shape((pair // 2, deep), F32),
        shape((pair // 2, deep), BF16),
    ]
    kernel = functools.partial(down_kernel, spots)
    args = [*own, *sib]
    return call_whole(
        kernel, "feed_down", out, args, [act_own, act_sib], copies=2 * len(own)
    )


def feed_back_kernel(
    g0, g1, slope_own, slope_sib, up_ref, down_ref,
    gt_ref, gup_own, gup_sib, bias_ref, near_ref, far_ref, g_ref,
):
    rows, deep = g0.shape
    g_ref[:rows, :] = g0[...]
    g_ref[rows:, :] = g1[...]
    units = gup_own.shape[1]
    step = units // 2
    for c in range(4):
        slope_ref, gup_ref = ((slope_own, gup_own), (slope_sib, gup_sib))[c // 2]
        at = slice((c % 2) * step, (c % 2 + 1) * step)
        grad = dot(g_ref[...], down_ref[:, c * step : (c + 1) * step])
        grad = (grad * slope_ref[:, at].astype(F32)).astype(BF16)
        gup_ref[:, at] = grad
        bias_ref[0:1, c * step : (c + 1) * step] = jnp.sum(
            grad.astype(F32), axis=0, keepdims=True
        )
    for c in range(4):
        at = slice(c * deep // 4, (c + 1) * deep // 4)
        out = dot(gup_own[...], up_ref[at, :units], NT) + dot(gup_sib[...], up_ref[at, units:], NT)
        split_store(out, near_ref, far_ref, at)
    gt_ref[...] = g_ref[...].T


def feed_back(g0, g1, slope_own, slope_sib, up_all, down_all):
    rows, deep = g0.shape
    units = slope_own.shape[1]
    out = [shape((deep, 2 * rows), BF16)]
    out += [shape((2 * rows, units), BF16)] * 2
    out += [shape((1, 2 * units), F32), shape((rows, deep), F32), shape((rows, deep), BF16)]
    args = [g0, g1, slope_own, slope_sib, up_all, down_all]
    scratch = [pltpu.VMEM((2 * rows, deep), BF16)]
    return call_whole(feed_back_kernel, "feed_back", out, [], args, scratch)


def row_mean(values):
    return jnp.mean(values, axis=-1, keepdims=True)


def col_sum(values):
    return jnp.sum(values, axis=0, keepdims=True)


def normalize(values):
    centered = values - row_mean(values)
    inverse = lax.rsqrt(row_mean(centered * centered) + NORM_EPSILON)
    return centered * inverse, inverse


def norm_back(grad_out, normed, inverse, gain):
    grad = grad_out * gain
    return inverse * (grad - row_mean(grad) - normed * row_mean(grad * normed))


def norm_one_kernel(own, part, recv, vec, first_ref, low_ref, normed_ref, inverse_ref):
    attn_out = part[...] + recv[...].astype(F32) + vec[4:5, :]
    normed, inverse = normalize(own[...].astype(F32) + attn_out)
    first = normed * vec[0:1, :] + vec[1:2, :]
    first_ref[...] = first
    low_ref[...] = first.astype(BF16)
    normed_ref[...] = normed
    inverse_ref[...] = inverse


def norm_one(own, part, recv, vec):
    rows, deep = own.shape
    out = [shape((rows, deep), t) for t in (F32, BF16, F32)] + [shape((rows, 1), F32)]
    return call_whole(norm_one_kernel, "norm_one", out, [], [own, part, recv, vec])


def norm_two_kernel(first, part, recv, cotangent, vec, out_ref, grad_ref, low_ref, sums_ref):
    down_out = part[...] + recv[...].astype(F32) + vec[5:6, :]
    normed, inverse = normalize(first[...] + down_out)
    out_ref[...] = (normed * vec[2:3, :] + vec[3:4, :]).astype(BF16)
    given = cotangent[...].astype(F32)
    grad = norm_back(given, normed, inverse, vec[2:3, :])
    grad_ref[...] = grad
    low = grad.astype(BF16)
    low_ref[...] = low
    sums_ref[0:1, :] = col_sum(given * normed)
    sums_ref[1:2, :] = col_sum(given)
    sums_ref[2:3, :] = col_sum(low.astype(F32))


def norm_two(first, part, recv, cotangent, vec):
    rows, deep = first.shape
    out = [shape((rows, deep), t) for t in (BF16, F32, BF16)] + [shape((3, deep), F32)]
    return call_whole(norm_two_kernel, "norm_two", out, [], [first, part, recv, cotangent, vec])


def norm_one_back_kernel(
    grad_second, part, recv, normed, inverse, vec, grad_ref, low_ref, sums_ref
):
    given = grad_second[...] + part[...] + recv[...].astype(F32)
    grad = norm_back(given, normed[...], inverse[...], vec[0:1, :])
    grad_ref[...] = grad
    low = grad.astype(BF16)
    low_ref[...] = low
    sums_ref[0:1, :] = col_sum(given * normed[...])
    sums_ref[1:2, :] = col_sum(given)
    sums_ref[2:3, :] = col_sum(low.astype(F32))


def norm_one_back(grad_second, part, recv, normed, inverse, vec):
    rows, deep = part.shape
    out = [shape((rows, deep), t) for t in (F32, BF16)] + [shape((3, deep), F32)]
    args = [grad_second, part, recv, normed, inverse, vec]
    return call_whole(norm_one_back_kernel, "norm_one_back", out, [], args)


def nesterov(weights, momentum, average, gradient, step_rate):
    momentum_new = MOMENTUM * momentum + gradient
    weight_new = weights - step_rate * (gradient + MOMENTUM * momentum_new)
    return (weight_new, momentum_new, AVERAGE * average + (1.0 - AVERAGE) * weight_new)


def swap_tp(values, bit):
    size = lax.axis_size("tp")
    return lax.ppermute(values, "tp", [(i, i ^ bit) for i in range(size)])


def core(values):
    return swap_tp(values, 1)


def across(values):
    return swap_tp(values, 2)


def swap_ctx(values):
    return lax.ppermute(values, "ctx", [(0, 1), (1, 0)])


def swap_both(values):
    size = lax.axis_size("tp")
    return lax.ppermute(values, ("ctx", "tp"), [(i, i ^ (size + 2)) for i in range(2 * size)])


def sum_fsdp(values):
    size = lax.axis_size("fsdp")

    def swap(values, bit):
        return lax.ppermute(values, "fsdp", [(i, i ^ bit) for i in range(size)])

    if size == 4:
        one, two, three = (swap(values, bit) for bit in (1, 2, 3))
        return (values + one) + (two + three)
    bit = 1
    while bit < size:
        values = values + swap(values, bit)
        bit *= 2
    return values


def gather_fsdp(shard, axis):
    return lax.all_gather(shard, "fsdp", axis=axis, tiled=True)


def ring():
    return lax.axis_size("fsdp") == 4


def shift_fsdp(values, step):
    size = lax.axis_size("fsdp")
    return lax.ppermute(values, "fsdp", [(i, (i + step) % size) for i in range(size)])


def gather_pieces(shard, axis):
    if not ring():
        return [gather_fsdp(shard, axis)]
    return [shard] + [shift_fsdp(shard, -s) for s in range(1, lax.axis_size("fsdp"))]


def scatter_fsdp(grads, axis):
    return lax.psum_scatter(grads, "fsdp", scatter_dimension=axis, tiled=True)


def halves(values, axis=-1):
    low, high = jnp.split(values, 2, axis=axis)
    first = lax.axis_index("ctx") == 0
    return jnp.where(first, low, high), jnp.where(first, high, low)


def join(mine, other, axis=-1):
    first = lax.axis_index("ctx") == 0
    low, high = jnp.where(first, mine, other), jnp.where(first, other, mine)
    return jnp.concatenate([low, high], axis=axis)


def quarters(mine):
    return jnp.stack(jnp.split(mine, 2, axis=1))


def after(values, *others):
    return lax.optimization_barrier((values,) + others)[0]


def on_device(
    tokens,
    cotangent,
    attn_weight,
    attn_momentum,
    attn_average,
    ffn_weight,
    ffn_momentum,
    ffn_average,
    vector_weight,
    vector_momentum,
    vector_average,
):
    tp_rank = lax.axis_index("tp")
    sib_rank = tp_rank ^ 1
    head_width = attn_weight.shape[2]
    unit_width = ffn_weight.shape[2]
    token_count = LEN * lax.axis_size("fsdp")
    matrix_rate = MATRIX_RATE / math.sqrt(token_count)
    vector_rate = VECTOR_RATE / math.sqrt(token_count)

    attn_low, attn_high = halves(attn_weight.astype(BF16))
    qkv_mine = gather_pieces(attn_low[:3], 1)

    own = tokens[0]
    rows = own.shape[0]
    pair = 2 * rows
    half = 4 * rows
    beside = across(own)
    facing = swap_ctx(own)
    diagonal = swap_both(own)
    if ring():
        others = swap_ctx(after(jnp.stack(qkv_mine[1:]), beside, facing))
        qkv_other = [attn_high[:3]] + [others[s] for s in range(len(qkv_mine) - 1)]
    else:
        qkv_other = [swap_ctx(qkv_mine[0])]
    up_low = quarters(halves(ffn_weight[0].astype(BF16))[0])
    out_low = jnp.concatenate([attn_low[3], attn_high[3]], axis=1)
    out_up_low = jnp.concatenate([out_low[None], up_low])
    out_up = gather_fsdp(after(out_up_low, *qkv_mine[-3:], beside, facing), 1)
    blocks = [own, beside, core(own), core(beside), facing, diagonal, core(facing), core(diagonal)]

    vec = vector_weight[: 6 * D].reshape(6, D)

    def columns(start, width):
        part = lax.dynamic_slice_in_dim(vector_weight, start, width)
        return jnp.concatenate(halves(part))

    biases = jnp.stack(
        [
            columns(6 * D + tp_rank * head_width, head_width),
            columns(7 * D + tp_rank * head_width, head_width),
        ]
    )
    bias_hidden = jnp.concatenate(
        [
            columns(8 * D + tp_rank * unit_width, unit_width),
            columns(8 * D + sib_rank * unit_width, unit_width),
        ]
    )[None]

    token_t, qkv_w, queries, keys, values = project(blocks, qkv_mine, qkv_other, biases)
    down_low = jnp.concatenate(halves(ffn_weight[1].astype(BF16)), axis=1)
    mixed_own, mixed_sib, lse = attend(queries, keys, values)
    down_low = after(down_low, mixed_own)
    if ring():
        low, high = jnp.split(down_low, 2, axis=1)
        spots = ((0, 0), (1, 0), (3, 0), (2, 0), (2, low.shape[1]))
        down_w = [down_low, shift_fsdp(down_low, -1), shift_fsdp(down_low, -3)]
        down_w += [shift_fsdp(low, -2), shift_fsdp(high, -2)]
    else:
        spots = ((0, 0),)
        down_w = [gather_fsdp(down_low, 0)]
    mixed_recv = core(mixed_sib)
    out_up = after(out_up, mixed_own)
    out_up_sib = core(out_up)
    up_other = swap_ctx(out_up[1:])
    out_w, attn_part, attn_far = out_project(mixed_own, mixed_recv, [out_up, out_up_sib])
    attn_recv = across(attn_far)
    if ring():
        attn_recv = after(attn_recv, down_w[1], down_w[2])
    first, first_low, normed_one, inverse_one = norm_one(own, attn_part, attn_recv, vec)
    first_beside = across(first_low)

    if ring():
        first_beside = after(first_beside, down_w[3])
    up_other = after(up_other, first_beside)
    first_t, up_all, hidden_own, hidden_sib, slope_own, slope_sib = feed_up(
        first_low, first_beside, [out_up, up_other, out_up_sib, core(up_other)], bias_hidden
    )
    if ring():
        down_w[4] = after(down_w[4], hidden_own)
    down_all, down_part, down_far = feed_down(
        hidden_own, hidden_sib, spots, down_w, [core(w) for w in down_w]
    )
    layer_out, grad_second, grad_down, sums_two = norm_two(
        first, down_part, across(down_far), cotangent[0], vec
    )
    grad_down_t, grad_up_own, grad_up_sib, grad_bias_hidden, first_part, first_far = feed_back(
        grad_down, across(grad_down), slope_own, slope_sib, up_all, down_all
    )
    down_sib = grad_send(grad_down_t, hidden_sib)
    up_sib = grad_send(first_t, grad_up_sib)
    first_recv = after(across(first_far), down_sib, up_sib)
    grad_res, grad_attn, sums_one = norm_one_back(
        grad_second, first_part, first_recv, normed_one, inverse_one, vec
    )
    grad_attn_beside = across(grad_attn)
    down_sum = grad_total(grad_down_t, hidden_own, after(core(down_sib), grad_attn))
    up_keep, up_send = grad_sum(first_t, grad_up_own, after(core(up_sib), grad_attn))

    def finish(mine):
        return join(mine, swap_ctx(mine)).astype(F32)

    def finish_whole(part):
        mine, other = jnp.split(part.astype(F32), 2, axis=1)
        recv_other, recv_mine = jnp.split(swap_ctx(part).astype(F32), 2, axis=1)
        return join(mine + recv_mine, other + recv_other)

    down_owned = scatter_fsdp(down_sum, 0)
    up_recv = swap_ctx(up_send)

    grad_attn_beside = after(grad_attn_beside, down_sum, up_send)
    grad_attn_t, grad_mixed_own, grad_mixed_sib = out_back(grad_attn, grad_attn_beside, out_w)
    grad_mixed = (grad_mixed_own, core(grad_mixed_sib))

    up_recv = after(up_recv, grad_mixed_sib)
    up_sum = (up_keep.astype(F32) + up_recv.astype(F32)).astype(BF16)
    up_owned = scatter_fsdp(up_sum, 0)
    mixed = (mixed_own, mixed_sib)
    heads = (queries, keys, values, mixed)
    query_other, kv_other = attend_back(*heads, grad_mixed, lse, 1)
    send = head_send(token_t, query_other, kv_other)
    out_sib = grad_send(after(grad_attn_t, query_other), mixed_recv)
    out_keep, out_send = grad_sum(grad_attn_t, mixed_own, core(out_sib))
    grad_mixed = (grad_mixed[0], after(grad_mixed[1], up_sum, send, out_send))
    recv = swap_ctx(send)
    query_mine, kv_mine = attend_back(*heads, grad_mixed, lse, 0)
    part = head_width // 2
    near, far, sibling = input_back(
        query_mine, query_other, kv_mine, kv_other, qkv_w, sums_one, sums_two, grad_bias_hidden
    )
    sib_recv = core(sibling)
    qkvo_sum = head_sum(token_t, query_mine, kv_mine, recv, out_keep, swap_ctx(out_send))
    qkvo_mine = scatter_fsdp(qkvo_sum, 0)
    sib_recv = after(sib_recv, qkvo_sum)
    input_part, to_x, to_y, to_d, vec_part = fold(near, far, sibling, sib_recv, grad_res)
    from_x, from_y, from_d = across(to_x), swap_ctx(to_y), swap_both(to_d)
    down_grad, up_grad = finish_whole(after(down_owned, to_y)), finish(after(up_owned, from_y))
    ffn_grad = jnp.stack([up_grad, down_grad])
    ffn_new, ffn_momentum_new, ffn_average_new = nesterov(
        ffn_weight, ffn_momentum, ffn_average, ffn_grad, matrix_rate
    )
    input_grad = input_part
    for term in (from_x, from_y, from_d):
        input_grad = input_grad + term[:rows].astype(F32)
    vec_x, vec_y, vec_d = (term[rows:].astype(F32) for term in (from_x, from_y, from_d))
    vec_plane = (vec_part.astype(F32) + vec_x) + (vec_y + vec_d)

    qkvo_mine = after(qkvo_mine, from_x, from_y, from_d)
    qkvo_other = swap_ctx(qkvo_mine)
    vector_grad = sum_fsdp(vec_plane[:12]).reshape(-1)
    attn_grad = jnp.stack(
        [
            join(qkvo_mine[:, j * part : (j + 1) * part], qkvo_other[:, j * part : (j + 1) * part])
            for j in range(4)
        ]
    ).astype(F32)
    vector_new, vector_momentum_new, vector_average_new = nesterov(
        vector_weight, vector_momentum, vector_average, vector_grad, vector_rate
    )
    attn_new, attn_momentum_new, attn_average_new = nesterov(
        attn_weight, attn_momentum, attn_average, attn_grad, matrix_rate
    )
    return (
        layer_out[None],
        input_grad[None],
        attn_grad,
        attn_new,
        attn_momentum_new,
        attn_average_new,
        attn_new.astype(BF16),
        ffn_grad,
        ffn_new,
        ffn_momentum_new,
        ffn_average_new,
        ffn_new.astype(BF16),
        vector_grad,
        vector_new,
        vector_momentum_new,
        vector_average_new,
    )


def solution(mesh):
    rows = P("fsdp", ("ctx", "tp"), None)
    weight = P(None, "fsdp", "tp")
    return jax.shard_map(
        on_device,
        mesh=mesh,
        in_specs=(rows, rows) + (weight,) * 6 + (P(),) * 3,
        out_specs=(rows, rows) + (weight,) * 10 + (P(),) * 4,
        check_vma=False,
    )
```

```python
import functools
import math

import jax
import jax.numpy as jnp
from jax import lax
from jax.experimental import pallas as pl
from jax.experimental.pallas import tpu as pltpu
from jax.sharding import PartitionSpec as P

D = 1024
FF = 4096
HEAD_DIM = 64
LEN = 2048

NORM_EPSILON = 1e-05
MOMENTUM = 0.5
AVERAGE = 0.5
MATRIX_RATE = 0.1
VECTOR_RATE = 0.3

SCALE = HEAD_DIM ** (-0.5)
LOG2E = math.log2(math.e)
F32 = jnp.float32
BF16 = jnp.bfloat16
NT = (((1,), (1,)), ((), ()))
TN = (((0,), (0,)), ((), ()))
NN = (((1,), (0,)), ((), ()))


def dot(left, right, dims=NN):
    return lax.dot_general(left, right, dims, preferred_element_type=F32)


VMEM = pl.BlockSpec(memory_space=pltpu.VMEM)
ANY = pl.BlockSpec(memory_space=pl.ANY)
MEGA = 1024 * 1024
WORK_UNIT = 1.2e10


WORK = {
    "project": 0.001,
    "attend": 0.001,
    "out_project": 0.001,
    "norm_one": 1.5,
    "feed_up": 8,
    "feed_down": 4,
    "norm_two": 2,
    "feed_back": 8,
    "grad_send": 10,
    "grad_sum": 3,
    "norm_one_back": 2,
    "out_back": 2,
    "attend_back": 12,
    "head_send": 3,
    "head_sum": 4,
    "input_back": 0.01,
    "fold": 1.5,
    "grad_total": 3,
}


def cost(name):
    flops = int(WORK[name] * WORK_UNIT)
    return pl.CostEstimate(flops=flops, bytes_accessed=1, transcendentals=0)


def shape(dims, dtype):
    return jax.ShapeDtypeStruct(tuple(dims), dtype)


def tile(i, size):
    return pl.ds(pl.multiple_of(i * size, size), size)


def call_whole(kernel, name, out_shape, far_args, near_args, scratch=(), copies=0):
    scratch = list(scratch)
    if copies:
        scratch.append(pltpu.SemaphoreType.DMA((copies,)))
    return pl.pallas_call(
        kernel,
        in_specs=[ANY] * len(far_args) + [VMEM] * len(near_args),
        out_specs=[VMEM] * len(out_shape),
        out_shape=list(out_shape),
        scratch_shapes=scratch,
        compiler_params=pltpu.CompilerParams(vmem_limit_bytes=8 * MEGA),
        cost_estimate=cost(name),
        name=name,
    )(*far_args, *near_args)


def start_all(pairs, sems):
    copies = [pltpu.make_async_copy(src, dst, sems.at[i]) for i, (src, dst) in enumerate(pairs)]
    for copy in copies:
        copy.start()
    return copies


def head_masks(width):
    lane = lax.broadcasted_iota(jnp.int32, (1, width), 1) // HEAD_DIM
    return [(lane == h).astype(BF16) for h in range(width // HEAD_DIM)]


def attend_kernel(chunk, q_ref, k_ref, v_ref, own_ref, sib_ref, lse_ref, vt_ref):
    heads = q_ref.shape[1] // HEAD_DIM
    count = k_ref.shape[0]
    step = pl.program_id(0)

    @pl.when(step == 0)
    def _():
        vt_ref[...] = v_ref[...].T

    queries = q_ref[...]
    masked = [queries * mask for mask in head_masks(q_ref.shape[1])]
    units = [(h, c) for h in range(heads) for c in range(0, count, chunk)]

    def scores_of(unit):
        h, c = unit
        return dot(k_ref[c : c + chunk, :], masked[h], NT)

    tops, totals, outs = {}, {}, {}
    scores = scores_of(units[0])
    for i, unit in enumerate(units):
        current = scores
        if i + 1 < len(units):
            scores = scores_of(units[i + 1])
        h, c = unit
        top = jnp.max(current, axis=0, keepdims=True)
        weights = jnp.exp2((current - top) * (SCALE * LOG2E))
        tops[unit] = top
        totals[unit] = jnp.sum(weights, axis=0, keepdims=True)
        outs[unit] = dot(
            vt_ref[h * HEAD_DIM : (h + 1) * HEAD_DIM, c : c + chunk], weights.astype(BF16)
        )
    heads_out = []
    for h in range(heads):
        mine = [(h, c) for c in range(0, count, chunk)]
        top = functools.reduce(jnp.maximum, [tops[u] for u in mine])
        share = [jnp.exp2((tops[u] - top) * (SCALE * LOG2E)) for u in mine]
        total = sum(totals[u] * f for u, f in zip(mine, share))
        out = sum(outs[u] * f for u, f in zip(mine, share))
        heads_out.append(out / total)
        lse_ref[h : h + 1, :] = top * (SCALE * LOG2E) + jnp.log2(total)
    mixed = jnp.concatenate(heads_out, axis=0).T.astype(BF16)
    steps = pl.num_programs(0)

    @pl.when(step < steps // 2)
    def _():
        own_ref[...] = mixed

    @pl.when(step >= steps // 2)
    def _():
        sib_ref[...] = mixed


def attend(queries, keys, values):
    rows, width = queries.shape
    block = min(256, rows // 2)
    steps = rows // block
    heads = width // HEAD_DIM
    half_blocks = steps // 2
    return pl.pallas_call(
        functools.partial(attend_kernel, min(512, keys.shape[0])),
        grid=(steps,),
        in_specs=[
            pl.BlockSpec((block, width), lambda i: (i, 0)),
            pl.BlockSpec(keys.shape, lambda i: (0, 0)),
            pl.BlockSpec(values.shape, lambda i: (0, 0)),
        ],
        out_specs=[
            pl.BlockSpec((block, width), lambda i: (jnp.minimum(i, half_blocks - 1), 0)),
            pl.BlockSpec((block, width), lambda i: (jnp.maximum(i - half_blocks, 0), 0)),
            pl.BlockSpec((heads, block), lambda i: (0, i)),
        ],
        out_shape=[
            shape((rows // 2, width), BF16),
            shape((rows // 2, width), BF16),
            shape((heads, rows), F32),
        ],
        scratch_shapes=[pltpu.VMEM((width, keys.shape[0]), BF16)],
        compiler_params=pltpu.CompilerParams(vmem_limit_bytes=16 * MEGA),
        cost_estimate=cost("attend"),
        name="attend",
    )(queries, keys, values)


def attend_back_kernel(
    part, q_ref, k_ref, v_ref, o0_ref, o1_ref, g0_ref, g1_ref, lse_ref,
    dq_ref, dkv_ref, kt_ref, dk_acc, dv_acc, o_ref, g_ref,
):
    width = q_ref.shape[1]
    heads = width // HEAD_DIM
    step = pl.program_id(0)
    steps = pl.num_programs(0)

    @pl.when(step == 0)
    def _():
        kt_ref[...] = k_ref[...].T
        dk_acc[...] = jnp.zeros_like(dk_acc)
        dv_acc[...] = jnp.zeros_like(dv_acc)

    @pl.when(step < steps // 2)
    def _():
        o_ref[...] = o0_ref[...]
        g_ref[...] = g0_ref[...]

    @pl.when(step >= steps // 2)
    def _():
        o_ref[...] = o1_ref[...]
        g_ref[...] = g1_ref[...]

    queries = q_ref[...]
    grads = g_ref[...]
    masks = head_masks(width)
    product = (o_ref[...].astype(F32) * grads.astype(F32)).T
    outs, probs, gscores, qms, gms = [], [], [], [], []
    for h in range(heads):
        qm = queries * masks[h]
        gm = grads * masks[h]
        delta = jnp.sum(product[h * HEAD_DIM : (h + 1) * HEAD_DIM, :], axis=0, keepdims=True)
        scores = dot(k_ref[...], qm, NT)
        row = part * heads + h
        prob = jnp.exp2(scores * (SCALE * LOG2E) - lse_ref[row : row + 1, :])
        grad_prob = dot(v_ref[...], gm, NT)
        gscore = (prob * (grad_prob - delta)).astype(BF16)
        outs.append(dot(kt_ref[h * HEAD_DIM : (h + 1) * HEAD_DIM, :], gscore))
        probs.append(prob.astype(BF16))
        gscores.append(gscore)
        qms.append(qm)
        gms.append(gm)
    dv_acc[...] += dot(jnp.concatenate(probs, axis=1), jnp.concatenate(gms, axis=0))
    dk_acc[...] += dot(jnp.concatenate(gscores, axis=1), jnp.concatenate(qms, axis=0))
    dq_ref[...] = (jnp.concatenate(outs, axis=0).T * SCALE).astype(BF16)

    @pl.when(step == steps - 1)
    def _():
        dkv_ref[:, :width] = (dk_acc[...] * SCALE).astype(BF16)
        dkv_ref[:, width:] = dv_acc[...].astype(BF16)


def attend_back(queries, keys, values, mixed, grads, lse, part):
    rows, both = queries.shape
    count = keys.shape[0]
    width = both // 2
    block = min(256, rows // 2)
    half_blocks = rows // 2 // block
    row_spec = pl.BlockSpec((block, width), lambda i: (i, part))
    own_spec = pl.BlockSpec((block, width), lambda i: (jnp.minimum(i, half_blocks - 1), part))
    sib_spec = pl.BlockSpec((block, width), lambda i: (jnp.maximum(i - half_blocks, 0), part))
    full_spec = pl.BlockSpec((count, width), lambda i: (0, part))
    lse_spec = pl.BlockSpec((lse.shape[0], block), lambda i: (0, i))
    return pl.pallas_call(
        functools.partial(attend_back_kernel, part),
        grid=(rows // block,),
        in_specs=[row_spec, full_spec, full_spec] + [own_spec, sib_spec] * 2 + [lse_spec],
        out_specs=[
            pl.BlockSpec((block, width), lambda i: (i, 0)),
            pl.BlockSpec((count, both), lambda i: (0, 0)),
        ],
        out_shape=[shape((rows, width), BF16), shape((count, both), BF16)],
        scratch_shapes=[
            pltpu.VMEM((width, count), BF16),
            pltpu.VMEM((count, width), F32),
            pltpu.VMEM((count, width), F32),
            pltpu.VMEM((block, width), BF16),
            pltpu.VMEM((block, width), BF16),
        ],
        compiler_params=pltpu.CompilerParams(vmem_limit_bytes=16 * MEGA),
        cost_estimate=cost("attend_back"),
        name="attend_back",
    )(queries, keys, values, *mixed, *grads, lse)


def ring_rows(count, deep):
    size = deep // count
    rank = lax.axis_index("fsdp")
    return [tile(lax.rem(rank + s, count), size) if count > 1 else tile(0, size) for s in range(count)]


def project_kernel(count, *refs):
    blocks, refs = refs[:8], refs[8:]
    mine, refs = refs[:count], refs[count:]
    other, refs = refs[:count], refs[count:]
    bias_ref, xt_ref, w_ref, q_ref, k_ref, v_ref, x_ref, sems = refs
    rows = blocks[0].shape[0]
    deep = x_ref.shape[1]
    part = mine[0].shape[2]
    width = 2 * part
    pairs = []
    for at, low, high in zip(ring_rows(count, deep), mine, other):
        for j in range(3):
            pairs.append((low.at[j], w_ref.at[at, j * width : j * width + part]))
            pairs.append((high.at[j], w_ref.at[at, j * width + part : (j + 1) * width]))
    weights = len(pairs)
    for i in range(8):
        pairs.append((blocks[i], x_ref.at[i * rows : (i + 1) * rows, :]))
    copies = start_all(pairs, sems)
    for copy in copies[:weights]:
        copy.wait()
    for i in range(4):
        at = slice(i * 2 * rows, (i + 1) * 2 * rows)
        for copy in copies[weights + 2 * i : weights + 2 * i + 2]:
            copy.wait()
        x = x_ref[at, :]
        if i < 2:
            out = dot(x, w_ref[...])
            q_ref[at, :] = (out[:, :width] + bias_ref[0:1, :]).astype(BF16)
            out = out[:, width:]
        else:
            out = dot(x, w_ref[:, width:])
        k_ref[at, :] = out[:, :width].astype(BF16)
        v_ref[at, :] = (out[:, width:] + bias_ref[1:2, :]).astype(BF16)
        xt_ref[:, at] = x.T


def project(blocks, mine, other, biases):
    rows, deep = blocks[0].shape
    width = biases.shape[1]
    out = [
        shape((deep, 8 * rows), BF16),
        shape((deep, 3 * width), BF16),
        shape((4 * rows, width), BF16),
        shape((8 * rows, width), BF16),
        shape((8 * rows, width), BF16),
    ]
    scratch = [pltpu.VMEM((8 * rows, deep), BF16)]
    kernel = functools.partial(project_kernel, len(mine))
    args = [*blocks, *mine, *other]
    return call_whole(kernel, "project", out, args, [biases], scratch, 8 + 6 * len(mine))


def split_store(out, near_ref, far_ref, at):
    rows = near_ref.shape[0]
    near_ref[:, at] = out[:rows]
    far_ref[:, at] = out[rows:].astype(BF16)


def out_kernel(w0, w1, own, sib, w_ref, near_ref, far_ref, sems):
    width = own.shape[1]
    deep = w_ref.shape[0]
    pairs = [(w0.at[0], w_ref.at[:, :width]), (w1.at[0], w_ref.at[:, width:])]
    for copy in start_all(pairs, sems):
        copy.wait()
    for c in range(4):
        at = slice(c * deep // 4, (c + 1) * deep // 4)
        out = dot(own[...], w_ref[at, :width], NT) + dot(sib[...], w_ref[at, width:], NT)
        split_store(out, near_ref, far_ref, at)


def out_project(own, sib, pieces):
    pair, width = own.shape
    deep = pieces[0].shape[1]
    out = [
        shape((deep, 2 * width), BF16),
        shape((pair // 2, deep), F32),
        shape((pair // 2, deep), BF16),
    ]
    return call_whole(out_kernel, "out_project", out, pieces, [own, sib], copies=2)


def out_back_kernel(g0, g1, w_ref, gt_ref, own_ref, sib_ref):
    rows = g0.shape[0]
    width = own_ref.shape[1]
    for i, ref in enumerate((g0, g1)):
        at = slice(i * rows, (i + 1) * rows)
        g = ref[...]
        out = dot(g, w_ref[...])
        own_ref[at, :] = out[:, :width].astype(BF16)
        sib_ref[at, :] = out[:, width:].astype(BF16)
        gt_ref[:, at] = g.T


def out_back(g0, g1, weights):
    rows, deep = g0.shape
    width = weights.shape[1] // 2
    out = [
        shape((deep, 2 * rows), BF16),
        shape((2 * rows, width), BF16),
        shape((2 * rows, width), BF16),
    ]
    return call_whole(out_back_kernel, "out_back", out, [], [g0, g1, weights])


EXTRA = 16


def pack_rows(out_ref, one, two, q0, q1, kv0, kv1, hidden):
    rank = lax.axis_index("tp")
    size = lax.axis_size("tp")
    first = lax.axis_index("ctx") == 0
    part = q0.shape[1]
    units = hidden.shape[1] // 2
    out_ref[...] = jnp.zeros_like(out_ref)
    out_ref[0:2, :] = one[0:2, :]
    out_ref[2:4, :] = two[0:2, :]
    out_ref[4:5, :] = one[2:3, :]
    out_ref[5:6, :] = two[2:3, :]
    for row, (mine, other, at) in ((6, (q0, q1, 0)), (7, (kv0, kv1, part))):
        mine = col_sum(mine[:, at : at + part].astype(F32))
        other = col_sum(other[:, at : at + part].astype(F32))
        low, high = jnp.where(first, mine, other), jnp.where(first, other, mine)
        for t in range(size):
            keep = rank == t
            start = 2 * t * part
            out_ref[row : row + 1, start : start + part] = jnp.where(keep, low, 0.0)
            out_ref[row : row + 1, start + part : start + 2 * part] = jnp.where(keep, high, 0.0)
    for t in range(size):
        row = 8 + t
        total = jnp.where(rank == t, hidden[:, :units], 0.0)
        total = total + jnp.where((rank ^ 1) == t, hidden[:, units:], 0.0)
        mine, other = total[:, : units // 2], total[:, units // 2 :]
        out_ref[row : row + 1, : units // 2] = jnp.where(first, mine, other)
        out_ref[row : row + 1, units // 2 :] = jnp.where(first, other, mine)


def input_back_kernel(
    q0, q1, kv0, kv1, w_ref, one, two, hidden, near_ref, far_ref, sib_ref, cat_ref, vec_ref
):
    half, part = q0.shape
    pair, deep = near_ref.shape
    for j, (ref, at) in enumerate(((q0, 0), (q1, 0), (kv0, 0), (kv1, 0), (kv0, part), (kv1, part))):
        count = ref.shape[0]
        cat_ref[:count, j * part : (j + 1) * part] = ref[:, at : at + part]
    sib_ref[:pair, :] = dot(cat_ref[pair:half, :], w_ref[...], NT).astype(BF16)
    out = dot(cat_ref[half + pair :, 2 * part :], w_ref[:, 2 * part :], NT)
    sib_ref[pair:half, :] = out.astype(BF16)
    near_ref[...] = dot(cat_ref[:pair, :], w_ref[...], NT)
    far_ref[...] = dot(cat_ref[half : half + pair, 2 * part :], w_ref[:, 2 * part :], NT)
    pack_rows(vec_ref, one, two, q0, q1, kv0, kv1, hidden)
    sib_ref[half:, :] = vec_ref[...].astype(BF16)


def input_back(q0, q1, kv0, kv1, weights, one, two, hidden):
    half, part = q0.shape
    deep = weights.shape[0]
    pair = half // 2
    out = [shape((pair, deep), F32), shape((pair, deep), F32), shape((half + EXTRA, deep), BF16)]
    scratch = [pltpu.VMEM((kv0.shape[0], 6 * part), BF16), pltpu.VMEM((EXTRA, deep), F32)]
    args = [q0, q1, kv0, kv1, weights, one, two, hidden]
    return call_whole(input_back_kernel, "input_back", out, [], args, scratch)


def fold_kernel(near, far, sent, recv, rest, own_ref, x_ref, y_ref, d_ref, vec_ref):
    rows = own_ref.shape[0]
    pair = 2 * rows
    own_ref[...] = rest[...] + near[:rows, :] + recv[:rows, :].astype(F32)
    vec = sent[2 * pair :, :].astype(F32) + recv[2 * pair :, :].astype(F32)
    vec_ref[...] = vec.astype(BF16)
    for ref, term, at in ((x_ref, near, rows), (y_ref, far, 0), (d_ref, far, rows)):
        start = at if term is near else pair + at
        total = term[at : at + rows, :] + recv[start : start + rows, :].astype(F32)
        ref[:rows, :] = total.astype(BF16)
        ref[rows:, :] = vec.astype(BF16)


def fold(near, far, sent, recv, rest):
    rows, deep = rest.shape
    out = [shape((rows, deep), F32)] + [shape((rows + EXTRA, deep), BF16)] * 3
    out += [shape((EXTRA, deep), BF16)]
    return call_whole(fold_kernel, "fold", out, [], [near, far, sent, recv, rest])


def grad_send_kernel(left, right, out_ref):
    out_ref[...] = dot(left[...], right[...]).astype(BF16)


def grad_send(left, right):
    out = [shape((left.shape[0], right.shape[1]), BF16)]
    return call_whole(grad_send_kernel, "grad_send", out, [], [left, right])[0]


def grad_sum_kernel(left, right, recv, keep_ref, send_ref):
    part = keep_ref.shape[1]
    for ref, at in ((send_ref, slice(part, 2 * part)), (keep_ref, slice(0, part))):
        ref[...] = (dot(left[...], right[:, at]) + recv[:, at].astype(F32)).astype(BF16)


def grad_sum(left, right, recv):
    half = shape((left.shape[0], right.shape[1] // 2), BF16)
    return call_whole(grad_sum_kernel, "grad_sum", [half, half], [], [left, right, recv])


def head_grads(left, query, pair):
    half = query.shape[0]
    return jnp.concatenate([dot(left[:, :half], query[...]), dot(left[...], pair[...])], axis=1)


def head_send_kernel(left, query, pair, out_ref):
    out_ref[...] = head_grads(left, query, pair).astype(BF16)


def head_send(left, query, pair):
    out = [shape((left.shape[0], query.shape[1] + pair.shape[1]), BF16)]
    return call_whole(head_send_kernel, "head_send", out, [], [left, query, pair])[0]


def head_sum_kernel(left, query, pair, recv, keep, keep_recv, out_ref):
    width = recv.shape[1]
    total = head_grads(left, query, pair) + recv[...].astype(F32)
    out_ref[:, :width] = total.astype(BF16)
    out_ref[:, width:] = (keep[...].astype(F32) + keep_recv[...].astype(F32)).astype(BF16)


def head_sum(left, query, pair, recv, keep, keep_recv):
    out = [shape((left.shape[0], recv.shape[1] + keep.shape[1]), BF16)]
    args = [left, query, pair, recv, keep, keep_recv]
    return call_whole(head_sum_kernel, "head_sum", out, [], args)[0]


def gelu_pair(values):
    size = jnp.abs(values)
    t = 1.0 / (1.0 + (0.3275911 * math.sqrt(0.5)) * size)
    bell = jnp.exp2(values * values * (-0.5 * LOG2E))
    poly = t * (
        0.5 * 0.254829592
        + t
        * (
            0.5 * -0.284496736
            + t * (0.5 * 1.421413741 + t * (0.5 * -1.453152027 + t * (0.5 * 1.061405429)))
        )
    )
    tail = poly * bell
    cdf = jnp.where(values < 0, tail, 1.0 - tail)
    return values * cdf, cdf + values * bell * (1.0 / math.sqrt(2.0 * math.pi))


def gather_units(refs, w_ref):
    pairs = []
    part = refs[0][0].shape[2]
    for ref, first in refs:
        for j in range(first, ref.shape[0]):
            at = len(pairs) * part
            pairs.append((ref.at[j], w_ref.at[:, at : at + part]))
    return pairs


def up_kernel(
    x0, x1, mine, other, mine_sib, other_sib, bias_ref,
    xt_ref, w_ref, act_own, act_sib, slope_own, slope_sib, x_ref, sems,
):
    rows = x0.shape[0]
    pairs = [(x0, x_ref.at[:rows, :]), (x1, x_ref.at[rows:, :])]
    pairs += gather_units(((mine, 1), (other, 0), (mine_sib, 1), (other_sib, 0)), w_ref)
    copies = start_all(pairs, sems)
    copies[0].wait()
    copies[1].wait()
    units = act_own.shape[1]
    step = mine.shape[2]

    def matmul(c):
        copies[2 + c].wait()
        return dot(x_ref[...], w_ref[:, c * step : (c + 1) * step])

    following = matmul(0)
    for c in range(8):
        pre = following
        if c < 7:
            following = matmul(c + 1)
        act_ref, slope_ref = ((act_own, slope_own), (act_sib, slope_sib))[c // 4]
        at = slice((c % 4) * step, (c % 4 + 1) * step)
        act, slope = gelu_pair(pre + bias_ref[0:1, c * step : (c + 1) * step])
        act_ref[:, at] = act.astype(BF16)
        slope_ref[:, at] = slope.astype(BF16)
    xt_ref[...] = x_ref[...].T


def feed_up(x0, x1, pieces, bias):
    rows, deep = x0.shape
    units = bias.shape[1]
    out = [shape((deep, 2 * rows), BF16), shape((deep, units), BF16)]
    out += [shape((2 * rows, units // 2), BF16)] * 4
    scratch = [pltpu.VMEM((2 * rows, deep), BF16)]
    return call_whole(up_kernel, "feed_up", out, [x0, x1, *pieces], [bias], scratch, 10)


def down_kernel(spots, *refs):
    count = len(spots)
    own, sib, refs = refs[:count], refs[count : 2 * count], refs[2 * count :]
    act_own, act_sib, w_ref, near_ref, far_ref, sems = refs
    deep = near_ref.shape[1]
    units = act_own.shape[1]
    pairs = []
    rows = ring_rows(deep // own[0].shape[0], deep)
    for (piece, start), left, right in zip(spots, own, sib):
        width = left.shape[1]
        pairs.append((left, w_ref.at[rows[piece], start : start + width]))
        pairs.append((right, w_ref.at[rows[piece], units + start : units + start + width]))
    for copy in start_all(pairs, sems):
        copy.wait()
    for c in range(4):
        at = slice(c * deep // 4, (c + 1) * deep // 4)
        out = dot(act_own[...], w_ref[at, :units], NT) + dot(act_sib[...], w_ref[at, units:], NT)
        split_store(out, near_ref, far_ref, at)


def feed_down(act_own, act_sib, spots, own, sib):
    pair, units = act_own.shape
    deep = D
    out = [
        shape((deep, 2 * units), BF16),
        shape((pair // 2, deep), F32),
        shape((pair // 2, deep), BF16),
    ]
    kernel = functools.partial(down_kernel, spots)
    args = [*own, *sib]
    return call_whole(
        kernel, "feed_down", out, args, [act_own, act_sib], copies=2 * len(own)
    )


def feed_back_kernel(
    g0, g1, slope_own, slope_sib, up_ref, down_ref,
    gt_ref, gup_own, gup_sib, bias_ref, near_ref, far_ref, g_ref,
):
    rows, deep = g0.shape
    g_ref[:rows, :] = g0[...]
    g_ref[rows:, :] = g1[...]
    units = gup_own.shape[1]
    step = units // 2
    for c in range(4):
        slope_ref, gup_ref = ((slope_own, gup_own), (slope_sib, gup_sib))[c // 2]
        at = slice((c % 2) * step, (c % 2 + 1) * step)
        grad = dot(g_ref[...], down_ref[:, c * step : (c + 1) * step])
        grad = (grad * slope_ref[:, at].astype(F32)).astype(BF16)
        gup_ref[:, at] = grad
        bias_ref[0:1, c * step : (c + 1) * step] = jnp.sum(
            grad.astype(F32), axis=0, keepdims=True
        )
    for c in range(4):
        at = slice(c * deep // 4, (c + 1) * deep // 4)
        out = dot(gup_own[...], up_ref[at, :units], NT) + dot(gup_sib[...], up_ref[at, units:], NT)
        split_store(out, near_ref, far_ref, at)
    gt_ref[...] = g_ref[...].T


def feed_back(g0, g1, slope_own, slope_sib, up_all, down_all):
    rows, deep = g0.shape
    units = slope_own.shape[1]
    out = [shape((deep, 2 * rows), BF16)]
    out += [shape((2 * rows, units), BF16)] * 2
    out += [shape((1, 2 * units), F32), shape((rows, deep), F32), shape((rows, deep), BF16)]
    args = [g0, g1, slope_own, slope_sib, up_all, down_all]
    scratch = [pltpu.VMEM((2 * rows, deep), BF16)]
    return call_whole(feed_back_kernel, "feed_back", out, [], args, scratch)


def row_mean(values):
    return jnp.mean(values, axis=-1, keepdims=True)


def col_sum(values):
    return jnp.sum(values, axis=0, keepdims=True)


def normalize(values):
    centered = values - row_mean(values)
    inverse = lax.rsqrt(row_mean(centered * centered) + NORM_EPSILON)
    return centered * inverse, inverse


def norm_back(grad_out, normed, inverse, gain):
    grad = grad_out * gain
    return inverse * (grad - row_mean(grad) - normed * row_mean(grad * normed))


def norm_one_kernel(own, part, recv, vec, first_ref, low_ref, normed_ref, inverse_ref):
    attn_out = part[...] + recv[...].astype(F32) + vec[4:5, :]
    normed, inverse = normalize(own[...].astype(F32) + attn_out)
    first = normed * vec[0:1, :] + vec[1:2, :]
    first_ref[...] = first
    low_ref[...] = first.astype(BF16)
    normed_ref[...] = normed
    inverse_ref[...] = inverse


def norm_one(own, part, recv, vec):
    rows, deep = own.shape
    out = [shape((rows, deep), t) for t in (F32, BF16, F32)] + [shape((rows, 1), F32)]
    return call_whole(norm_one_kernel, "norm_one", out, [], [own, part, recv, vec])


def norm_two_kernel(first, part, recv, cotangent, vec, out_ref, grad_ref, low_ref, sums_ref):
    down_out = part[...] + recv[...].astype(F32) + vec[5:6, :]
    normed, inverse = normalize(first[...] + down_out)
    out_ref[...] = (normed * vec[2:3, :] + vec[3:4, :]).astype(BF16)
    given = cotangent[...].astype(F32)
    grad = norm_back(given, normed, inverse, vec[2:3, :])
    grad_ref[...] = grad
    low = grad.astype(BF16)
    low_ref[...] = low
    sums_ref[0:1, :] = col_sum(given * normed)
    sums_ref[1:2, :] = col_sum(given)
    sums_ref[2:3, :] = col_sum(low.astype(F32))


def norm_two(first, part, recv, cotangent, vec):
    rows, deep = first.shape
    out = [shape((rows, deep), t) for t in (BF16, F32, BF16)] + [shape((3, deep), F32)]
    return call_whole(norm_two_kernel, "norm_two", out, [], [first, part, recv, cotangent, vec])


def norm_one_back_kernel(
    grad_second, part, recv, normed, inverse, vec, grad_ref, low_ref, sums_ref
):
    given = grad_second[...] + part[...] + recv[...].astype(F32)
    grad = norm_back(given, normed[...], inverse[...], vec[0:1, :])
    grad_ref[...] = grad
    low = grad.astype(BF16)
    low_ref[...] = low
    sums_ref[0:1, :] = col_sum(given * normed[...])
    sums_ref[1:2, :] = col_sum(given)
    sums_ref[2:3, :] = col_sum(low.astype(F32))


def norm_one_back(grad_second, part, recv, normed, inverse, vec):
    rows, deep = part.shape
    out = [shape((rows, deep), t) for t in (F32, BF16)] + [shape((3, deep), F32)]
    args = [grad_second, part, recv, normed, inverse, vec]
    return call_whole(norm_one_back_kernel, "norm_one_back", out, [], args)


def nesterov(weights, momentum, average, gradient, step_rate):
    momentum_new = MOMENTUM * momentum + gradient
    weight_new = weights - step_rate * (gradient + MOMENTUM * momentum_new)
    return (weight_new, momentum_new, AVERAGE * average + (1.0 - AVERAGE) * weight_new)


def swap_tp(values, bit):
    size = lax.axis_size("tp")
    return lax.ppermute(values, "tp", [(i, i ^ bit) for i in range(size)])


def core(values):
    return swap_tp(values, 1)


def across(values):
    return swap_tp(values, 2)


def swap_ctx(values):
    return lax.ppermute(values, "ctx", [(0, 1), (1, 0)])


def swap_both(values):
    size = lax.axis_size("tp")
    return lax.ppermute(values, ("ctx", "tp"), [(i, i ^ (size + 2)) for i in range(2 * size)])


def sum_fsdp(values):
    size = lax.axis_size("fsdp")

    def swap(values, bit):
        return lax.ppermute(values, "fsdp", [(i, i ^ bit) for i in range(size)])

    if size == 4:
        one, two, three = (swap(values, bit) for bit in (1, 2, 3))
        return (values + one) + (two + three)
    bit = 1
    while bit < size:
        values = values + swap(values, bit)
        bit *= 2
    return values


def gather_fsdp(shard, axis):
    return lax.all_gather(shard, "fsdp", axis=axis, tiled=True)


def ring():
    return lax.axis_size("fsdp") == 4


def shift_fsdp(values, step):
    size = lax.axis_size("fsdp")
    return lax.ppermute(values, "fsdp", [(i, (i + step) % size) for i in range(size)])


def gather_pieces(shard, axis):
    if not ring():
        return [gather_fsdp(shard, axis)]
    return [shard] + [shift_fsdp(shard, -s) for s in range(1, lax.axis_size("fsdp"))]


def scatter_fsdp(grads, axis):
    return lax.psum_scatter(grads, "fsdp", scatter_dimension=axis, tiled=True)


def halves(values, axis=-1):
    low, high = jnp.split(values, 2, axis=axis)
    first = lax.axis_index("ctx") == 0
    return jnp.where(first, low, high), jnp.where(first, high, low)


def join(mine, other, axis=-1):
    first = lax.axis_index("ctx") == 0
    low, high = jnp.where(first, mine, other), jnp.where(first, other, mine)
    return jnp.concatenate([low, high], axis=axis)


def quarters(mine):
    return jnp.stack(jnp.split(mine, 2, axis=1))


def after(values, *others):
    return lax.optimization_barrier((values,) + others)[0]


def on_device(
    tokens,
    cotangent,
    attn_weight,
    attn_momentum,
    attn_average,
    ffn_weight,
    ffn_momentum,
    ffn_average,
    vector_weight,
    vector_momentum,
    vector_average,
):
    tp_rank = lax.axis_index("tp")
    sib_rank = tp_rank ^ 1
    head_width = attn_weight.shape[2]
    unit_width = ffn_weight.shape[2]
    token_count = LEN * lax.axis_size("fsdp")
    matrix_rate = MATRIX_RATE / math.sqrt(token_count)
    vector_rate = VECTOR_RATE / math.sqrt(token_count)

    attn_low, attn_high = halves(attn_weight.astype(BF16))
    qkv_mine = gather_pieces(attn_low[:3], 1)

    own = tokens[0]
    rows = own.shape[0]
    pair = 2 * rows
    half = 4 * rows
    beside = across(own)
    facing = swap_ctx(own)
    diagonal = swap_both(own)
    if ring():
        others = swap_ctx(after(jnp.stack(qkv_mine[1:]), beside, facing))
        qkv_other = [attn_high[:3]] + [others[s] for s in range(len(qkv_mine) - 1)]
    else:
        qkv_other = [swap_ctx(qkv_mine[0])]
    up_low = quarters(halves(ffn_weight[0].astype(BF16))[0])
    out_low = jnp.concatenate([attn_low[3], attn_high[3]], axis=1)
    out_up_low = jnp.concatenate([out_low[None], up_low])
    out_up = gather_fsdp(after(out_up_low, *qkv_mine[-3:], beside, facing), 1)
    blocks = [own, beside, core(own), core(beside), facing, diagonal, core(facing), core(diagonal)]

    vec = vector_weight[: 6 * D].reshape(6, D)

    def columns(start, width):
        part = lax.dynamic_slice_in_dim(vector_weight, start, width)
        return jnp.concatenate(halves(part))

    biases = jnp.stack(
        [
            columns(6 * D + tp_rank * head_width, head_width),
            columns(7 * D + tp_rank * head_width, head_width),
        ]
    )
    bias_hidden = jnp.concatenate(
        [
            columns(8 * D + tp_rank * unit_width, unit_width),
            columns(8 * D + sib_rank * unit_width, unit_width),
        ]
    )[None]

    token_t, qkv_w, queries, keys, values = project(blocks, qkv_mine, qkv_other, biases)
    down_low = jnp.concatenate(halves(ffn_weight[1].astype(BF16)), axis=1)
    mixed_own, mixed_sib, lse = attend(queries, keys, values)
    down_low = after(down_low, mixed_own)
    if ring():
        low, high = jnp.split(down_low, 2, axis=1)
        spots = ((0, 0), (1, 0), (3, 0), (2, 0), (2, low.shape[1]))
        down_w = [down_low, shift_fsdp(down_low, -1), shift_fsdp(down_low, -3)]
        down_w += [shift_fsdp(low, -2), shift_fsdp(high, -2)]
    else:
        spots = ((0, 0),)
        down_w = [gather_fsdp(down_low, 0)]
    mixed_recv = core(mixed_sib)
    out_up = after(out_up, mixed_own)
    out_up_sib = core(out_up)
    up_other = swap_ctx(out_up[1:])
    out_w, attn_part, attn_far = out_project(mixed_own, mixed_recv, [out_up, out_up_sib])
    attn_recv = across(attn_far)
    if ring():
        attn_recv = after(attn_recv, down_w[1], down_w[2])
    first, first_low, normed_one, inverse_one = norm_one(own, attn_part, attn_recv, vec)
    first_beside = across(first_low)

    if ring():
        first_beside = after(first_beside, down_w[3])
    up_other = after(up_other, first_beside)
    first_t, up_all, hidden_own, hidden_sib, slope_own, slope_sib = feed_up(
        first_low, first_beside, [out_up, up_other, out_up_sib, core(up_other)], bias_hidden
    )
    if ring():
        down_w[4] = after(down_w[4], hidden_own)
    down_all, down_part, down_far = feed_down(
        hidden_own, hidden_sib, spots, down_w, [core(w) for w in down_w]
    )
    layer_out, grad_second, grad_down, sums_two = norm_two(
        first, down_part, across(down_far), cotangent[0], vec
    )
    grad_down_t, grad_up_own, grad_up_sib, grad_bias_hidden, first_part, first_far = feed_back(
        grad_down, across(grad_down), slope_own, slope_sib, up_all, down_all
    )
    down_sib = grad_send(grad_down_t, hidden_sib)
    up_sib = grad_send(first_t, grad_up_sib)
    first_recv = after(across(first_far), down_sib, up_sib)
    grad_res, grad_attn, sums_one = norm_one_back(
        grad_second, first_part, first_recv, normed_one, inverse_one, vec
    )
    grad_attn_beside = across(grad_attn)
    down_mine, down_rest = grad_sum(grad_down_t, hidden_own, after(core(down_sib), grad_attn))
    up_keep, up_send = grad_sum(first_t, grad_up_own, after(core(up_sib), grad_attn))

    def finish(mine):
        return join(mine, swap_ctx(mine)).astype(F32)

    mine_owned = scatter_fsdp(down_mine, 0)
    rest_owned = scatter_fsdp(down_rest, 0)
    up_recv = swap_ctx(up_send)

    grad_attn_beside = after(grad_attn_beside, down_mine, up_send)
    grad_attn_t, grad_mixed_own, grad_mixed_sib = out_back(grad_attn, grad_attn_beside, out_w)
    grad_mixed = (grad_mixed_own, core(grad_mixed_sib))

    up_recv = after(up_recv, grad_mixed_sib)
    up_sum = (up_keep.astype(F32) + up_recv.astype(F32)).astype(BF16)
    up_owned = scatter_fsdp(up_sum, 0)
    mixed = (mixed_own, mixed_sib)
    heads = (queries, keys, values, mixed)
    query_other, kv_other = attend_back(*heads, grad_mixed, lse, 1)
    send = head_send(token_t, query_other, kv_other)
    out_sib = grad_send(after(grad_attn_t, query_other), mixed_recv)
    out_keep, out_send = grad_sum(grad_attn_t, mixed_own, core(out_sib))
    grad_mixed = (grad_mixed[0], after(grad_mixed[1], up_sum, send, out_send, mine_owned))
    recv = swap_ctx(send)
    query_mine, kv_mine = attend_back(*heads, grad_mixed, lse, 0)
    part = head_width // 2
    near, far, sibling = input_back(
        query_mine, query_other, kv_mine, kv_other, qkv_w, sums_one, sums_two, grad_bias_hidden
    )
    sib_recv = core(sibling)
    qkvo_sum = head_sum(token_t, query_mine, after(kv_mine, rest_owned), recv, out_keep, swap_ctx(out_send))
    qkvo_mine = scatter_fsdp(qkvo_sum, 0)
    sib_recv = after(sib_recv, qkvo_sum)
    input_part, to_x, to_y, to_d, vec_part = fold(near, far, sibling, sib_recv, grad_res)
    from_x, from_y, from_d = across(to_x), swap_ctx(to_y), swap_both(to_d)
    mine_recv, rest_recv = swap_ctx(after(mine_owned, to_y)), swap_ctx(after(rest_owned, from_y))
    down_grad = join(
        mine_owned.astype(F32) + rest_recv.astype(F32),
        rest_owned.astype(F32) + mine_recv.astype(F32),
    )
    up_grad = finish(after(up_owned, from_y))
    ffn_grad = jnp.stack([up_grad, down_grad])
    ffn_new, ffn_momentum_new, ffn_average_new = nesterov(
        ffn_weight, ffn_momentum, ffn_average, ffn_grad, matrix_rate
    )
    input_grad = input_part
    for term in (from_x, from_y, from_d):
        input_grad = input_grad + term[:rows].astype(F32)
    vec_x, vec_y, vec_d = (term[rows:].astype(F32) for term in (from_x, from_y, from_d))
    vec_plane = (vec_part.astype(F32) + vec_x) + (vec_y + vec_d)

    qkvo_mine = after(qkvo_mine, from_x, from_y, from_d)
    qkvo_other = swap_ctx(qkvo_mine)
    vector_grad = sum_fsdp(vec_plane[:12]).reshape(-1)
    attn_grad = jnp.stack(
        [
            join(qkvo_mine[:, j * part : (j + 1) * part], qkvo_other[:, j * part : (j + 1) * part])
            for j in range(4)
        ]
    ).astype(F32)
    vector_new, vector_momentum_new, vector_average_new = nesterov(
        vector_weight, vector_momentum, vector_average, vector_grad, vector_rate
    )
    attn_new, attn_momentum_new, attn_average_new = nesterov(
        attn_weight, attn_momentum, attn_average, attn_grad, matrix_rate
    )
    return (
        layer_out[None],
        input_grad[None],
        attn_grad,
        attn_new,
        attn_momentum_new,
        attn_average_new,
        attn_new.astype(BF16),
        ffn_grad,
        ffn_new,
        ffn_momentum_new,
        ffn_average_new,
        ffn_new.astype(BF16),
        vector_grad,
        vector_new,
        vector_momentum_new,
        vector_average_new,
    )


def solution(mesh):
    rows = P("fsdp", ("ctx", "tp"), None)
    weight = P(None, "fsdp", "tp")
    return jax.shard_map(
        on_device,
        mesh=mesh,
        in_specs=(rows, rows) + (weight,) * 6 + (P(),) * 3,
        out_specs=(rows, rows) + (weight,) * 10 + (P(),) * 4,
        check_vma=False,
    )
```

```python
import functools
import math

import jax
import jax.numpy as jnp
from jax import lax
from jax.experimental import pallas as pl
from jax.experimental.pallas import tpu as pltpu
from jax.sharding import PartitionSpec as P

D = 1024
FF = 4096
HEAD_DIM = 64
LEN = 2048

NORM_EPSILON = 1e-05
MOMENTUM = 0.5
AVERAGE = 0.5
MATRIX_RATE = 0.1
VECTOR_RATE = 0.3

SCALE = HEAD_DIM ** (-0.5)
LOG2E = math.log2(math.e)
F32 = jnp.float32
BF16 = jnp.bfloat16
NT = (((1,), (1,)), ((), ()))
TN = (((0,), (0,)), ((), ()))
NN = (((1,), (0,)), ((), ()))


def dot(left, right, dims=NN):
    return lax.dot_general(left, right, dims, preferred_element_type=F32)


VMEM = pl.BlockSpec(memory_space=pltpu.VMEM)
ANY = pl.BlockSpec(memory_space=pl.ANY)
MEGA = 1024 * 1024
WORK_UNIT = 1.2e10


WORK = {
    "project": 0.001,
    "attend": 0.001,
    "out_project": 0.001,
    "norm_one": 1.5,
    "feed_up": 8,
    "feed_down": 4,
    "norm_two": 2,
    "feed_back": 8,
    "grad_send": 10,
    "grad_sum": 3,
    "norm_one_back": 2,
    "out_back": 2,
    "attend_back": 12,
    "head_send": 3,
    "head_sum": 4,
    "input_back": 0.01,
    "fold": 1.5,
    "grad_total": 3,
}


def cost(name):
    flops = int(WORK[name] * WORK_UNIT)
    return pl.CostEstimate(flops=flops, bytes_accessed=1, transcendentals=0)


def shape(dims, dtype):
    return jax.ShapeDtypeStruct(tuple(dims), dtype)


def tile(i, size):
    return pl.ds(pl.multiple_of(i * size, size), size)


def call_whole(kernel, name, out_shape, far_args, near_args, scratch=(), copies=0):
    scratch = list(scratch)
    if copies:
        scratch.append(pltpu.SemaphoreType.DMA((copies,)))
    return pl.pallas_call(
        kernel,
        in_specs=[ANY] * len(far_args) + [VMEM] * len(near_args),
        out_specs=[VMEM] * len(out_shape),
        out_shape=list(out_shape),
        scratch_shapes=scratch,
        compiler_params=pltpu.CompilerParams(vmem_limit_bytes=6 * MEGA),
        cost_estimate=cost(name),
        name=name,
    )(*far_args, *near_args)


def start_all(pairs, sems):
    copies = [pltpu.make_async_copy(src, dst, sems.at[i]) for i, (src, dst) in enumerate(pairs)]
    for copy in copies:
        copy.start()
    return copies


def head_masks(width):
    lane = lax.broadcasted_iota(jnp.int32, (1, width), 1) // HEAD_DIM
    return [(lane == h).astype(BF16) for h in range(width // HEAD_DIM)]


def attend_kernel(chunk, q_ref, k_ref, v_ref, own_ref, sib_ref, lse_ref, vt_ref):
    heads = q_ref.shape[1] // HEAD_DIM
    count = k_ref.shape[0]
    step = pl.program_id(0)

    @pl.when(step == 0)
    def _():
        vt_ref[...] = v_ref[...].T

    queries = q_ref[...]
    masked = [queries * mask for mask in head_masks(q_ref.shape[1])]
    units = [(h, c) for h in range(heads) for c in range(0, count, chunk)]

    def scores_of(unit):
        h, c = unit
        return dot(k_ref[c : c + chunk, :], masked[h], NT)

    tops, totals, outs = {}, {}, {}
    scores = scores_of(units[0])
    for i, unit in enumerate(units):
        current = scores
        if i + 1 < len(units):
            scores = scores_of(units[i + 1])
        h, c = unit
        top = jnp.max(current, axis=0, keepdims=True)
        weights = jnp.exp2((current - top) * (SCALE * LOG2E))
        tops[unit] = top
        totals[unit] = jnp.sum(weights, axis=0, keepdims=True)
        outs[unit] = dot(
            vt_ref[h * HEAD_DIM : (h + 1) * HEAD_DIM, c : c + chunk], weights.astype(BF16)
        )
    heads_out = []
    for h in range(heads):
        mine = [(h, c) for c in range(0, count, chunk)]
        top = functools.reduce(jnp.maximum, [tops[u] for u in mine])
        share = [jnp.exp2((tops[u] - top) * (SCALE * LOG2E)) for u in mine]
        total = sum(totals[u] * f for u, f in zip(mine, share))
        out = sum(outs[u] * f for u, f in zip(mine, share))
        heads_out.append(out / total)
        lse_ref[h : h + 1, :] = top * (SCALE * LOG2E) + jnp.log2(total)
    mixed = jnp.concatenate(heads_out, axis=0).T.astype(BF16)
    steps = pl.num_programs(0)

    @pl.when(step < steps // 2)
    def _():
        own_ref[...] = mixed

    @pl.when(step >= steps // 2)
    def _():
        sib_ref[...] = mixed


def attend(queries, keys, values):
    rows, width = queries.shape
    block = min(256, rows // 2)
    steps = rows // block
    heads = width // HEAD_DIM
    half_blocks = steps // 2
    return pl.pallas_call(
        functools.partial(attend_kernel, min(512, keys.shape[0])),
        grid=(steps,),
        in_specs=[
            pl.BlockSpec((block, width), lambda i: (i, 0)),
            pl.BlockSpec(keys.shape, lambda i: (0, 0)),
            pl.BlockSpec(values.shape, lambda i: (0, 0)),
        ],
        out_specs=[
            pl.BlockSpec((block, width), lambda i: (jnp.minimum(i, half_blocks - 1), 0)),
            pl.BlockSpec((block, width), lambda i: (jnp.maximum(i - half_blocks, 0), 0)),
            pl.BlockSpec((heads, block), lambda i: (0, i)),
        ],
        out_shape=[
            shape((rows // 2, width), BF16),
            shape((rows // 2, width), BF16),
            shape((heads, rows), F32),
        ],
        scratch_shapes=[pltpu.VMEM((width, keys.shape[0]), BF16)],
        compiler_params=pltpu.CompilerParams(vmem_limit_bytes=12 * MEGA),
        cost_estimate=cost("attend"),
        name="attend",
    )(queries, keys, values)


def attend_back_kernel(
    part, q_ref, k_ref, v_ref, o0_ref, o1_ref, g0_ref, g1_ref, lse_ref,
    dq_ref, dkv_ref, kt_ref, dk_acc, dv_acc, o_ref, g_ref,
):
    width = q_ref.shape[1]
    heads = width // HEAD_DIM
    step = pl.program_id(0)
    steps = pl.num_programs(0)

    @pl.when(step == 0)
    def _():
        kt_ref[...] = k_ref[...].T
        dk_acc[...] = jnp.zeros_like(dk_acc)
        dv_acc[...] = jnp.zeros_like(dv_acc)

    @pl.when(step < steps // 2)
    def _():
        o_ref[...] = o0_ref[...]
        g_ref[...] = g0_ref[...]

    @pl.when(step >= steps // 2)
    def _():
        o_ref[...] = o1_ref[...]
        g_ref[...] = g1_ref[...]

    queries = q_ref[...]
    grads = g_ref[...]
    masks = head_masks(width)
    product = (o_ref[...].astype(F32) * grads.astype(F32)).T
    outs, probs, gscores, qms, gms = [], [], [], [], []
    for h in range(heads):
        qm = queries * masks[h]
        gm = grads * masks[h]
        delta = jnp.sum(product[h * HEAD_DIM : (h + 1) * HEAD_DIM, :], axis=0, keepdims=True)
        scores = dot(k_ref[...], qm, NT)
        row = part * heads + h
        prob = jnp.exp2(scores * (SCALE * LOG2E) - lse_ref[row : row + 1, :])
        grad_prob = dot(v_ref[...], gm, NT)
        gscore = (prob * (grad_prob - delta)).astype(BF16)
        outs.append(dot(kt_ref[h * HEAD_DIM : (h + 1) * HEAD_DIM, :], gscore))
        probs.append(prob.astype(BF16))
        gscores.append(gscore)
        qms.append(qm)
        gms.append(gm)
    dv_acc[...] += dot(jnp.concatenate(probs, axis=1), jnp.concatenate(gms, axis=0))
    dk_acc[...] += dot(jnp.concatenate(gscores, axis=1), jnp.concatenate(qms, axis=0))
    dq_ref[...] = (jnp.concatenate(outs, axis=0).T * SCALE).astype(BF16)

    @pl.when(step == steps - 1)
    def _():
        dkv_ref[:, :width] = (dk_acc[...] * SCALE).astype(BF16)
        dkv_ref[:, width:] = dv_acc[...].astype(BF16)


def attend_back(queries, keys, values, mixed, grads, lse, part):
    rows, both = queries.shape
    count = keys.shape[0]
    width = both // 2
    block = min(256, rows // 2)
    half_blocks = rows // 2 // block
    row_spec = pl.BlockSpec((block, width), lambda i: (i, part))
    own_spec = pl.BlockSpec((block, width), lambda i: (jnp.minimum(i, half_blocks - 1), part))
    sib_spec = pl.BlockSpec((block, width), lambda i: (jnp.maximum(i - half_blocks, 0), part))
    full_spec = pl.BlockSpec((count, width), lambda i: (0, part))
    lse_spec = pl.BlockSpec((lse.shape[0], block), lambda i: (0, i))
    return pl.pallas_call(
        functools.partial(attend_back_kernel, part),
        grid=(rows // block,),
        in_specs=[row_spec, full_spec, full_spec] + [own_spec, sib_spec] * 2 + [lse_spec],
        out_specs=[
            pl.BlockSpec((block, width), lambda i: (i, 0)),
            pl.BlockSpec((count, both), lambda i: (0, 0)),
        ],
        out_shape=[shape((rows, width), BF16), shape((count, both), BF16)],
        scratch_shapes=[
            pltpu.VMEM((width, count), BF16),
            pltpu.VMEM((count, width), F32),
            pltpu.VMEM((count, width), F32),
            pltpu.VMEM((block, width), BF16),
            pltpu.VMEM((block, width), BF16),
        ],
        compiler_params=pltpu.CompilerParams(vmem_limit_bytes=12 * MEGA),
        cost_estimate=cost("attend_back"),
        name="attend_back",
    )(queries, keys, values, *mixed, *grads, lse)


def ring_rows(count, deep):
    size = deep // count
    rank = lax.axis_index("fsdp")
    return [tile(lax.rem(rank + s, count), size) if count > 1 else tile(0, size) for s in range(count)]


def project_kernel(count, *refs):
    blocks, refs = refs[:8], refs[8:]
    mine, refs = refs[:count], refs[count:]
    other, refs = refs[:count], refs[count:]
    bias_ref, xt_ref, w_ref, q_ref, k_ref, v_ref, x_ref, sems = refs
    rows = blocks[0].shape[0]
    deep = x_ref.shape[1]
    part = mine[0].shape[2]
    width = 2 * part
    pairs = []
    for at, low, high in zip(ring_rows(count, deep), mine, other):
        for j in range(3):
            pairs.append((low.at[j], w_ref.at[at, j * width : j * width + part]))
            pairs.append((high.at[j], w_ref.at[at, j * width + part : (j + 1) * width]))
    weights = len(pairs)
    for i in range(8):
        pairs.append((blocks[i], x_ref.at[i * rows : (i + 1) * rows, :]))
    copies = start_all(pairs, sems)
    for copy in copies[:weights]:
        copy.wait()
    for i in range(4):
        at = slice(i * 2 * rows, (i + 1) * 2 * rows)
        for copy in copies[weights + 2 * i : weights + 2 * i + 2]:
            copy.wait()
        x = x_ref[at, :]
        if i < 2:
            out = dot(x, w_ref[...])
            q_ref[at, :] = (out[:, :width] + bias_ref[0:1, :]).astype(BF16)
            out = out[:, width:]
        else:
            out = dot(x, w_ref[:, width:])
        k_ref[at, :] = out[:, :width].astype(BF16)
        v_ref[at, :] = (out[:, width:] + bias_ref[1:2, :]).astype(BF16)
        xt_ref[:, at] = x.T


def project(blocks, mine, other, biases):
    rows, deep = blocks[0].shape
    width = biases.shape[1]
    out = [
        shape((deep, 8 * rows), BF16),
        shape((deep, 3 * width), BF16),
        shape((4 * rows, width), BF16),
        shape((8 * rows, width), BF16),
        shape((8 * rows, width), BF16),
    ]
    scratch = [pltpu.VMEM((8 * rows, deep), BF16)]
    kernel = functools.partial(project_kernel, len(mine))
    args = [*blocks, *mine, *other]
    return call_whole(kernel, "project", out, args, [biases], scratch, 8 + 6 * len(mine))


def split_store(out, near_ref, far_ref, at):
    rows = near_ref.shape[0]
    near_ref[:, at] = out[:rows]
    far_ref[:, at] = out[rows:].astype(BF16)


def out_kernel(w0, w1, own, sib, w_ref, near_ref, far_ref, sems):
    width = own.shape[1]
    deep = w_ref.shape[0]
    pairs = [(w0.at[0], w_ref.at[:, :width]), (w1.at[0], w_ref.at[:, width:])]
    for copy in start_all(pairs, sems):
        copy.wait()
    for c in range(4):
        at = slice(c * deep // 4, (c + 1) * deep // 4)
        out = dot(own[...], w_ref[at, :width], NT) + dot(sib[...], w_ref[at, width:], NT)
        split_store(out, near_ref, far_ref, at)


def out_project(own, sib, pieces):
    pair, width = own.shape
    deep = pieces[0].shape[1]
    out = [
        shape((deep, 2 * width), BF16),
        shape((pair // 2, deep), F32),
        shape((pair // 2, deep), BF16),
    ]
    return call_whole(out_kernel, "out_project", out, pieces, [own, sib], copies=2)


def out_back_kernel(g0, g1, w_ref, gt_ref, own_ref, sib_ref):
    rows = g0.shape[0]
    width = own_ref.shape[1]
    for i, ref in enumerate((g0, g1)):
        at = slice(i * rows, (i + 1) * rows)
        g = ref[...]
        out = dot(g, w_ref[...])
        own_ref[at, :] = out[:, :width].astype(BF16)
        sib_ref[at, :] = out[:, width:].astype(BF16)
        gt_ref[:, at] = g.T


def out_back(g0, g1, weights):
    rows, deep = g0.shape
    width = weights.shape[1] // 2
    out = [
        shape((deep, 2 * rows), BF16),
        shape((2 * rows, width), BF16),
        shape((2 * rows, width), BF16),
    ]
    return call_whole(out_back_kernel, "out_back", out, [], [g0, g1, weights])


EXTRA = 16


def pack_rows(out_ref, one, two, q0, q1, kv0, kv1, hidden):
    rank = lax.axis_index("tp")
    size = lax.axis_size("tp")
    first = lax.axis_index("ctx") == 0
    part = q0.shape[1]
    units = hidden.shape[1] // 2
    out_ref[...] = jnp.zeros_like(out_ref)
    out_ref[0:2, :] = one[0:2, :]
    out_ref[2:4, :] = two[0:2, :]
    out_ref[4:5, :] = one[2:3, :]
    out_ref[5:6, :] = two[2:3, :]
    for row, (mine, other, at) in ((6, (q0, q1, 0)), (7, (kv0, kv1, part))):
        mine = col_sum(mine[:, at : at + part].astype(F32))
        other = col_sum(other[:, at : at + part].astype(F32))
        low, high = jnp.where(first, mine, other), jnp.where(first, other, mine)
        for t in range(size):
            keep = rank == t
            start = 2 * t * part
            out_ref[row : row + 1, start : start + part] = jnp.where(keep, low, 0.0)
            out_ref[row : row + 1, start + part : start + 2 * part] = jnp.where(keep, high, 0.0)
    for t in range(size):
        row = 8 + t
        total = jnp.where(rank == t, hidden[:, :units], 0.0)
        total = total + jnp.where((rank ^ 1) == t, hidden[:, units:], 0.0)
        mine, other = total[:, : units // 2], total[:, units // 2 :]
        out_ref[row : row + 1, : units // 2] = jnp.where(first, mine, other)
        out_ref[row : row + 1, units // 2 :] = jnp.where(first, other, mine)


def input_back_kernel(
    q0, q1, kv0, kv1, w_ref, one, two, hidden, near_ref, far_ref, sib_ref, cat_ref, vec_ref
):
    half, part = q0.shape
    pair, deep = near_ref.shape
    for j, (ref, at) in enumerate(((q0, 0), (q1, 0), (kv0, 0), (kv1, 0), (kv0, part), (kv1, part))):
        count = ref.shape[0]
        cat_ref[:count, j * part : (j + 1) * part] = ref[:, at : at + part]
    sib_ref[:pair, :] = dot(cat_ref[pair:half, :], w_ref[...], NT).astype(BF16)
    out = dot(cat_ref[half + pair :, 2 * part :], w_ref[:, 2 * part :], NT)
    sib_ref[pair:half, :] = out.astype(BF16)
    near_ref[...] = dot(cat_ref[:pair, :], w_ref[...], NT)
    far_ref[...] = dot(cat_ref[half : half + pair, 2 * part :], w_ref[:, 2 * part :], NT)
    pack_rows(vec_ref, one, two, q0, q1, kv0, kv1, hidden)
    sib_ref[half:, :] = vec_ref[...].astype(BF16)


def input_back(q0, q1, kv0, kv1, weights, one, two, hidden):
    half, part = q0.shape
    deep = weights.shape[0]
    pair = half // 2
    out = [shape((pair, deep), F32), shape((pair, deep), F32), shape((half + EXTRA, deep), BF16)]
    scratch = [pltpu.VMEM((kv0.shape[0], 6 * part), BF16), pltpu.VMEM((EXTRA, deep), F32)]
    args = [q0, q1, kv0, kv1, weights, one, two, hidden]
    return call_whole(input_back_kernel, "input_back", out, [], args, scratch)


def fold_kernel(near, far, sent, recv, rest, own_ref, x_ref, y_ref, d_ref, vec_ref):
    rows = own_ref.shape[0]
    pair = 2 * rows
    own_ref[...] = rest[...] + near[:rows, :] + recv[:rows, :].astype(F32)
    vec = sent[2 * pair :, :].astype(F32) + recv[2 * pair :, :].astype(F32)
    vec_ref[...] = vec.astype(BF16)
    for ref, term, at in ((x_ref, near, rows), (y_ref, far, 0), (d_ref, far, rows)):
        start = at if term is near else pair + at
        total = term[at : at + rows, :] + recv[start : start + rows, :].astype(F32)
        ref[:rows, :] = total.astype(BF16)
        ref[rows:, :] = vec.astype(BF16)


def fold(near, far, sent, recv, rest):
    rows, deep = rest.shape
    out = [shape((rows, deep), F32)] + [shape((rows + EXTRA, deep), BF16)] * 3
    out += [shape((EXTRA, deep), BF16)]
    return call_whole(fold_kernel, "fold", out, [], [near, far, sent, recv, rest])


def grad_send_kernel(left, right, out_ref):
    out_ref[...] = dot(left[...], right[...]).astype(BF16)


def grad_send(left, right):
    out = [shape((left.shape[0], right.shape[1]), BF16)]
    return call_whole(grad_send_kernel, "grad_send", out, [], [left, right])[0]


def grad_sum_kernel(left, right, recv, keep_ref, send_ref):
    part = keep_ref.shape[1]
    for ref, at in ((send_ref, slice(part, 2 * part)), (keep_ref, slice(0, part))):
        ref[...] = (dot(left[...], right[:, at]) + recv[:, at].astype(F32)).astype(BF16)


def grad_sum(left, right, recv):
    half = shape((left.shape[0], right.shape[1] // 2), BF16)
    return call_whole(grad_sum_kernel, "grad_sum", [half, half], [], [left, right, recv])


def head_grads(left, query, pair):
    half = query.shape[0]
    return jnp.concatenate([dot(left[:, :half], query[...]), dot(left[...], pair[...])], axis=1)


def head_send_kernel(left, query, pair, out_ref):
    out_ref[...] = head_grads(left, query, pair).astype(BF16)


def head_send(left, query, pair):
    out = [shape((left.shape[0], query.shape[1] + pair.shape[1]), BF16)]
    return call_whole(head_send_kernel, "head_send", out, [], [left, query, pair])[0]


def head_sum_kernel(left, query, pair, recv, keep, keep_recv, out_ref):
    width = recv.shape[1]
    total = head_grads(left, query, pair) + recv[...].astype(F32)
    out_ref[:, :width] = total.astype(BF16)
    out_ref[:, width:] = (keep[...].astype(F32) + keep_recv[...].astype(F32)).astype(BF16)


def head_sum(left, query, pair, recv, keep, keep_recv):
    out = [shape((left.shape[0], recv.shape[1] + keep.shape[1]), BF16)]
    args = [left, query, pair, recv, keep, keep_recv]
    return call_whole(head_sum_kernel, "head_sum", out, [], args)[0]


def gelu_pair(values):
    size = jnp.abs(values)
    t = 1.0 / (1.0 + (0.3275911 * math.sqrt(0.5)) * size)
    bell = jnp.exp2(values * values * (-0.5 * LOG2E))
    poly = t * (
        0.5 * 0.254829592
        + t
        * (
            0.5 * -0.284496736
            + t * (0.5 * 1.421413741 + t * (0.5 * -1.453152027 + t * (0.5 * 1.061405429)))
        )
    )
    tail = poly * bell
    cdf = jnp.where(values < 0, tail, 1.0 - tail)
    return values * cdf, cdf + values * bell * (1.0 / math.sqrt(2.0 * math.pi))


def gather_units(refs, w_ref):
    pairs = []
    part = refs[0][0].shape[2]
    for ref, first in refs:
        for j in range(first, ref.shape[0]):
            at = len(pairs) * part
            pairs.append((ref.at[j], w_ref.at[:, at : at + part]))
    return pairs


def up_kernel(
    x0, x1, mine, other, mine_sib, other_sib, bias_ref,
    xt_ref, w_ref, act_own, act_sib, slope_own, slope_sib, x_ref, sems,
):
    rows = x0.shape[0]
    pairs = [(x0, x_ref.at[:rows, :]), (x1, x_ref.at[rows:, :])]
    pairs += gather_units(((mine, 1), (other, 0), (mine_sib, 1), (other_sib, 0)), w_ref)
    copies = start_all(pairs, sems)
    copies[0].wait()
    copies[1].wait()
    units = act_own.shape[1]
    step = mine.shape[2]

    def matmul(c):
        copies[2 + c].wait()
        return dot(x_ref[...], w_ref[:, c * step : (c + 1) * step])

    following = matmul(0)
    for c in range(8):
        pre = following
        if c < 7:
            following = matmul(c + 1)
        act_ref, slope_ref = ((act_own, slope_own), (act_sib, slope_sib))[c // 4]
        at = slice((c % 4) * step, (c % 4 + 1) * step)
        act, slope = gelu_pair(pre + bias_ref[0:1, c * step : (c + 1) * step])
        act_ref[:, at] = act.astype(BF16)
        slope_ref[:, at] = slope.astype(BF16)
    xt_ref[...] = x_ref[...].T


def feed_up(x0, x1, pieces, bias):
    rows, deep = x0.shape
    units = bias.shape[1]
    out = [shape((deep, 2 * rows), BF16), shape((deep, units), BF16)]
    out += [shape((2 * rows, units // 2), BF16)] * 4
    scratch = [pltpu.VMEM((2 * rows, deep), BF16)]
    return call_whole(up_kernel, "feed_up", out, [x0, x1, *pieces], [bias], scratch, 10)


def down_kernel(spots, *refs):
    count = len(spots)
    own, sib, refs = refs[:count], refs[count : 2 * count], refs[2 * count :]
    act_own, act_sib, w_ref, near_ref, far_ref, sems = refs
    deep = near_ref.shape[1]
    units = act_own.shape[1]
    pairs = []
    rows = ring_rows(deep // own[0].shape[0], deep)
    for (piece, start), left, right in zip(spots, own, sib):
        width = left.shape[1]
        pairs.append((left, w_ref.at[rows[piece], start : start + width]))
        pairs.append((right, w_ref.at[rows[piece], units + start : units + start + width]))
    for copy in start_all(pairs, sems):
        copy.wait()
    for c in range(4):
        at = slice(c * deep // 4, (c + 1) * deep // 4)
        out = dot(act_own[...], w_ref[at, :units], NT) + dot(act_sib[...], w_ref[at, units:], NT)
        split_store(out, near_ref, far_ref, at)


def feed_down(act_own, act_sib, spots, own, sib):
    pair, units = act_own.shape
    deep = D
    out = [
        shape((deep, 2 * units), BF16),
        shape((pair // 2, deep), F32),
        shape((pair // 2, deep), BF16),
    ]
    kernel = functools.partial(down_kernel, spots)
    args = [*own, *sib]
    return call_whole(
        kernel, "feed_down", out, args, [act_own, act_sib], copies=2 * len(own)
    )


def feed_back_kernel(
    g0, g1, slope_own, slope_sib, up_ref, down_ref,
    gt_ref, gup_own, gup_sib, bias_ref, near_ref, far_ref, g_ref,
):
    rows, deep = g0.shape
    g_ref[:rows, :] = g0[...]
    g_ref[rows:, :] = g1[...]
    units = gup_own.shape[1]
    step = units // 2
    for c in range(4):
        slope_ref, gup_ref = ((slope_own, gup_own), (slope_sib, gup_sib))[c // 2]
        at = slice((c % 2) * step, (c % 2 + 1) * step)
        grad = dot(g_ref[...], down_ref[:, c * step : (c + 1) * step])
        grad = (grad * slope_ref[:, at].astype(F32)).astype(BF16)
        gup_ref[:, at] = grad
        bias_ref[0:1, c * step : (c + 1) * step] = jnp.sum(
            grad.astype(F32), axis=0, keepdims=True
        )
    for c in range(4):
        at = slice(c * deep // 4, (c + 1) * deep // 4)
        out = dot(gup_own[...], up_ref[at, :units], NT) + dot(gup_sib[...], up_ref[at, units:], NT)
        split_store(out, near_ref, far_ref, at)
    gt_ref[...] = g_ref[...].T


def feed_back(g0, g1, slope_own, slope_sib, up_all, down_all):
    rows, deep = g0.shape
    units = slope_own.shape[1]
    out = [shape((deep, 2 * rows), BF16)]
    out += [shape((2 * rows, units), BF16)] * 2
    out += [shape((1, 2 * units), F32), shape((rows, deep), F32), shape((rows, deep), BF16)]
    args = [g0, g1, slope_own, slope_sib, up_all, down_all]
    scratch = [pltpu.VMEM((2 * rows, deep), BF16)]
    return call_whole(feed_back_kernel, "feed_back", out, [], args, scratch)


def row_mean(values):
    return jnp.mean(values, axis=-1, keepdims=True)


def col_sum(values):
    return jnp.sum(values, axis=0, keepdims=True)


def normalize(values):
    centered = values - row_mean(values)
    inverse = lax.rsqrt(row_mean(centered * centered) + NORM_EPSILON)
    return centered * inverse, inverse


def norm_back(grad_out, normed, inverse, gain):
    grad = grad_out * gain
    return inverse * (grad - row_mean(grad) - normed * row_mean(grad * normed))


def norm_one_kernel(own, part, recv, vec, first_ref, low_ref, normed_ref, inverse_ref):
    attn_out = part[...] + recv[...].astype(F32) + vec[4:5, :]
    normed, inverse = normalize(own[...].astype(F32) + attn_out)
    first = normed * vec[0:1, :] + vec[1:2, :]
    first_ref[...] = first
    low_ref[...] = first.astype(BF16)
    normed_ref[...] = normed
    inverse_ref[...] = inverse


def norm_one(own, part, recv, vec):
    rows, deep = own.shape
    out = [shape((rows, deep), t) for t in (F32, BF16, F32)] + [shape((rows, 1), F32)]
    return call_whole(norm_one_kernel, "norm_one", out, [], [own, part, recv, vec])


def norm_two_kernel(first, part, recv, cotangent, vec, out_ref, grad_ref, low_ref, sums_ref):
    down_out = part[...] + recv[...].astype(F32) + vec[5:6, :]
    normed, inverse = normalize(first[...] + down_out)
    out_ref[...] = (normed * vec[2:3, :] + vec[3:4, :]).astype(BF16)
    given = cotangent[...].astype(F32)
    grad = norm_back(given, normed, inverse, vec[2:3, :])
    grad_ref[...] = grad
    low = grad.astype(BF16)
    low_ref[...] = low
    sums_ref[0:1, :] = col_sum(given * normed)
    sums_ref[1:2, :] = col_sum(given)
    sums_ref[2:3, :] = col_sum(low.astype(F32))


def norm_two(first, part, recv, cotangent, vec):
    rows, deep = first.shape
    out = [shape((rows, deep), t) for t in (BF16, F32, BF16)] + [shape((3, deep), F32)]
    return call_whole(norm_two_kernel, "norm_two", out, [], [first, part, recv, cotangent, vec])


def norm_one_back_kernel(
    grad_second, part, recv, normed, inverse, vec, grad_ref, low_ref, sums_ref
):
    given = grad_second[...] + part[...] + recv[...].astype(F32)
    grad = norm_back(given, normed[...], inverse[...], vec[0:1, :])
    grad_ref[...] = grad
    low = grad.astype(BF16)
    low_ref[...] = low
    sums_ref[0:1, :] = col_sum(given * normed[...])
    sums_ref[1:2, :] = col_sum(given)
    sums_ref[2:3, :] = col_sum(low.astype(F32))


def norm_one_back(grad_second, part, recv, normed, inverse, vec):
    rows, deep = part.shape
    out = [shape((rows, deep), t) for t in (F32, BF16)] + [shape((3, deep), F32)]
    args = [grad_second, part, recv, normed, inverse, vec]
    return call_whole(norm_one_back_kernel, "norm_one_back", out, [], args)


def nesterov(weights, momentum, average, gradient, step_rate):
    momentum_new = MOMENTUM * momentum + gradient
    weight_new = weights - step_rate * (gradient + MOMENTUM * momentum_new)
    return (weight_new, momentum_new, AVERAGE * average + (1.0 - AVERAGE) * weight_new)


def swap_tp(values, bit):
    size = lax.axis_size("tp")
    return lax.ppermute(values, "tp", [(i, i ^ bit) for i in range(size)])


def core(values):
    return swap_tp(values, 1)


def across(values):
    return swap_tp(values, 2)


def swap_ctx(values):
    return lax.ppermute(values, "ctx", [(0, 1), (1, 0)])


def swap_both(values):
    size = lax.axis_size("tp")
    return lax.ppermute(values, ("ctx", "tp"), [(i, i ^ (size + 2)) for i in range(2 * size)])


def sum_fsdp(values):
    size = lax.axis_size("fsdp")

    def swap(values, bit):
        return lax.ppermute(values, "fsdp", [(i, i ^ bit) for i in range(size)])

    if size == 4:
        one, two, three = (swap(values, bit) for bit in (1, 2, 3))
        return (values + one) + (two + three)
    bit = 1
    while bit < size:
        values = values + swap(values, bit)
        bit *= 2
    return values


def gather_fsdp(shard, axis):
    return lax.all_gather(shard, "fsdp", axis=axis, tiled=True)


def ring():
    return lax.axis_size("fsdp") == 4


def shift_fsdp(values, step):
    size = lax.axis_size("fsdp")
    return lax.ppermute(values, "fsdp", [(i, (i + step) % size) for i in range(size)])


def gather_pieces(shard, axis):
    if not ring():
        return [gather_fsdp(shard, axis)]
    return [shard] + [shift_fsdp(shard, -s) for s in range(1, lax.axis_size("fsdp"))]


def scatter_fsdp(grads, axis):
    return lax.psum_scatter(grads, "fsdp", scatter_dimension=axis, tiled=True)


def halves(values, axis=-1):
    low, high = jnp.split(values, 2, axis=axis)
    first = lax.axis_index("ctx") == 0
    return jnp.where(first, low, high), jnp.where(first, high, low)


def join(mine, other, axis=-1):
    first = lax.axis_index("ctx") == 0
    low, high = jnp.where(first, mine, other), jnp.where(first, other, mine)
    return jnp.concatenate([low, high], axis=axis)


def quarters(mine):
    return jnp.stack(jnp.split(mine, 2, axis=1))


def after(values, *others):
    return lax.optimization_barrier((values,) + others)[0]


def on_device(
    tokens,
    cotangent,
    attn_weight,
    attn_momentum,
    attn_average,
    ffn_weight,
    ffn_momentum,
    ffn_average,
    vector_weight,
    vector_momentum,
    vector_average,
):
    tp_rank = lax.axis_index("tp")
    sib_rank = tp_rank ^ 1
    head_width = attn_weight.shape[2]
    unit_width = ffn_weight.shape[2]
    token_count = LEN * lax.axis_size("fsdp")
    matrix_rate = MATRIX_RATE / math.sqrt(token_count)
    vector_rate = VECTOR_RATE / math.sqrt(token_count)

    attn_low, attn_high = halves(attn_weight.astype(BF16))
    qkv_mine = gather_pieces(attn_low[:3], 1)

    own = tokens[0]
    rows = own.shape[0]
    pair = 2 * rows
    half = 4 * rows
    beside = across(own)
    facing = swap_ctx(own)
    diagonal = swap_both(own)
    if ring():
        others = swap_ctx(after(jnp.stack(qkv_mine[1:]), beside, facing))
        qkv_other = [attn_high[:3]] + [others[s] for s in range(len(qkv_mine) - 1)]
    else:
        qkv_other = [swap_ctx(qkv_mine[0])]
    up_low = quarters(halves(ffn_weight[0].astype(BF16))[0])
    out_low = jnp.concatenate([attn_low[3], attn_high[3]], axis=1)
    out_up_low = jnp.concatenate([out_low[None], up_low])
    out_up = gather_fsdp(after(out_up_low, *qkv_mine[-3:], beside, facing), 1)
    blocks = [own, beside, core(own), core(beside), facing, diagonal, core(facing), core(diagonal)]

    vec = vector_weight[: 6 * D].reshape(6, D)

    def columns(start, width):
        part = lax.dynamic_slice_in_dim(vector_weight, start, width)
        return jnp.concatenate(halves(part))

    biases = jnp.stack(
        [
            columns(6 * D + tp_rank * head_width, head_width),
            columns(7 * D + tp_rank * head_width, head_width),
        ]
    )
    bias_hidden = jnp.concatenate(
        [
            columns(8 * D + tp_rank * unit_width, unit_width),
            columns(8 * D + sib_rank * unit_width, unit_width),
        ]
    )[None]

    token_t, qkv_w, queries, keys, values = project(blocks, qkv_mine, qkv_other, biases)
    down_low = jnp.concatenate(halves(ffn_weight[1].astype(BF16)), axis=1)
    mixed_own, mixed_sib, lse = attend(queries, keys, values)
    down_low = after(down_low, mixed_own)
    if ring():
        low, high = jnp.split(down_low, 2, axis=1)
        spots = ((0, 0), (1, 0), (3, 0), (2, 0), (2, low.shape[1]))
        down_w = [down_low, shift_fsdp(down_low, -1), shift_fsdp(down_low, -3)]
        down_w += [shift_fsdp(low, -2), shift_fsdp(high, -2)]
    else:
        spots = ((0, 0),)
        down_w = [gather_fsdp(down_low, 0)]
    mixed_recv = core(mixed_sib)
    out_up = after(out_up, mixed_own)
    out_up_sib = core(out_up)
    up_other = swap_ctx(out_up[1:])
    out_w, attn_part, attn_far = out_project(mixed_own, mixed_recv, [out_up, out_up_sib])
    attn_recv = across(attn_far)
    if ring():
        attn_recv = after(attn_recv, down_w[1], down_w[2])
    first, first_low, normed_one, inverse_one = norm_one(own, attn_part, attn_recv, vec)
    first_beside = across(first_low)

    if ring():
        first_beside = after(first_beside, down_w[3])
    up_other = after(up_other, first_beside)
    first_t, up_all, hidden_own, hidden_sib, slope_own, slope_sib = feed_up(
        first_low, first_beside, [out_up, up_other, out_up_sib, core(up_other)], bias_hidden
    )
    if ring():
        down_w[4] = after(down_w[4], hidden_own)
    down_all, down_part, down_far = feed_down(
        hidden_own, hidden_sib, spots, down_w, [core(w) for w in down_w]
    )
    layer_out, grad_second, grad_down, sums_two = norm_two(
        first, down_part, across(down_far), cotangent[0], vec
    )
    grad_down_t, grad_up_own, grad_up_sib, grad_bias_hidden, first_part, first_far = feed_back(
        grad_down, across(grad_down), slope_own, slope_sib, up_all, down_all
    )
    down_sib = grad_send(grad_down_t, hidden_sib)
    up_sib = grad_send(first_t, grad_up_sib)
    first_recv = after(across(first_far), down_sib, up_sib)
    grad_res, grad_attn, sums_one = norm_one_back(
        grad_second, first_part, first_recv, normed_one, inverse_one, vec
    )
    grad_attn_beside = across(grad_attn)
    down_mine, down_rest = grad_sum(grad_down_t, hidden_own, after(core(down_sib), grad_attn))
    up_keep, up_send = grad_sum(first_t, grad_up_own, after(core(up_sib), grad_attn))

    def finish(mine):
        return join(mine, swap_ctx(mine)).astype(F32)

    mine_owned = scatter_fsdp(down_mine, 0)
    rest_owned = scatter_fsdp(down_rest, 0)
    up_recv = swap_ctx(up_send)

    grad_attn_beside = after(grad_attn_beside, down_mine, up_send)
    grad_attn_t, grad_mixed_own, grad_mixed_sib = out_back(grad_attn, grad_attn_beside, out_w)
    grad_mixed = (grad_mixed_own, core(grad_mixed_sib))

    up_recv = after(up_recv, grad_mixed_sib)
    up_sum = (up_keep.astype(F32) + up_recv.astype(F32)).astype(BF16)
    up_owned = scatter_fsdp(up_sum, 0)
    mixed = (mixed_own, mixed_sib)
    heads = (queries, keys, values, mixed)
    query_other, kv_other = attend_back(*heads, grad_mixed, lse, 1)
    send = head_send(token_t, query_other, kv_other)
    out_sib = grad_send(after(grad_attn_t, query_other), mixed_recv)
    out_keep, out_send = grad_sum(grad_attn_t, mixed_own, core(out_sib))
    grad_mixed = (grad_mixed[0], after(grad_mixed[1], up_sum, send, out_send, mine_owned))
    recv = swap_ctx(send)
    query_mine, kv_mine = attend_back(*heads, grad_mixed, lse, 0)
    part = head_width // 2
    near, far, sibling = input_back(
        query_mine, query_other, kv_mine, kv_other, qkv_w, sums_one, sums_two, grad_bias_hidden
    )
    sib_recv = core(sibling)
    qkvo_sum = head_sum(token_t, query_mine, after(kv_mine, rest_owned), recv, out_keep, swap_ctx(out_send))
    qkvo_mine = scatter_fsdp(qkvo_sum, 0)
    sib_recv = after(sib_recv, qkvo_sum, up_owned)
    input_part, to_x, to_y, to_d, vec_part = fold(near, far, sibling, sib_recv, grad_res)
    from_x, from_y, from_d = across(to_x), swap_ctx(to_y), swap_both(to_d)
    mine_recv, rest_recv = swap_ctx(after(mine_owned, to_y)), swap_ctx(after(rest_owned, from_y))
    down_grad = join(
        mine_owned.astype(F32) + rest_recv.astype(F32),
        rest_owned.astype(F32) + mine_recv.astype(F32),
    )
    up_grad = finish(after(up_owned, to_y))
    ffn_grad = jnp.stack([up_grad, down_grad])
    ffn_new, ffn_momentum_new, ffn_average_new = nesterov(
        ffn_weight, ffn_momentum, ffn_average, ffn_grad, matrix_rate
    )
    input_grad = input_part
    for term in (from_x, from_y, from_d):
        input_grad = input_grad + term[:rows].astype(F32)
    vec_x, vec_y, vec_d = (term[rows:].astype(F32) for term in (from_x, from_y, from_d))
    vec_plane = (vec_part.astype(F32) + vec_x) + (vec_y + vec_d)

    qkvo_mine = after(qkvo_mine, from_x, from_y, from_d)
    qkvo_other = swap_ctx(qkvo_mine)
    vector_grad = sum_fsdp(vec_plane[:12]).reshape(-1)
    attn_grad = jnp.stack(
        [
            join(qkvo_mine[:, j * part : (j + 1) * part], qkvo_other[:, j * part : (j + 1) * part])
            for j in range(4)
        ]
    ).astype(F32)
    vector_new, vector_momentum_new, vector_average_new = nesterov(
        vector_weight, vector_momentum, vector_average, vector_grad, vector_rate
    )
    attn_new, attn_momentum_new, attn_average_new = nesterov(
        attn_weight, attn_momentum, attn_average, attn_grad, matrix_rate
    )
    return (
        layer_out[None],
        input_grad[None],
        attn_grad,
        attn_new,
        attn_momentum_new,
        attn_average_new,
        attn_new.astype(BF16),
        ffn_grad,
        ffn_new,
        ffn_momentum_new,
        ffn_average_new,
        ffn_new.astype(BF16),
        vector_grad,
        vector_new,
        vector_momentum_new,
        vector_average_new,
    )


def solution(mesh):
    rows = P("fsdp", ("ctx", "tp"), None)
    weight = P(None, "fsdp", "tp")
    return jax.shard_map(
        on_device,
        mesh=mesh,
        in_specs=(rows, rows) + (weight,) * 6 + (P(),) * 3,
        out_specs=(rows, rows) + (weight,) * 10 + (P(),) * 4,
        check_vma=False,
    )
```

```python
import functools
import math

import jax
import jax.numpy as jnp
from jax import lax
from jax.experimental import pallas as pl
from jax.experimental.pallas import tpu as pltpu
from jax.sharding import PartitionSpec as P

D = 1024
FF = 4096
HEAD_DIM = 64
LEN = 2048

NORM_EPSILON = 1e-05
MOMENTUM = 0.5
AVERAGE = 0.5
MATRIX_RATE = 0.1
VECTOR_RATE = 0.3

SCALE = HEAD_DIM ** (-0.5)
LOG2E = math.log2(math.e)
F32 = jnp.float32
BF16 = jnp.bfloat16
NT = (((1,), (1,)), ((), ()))
TN = (((0,), (0,)), ((), ()))
NN = (((1,), (0,)), ((), ()))


def dot(left, right, dims=NN):
    return lax.dot_general(left, right, dims, preferred_element_type=F32)


VMEM = pl.BlockSpec(memory_space=pltpu.VMEM)
ANY = pl.BlockSpec(memory_space=pl.ANY)
MEGA = 1024 * 1024
WORK_UNIT = 1.2e10


WORK = {
    "project": 0.001,
    "attend": 0.001,
    "out_project": 0.001,
    "norm_one": 1.5,
    "feed_up": 8,
    "feed_down": 4,
    "norm_two": 2,
    "feed_back": 8,
    "grad_send": 10,
    "grad_sum": 3,
    "norm_one_back": 2,
    "out_back": 2,
    "attend_back": 12,
    "head_send": 3,
    "head_sum": 4,
    "input_back": 0.01,
    "fold": 1.5,
    "grad_total": 3,
}


def cost(name):
    flops = int(WORK[name] * WORK_UNIT)
    return pl.CostEstimate(flops=flops, bytes_accessed=1, transcendentals=0)


def shape(dims, dtype):
    return jax.ShapeDtypeStruct(tuple(dims), dtype)


def tile(i, size):
    return pl.ds(pl.multiple_of(i * size, size), size)


def call_whole(kernel, name, out_shape, far_args, near_args, scratch=(), copies=0):
    scratch = list(scratch)
    if copies:
        scratch.append(pltpu.SemaphoreType.DMA((copies,)))
    return pl.pallas_call(
        kernel,
        in_specs=[ANY] * len(far_args) + [VMEM] * len(near_args),
        out_specs=[VMEM] * len(out_shape),
        out_shape=list(out_shape),
        scratch_shapes=scratch,
        compiler_params=pltpu.CompilerParams(vmem_limit_bytes=6 * MEGA),
        cost_estimate=cost(name),
        name=name,
    )(*far_args, *near_args)


def start_all(pairs, sems):
    copies = [pltpu.make_async_copy(src, dst, sems.at[i]) for i, (src, dst) in enumerate(pairs)]
    for copy in copies:
        copy.start()
    return copies


def head_masks(width):
    lane = lax.broadcasted_iota(jnp.int32, (1, width), 1) // HEAD_DIM
    return [(lane == h).astype(BF16) for h in range(width // HEAD_DIM)]


def attend_kernel(chunk, q_ref, k_ref, v_ref, own_ref, sib_ref, lse_ref, vt_ref):
    heads = q_ref.shape[1] // HEAD_DIM
    count = k_ref.shape[0]
    step = pl.program_id(0)

    @pl.when(step == 0)
    def _():
        vt_ref[...] = v_ref[...].T

    queries = q_ref[...]
    masked = [queries * mask for mask in head_masks(q_ref.shape[1])]
    units = [(h, c) for h in range(heads) for c in range(0, count, chunk)]

    def scores_of(unit):
        h, c = unit
        return dot(k_ref[c : c + chunk, :], masked[h], NT)

    tops, totals, outs = {}, {}, {}
    scores = scores_of(units[0])
    for i, unit in enumerate(units):
        current = scores
        if i + 1 < len(units):
            scores = scores_of(units[i + 1])
        h, c = unit
        top = jnp.max(current, axis=0, keepdims=True)
        weights = jnp.exp2((current - top) * (SCALE * LOG2E))
        tops[unit] = top
        totals[unit] = jnp.sum(weights, axis=0, keepdims=True)
        outs[unit] = dot(
            vt_ref[h * HEAD_DIM : (h + 1) * HEAD_DIM, c : c + chunk], weights.astype(BF16)
        )
    heads_out = []
    for h in range(heads):
        mine = [(h, c) for c in range(0, count, chunk)]
        top = functools.reduce(jnp.maximum, [tops[u] for u in mine])
        share = [jnp.exp2((tops[u] - top) * (SCALE * LOG2E)) for u in mine]
        total = sum(totals[u] * f for u, f in zip(mine, share))
        out = sum(outs[u] * f for u, f in zip(mine, share))
        heads_out.append(out / total)
        lse_ref[h : h + 1, :] = top * (SCALE * LOG2E) + jnp.log2(total)
    mixed = jnp.concatenate(heads_out, axis=0).T.astype(BF16)
    steps = pl.num_programs(0)

    @pl.when(step < steps // 2)
    def _():
        own_ref[...] = mixed

    @pl.when(step >= steps // 2)
    def _():
        sib_ref[...] = mixed


def attend(queries, keys, values):
    rows, width = queries.shape
    block = min(256, rows // 2)
    steps = rows // block
    heads = width // HEAD_DIM
    half_blocks = steps // 2
    return pl.pallas_call(
        functools.partial(attend_kernel, min(512, keys.shape[0])),
        grid=(steps,),
        in_specs=[
            pl.BlockSpec((block, width), lambda i: (i, 0)),
            pl.BlockSpec(keys.shape, lambda i: (0, 0)),
            pl.BlockSpec(values.shape, lambda i: (0, 0)),
        ],
        out_specs=[
            pl.BlockSpec((block, width), lambda i: (jnp.minimum(i, half_blocks - 1), 0)),
            pl.BlockSpec((block, width), lambda i: (jnp.maximum(i - half_blocks, 0), 0)),
            pl.BlockSpec((heads, block), lambda i: (0, i)),
        ],
        out_shape=[
            shape((rows // 2, width), BF16),
            shape((rows // 2, width), BF16),
            shape((heads, rows), F32),
        ],
        scratch_shapes=[pltpu.VMEM((width, keys.shape[0]), BF16)],
        compiler_params=pltpu.CompilerParams(vmem_limit_bytes=12 * MEGA),
        cost_estimate=cost("attend"),
        name="attend",
    )(queries, keys, values)


def attend_back_kernel(
    part, q_ref, k_ref, v_ref, o0_ref, o1_ref, g0_ref, g1_ref, lse_ref,
    dq_ref, dkv_ref, kt_ref, dk_acc, dv_acc, o_ref, g_ref,
):
    width = q_ref.shape[1]
    heads = width // HEAD_DIM
    step = pl.program_id(0)
    steps = pl.num_programs(0)

    @pl.when(step == 0)
    def _():
        kt_ref[...] = k_ref[...].T
        dk_acc[...] = jnp.zeros_like(dk_acc)
        dv_acc[...] = jnp.zeros_like(dv_acc)

    @pl.when(step < steps // 2)
    def _():
        o_ref[...] = o0_ref[...]
        g_ref[...] = g0_ref[...]

    @pl.when(step >= steps // 2)
    def _():
        o_ref[...] = o1_ref[...]
        g_ref[...] = g1_ref[...]

    queries = q_ref[...]
    grads = g_ref[...]
    masks = head_masks(width)
    product = (o_ref[...].astype(F32) * grads.astype(F32)).T
    outs, probs, gscores, qms, gms = [], [], [], [], []
    for h in range(heads):
        qm = queries * masks[h]
        gm = grads * masks[h]
        delta = jnp.sum(product[h * HEAD_DIM : (h + 1) * HEAD_DIM, :], axis=0, keepdims=True)
        scores = dot(k_ref[...], qm, NT)
        row = part * heads + h
        prob = jnp.exp2(scores * (SCALE * LOG2E) - lse_ref[row : row + 1, :])
        grad_prob = dot(v_ref[...], gm, NT)
        gscore = (prob * (grad_prob - delta)).astype(BF16)
        outs.append(dot(kt_ref[h * HEAD_DIM : (h + 1) * HEAD_DIM, :], gscore))
        probs.append(prob.astype(BF16))
        gscores.append(gscore)
        qms.append(qm)
        gms.append(gm)
    dv_acc[...] += dot(jnp.concatenate(probs, axis=1), jnp.concatenate(gms, axis=0))
    dk_acc[...] += dot(jnp.concatenate(gscores, axis=1), jnp.concatenate(qms, axis=0))
    dq_ref[...] = (jnp.concatenate(outs, axis=0).T * SCALE).astype(BF16)

    @pl.when(step == steps - 1)
    def _():
        dkv_ref[:, :width] = (dk_acc[...] * SCALE).astype(BF16)
        dkv_ref[:, width:] = dv_acc[...].astype(BF16)


def attend_back(queries, keys, values, mixed, grads, lse, part):
    rows, both = queries.shape
    count = keys.shape[0]
    width = both // 2
    block = min(256, rows // 2)
    half_blocks = rows // 2 // block
    row_spec = pl.BlockSpec((block, width), lambda i: (i, part))
    own_spec = pl.BlockSpec((block, width), lambda i: (jnp.minimum(i, half_blocks - 1), part))
    sib_spec = pl.BlockSpec((block, width), lambda i: (jnp.maximum(i - half_blocks, 0), part))
    full_spec = pl.BlockSpec((count, width), lambda i: (0, part))
    lse_spec = pl.BlockSpec((lse.shape[0], block), lambda i: (0, i))
    return pl.pallas_call(
        functools.partial(attend_back_kernel, part),
        grid=(rows // block,),
        in_specs=[row_spec, full_spec, full_spec] + [own_spec, sib_spec] * 2 + [lse_spec],
        out_specs=[
            pl.BlockSpec((block, width), lambda i: (i, 0)),
            pl.BlockSpec((count, both), lambda i: (0, 0)),
        ],
        out_shape=[shape((rows, width), BF16), shape((count, both), BF16)],
        scratch_shapes=[
            pltpu.VMEM((width, count), BF16),
            pltpu.VMEM((count, width), F32),
            pltpu.VMEM((count, width), F32),
            pltpu.VMEM((block, width), BF16),
            pltpu.VMEM((block, width), BF16),
        ],
        compiler_params=pltpu.CompilerParams(vmem_limit_bytes=12 * MEGA),
        cost_estimate=cost("attend_back"),
        name="attend_back",
    )(queries, keys, values, *mixed, *grads, lse)


def ring_rows(count, deep):
    size = deep // count
    rank = lax.axis_index("fsdp")
    return [tile(lax.rem(rank + s, count), size) if count > 1 else tile(0, size) for s in range(count)]


def project_kernel(count, *refs):
    blocks, refs = refs[:8], refs[8:]
    mine, refs = refs[:count], refs[count:]
    other, refs = refs[:count], refs[count:]
    bias_ref, xt_ref, w_ref, q_ref, k_ref, v_ref, x_ref, sems = refs
    rows = blocks[0].shape[0]
    deep = x_ref.shape[1]
    part = mine[0].shape[2]
    width = 2 * part
    pairs = []
    for at, low, high in zip(ring_rows(count, deep), mine, other):
        for j in range(3):
            pairs.append((low.at[j], w_ref.at[at, j * width : j * width + part]))
            pairs.append((high.at[j], w_ref.at[at, j * width + part : (j + 1) * width]))
    weights = len(pairs)
    for i in range(8):
        pairs.append((blocks[i], x_ref.at[i * rows : (i + 1) * rows, :]))
    copies = start_all(pairs, sems)
    for copy in copies[:weights]:
        copy.wait()
    for i in range(4):
        at = slice(i * 2 * rows, (i + 1) * 2 * rows)
        for copy in copies[weights + 2 * i : weights + 2 * i + 2]:
            copy.wait()
        x = x_ref[at, :]
        if i < 2:
            out = dot(x, w_ref[...])
            q_ref[at, :] = (out[:, :width] + bias_ref[0:1, :]).astype(BF16)
            out = out[:, width:]
        else:
            out = dot(x, w_ref[:, width:])
        k_ref[at, :] = out[:, :width].astype(BF16)
        v_ref[at, :] = (out[:, width:] + bias_ref[1:2, :]).astype(BF16)
        xt_ref[:, at] = x.T


def project(blocks, mine, other, biases):
    rows, deep = blocks[0].shape
    width = biases.shape[1]
    out = [
        shape((deep, 8 * rows), BF16),
        shape((deep, 3 * width), BF16),
        shape((4 * rows, width), BF16),
        shape((8 * rows, width), BF16),
        shape((8 * rows, width), BF16),
    ]
    scratch = [pltpu.VMEM((8 * rows, deep), BF16)]
    kernel = functools.partial(project_kernel, len(mine))
    args = [*blocks, *mine, *other]
    return call_whole(kernel, "project", out, args, [biases], scratch, 8 + 6 * len(mine))


def split_store(out, near_ref, far_ref, at):
    rows = near_ref.shape[0]
    near_ref[:, at] = out[:rows]
    far_ref[:, at] = out[rows:].astype(BF16)


def out_kernel(w0, w1, own, sib, w_ref, near_ref, far_ref, sems):
    width = own.shape[1]
    deep = w_ref.shape[0]
    pairs = [(w0.at[0], w_ref.at[:, :width]), (w1.at[0], w_ref.at[:, width:])]
    for copy in start_all(pairs, sems):
        copy.wait()
    for c in range(4):
        at = slice(c * deep // 4, (c + 1) * deep // 4)
        out = dot(own[...], w_ref[at, :width], NT) + dot(sib[...], w_ref[at, width:], NT)
        split_store(out, near_ref, far_ref, at)


def out_project(own, sib, pieces):
    pair, width = own.shape
    deep = pieces[0].shape[1]
    out = [
        shape((deep, 2 * width), BF16),
        shape((pair // 2, deep), F32),
        shape((pair // 2, deep), BF16),
    ]
    return call_whole(out_kernel, "out_project", out, pieces, [own, sib], copies=2)


def out_back_kernel(g0, g1, w_ref, gt_ref, own_ref, sib_ref):
    rows = g0.shape[0]
    width = own_ref.shape[1]
    for i, ref in enumerate((g0, g1)):
        at = slice(i * rows, (i + 1) * rows)
        g = ref[...]
        out = dot(g, w_ref[...])
        own_ref[at, :] = out[:, :width].astype(BF16)
        sib_ref[at, :] = out[:, width:].astype(BF16)
        gt_ref[:, at] = g.T


def out_back(g0, g1, weights):
    rows, deep = g0.shape
    width = weights.shape[1] // 2
    out = [
        shape((deep, 2 * rows), BF16),
        shape((2 * rows, width), BF16),
        shape((2 * rows, width), BF16),
    ]
    return call_whole(out_back_kernel, "out_back", out, [], [g0, g1, weights])


EXTRA = 16


def pack_rows(out_ref, one, two, q0, q1, kv0, kv1, hidden):
    rank = lax.axis_index("tp")
    size = lax.axis_size("tp")
    first = lax.axis_index("ctx") == 0
    part = q0.shape[1]
    units = hidden.shape[1] // 2
    out_ref[...] = jnp.zeros_like(out_ref)
    out_ref[0:2, :] = one[0:2, :]
    out_ref[2:4, :] = two[0:2, :]
    out_ref[4:5, :] = one[2:3, :]
    out_ref[5:6, :] = two[2:3, :]
    for row, (mine, other, at) in ((6, (q0, q1, 0)), (7, (kv0, kv1, part))):
        mine = col_sum(mine[:, at : at + part].astype(F32))
        other = col_sum(other[:, at : at + part].astype(F32))
        low, high = jnp.where(first, mine, other), jnp.where(first, other, mine)
        for t in range(size):
            keep = rank == t
            start = 2 * t * part
            out_ref[row : row + 1, start : start + part] = jnp.where(keep, low, 0.0)
            out_ref[row : row + 1, start + part : start + 2 * part] = jnp.where(keep, high, 0.0)
    for t in range(size):
        row = 8 + t
        total = jnp.where(rank == t, hidden[:, :units], 0.0)
        total = total + jnp.where((rank ^ 1) == t, hidden[:, units:], 0.0)
        mine, other = total[:, : units // 2], total[:, units // 2 :]
        out_ref[row : row + 1, : units // 2] = jnp.where(first, mine, other)
        out_ref[row : row + 1, units // 2 :] = jnp.where(first, other, mine)


def input_back_kernel(
    q0, q1, kv0, kv1, w_ref, one, two, hidden, near_ref, far_ref, sib_ref, cat_ref, vec_ref
):
    half, part = q0.shape
    pair, deep = near_ref.shape
    for j, (ref, at) in enumerate(((q0, 0), (q1, 0), (kv0, 0), (kv1, 0), (kv0, part), (kv1, part))):
        count = ref.shape[0]
        cat_ref[:count, j * part : (j + 1) * part] = ref[:, at : at + part]
    sib_ref[:pair, :] = dot(cat_ref[pair:half, :], w_ref[...], NT).astype(BF16)
    out = dot(cat_ref[half + pair :, 2 * part :], w_ref[:, 2 * part :], NT)
    sib_ref[pair:half, :] = out.astype(BF16)
    near_ref[...] = dot(cat_ref[:pair, :], w_ref[...], NT)
    far_ref[...] = dot(cat_ref[half : half + pair, 2 * part :], w_ref[:, 2 * part :], NT)
    pack_rows(vec_ref, one, two, q0, q1, kv0, kv1, hidden)
    sib_ref[half:, :] = vec_ref[...].astype(BF16)


def input_back(q0, q1, kv0, kv1, weights, one, two, hidden):
    half, part = q0.shape
    deep = weights.shape[0]
    pair = half // 2
    out = [shape((pair, deep), F32), shape((pair, deep), F32), shape((half + EXTRA, deep), BF16)]
    scratch = [pltpu.VMEM((kv0.shape[0], 6 * part), BF16), pltpu.VMEM((EXTRA, deep), F32)]
    args = [q0, q1, kv0, kv1, weights, one, two, hidden]
    return call_whole(input_back_kernel, "input_back", out, [], args, scratch)


def fold_kernel(near, far, sent, recv, rest, own_ref, x_ref, y_ref, d_ref, vec_ref):
    rows = own_ref.shape[0]
    pair = 2 * rows
    own_ref[...] = rest[...] + near[:rows, :] + recv[:rows, :].astype(F32)
    vec = sent[2 * pair :, :].astype(F32) + recv[2 * pair :, :].astype(F32)
    vec_ref[...] = vec.astype(BF16)
    for ref, term, at in ((x_ref, near, rows), (y_ref, far, 0), (d_ref, far, rows)):
        start = at if term is near else pair + at
        total = term[at : at + rows, :] + recv[start : start + rows, :].astype(F32)
        ref[:rows, :] = total.astype(BF16)
        ref[rows:, :] = vec.astype(BF16)


def fold(near, far, sent, recv, rest):
    rows, deep = rest.shape
    out = [shape((rows, deep), F32)] + [shape((rows + EXTRA, deep), BF16)] * 3
    out += [shape((EXTRA, deep), BF16)]
    return call_whole(fold_kernel, "fold", out, [], [near, far, sent, recv, rest])


def grad_send_kernel(left, right, out_ref):
    out_ref[...] = dot(left[...], right[...]).astype(BF16)


def grad_send(left, right):
    out = [shape((left.shape[0], right.shape[1]), BF16)]
    return call_whole(grad_send_kernel, "grad_send", out, [], [left, right])[0]


def grad_sum_kernel(left, right, recv, keep_ref, send_ref):
    part = keep_ref.shape[1]
    for ref, at in ((send_ref, slice(part, 2 * part)), (keep_ref, slice(0, part))):
        ref[...] = (dot(left[...], right[:, at]) + recv[:, at].astype(F32)).astype(BF16)


def grad_sum(left, right, recv):
    half = shape((left.shape[0], right.shape[1] // 2), BF16)
    return call_whole(grad_sum_kernel, "grad_sum", [half, half], [], [left, right, recv])


def head_grads(left, query, pair):
    half = query.shape[0]
    return jnp.concatenate([dot(left[:, :half], query[...]), dot(left[...], pair[...])], axis=1)


def head_send_kernel(left, query, pair, out_ref):
    out_ref[...] = head_grads(left, query, pair).astype(BF16)


def head_send(left, query, pair):
    out = [shape((left.shape[0], query.shape[1] + pair.shape[1]), BF16)]
    return call_whole(head_send_kernel, "head_send", out, [], [left, query, pair])[0]


def head_sum_kernel(left, query, pair, recv, keep, keep_recv, out_ref):
    width = recv.shape[1]
    total = head_grads(left, query, pair) + recv[...].astype(F32)
    out_ref[:, :width] = total.astype(BF16)
    out_ref[:, width:] = (keep[...].astype(F32) + keep_recv[...].astype(F32)).astype(BF16)


def head_sum(left, query, pair, recv, keep, keep_recv):
    out = [shape((left.shape[0], recv.shape[1] + keep.shape[1]), BF16)]
    args = [left, query, pair, recv, keep, keep_recv]
    return call_whole(head_sum_kernel, "head_sum", out, [], args)[0]


def gelu_pair(values):
    size = jnp.abs(values)
    t = 1.0 / (1.0 + (0.3275911 * math.sqrt(0.5)) * size)
    bell = jnp.exp2(values * values * (-0.5 * LOG2E))
    poly = t * (
        0.5 * 0.254829592
        + t
        * (
            0.5 * -0.284496736
            + t * (0.5 * 1.421413741 + t * (0.5 * -1.453152027 + t * (0.5 * 1.061405429)))
        )
    )
    tail = poly * bell
    cdf = jnp.where(values < 0, tail, 1.0 - tail)
    return values * cdf, cdf + values * bell * (1.0 / math.sqrt(2.0 * math.pi))


def gather_units(refs, w_ref):
    pairs = []
    part = refs[0][0].shape[2]
    for ref, first in refs:
        for j in range(first, ref.shape[0]):
            at = len(pairs) * part
            pairs.append((ref.at[j], w_ref.at[:, at : at + part]))
    return pairs


def up_kernel(
    x0, x1, mine, other, mine_sib, other_sib, bias_ref,
    xt_ref, w_ref, act_own, act_sib, slope_own, slope_sib, x_ref, sems,
):
    rows = x0.shape[0]
    pairs = [(x0, x_ref.at[:rows, :]), (x1, x_ref.at[rows:, :])]
    pairs += gather_units(((mine, 1), (other, 0), (mine_sib, 1), (other_sib, 0)), w_ref)
    copies = start_all(pairs, sems)
    copies[0].wait()
    copies[1].wait()
    units = act_own.shape[1]
    step = mine.shape[2]

    def matmul(c):
        copies[2 + c].wait()
        return dot(x_ref[...], w_ref[:, c * step : (c + 1) * step])

    following = matmul(0)
    for c in range(8):
        pre = following
        if c < 7:
            following = matmul(c + 1)
        act_ref, slope_ref = ((act_own, slope_own), (act_sib, slope_sib))[c // 4]
        at = slice((c % 4) * step, (c % 4 + 1) * step)
        act, slope = gelu_pair(pre + bias_ref[0:1, c * step : (c + 1) * step])
        act_ref[:, at] = act.astype(BF16)
        slope_ref[:, at] = slope.astype(BF16)
    xt_ref[...] = x_ref[...].T


def feed_up(x0, x1, pieces, bias):
    rows, deep = x0.shape
    units = bias.shape[1]
    out = [shape((deep, 2 * rows), BF16), shape((deep, units), BF16)]
    out += [shape((2 * rows, units // 2), BF16)] * 4
    scratch = [pltpu.VMEM((2 * rows, deep), BF16)]
    return call_whole(up_kernel, "feed_up", out, [x0, x1, *pieces], [bias], scratch, 10)


def down_kernel(spots, *refs):
    count = len(spots)
    own, sib, refs = refs[:count], refs[count : 2 * count], refs[2 * count :]
    act_own, act_sib, w_ref, near_ref, far_ref, sems = refs
    deep = near_ref.shape[1]
    units = act_own.shape[1]
    pairs = []
    rows = ring_rows(deep // own[0].shape[0], deep)
    for (piece, start), left, right in zip(spots, own, sib):
        width = left.shape[1]
        pairs.append((left, w_ref.at[rows[piece], start : start + width]))
        pairs.append((right, w_ref.at[rows[piece], units + start : units + start + width]))
    for copy in start_all(pairs, sems):
        copy.wait()
    for c in range(4):
        at = slice(c * deep // 4, (c + 1) * deep // 4)
        out = dot(act_own[...], w_ref[at, :units], NT) + dot(act_sib[...], w_ref[at, units:], NT)
        split_store(out, near_ref, far_ref, at)


def feed_down(act_own, act_sib, spots, own, sib):
    pair, units = act_own.shape
    deep = D
    out = [
        shape((deep, 2 * units), BF16),
        shape((pair // 2, deep), F32),
        shape((pair // 2, deep), BF16),
    ]
    kernel = functools.partial(down_kernel, spots)
    args = [*own, *sib]
    return call_whole(
        kernel, "feed_down", out, args, [act_own, act_sib], copies=2 * len(own)
    )


def feed_back_kernel(
    g0, g1, slope_own, slope_sib, up_ref, down_ref,
    gt_ref, gup_own, gup_sib, bias_ref, near_ref, far_ref, g_ref,
):
    rows, deep = g0.shape
    g_ref[:rows, :] = g0[...]
    g_ref[rows:, :] = g1[...]
    units = gup_own.shape[1]
    step = units // 2
    for c in range(4):
        slope_ref, gup_ref = ((slope_own, gup_own), (slope_sib, gup_sib))[c // 2]
        at = slice((c % 2) * step, (c % 2 + 1) * step)
        grad = dot(g_ref[...], down_ref[:, c * step : (c + 1) * step])
        grad = (grad * slope_ref[:, at].astype(F32)).astype(BF16)
        gup_ref[:, at] = grad
        bias_ref[0:1, c * step : (c + 1) * step] = jnp.sum(
            grad.astype(F32), axis=0, keepdims=True
        )
    for c in range(4):
        at = slice(c * deep // 4, (c + 1) * deep // 4)
        out = dot(gup_own[...], up_ref[at, :units], NT) + dot(gup_sib[...], up_ref[at, units:], NT)
        split_store(out, near_ref, far_ref, at)
    gt_ref[...] = g_ref[...].T


def feed_back(g0, g1, slope_own, slope_sib, up_all, down_all):
    rows, deep = g0.shape
    units = slope_own.shape[1]
    out = [shape((deep, 2 * rows), BF16)]
    out += [shape((2 * rows, units), BF16)] * 2
    out += [shape((1, 2 * units), F32), shape((rows, deep), F32), shape((rows, deep), BF16)]
    args = [g0, g1, slope_own, slope_sib, up_all, down_all]
    scratch = [pltpu.VMEM((2 * rows, deep), BF16)]
    return call_whole(feed_back_kernel, "feed_back", out, [], args, scratch)


def row_mean(values):
    return jnp.mean(values, axis=-1, keepdims=True)


def col_sum(values):
    return jnp.sum(values, axis=0, keepdims=True)


def normalize(values):
    centered = values - row_mean(values)
    inverse = lax.rsqrt(row_mean(centered * centered) + NORM_EPSILON)
    return centered * inverse, inverse


def norm_back(grad_out, normed, inverse, gain):
    grad = grad_out * gain
    return inverse * (grad - row_mean(grad) - normed * row_mean(grad * normed))


def norm_one_kernel(own, part, recv, vec, first_ref, low_ref, normed_ref, inverse_ref):
    attn_out = part[...] + recv[...].astype(F32) + vec[4:5, :]
    normed, inverse = normalize(own[...].astype(F32) + attn_out)
    first = normed * vec[0:1, :] + vec[1:2, :]
    first_ref[...] = first
    low_ref[...] = first.astype(BF16)
    normed_ref[...] = normed
    inverse_ref[...] = inverse


def norm_one(own, part, recv, vec):
    rows, deep = own.shape
    out = [shape((rows, deep), t) for t in (F32, BF16, F32)] + [shape((rows, 1), F32)]
    return call_whole(norm_one_kernel, "norm_one", out, [], [own, part, recv, vec])


def norm_two_kernel(first, part, recv, cotangent, vec, out_ref, grad_ref, low_ref, sums_ref):
    down_out = part[...] + recv[...].astype(F32) + vec[5:6, :]
    normed, inverse = normalize(first[...] + down_out)
    out_ref[...] = (normed * vec[2:3, :] + vec[3:4, :]).astype(BF16)
    given = cotangent[...].astype(F32)
    grad = norm_back(given, normed, inverse, vec[2:3, :])
    grad_ref[...] = grad
    low = grad.astype(BF16)
    low_ref[...] = low
    sums_ref[0:1, :] = col_sum(given * normed)
    sums_ref[1:2, :] = col_sum(given)
    sums_ref[2:3, :] = col_sum(low.astype(F32))


def norm_two(first, part, recv, cotangent, vec):
    rows, deep = first.shape
    out = [shape((rows, deep), t) for t in (BF16, F32, BF16)] + [shape((3, deep), F32)]
    return call_whole(norm_two_kernel, "norm_two", out, [], [first, part, recv, cotangent, vec])


def norm_one_back_kernel(
    grad_second, part, recv, normed, inverse, vec, grad_ref, low_ref, sums_ref
):
    given = grad_second[...] + part[...] + recv[...].astype(F32)
    grad = norm_back(given, normed[...], inverse[...], vec[0:1, :])
    grad_ref[...] = grad
    low = grad.astype(BF16)
    low_ref[...] = low
    sums_ref[0:1, :] = col_sum(given * normed[...])
    sums_ref[1:2, :] = col_sum(given)
    sums_ref[2:3, :] = col_sum(low.astype(F32))


def norm_one_back(grad_second, part, recv, normed, inverse, vec):
    rows, deep = part.shape
    out = [shape((rows, deep), t) for t in (F32, BF16)] + [shape((3, deep), F32)]
    args = [grad_second, part, recv, normed, inverse, vec]
    return call_whole(norm_one_back_kernel, "norm_one_back", out, [], args)


def nesterov(weights, momentum, average, gradient, step_rate):
    momentum_new = MOMENTUM * momentum + gradient
    weight_new = weights - step_rate * (gradient + MOMENTUM * momentum_new)
    return (weight_new, momentum_new, AVERAGE * average + (1.0 - AVERAGE) * weight_new)


def swap_tp(values, bit):
    size = lax.axis_size("tp")
    return lax.ppermute(values, "tp", [(i, i ^ bit) for i in range(size)])


def core(values):
    return swap_tp(values, 1)


def across(values):
    return swap_tp(values, 2)


def swap_ctx(values):
    return lax.ppermute(values, "ctx", [(0, 1), (1, 0)])


def swap_both(values):
    size = lax.axis_size("tp")
    return lax.ppermute(values, ("ctx", "tp"), [(i, i ^ (size + 2)) for i in range(2 * size)])


def sum_fsdp(values):
    size = lax.axis_size("fsdp")

    def swap(values, bit):
        return lax.ppermute(values, "fsdp", [(i, i ^ bit) for i in range(size)])

    if size == 4:
        one, two, three = (swap(values, bit) for bit in (1, 2, 3))
        return (values + one) + (two + three)
    bit = 1
    while bit < size:
        values = values + swap(values, bit)
        bit *= 2
    return values


def gather_fsdp(shard, axis):
    return lax.all_gather(shard, "fsdp", axis=axis, tiled=True)


def ring():
    return lax.axis_size("fsdp") == 4


def shift_fsdp(values, step):
    size = lax.axis_size("fsdp")
    return lax.ppermute(values, "fsdp", [(i, (i + step) % size) for i in range(size)])


def gather_pieces(shard, axis):
    if not ring():
        return [gather_fsdp(shard, axis)]
    return [shard] + [shift_fsdp(shard, -s) for s in range(1, lax.axis_size("fsdp"))]


def scatter_fsdp(grads, axis):
    return lax.psum_scatter(grads, "fsdp", scatter_dimension=axis, tiled=True)


def halves(values, axis=-1):
    low, high = jnp.split(values, 2, axis=axis)
    first = lax.axis_index("ctx") == 0
    return jnp.where(first, low, high), jnp.where(first, high, low)


def join(mine, other, axis=-1):
    first = lax.axis_index("ctx") == 0
    low, high = jnp.where(first, mine, other), jnp.where(first, other, mine)
    return jnp.concatenate([low, high], axis=axis)


def quarters(mine):
    return jnp.stack(jnp.split(mine, 2, axis=1))


def after(values, *others):
    return lax.optimization_barrier((values,) + others)[0]


def on_device(
    tokens,
    cotangent,
    attn_weight,
    attn_momentum,
    attn_average,
    ffn_weight,
    ffn_momentum,
    ffn_average,
    vector_weight,
    vector_momentum,
    vector_average,
):
    tp_rank = lax.axis_index("tp")
    sib_rank = tp_rank ^ 1
    head_width = attn_weight.shape[2]
    unit_width = ffn_weight.shape[2]
    token_count = LEN * lax.axis_size("fsdp")
    matrix_rate = MATRIX_RATE / math.sqrt(token_count)
    vector_rate = VECTOR_RATE / math.sqrt(token_count)

    attn_low, attn_high = halves(attn_weight.astype(BF16))
    qkv_mine = gather_pieces(attn_low[:3], 1)

    own = tokens[0]
    rows = own.shape[0]
    pair = 2 * rows
    half = 4 * rows
    beside = across(own)
    facing = swap_ctx(own)
    diagonal = swap_both(own)
    if ring():
        others = swap_ctx(after(jnp.stack(qkv_mine[1:]), beside, facing))
        qkv_other = [attn_high[:3]] + [others[s] for s in range(len(qkv_mine) - 1)]
    else:
        qkv_other = [swap_ctx(qkv_mine[0])]
    up_low = quarters(halves(ffn_weight[0].astype(BF16))[0])
    out_low = jnp.concatenate([attn_low[3], attn_high[3]], axis=1)
    out_up_low = jnp.concatenate([out_low[None], up_low])
    out_up = gather_fsdp(after(out_up_low, *qkv_mine[-3:], beside, facing), 1)
    blocks = [own, beside, core(own), core(beside), facing, diagonal, core(facing), core(diagonal)]

    vec = vector_weight[: 6 * D].reshape(6, D)

    def columns(start, width):
        part = lax.dynamic_slice_in_dim(vector_weight, start, width)
        return jnp.concatenate(halves(part))

    biases = jnp.stack(
        [
            columns(6 * D + tp_rank * head_width, head_width),
            columns(7 * D + tp_rank * head_width, head_width),
        ]
    )
    bias_hidden = jnp.concatenate(
        [
            columns(8 * D + tp_rank * unit_width, unit_width),
            columns(8 * D + sib_rank * unit_width, unit_width),
        ]
    )[None]

    token_t, qkv_w, queries, keys, values = project(blocks, qkv_mine, qkv_other, biases)
    down_low = jnp.concatenate(halves(ffn_weight[1].astype(BF16)), axis=1)
    mixed_own, mixed_sib, lse = attend(queries, keys, values)
    down_low = after(down_low, mixed_own)
    if ring():
        low, high = jnp.split(down_low, 2, axis=1)
        spots = ((0, 0), (1, 0), (3, 0), (2, 0), (2, low.shape[1]))
        down_w = [down_low, shift_fsdp(down_low, -1), shift_fsdp(down_low, -3)]
        down_w += [shift_fsdp(low, -2), shift_fsdp(high, -2)]
    else:
        spots = ((0, 0),)
        down_w = [gather_fsdp(down_low, 0)]
    mixed_recv = core(mixed_sib)
    out_up = after(out_up, mixed_own)
    out_up_sib = core(out_up)
    up_other = swap_ctx(out_up[1:])
    out_w, attn_part, attn_far = out_project(mixed_own, mixed_recv, [out_up, out_up_sib])
    attn_recv = across(attn_far)
    if ring():
        attn_recv = after(attn_recv, down_w[1], down_w[2])
    first, first_low, normed_one, inverse_one = norm_one(own, attn_part, attn_recv, vec)
    first_beside = across(first_low)

    if ring():
        first_beside = after(first_beside, down_w[3])
    up_other = after(up_other, first_beside)
    first_t, up_all, hidden_own, hidden_sib, slope_own, slope_sib = feed_up(
        first_low, first_beside, [out_up, up_other, out_up_sib, core(up_other)], bias_hidden
    )
    if ring():
        down_w[4] = after(down_w[4], hidden_own)
    down_all, down_part, down_far = feed_down(
        hidden_own, hidden_sib, spots, down_w, [core(w) for w in down_w]
    )
    layer_out, grad_second, grad_down, sums_two = norm_two(
        first, down_part, across(down_far), cotangent[0], vec
    )
    grad_down_t, grad_up_own, grad_up_sib, grad_bias_hidden, first_part, first_far = feed_back(
        grad_down, across(grad_down), slope_own, slope_sib, up_all, down_all
    )
    down_sib = grad_send(grad_down_t, hidden_sib)
    up_sib = grad_send(first_t, grad_up_sib)
    first_recv = after(across(first_far), down_sib, up_sib)
    grad_res, grad_attn, sums_one = norm_one_back(
        grad_second, first_part, first_recv, normed_one, inverse_one, vec
    )
    grad_attn_beside = across(grad_attn)
    down_mine, down_rest = grad_sum(grad_down_t, hidden_own, after(core(down_sib), grad_attn))
    up_keep, up_send = grad_sum(first_t, grad_up_own, after(core(up_sib), grad_attn))

    def finish(mine):
        return join(mine, swap_ctx(mine)).astype(F32)

    mine_owned = scatter_fsdp(down_mine, 0)
    rest_owned = scatter_fsdp(down_rest, 0)
    up_recv = swap_ctx(up_send)

    grad_attn_beside = after(grad_attn_beside, down_mine, up_send)
    grad_attn_t, grad_mixed_own, grad_mixed_sib = out_back(grad_attn, grad_attn_beside, out_w)
    grad_mixed = (grad_mixed_own, core(grad_mixed_sib))

    up_recv = after(up_recv, grad_mixed_sib)
    up_sum = (up_keep.astype(F32) + up_recv.astype(F32)).astype(BF16)
    up_owned = scatter_fsdp(up_sum, 0)
    mixed = (mixed_own, mixed_sib)
    heads = (queries, keys, values, mixed)
    query_other, kv_other = attend_back(*heads, grad_mixed, lse, 1)
    send = head_send(token_t, query_other, kv_other)
    out_sib = grad_send(after(grad_attn_t, query_other), mixed_recv)
    out_keep, out_send = grad_sum(grad_attn_t, mixed_own, core(out_sib))
    grad_mixed = (grad_mixed[0], after(grad_mixed[1], up_sum, send, out_send, mine_owned))
    recv = swap_ctx(send)
    query_mine, kv_mine = attend_back(*heads, grad_mixed, lse, 0)
    part = head_width // 2
    near, far, sibling = input_back(
        query_mine, query_other, kv_mine, kv_other, qkv_w, sums_one, sums_two, grad_bias_hidden
    )
    sib_recv = core(sibling)
    qkvo_sum = head_sum(token_t, query_mine, after(kv_mine, rest_owned), recv, out_keep, swap_ctx(out_send))
    qkvo_mine = scatter_fsdp(qkvo_sum, 0)
    mine_recv, rest_recv = swap_ctx(mine_owned), swap_ctx(rest_owned)
    sib_recv = after(sib_recv, qkvo_sum, up_owned, mine_recv, rest_recv)
    input_part, to_x, to_y, to_d, vec_part = fold(near, far, sibling, sib_recv, grad_res)
    from_x, from_y, from_d = across(to_x), swap_ctx(to_y), swap_both(to_d)
    down_grad = join(
        mine_owned.astype(F32) + rest_recv.astype(F32),
        rest_owned.astype(F32) + mine_recv.astype(F32),
    )
    up_grad = finish(after(up_owned, to_y))
    ffn_grad = jnp.stack([up_grad, down_grad])
    ffn_new, ffn_momentum_new, ffn_average_new = nesterov(
        ffn_weight, ffn_momentum, ffn_average, ffn_grad, matrix_rate
    )
    input_grad = input_part
    for term in (from_x, from_y, from_d):
        input_grad = input_grad + term[:rows].astype(F32)
    vec_x, vec_y, vec_d = (term[rows:].astype(F32) for term in (from_x, from_y, from_d))
    vec_plane = (vec_part.astype(F32) + vec_x) + (vec_y + vec_d)

    qkvo_mine = after(qkvo_mine, from_x, from_y, from_d)
    qkvo_other = swap_ctx(qkvo_mine)
    vector_grad = sum_fsdp(vec_plane[:12]).reshape(-1)
    attn_grad = jnp.stack(
        [
            join(qkvo_mine[:, j * part : (j + 1) * part], qkvo_other[:, j * part : (j + 1) * part])
            for j in range(4)
        ]
    ).astype(F32)
    vector_new, vector_momentum_new, vector_average_new = nesterov(
        vector_weight, vector_momentum, vector_average, vector_grad, vector_rate
    )
    attn_new, attn_momentum_new, attn_average_new = nesterov(
        attn_weight, attn_momentum, attn_average, attn_grad, matrix_rate
    )
    return (
        layer_out[None],
        input_grad[None],
        attn_grad,
        attn_new,
        attn_momentum_new,
        attn_average_new,
        attn_new.astype(BF16),
        ffn_grad,
        ffn_new,
        ffn_momentum_new,
        ffn_average_new,
        ffn_new.astype(BF16),
        vector_grad,
        vector_new,
        vector_momentum_new,
        vector_average_new,
    )


def solution(mesh):
    rows = P("fsdp", ("ctx", "tp"), None)
    weight = P(None, "fsdp", "tp")
    return jax.shard_map(
        on_device,
        mesh=mesh,
        in_specs=(rows, rows) + (weight,) * 6 + (P(),) * 3,
        out_specs=(rows, rows) + (weight,) * 10 + (P(),) * 4,
        check_vma=False,
    )
```

```python
import functools
import math

import jax
import jax.numpy as jnp
from jax import lax
from jax.experimental import pallas as pl
from jax.experimental.pallas import tpu as pltpu
from jax.sharding import PartitionSpec as P

D = 1024
FF = 4096
HEAD_DIM = 64
LEN = 2048

NORM_EPSILON = 1e-05
MOMENTUM = 0.5
AVERAGE = 0.5
MATRIX_RATE = 0.1
VECTOR_RATE = 0.3

SCALE = HEAD_DIM ** (-0.5)
LOG2E = math.log2(math.e)
F32 = jnp.float32
BF16 = jnp.bfloat16
NT = (((1,), (1,)), ((), ()))
TN = (((0,), (0,)), ((), ()))
NN = (((1,), (0,)), ((), ()))


def dot(left, right, dims=NN):
    return lax.dot_general(left, right, dims, preferred_element_type=F32)


VMEM = pl.BlockSpec(memory_space=pltpu.VMEM)
ANY = pl.BlockSpec(memory_space=pl.ANY)
MEGA = 1024 * 1024
WORK_UNIT = 1.2e10


WORK = {
    "project": 0.001,
    "attend": 0.001,
    "out_project": 0.001,
    "norm_one": 1.5,
    "feed_up": 8,
    "feed_down": 4,
    "norm_two": 2,
    "feed_back": 8,
    "grad_send": 10,
    "grad_sum": 3,
    "norm_one_back": 2,
    "out_back": 2,
    "attend_back": 12,
    "head_send": 3,
    "head_sum": 4,
    "input_back": 0.01,
    "fold": 1.5,
    "grad_total": 3,
}


def cost(name):
    flops = int(WORK[name] * WORK_UNIT)
    return pl.CostEstimate(flops=flops, bytes_accessed=1, transcendentals=0)


def shape(dims, dtype):
    return jax.ShapeDtypeStruct(tuple(dims), dtype)


def tile(i, size):
    return pl.ds(pl.multiple_of(i * size, size), size)


def call_whole(kernel, name, out_shape, far_args, near_args, scratch=(), copies=0):
    scratch = list(scratch)
    if copies:
        scratch.append(pltpu.SemaphoreType.DMA((copies,)))
    return pl.pallas_call(
        kernel,
        in_specs=[ANY] * len(far_args) + [VMEM] * len(near_args),
        out_specs=[VMEM] * len(out_shape),
        out_shape=list(out_shape),
        scratch_shapes=scratch,
        compiler_params=pltpu.CompilerParams(vmem_limit_bytes=6 * MEGA),
        cost_estimate=cost(name),
        name=name,
    )(*far_args, *near_args)


def start_all(pairs, sems):
    copies = [pltpu.make_async_copy(src, dst, sems.at[i]) for i, (src, dst) in enumerate(pairs)]
    for copy in copies:
        copy.start()
    return copies


def head_masks(width):
    lane = lax.broadcasted_iota(jnp.int32, (1, width), 1) // HEAD_DIM
    return [(lane == h).astype(BF16) for h in range(width // HEAD_DIM)]


def attend_kernel(chunk, q_ref, k_ref, v_ref, own_ref, sib_ref, lse_ref, vt_ref):
    heads = q_ref.shape[1] // HEAD_DIM
    count = k_ref.shape[0]
    step = pl.program_id(0)

    @pl.when(step == 0)
    def _():
        vt_ref[...] = v_ref[...].T

    queries = q_ref[...]
    masked = [queries * mask for mask in head_masks(q_ref.shape[1])]
    units = [(h, c) for h in range(heads) for c in range(0, count, chunk)]

    def scores_of(unit):
        h, c = unit
        return dot(k_ref[c : c + chunk, :], masked[h], NT)

    tops, totals, outs = {}, {}, {}
    scores = scores_of(units[0])
    for i, unit in enumerate(units):
        current = scores
        if i + 1 < len(units):
            scores = scores_of(units[i + 1])
        h, c = unit
        top = jnp.max(current, axis=0, keepdims=True)
        weights = jnp.exp2((current - top) * (SCALE * LOG2E))
        tops[unit] = top
        totals[unit] = jnp.sum(weights, axis=0, keepdims=True)
        outs[unit] = dot(
            vt_ref[h * HEAD_DIM : (h + 1) * HEAD_DIM, c : c + chunk], weights.astype(BF16)
        )
    heads_out = []
    for h in range(heads):
        mine = [(h, c) for c in range(0, count, chunk)]
        top = functools.reduce(jnp.maximum, [tops[u] for u in mine])
        share = [jnp.exp2((tops[u] - top) * (SCALE * LOG2E)) for u in mine]
        total = sum(totals[u] * f for u, f in zip(mine, share))
        out = sum(outs[u] * f for u, f in zip(mine, share))
        heads_out.append(out / total)
        lse_ref[h : h + 1, :] = top * (SCALE * LOG2E) + jnp.log2(total)
    mixed = jnp.concatenate(heads_out, axis=0).T.astype(BF16)
    steps = pl.num_programs(0)

    @pl.when(step < steps // 2)
    def _():
        own_ref[...] = mixed

    @pl.when(step >= steps // 2)
    def _():
        sib_ref[...] = mixed


def attend(queries, keys, values):
    rows, width = queries.shape
    block = min(256, rows // 2)
    steps = rows // block
    heads = width // HEAD_DIM
    half_blocks = steps // 2
    return pl.pallas_call(
        functools.partial(attend_kernel, min(512, keys.shape[0])),
        grid=(steps,),
        in_specs=[
            pl.BlockSpec((block, width), lambda i: (i, 0)),
            pl.BlockSpec(keys.shape, lambda i: (0, 0)),
            pl.BlockSpec(values.shape, lambda i: (0, 0)),
        ],
        out_specs=[
            pl.BlockSpec((block, width), lambda i: (jnp.minimum(i, half_blocks - 1), 0)),
            pl.BlockSpec((block, width), lambda i: (jnp.maximum(i - half_blocks, 0), 0)),
            pl.BlockSpec((heads, block), lambda i: (0, i)),
        ],
        out_shape=[
            shape((rows // 2, width), BF16),
            shape((rows // 2, width), BF16),
            shape((heads, rows), F32),
        ],
        scratch_shapes=[pltpu.VMEM((width, keys.shape[0]), BF16)],
        compiler_params=pltpu.CompilerParams(vmem_limit_bytes=12 * MEGA),
        cost_estimate=cost("attend"),
        name="attend",
    )(queries, keys, values)


def attend_back_kernel(
    part, q_ref, k_ref, v_ref, o0_ref, o1_ref, g0_ref, g1_ref, lse_ref,
    dq_ref, dkv_ref, kt_ref, dk_acc, dv_acc, o_ref, g_ref,
):
    width = q_ref.shape[1]
    heads = width // HEAD_DIM
    step = pl.program_id(0)
    steps = pl.num_programs(0)

    @pl.when(step == 0)
    def _():
        kt_ref[...] = k_ref[...].T
        dk_acc[...] = jnp.zeros_like(dk_acc)
        dv_acc[...] = jnp.zeros_like(dv_acc)

    @pl.when(step < steps // 2)
    def _():
        o_ref[...] = o0_ref[...]
        g_ref[...] = g0_ref[...]

    @pl.when(step >= steps // 2)
    def _():
        o_ref[...] = o1_ref[...]
        g_ref[...] = g1_ref[...]

    queries = q_ref[...]
    grads = g_ref[...]
    masks = head_masks(width)
    product = (o_ref[...].astype(F32) * grads.astype(F32)).T
    outs, probs, gscores, qms, gms = [], [], [], [], []
    for h in range(heads):
        qm = queries * masks[h]
        gm = grads * masks[h]
        delta = jnp.sum(product[h * HEAD_DIM : (h + 1) * HEAD_DIM, :], axis=0, keepdims=True)
        scores = dot(k_ref[...], qm, NT)
        row = part * heads + h
        prob = jnp.exp2(scores * (SCALE * LOG2E) - lse_ref[row : row + 1, :])
        grad_prob = dot(v_ref[...], gm, NT)
        gscore = (prob * (grad_prob - delta)).astype(BF16)
        outs.append(dot(kt_ref[h * HEAD_DIM : (h + 1) * HEAD_DIM, :], gscore))
        probs.append(prob.astype(BF16))
        gscores.append(gscore)
        qms.append(qm)
        gms.append(gm)
    dv_acc[...] += dot(jnp.concatenate(probs, axis=1), jnp.concatenate(gms, axis=0))
    dk_acc[...] += dot(jnp.concatenate(gscores, axis=1), jnp.concatenate(qms, axis=0))
    dq_ref[...] = (jnp.concatenate(outs, axis=0).T * SCALE).astype(BF16)

    @pl.when(step == steps - 1)
    def _():
        dkv_ref[:, :width] = (dk_acc[...] * SCALE).astype(BF16)
        dkv_ref[:, width:] = dv_acc[...].astype(BF16)


def attend_back(queries, keys, values, mixed, grads, lse, part):
    rows, both = queries.shape
    count = keys.shape[0]
    width = both // 2
    block = min(256, rows // 2)
    half_blocks = rows // 2 // block
    row_spec = pl.BlockSpec((block, width), lambda i: (i, part))
    own_spec = pl.BlockSpec((block, width), lambda i: (jnp.minimum(i, half_blocks - 1), part))
    sib_spec = pl.BlockSpec((block, width), lambda i: (jnp.maximum(i - half_blocks, 0), part))
    full_spec = pl.BlockSpec((count, width), lambda i: (0, part))
    lse_spec = pl.BlockSpec((lse.shape[0], block), lambda i: (0, i))
    return pl.pallas_call(
        functools.partial(attend_back_kernel, part),
        grid=(rows // block,),
        in_specs=[row_spec, full_spec, full_spec] + [own_spec, sib_spec] * 2 + [lse_spec],
        out_specs=[
            pl.BlockSpec((block, width), lambda i: (i, 0)),
            pl.BlockSpec((count, both), lambda i: (0, 0)),
        ],
        out_shape=[shape((rows, width), BF16), shape((count, both), BF16)],
        scratch_shapes=[
            pltpu.VMEM((width, count), BF16),
            pltpu.VMEM((count, width), F32),
            pltpu.VMEM((count, width), F32),
            pltpu.VMEM((block, width), BF16),
            pltpu.VMEM((block, width), BF16),
        ],
        compiler_params=pltpu.CompilerParams(vmem_limit_bytes=12 * MEGA),
        cost_estimate=cost("attend_back"),
        name="attend_back",
    )(queries, keys, values, *mixed, *grads, lse)


def ring_rows(count, deep):
    size = deep // count
    rank = lax.axis_index("fsdp")
    return [tile(lax.rem(rank + s, count), size) if count > 1 else tile(0, size) for s in range(count)]


def project_kernel(count, *refs):
    blocks, refs = refs[:8], refs[8:]
    mine, refs = refs[:count], refs[count:]
    other, refs = refs[:count], refs[count:]
    bias_ref, xt_ref, w_ref, q_ref, k_ref, v_ref, x_ref, sems = refs
    rows = blocks[0].shape[0]
    deep = x_ref.shape[1]
    part = mine[0].shape[2]
    width = 2 * part
    pairs = []
    for at, low, high in zip(ring_rows(count, deep), mine, other):
        for j in range(3):
            pairs.append((low.at[j], w_ref.at[at, j * width : j * width + part]))
            pairs.append((high.at[j], w_ref.at[at, j * width + part : (j + 1) * width]))
    weights = len(pairs)
    for i in range(8):
        pairs.append((blocks[i], x_ref.at[i * rows : (i + 1) * rows, :]))
    copies = start_all(pairs, sems)
    for copy in copies[:weights]:
        copy.wait()
    for i in range(4):
        at = slice(i * 2 * rows, (i + 1) * 2 * rows)
        for copy in copies[weights + 2 * i : weights + 2 * i + 2]:
            copy.wait()
        x = x_ref[at, :]
        if i < 2:
            out = dot(x, w_ref[...])
            q_ref[at, :] = (out[:, :width] + bias_ref[0:1, :]).astype(BF16)
            out = out[:, width:]
        else:
            out = dot(x, w_ref[:, width:])
        k_ref[at, :] = out[:, :width].astype(BF16)
        v_ref[at, :] = (out[:, width:] + bias_ref[1:2, :]).astype(BF16)
        xt_ref[:, at] = x.T


def project(blocks, mine, other, biases):
    rows, deep = blocks[0].shape
    width = biases.shape[1]
    out = [
        shape((deep, 8 * rows), BF16),
        shape((deep, 3 * width), BF16),
        shape((4 * rows, width), BF16),
        shape((8 * rows, width), BF16),
        shape((8 * rows, width), BF16),
    ]
    scratch = [pltpu.VMEM((8 * rows, deep), BF16)]
    kernel = functools.partial(project_kernel, len(mine))
    args = [*blocks, *mine, *other]
    return call_whole(kernel, "project", out, args, [biases], scratch, 8 + 6 * len(mine))


def split_store(out, near_ref, far_ref, at):
    rows = near_ref.shape[0]
    near_ref[:, at] = out[:rows]
    far_ref[:, at] = out[rows:].astype(BF16)


def out_kernel(w0, w1, own, sib, w_ref, near_ref, far_ref, sems):
    width = own.shape[1]
    deep = w_ref.shape[0]
    pairs = [(w0.at[0], w_ref.at[:, :width]), (w1.at[0], w_ref.at[:, width:])]
    for copy in start_all(pairs, sems):
        copy.wait()
    for c in range(4):
        at = slice(c * deep // 4, (c + 1) * deep // 4)
        out = dot(own[...], w_ref[at, :width], NT) + dot(sib[...], w_ref[at, width:], NT)
        split_store(out, near_ref, far_ref, at)


def out_project(own, sib, pieces):
    pair, width = own.shape
    deep = pieces[0].shape[1]
    out = [
        shape((deep, 2 * width), BF16),
        shape((pair // 2, deep), F32),
        shape((pair // 2, deep), BF16),
    ]
    return call_whole(out_kernel, "out_project", out, pieces, [own, sib], copies=2)


def out_back_kernel(g0, g1, w_ref, gt_ref, own_ref, sib_ref):
    rows = g0.shape[0]
    width = own_ref.shape[1]
    for i, ref in enumerate((g0, g1)):
        at = slice(i * rows, (i + 1) * rows)
        g = ref[...]
        out = dot(g, w_ref[...])
        own_ref[at, :] = out[:, :width].astype(BF16)
        sib_ref[at, :] = out[:, width:].astype(BF16)
        gt_ref[:, at] = g.T


def out_back(g0, g1, weights):
    rows, deep = g0.shape
    width = weights.shape[1] // 2
    out = [
        shape((deep, 2 * rows), BF16),
        shape((2 * rows, width), BF16),
        shape((2 * rows, width), BF16),
    ]
    return call_whole(out_back_kernel, "out_back", out, [], [g0, g1, weights])


EXTRA = 16


def pack_rows(out_ref, one, two, q0, q1, kv0, kv1, hidden):
    rank = lax.axis_index("tp")
    size = lax.axis_size("tp")
    first = lax.axis_index("ctx") == 0
    part = q0.shape[1]
    units = hidden.shape[1] // 2
    out_ref[...] = jnp.zeros_like(out_ref)
    out_ref[0:2, :] = one[0:2, :]
    out_ref[2:4, :] = two[0:2, :]
    out_ref[4:5, :] = one[2:3, :]
    out_ref[5:6, :] = two[2:3, :]
    for row, (mine, other, at) in ((6, (q0, q1, 0)), (7, (kv0, kv1, part))):
        mine = col_sum(mine[:, at : at + part].astype(F32))
        other = col_sum(other[:, at : at + part].astype(F32))
        low, high = jnp.where(first, mine, other), jnp.where(first, other, mine)
        for t in range(size):
            keep = rank == t
            start = 2 * t * part
            out_ref[row : row + 1, start : start + part] = jnp.where(keep, low, 0.0)
            out_ref[row : row + 1, start + part : start + 2 * part] = jnp.where(keep, high, 0.0)
    for t in range(size):
        row = 8 + t
        total = jnp.where(rank == t, hidden[:, :units], 0.0)
        total = total + jnp.where((rank ^ 1) == t, hidden[:, units:], 0.0)
        mine, other = total[:, : units // 2], total[:, units // 2 :]
        out_ref[row : row + 1, : units // 2] = jnp.where(first, mine, other)
        out_ref[row : row + 1, units // 2 :] = jnp.where(first, other, mine)


def input_back_kernel(
    q0, q1, kv0, kv1, w_ref, one, two, hidden, near_ref, far_ref, sib_ref, cat_ref, vec_ref
):
    half, part = q0.shape
    pair, deep = near_ref.shape
    for j, (ref, at) in enumerate(((q0, 0), (q1, 0), (kv0, 0), (kv1, 0), (kv0, part), (kv1, part))):
        count = ref.shape[0]
        cat_ref[:count, j * part : (j + 1) * part] = ref[:, at : at + part]
    sib_ref[:pair, :] = dot(cat_ref[pair:half, :], w_ref[...], NT).astype(BF16)
    out = dot(cat_ref[half + pair :, 2 * part :], w_ref[:, 2 * part :], NT)
    sib_ref[pair:half, :] = out.astype(BF16)
    near_ref[...] = dot(cat_ref[:pair, :], w_ref[...], NT)
    far_ref[...] = dot(cat_ref[half : half + pair, 2 * part :], w_ref[:, 2 * part :], NT)
    pack_rows(vec_ref, one, two, q0, q1, kv0, kv1, hidden)
    sib_ref[half:, :] = vec_ref[...].astype(BF16)


def input_back(q0, q1, kv0, kv1, weights, one, two, hidden):
    half, part = q0.shape
    deep = weights.shape[0]
    pair = half // 2
    out = [shape((pair, deep), F32), shape((pair, deep), F32), shape((half + EXTRA, deep), BF16)]
    scratch = [pltpu.VMEM((kv0.shape[0], 6 * part), BF16), pltpu.VMEM((EXTRA, deep), F32)]
    args = [q0, q1, kv0, kv1, weights, one, two, hidden]
    return call_whole(input_back_kernel, "input_back", out, [], args, scratch)


def fold_kernel(near, far, sent, recv, rest, own_ref, x_ref, y_ref, d_ref, vec_ref):
    rows = own_ref.shape[0]
    pair = 2 * rows
    own_ref[...] = rest[...] + near[:rows, :] + recv[:rows, :].astype(F32)
    vec = sent[2 * pair :, :].astype(F32) + recv[2 * pair :, :].astype(F32)
    vec_ref[...] = vec.astype(BF16)
    for ref, term, at in ((x_ref, near, rows), (y_ref, far, 0), (d_ref, far, rows)):
        start = at if term is near else pair + at
        total = term[at : at + rows, :] + recv[start : start + rows, :].astype(F32)
        ref[:rows, :] = total.astype(BF16)
        ref[rows:, :] = vec.astype(BF16)


def fold(near, far, sent, recv, rest):
    rows, deep = rest.shape
    out = [shape((rows, deep), F32)] + [shape((rows + EXTRA, deep), BF16)] * 3
    out += [shape((EXTRA, deep), BF16)]
    return call_whole(fold_kernel, "fold", out, [], [near, far, sent, recv, rest])


def grad_send_kernel(left, right, out_ref):
    out_ref[...] = dot(left[...], right[...]).astype(BF16)


def grad_send(left, right):
    out = [shape((left.shape[0], right.shape[1]), BF16)]
    return call_whole(grad_send_kernel, "grad_send", out, [], [left, right])[0]


def grad_sum_kernel(left, right, recv, keep_ref, send_ref):
    part = keep_ref.shape[1]
    for ref, at in ((send_ref, slice(part, 2 * part)), (keep_ref, slice(0, part))):
        ref[...] = (dot(left[...], right[:, at]) + recv[:, at].astype(F32)).astype(BF16)


def grad_sum(left, right, recv):
    half = shape((left.shape[0], right.shape[1] // 2), BF16)
    return call_whole(grad_sum_kernel, "grad_sum", [half, half], [], [left, right, recv])


def head_grads(left, query, pair):
    half = query.shape[0]
    return jnp.concatenate([dot(left[:, :half], query[...]), dot(left[...], pair[...])], axis=1)


def head_send_kernel(left, query, pair, out_ref):
    out_ref[...] = head_grads(left, query, pair).astype(BF16)


def head_send(left, query, pair):
    out = [shape((left.shape[0], query.shape[1] + pair.shape[1]), BF16)]
    return call_whole(head_send_kernel, "head_send", out, [], [left, query, pair])[0]


def head_sum_kernel(left, query, pair, recv, keep, keep_recv, out_ref):
    width = recv.shape[1]
    total = head_grads(left, query, pair) + recv[...].astype(F32)
    out_ref[:, :width] = total.astype(BF16)
    out_ref[:, width:] = (keep[...].astype(F32) + keep_recv[...].astype(F32)).astype(BF16)


def head_sum(left, query, pair, recv, keep, keep_recv):
    out = [shape((left.shape[0], recv.shape[1] + keep.shape[1]), BF16)]
    args = [left, query, pair, recv, keep, keep_recv]
    return call_whole(head_sum_kernel, "head_sum", out, [], args)[0]


def gelu_pair(values):
    size = jnp.abs(values)
    t = 1.0 / (1.0 + (0.3275911 * math.sqrt(0.5)) * size)
    bell = jnp.exp2(values * values * (-0.5 * LOG2E))
    poly = t * (
        0.5 * 0.254829592
        + t
        * (
            0.5 * -0.284496736
            + t * (0.5 * 1.421413741 + t * (0.5 * -1.453152027 + t * (0.5 * 1.061405429)))
        )
    )
    tail = poly * bell
    cdf = jnp.where(values < 0, tail, 1.0 - tail)
    return values * cdf, cdf + values * bell * (1.0 / math.sqrt(2.0 * math.pi))


def gather_units(refs, w_ref):
    pairs = []
    part = refs[0][0].shape[2]
    for ref, first in refs:
        for j in range(first, ref.shape[0]):
            at = len(pairs) * part
            pairs.append((ref.at[j], w_ref.at[:, at : at + part]))
    return pairs


def up_kernel(
    x0, x1, mine, other, mine_sib, other_sib, bias_ref,
    xt_ref, w_ref, act_own, act_sib, slope_own, slope_sib, x_ref, sems,
):
    rows = x0.shape[0]
    pairs = [(x0, x_ref.at[:rows, :]), (x1, x_ref.at[rows:, :])]
    pairs += gather_units(((mine, 1), (other, 0), (mine_sib, 1), (other_sib, 0)), w_ref)
    copies = start_all(pairs, sems)
    copies[0].wait()
    copies[1].wait()
    units = act_own.shape[1]
    step = mine.shape[2]

    def matmul(c):
        copies[2 + c].wait()
        return dot(x_ref[...], w_ref[:, c * step : (c + 1) * step])

    following = matmul(0)
    for c in range(8):
        pre = following
        if c < 7:
            following = matmul(c + 1)
        act_ref, slope_ref = ((act_own, slope_own), (act_sib, slope_sib))[c // 4]
        at = slice((c % 4) * step, (c % 4 + 1) * step)
        act, slope = gelu_pair(pre + bias_ref[0:1, c * step : (c + 1) * step])
        act_ref[:, at] = act.astype(BF16)
        slope_ref[:, at] = slope.astype(BF16)
    xt_ref[...] = x_ref[...].T


def feed_up(x0, x1, pieces, bias):
    rows, deep = x0.shape
    units = bias.shape[1]
    out = [shape((deep, 2 * rows), BF16), shape((deep, units), BF16)]
    out += [shape((2 * rows, units // 2), BF16)] * 4
    scratch = [pltpu.VMEM((2 * rows, deep), BF16)]
    return call_whole(up_kernel, "feed_up", out, [x0, x1, *pieces], [bias], scratch, 10)


def down_kernel(spots, *refs):
    count = len(spots)
    own, sib, refs = refs[:count], refs[count : 2 * count], refs[2 * count :]
    act_own, act_sib, w_ref, near_ref, far_ref, sems = refs
    deep = near_ref.shape[1]
    units = act_own.shape[1]
    pairs = []
    rows = ring_rows(deep // own[0].shape[0], deep)
    for (piece, start), left, right in zip(spots, own, sib):
        width = left.shape[1]
        pairs.append((left, w_ref.at[rows[piece], start : start + width]))
        pairs.append((right, w_ref.at[rows[piece], units + start : units + start + width]))
    for copy in start_all(pairs, sems):
        copy.wait()
    for c in range(4):
        at = slice(c * deep // 4, (c + 1) * deep // 4)
        out = dot(act_own[...], w_ref[at, :units], NT) + dot(act_sib[...], w_ref[at, units:], NT)
        split_store(out, near_ref, far_ref, at)


def feed_down(act_own, act_sib, spots, own, sib):
    pair, units = act_own.shape
    deep = D
    out = [
        shape((deep, 2 * units), BF16),
        shape((pair // 2, deep), F32),
        shape((pair // 2, deep), BF16),
    ]
    kernel = functools.partial(down_kernel, spots)
    args = [*own, *sib]
    return call_whole(
        kernel, "feed_down", out, args, [act_own, act_sib], copies=2 * len(own)
    )


def feed_back_kernel(
    g0, g1, slope_own, slope_sib, up_ref, down_ref,
    gt_ref, gup_own, gup_sib, bias_ref, near_ref, far_ref, g_ref,
):
    rows, deep = g0.shape
    g_ref[:rows, :] = g0[...]
    g_ref[rows:, :] = g1[...]
    units = gup_own.shape[1]
    step = units // 2
    for c in range(4):
        slope_ref, gup_ref = ((slope_own, gup_own), (slope_sib, gup_sib))[c // 2]
        at = slice((c % 2) * step, (c % 2 + 1) * step)
        grad = dot(g_ref[...], down_ref[:, c * step : (c + 1) * step])
        grad = (grad * slope_ref[:, at].astype(F32)).astype(BF16)
        gup_ref[:, at] = grad
        bias_ref[0:1, c * step : (c + 1) * step] = jnp.sum(
            grad.astype(F32), axis=0, keepdims=True
        )
    for c in range(4):
        at = slice(c * deep // 4, (c + 1) * deep // 4)
        out = dot(gup_own[...], up_ref[at, :units], NT) + dot(gup_sib[...], up_ref[at, units:], NT)
        split_store(out, near_ref, far_ref, at)
    gt_ref[...] = g_ref[...].T


def feed_back(g0, g1, slope_own, slope_sib, up_all, down_all):
    rows, deep = g0.shape
    units = slope_own.shape[1]
    out = [shape((deep, 2 * rows), BF16)]
    out += [shape((2 * rows, units), BF16)] * 2
    out += [shape((1, 2 * units), F32), shape((rows, deep), F32), shape((rows, deep), BF16)]
    args = [g0, g1, slope_own, slope_sib, up_all, down_all]
    scratch = [pltpu.VMEM((2 * rows, deep), BF16)]
    return call_whole(feed_back_kernel, "feed_back", out, [], args, scratch)


def row_mean(values):
    return jnp.mean(values, axis=-1, keepdims=True)


def col_sum(values):
    return jnp.sum(values, axis=0, keepdims=True)


def normalize(values):
    centered = values - row_mean(values)
    inverse = lax.rsqrt(row_mean(centered * centered) + NORM_EPSILON)
    return centered * inverse, inverse


def norm_back(grad_out, normed, inverse, gain):
    grad = grad_out * gain
    return inverse * (grad - row_mean(grad) - normed * row_mean(grad * normed))


def norm_one_kernel(own, part, recv, vec, first_ref, low_ref, normed_ref, inverse_ref):
    attn_out = part[...] + recv[...].astype(F32) + vec[4:5, :]
    normed, inverse = normalize(own[...].astype(F32) + attn_out)
    first = normed * vec[0:1, :] + vec[1:2, :]
    first_ref[...] = first
    low_ref[...] = first.astype(BF16)
    normed_ref[...] = normed
    inverse_ref[...] = inverse


def norm_one(own, part, recv, vec):
    rows, deep = own.shape
    out = [shape((rows, deep), t) for t in (F32, BF16, F32)] + [shape((rows, 1), F32)]
    return call_whole(norm_one_kernel, "norm_one", out, [], [own, part, recv, vec])


def norm_two_kernel(first, part, recv, cotangent, vec, out_ref, grad_ref, low_ref, sums_ref):
    down_out = part[...] + recv[...].astype(F32) + vec[5:6, :]
    normed, inverse = normalize(first[...] + down_out)
    out_ref[...] = (normed * vec[2:3, :] + vec[3:4, :]).astype(BF16)
    given = cotangent[...].astype(F32)
    grad = norm_back(given, normed, inverse, vec[2:3, :])
    grad_ref[...] = grad
    low = grad.astype(BF16)
    low_ref[...] = low
    sums_ref[0:1, :] = col_sum(given * normed)
    sums_ref[1:2, :] = col_sum(given)
    sums_ref[2:3, :] = col_sum(low.astype(F32))


def norm_two(first, part, recv, cotangent, vec):
    rows, deep = first.shape
    out = [shape((rows, deep), t) for t in (BF16, F32, BF16)] + [shape((3, deep), F32)]
    return call_whole(norm_two_kernel, "norm_two", out, [], [first, part, recv, cotangent, vec])


def norm_one_back_kernel(
    grad_second, part, recv, normed, inverse, vec, grad_ref, low_ref, sums_ref
):
    given = grad_second[...] + part[...] + recv[...].astype(F32)
    grad = norm_back(given, normed[...], inverse[...], vec[0:1, :])
    grad_ref[...] = grad
    low = grad.astype(BF16)
    low_ref[...] = low
    sums_ref[0:1, :] = col_sum(given * normed[...])
    sums_ref[1:2, :] = col_sum(given)
    sums_ref[2:3, :] = col_sum(low.astype(F32))


def norm_one_back(grad_second, part, recv, normed, inverse, vec):
    rows, deep = part.shape
    out = [shape((rows, deep), t) for t in (F32, BF16)] + [shape((3, deep), F32)]
    args = [grad_second, part, recv, normed, inverse, vec]
    return call_whole(norm_one_back_kernel, "norm_one_back", out, [], args)


def nesterov(weights, momentum, average, gradient, step_rate):
    momentum_new = MOMENTUM * momentum + gradient
    weight_new = weights - step_rate * (gradient + MOMENTUM * momentum_new)
    return (weight_new, momentum_new, AVERAGE * average + (1.0 - AVERAGE) * weight_new)


def swap_tp(values, bit):
    size = lax.axis_size("tp")
    return lax.ppermute(values, "tp", [(i, i ^ bit) for i in range(size)])


def core(values):
    return swap_tp(values, 1)


def across(values):
    return swap_tp(values, 2)


def swap_ctx(values):
    return lax.ppermute(values, "ctx", [(0, 1), (1, 0)])


def swap_both(values):
    size = lax.axis_size("tp")
    return lax.ppermute(values, ("ctx", "tp"), [(i, i ^ (size + 2)) for i in range(2 * size)])


def sum_fsdp(values):
    size = lax.axis_size("fsdp")

    def swap(values, bit):
        return lax.ppermute(values, "fsdp", [(i, i ^ bit) for i in range(size)])

    if size == 4:
        one, two, three = (swap(values, bit) for bit in (1, 2, 3))
        return (values + one) + (two + three)
    bit = 1
    while bit < size:
        values = values + swap(values, bit)
        bit *= 2
    return values


def gather_fsdp(shard, axis):
    return lax.all_gather(shard, "fsdp", axis=axis, tiled=True)


def ring():
    return lax.axis_size("fsdp") == 4


def shift_fsdp(values, step):
    size = lax.axis_size("fsdp")
    return lax.ppermute(values, "fsdp", [(i, (i + step) % size) for i in range(size)])


def gather_pieces(shard, axis):
    if not ring():
        return [gather_fsdp(shard, axis)]
    return [shard] + [shift_fsdp(shard, -s) for s in range(1, lax.axis_size("fsdp"))]


def scatter_fsdp(grads, axis):
    return lax.psum_scatter(grads, "fsdp", scatter_dimension=axis, tiled=True)


def halves(values, axis=-1):
    low, high = jnp.split(values, 2, axis=axis)
    first = lax.axis_index("ctx") == 0
    return jnp.where(first, low, high), jnp.where(first, high, low)


def join(mine, other, axis=-1):
    first = lax.axis_index("ctx") == 0
    low, high = jnp.where(first, mine, other), jnp.where(first, other, mine)
    return jnp.concatenate([low, high], axis=axis)


def quarters(mine):
    return jnp.stack(jnp.split(mine, 2, axis=1))


def after(values, *others):
    return lax.optimization_barrier((values,) + others)[0]


def on_device(
    tokens,
    cotangent,
    attn_weight,
    attn_momentum,
    attn_average,
    ffn_weight,
    ffn_momentum,
    ffn_average,
    vector_weight,
    vector_momentum,
    vector_average,
):
    tp_rank = lax.axis_index("tp")
    sib_rank = tp_rank ^ 1
    head_width = attn_weight.shape[2]
    unit_width = ffn_weight.shape[2]
    token_count = LEN * lax.axis_size("fsdp")
    matrix_rate = MATRIX_RATE / math.sqrt(token_count)
    vector_rate = VECTOR_RATE / math.sqrt(token_count)

    attn_low, attn_high = halves(attn_weight.astype(BF16))
    qkv_mine = gather_pieces(attn_low[:3], 1)

    own = tokens[0]
    rows = own.shape[0]
    pair = 2 * rows
    half = 4 * rows
    beside = across(own)
    facing = swap_ctx(own)
    diagonal = swap_both(own)
    if ring():
        others = swap_ctx(after(jnp.stack(qkv_mine[1:]), beside, facing))
        qkv_other = [attn_high[:3]] + [others[s] for s in range(len(qkv_mine) - 1)]
    else:
        qkv_other = [swap_ctx(qkv_mine[0])]
    up_low = quarters(halves(ffn_weight[0].astype(BF16))[0])
    out_low = jnp.concatenate([attn_low[3], attn_high[3]], axis=1)
    out_up_low = jnp.concatenate([out_low[None], up_low])
    out_up = gather_fsdp(after(out_up_low, *qkv_mine[-3:], beside, facing), 1)
    blocks = [own, beside, core(own), core(beside), facing, diagonal, core(facing), core(diagonal)]

    vec = vector_weight[: 6 * D].reshape(6, D)

    def columns(start, width):
        part = lax.dynamic_slice_in_dim(vector_weight, start, width)
        return jnp.concatenate(halves(part))

    biases = jnp.stack(
        [
            columns(6 * D + tp_rank * head_width, head_width),
            columns(7 * D + tp_rank * head_width, head_width),
        ]
    )
    bias_hidden = jnp.concatenate(
        [
            columns(8 * D + tp_rank * unit_width, unit_width),
            columns(8 * D + sib_rank * unit_width, unit_width),
        ]
    )[None]

    token_t, qkv_w, queries, keys, values = project(blocks, qkv_mine, qkv_other, biases)
    down_low = jnp.concatenate(halves(ffn_weight[1].astype(BF16)), axis=1)
    mixed_own, mixed_sib, lse = attend(queries, keys, values)
    down_low = after(down_low, mixed_own)
    if ring():
        low, high = jnp.split(down_low, 2, axis=1)
        spots = ((0, 0), (1, 0), (3, 0), (2, 0), (2, low.shape[1]))
        down_w = [down_low, shift_fsdp(down_low, -1), shift_fsdp(down_low, -3)]
        down_w += [shift_fsdp(low, -2), shift_fsdp(high, -2)]
    else:
        spots = ((0, 0),)
        down_w = [gather_fsdp(down_low, 0)]
    mixed_recv = core(mixed_sib)
    out_up = after(out_up, mixed_own)
    out_up_sib = core(out_up)
    up_other = swap_ctx(out_up[1:])
    out_w, attn_part, attn_far = out_project(mixed_own, mixed_recv, [out_up, out_up_sib])
    attn_recv = across(attn_far)
    if ring():
        attn_recv = after(attn_recv, down_w[1], down_w[2])
    first, first_low, normed_one, inverse_one = norm_one(own, attn_part, attn_recv, vec)
    first_beside = across(first_low)

    if ring():
        first_beside = after(first_beside, down_w[3])
    up_other = after(up_other, first_beside)
    first_t, up_all, hidden_own, hidden_sib, slope_own, slope_sib = feed_up(
        first_low, first_beside, [out_up, up_other, out_up_sib, core(up_other)], bias_hidden
    )
    if ring():
        down_w[4] = after(down_w[4], hidden_own)
    down_all, down_part, down_far = feed_down(
        hidden_own, hidden_sib, spots, down_w, [core(w) for w in down_w]
    )
    layer_out, grad_second, grad_down, sums_two = norm_two(
        first, down_part, across(down_far), cotangent[0], vec
    )
    grad_down_t, grad_up_own, grad_up_sib, grad_bias_hidden, first_part, first_far = feed_back(
        grad_down, across(grad_down), slope_own, slope_sib, up_all, down_all
    )
    down_sib = grad_send(grad_down_t, hidden_sib)
    up_sib = grad_send(first_t, grad_up_sib)
    first_recv = after(across(first_far), down_sib, up_sib)
    grad_res, grad_attn, sums_one = norm_one_back(
        grad_second, first_part, first_recv, normed_one, inverse_one, vec
    )
    grad_attn_beside = across(grad_attn)
    down_mine, down_rest = grad_sum(grad_down_t, hidden_own, after(core(down_sib), grad_attn))
    up_keep, up_send = grad_sum(first_t, grad_up_own, after(core(up_sib), grad_attn))

    def finish(mine):
        return join(mine, swap_ctx(mine)).astype(F32)

    mine_owned = scatter_fsdp(down_mine, 0)
    rest_owned = scatter_fsdp(down_rest, 0)
    up_recv = swap_ctx(up_send)

    grad_attn_beside = after(grad_attn_beside, down_mine, up_send)
    grad_attn_t, grad_mixed_own, grad_mixed_sib = out_back(grad_attn, grad_attn_beside, out_w)
    grad_mixed = (grad_mixed_own, core(grad_mixed_sib))

    up_recv = after(up_recv, grad_mixed_sib)
    up_sum = (up_keep.astype(F32) + up_recv.astype(F32)).astype(BF16)
    up_owned = scatter_fsdp(up_sum, 0)
    mixed = (mixed_own, mixed_sib)
    heads = (queries, keys, values, mixed)
    query_other, kv_other = attend_back(*heads, grad_mixed, lse, 1)
    send = head_send(token_t, query_other, kv_other)
    out_sib = grad_send(after(grad_attn_t, query_other), mixed_recv)
    out_keep, out_send = grad_sum(grad_attn_t, mixed_own, core(out_sib))
    grad_mixed = (grad_mixed[0], after(grad_mixed[1], up_sum, send, out_send, mine_owned))
    recv = swap_ctx(send)
    query_mine, kv_mine = attend_back(*heads, grad_mixed, lse, 0)
    part = head_width // 2
    near, far, sibling = input_back(
        query_mine, query_other, kv_mine, kv_other, qkv_w, sums_one, sums_two, grad_bias_hidden
    )
    sib_recv = core(sibling)
    qkvo_sum = head_sum(token_t, query_mine, after(kv_mine, rest_owned), recv, out_keep, swap_ctx(out_send))
    qkvo_mine = scatter_fsdp(qkvo_sum, 0)
    mine_recv, rest_recv = swap_ctx(mine_owned), swap_ctx(rest_owned)
    sib_recv = after(sib_recv, qkvo_sum, up_owned, mine_recv, rest_recv)
    input_part, to_x, to_y, to_d, vec_part = fold(near, far, sibling, sib_recv, grad_res)
    from_x, from_y, from_d = across(to_x), swap_ctx(to_y), swap_both(to_d)
    down_grad = join(
        mine_owned.astype(F32) + rest_recv.astype(F32),
        rest_owned.astype(F32) + mine_recv.astype(F32),
    )
    up_grad = finish(after(up_owned, to_y))
    ffn_grad = jnp.stack([up_grad, down_grad])
    ffn_new, ffn_momentum_new, ffn_average_new = nesterov(
        ffn_weight, ffn_momentum, ffn_average, ffn_grad, matrix_rate
    )
    input_grad = input_part
    for term in (from_x, from_y, from_d):
        input_grad = input_grad + term[:rows].astype(F32)
    vec_x, vec_y, vec_d = (term[rows:].astype(F32) for term in (from_x, from_y, from_d))
    vec_plane = (vec_part.astype(F32) + vec_x) + (vec_y + vec_d)

    qkvo_mine = after(qkvo_mine, from_x)
    qkvo_other = swap_ctx(qkvo_mine)
    vector_grad = sum_fsdp(vec_plane[:12]).reshape(-1)
    attn_grad = jnp.stack(
        [
            join(qkvo_mine[:, j * part : (j + 1) * part], qkvo_other[:, j * part : (j + 1) * part])
            for j in range(4)
        ]
    ).astype(F32)
    vector_new, vector_momentum_new, vector_average_new = nesterov(
        vector_weight, vector_momentum, vector_average, vector_grad, vector_rate
    )
    attn_new, attn_momentum_new, attn_average_new = nesterov(
        attn_weight, attn_momentum, attn_average, attn_grad, matrix_rate
    )
    return (
        layer_out[None],
        input_grad[None],
        attn_grad,
        attn_new,
        attn_momentum_new,
        attn_average_new,
        attn_new.astype(BF16),
        ffn_grad,
        ffn_new,
        ffn_momentum_new,
        ffn_average_new,
        ffn_new.astype(BF16),
        vector_grad,
        vector_new,
        vector_momentum_new,
        vector_average_new,
    )


def solution(mesh):
    rows = P("fsdp", ("ctx", "tp"), None)
    weight = P(None, "fsdp", "tp")
    return jax.shard_map(
        on_device,
        mesh=mesh,
        in_specs=(rows, rows) + (weight,) * 6 + (P(),) * 3,
        out_specs=(rows, rows) + (weight,) * 10 + (P(),) * 4,
        check_vma=False,
    )
```
